32 devices in a mesh: fsdp: 16 (over z, y, x), seq: 2 (over core).
Axes of the slice: x: 2, y: 2, z: 4, core: 2. Of those that a mesh axis runs over, the one named last changes fastest.
Arguments:
- latent: bfloat16 [32, 256, 1408], P('fsdp', 'seq'), may hold values from -6 to 6
- skip_input: bfloat16 [32, 256, 1408], P('fsdp', 'seq'), may hold values from -6 to 6
- condition: bfloat16 [32, 1408], P('fsdp'), may hold values from -6 to 6
- text_encoder_states: bfloat16 [32, 256, 1024], P('fsdp'), may hold values from -6 to 6
- text_lengths: int32 [32], P('fsdp'), may hold values from 64 to 256, as said below
- out_grad: bfloat16 [32, 256, 1408], P('fsdp', 'seq'), may hold values from -6 to 6
- skip_gain: bfloat16 [2816], P('fsdp'), may hold values from 0.099609375 to 1.8984375
- norm_gains: bfloat16 [3, 1408], P(None, 'fsdp'), may hold values from 0.099609375 to 1.8984375
- skip_linear: bfloat16 [2816, 1408], P('fsdp'), may hold values from -0.109375 to 0.109375
- shift_linear: bfloat16 [1408, 1408], P('fsdp'), may hold values from -0.15625 to 0.15625
- self_qkv: bfloat16 [1408, 4224], P('fsdp'), may hold values from -0.15625 to 0.15625
- self_out: bfloat16 [1408, 1408], P('fsdp'), may hold values from -1.25 to 1.25
- cross_query: bfloat16 [1408, 1408], P('fsdp'), may hold values from -0.15625 to 0.15625
- cross_keyval: bfloat16 [1024, 2816], P('fsdp'), may hold values from -0.1875 to 0.1875
- cross_out: bfloat16 [1408, 1408], P('fsdp'), may hold values from -1.25 to 1.25
- mlp_up: bfloat16 [1408, 6144], P('fsdp'), may hold values from -0.15625 to 0.15625
- mlp_down: bfloat16 [6144, 1408], P('fsdp'), may hold values from -0.078125 to 0.078125
- thresholds: float32 [2, 16], replicated, may hold values from 1 to 3
Outputs:
- block_out: bfloat16 [32, 256, 1408], P('fsdp', 'seq')
- grad_latent: float32 [32, 256, 1408], P('fsdp', 'seq')
- grad_skip: float32 [32, 256, 1408], P('fsdp', 'seq')
- grad_condition: float32 [32, 1408], P('fsdp')
- grad_text: float32 [32, 256, 1024], P('fsdp', 'seq')
- grad_skip_gain: float32 [2816], P('fsdp')
- grad_norm_gains: float32 [3, 1408], P(None, 'fsdp')
- grad_skip_linear: float32 [2816, 1408], P('fsdp')
- grad_shift_linear: float32 [1408, 1408], P('fsdp')
- grad_self_qkv: float32 [1408, 4224], P('fsdp')
- grad_self_out: float32 [1408, 1408], P('fsdp')
- grad_cross_query: float32 [1408, 1408], P('fsdp')
- grad_cross_keyval: float32 [1024, 2816], P('fsdp')
- grad_cross_out: float32 [1408, 1408], P('fsdp')
- grad_mlp_up: float32 [1408, 6144], P('fsdp')
- grad_mlp_down: float32 [6144, 1408], P('fsdp')
- clipped_qkv: bfloat16 [1408, 4224], P('fsdp')
- clipped_query: bfloat16 [1408, 1408], P('fsdp')
- clipped_keyval: bfloat16 [1024, 2816], P('fsdp')
- logit_peaks: float32 [2, 16], replicated
The draws below stay inside these ranges and needn't reach their ends.
Inputs may be any that keep to these rules, and one draw needn't show every extreme that they name: `text_lengths`: number of real text tokens of each sample, the rest padding; some sample has all 256.
All inputs are finite; a program needn't handle non-finite values.
Results may differ from the reference program's by a relative error of at most 0.019.
Values may be sent and summed in bfloat16 or wider, within the bound.
A program may use at most 384 MiB of HBM per device.

```python
import math
import jax
import jax.numpy as jnp
from jax import lax

D = 1408
HEADS = 16
HD = 88
FF = 6144
TD = 1024
TXT = 256
GRID_W = 32
LEN = 256
SAMPLES = 32


def draw_text_lengths(key, part):
    key = jax.random.fold_in(key, 7)
    first_key, second_key = jax.random.split(key)
    drawn = jax.random.randint(first_key, (SAMPLES,), TXT // 4, TXT + 1)
    full_at = jax.random.randint(second_key, (), 0, SAMPLES)
    return jnp.where(jnp.arange(SAMPLES) == full_at, TXT, drawn).astype(jnp.int32)


def levels(key, extent, shards, least, top_value):
    level = 1.0
    for axis_at, blocks in shards:
        steps = jax.random.uniform(jax.random.fold_in(jax.random.fold_in(key, 6), axis_at), (blocks,), jnp.float32, least / len(shards), top_value / len(shards))
        level = level * jnp.repeat(jnp.exp(steps), extent[axis_at] // blocks).reshape((-1,) + (1,) * (len(extent) - 1 - axis_at))
    return level


def bell_draw(key, dims, deviation, limit, cuts=(), held_as=jnp.bfloat16):
    gain = levels(key, dims, cuts, -0.22, 0.18) if cuts else 1.0
    values = jax.random.normal(key, dims, jnp.float32) * deviation * gain
    return jnp.minimum(jnp.maximum(values, -limit), limit).astype(held_as)


def setup_inputs(seed: int = 0) -> dict:
    streams_of = jax.random.split(jax.random.key(seed), 19)
    latent = bell_draw(streams_of[0], (SAMPLES, LEN, D), 1.0, 6.0, ((0, 16), (1, 2)))
    skip_input = bell_draw(streams_of[1], (SAMPLES, LEN, D), 1.0, 6.0, ((0, 16), (1, 2)))
    condition = bell_draw(streams_of[2], (SAMPLES, D), 1.0, 6.0, ((0, 16),))
    text_encoder_states = bell_draw(streams_of[3], (SAMPLES, TXT, TD), 1.0, 6.0, ((0, 16),))
    text_lengths = draw_text_lengths(jax.random.fold_in(streams_of[18], 71), 0)
    out_grad = bell_draw(streams_of[5], (SAMPLES, LEN, D), 1.0, 6.0, ((0, 16), (1, 2)))
    skip_gain = jnp.clip(1.0 + 0.18 * jax.random.normal(streams_of[6], (2 * D,), jnp.float32), 0.099609375, 1.8984375).astype(jnp.bfloat16)
    norm_gains = jnp.clip(1.0 + 0.18 * jax.random.normal(streams_of[7], (3, D), jnp.float32), 0.099609375, 1.8984375).astype(jnp.bfloat16)
    skip_linear = bell_draw(streams_of[8], (2 * D, D), (2 * D) ** -0.5, 0.109375, ((0, 16),))
    shift_linear = bell_draw(streams_of[9], (D, D), D ** -0.5, 0.15625, ((0, 16),))
    self_qkv = bell_draw(streams_of[10], (D, 3 * D), D ** -0.5, 0.15625, ((0, 16),))
    self_out = bell_draw(streams_of[11], (D, D), (max(1, D * 4 // LEN)) ** -0.5, 1.25, ((0, 16),))
    cross_query = bell_draw(streams_of[12], (D, D), D ** -0.5, 0.15625, ((0, 16),))
    cross_keyval = bell_draw(streams_of[13], (TD, 2 * D), TD ** -0.5, 0.1875, ((0, 16),))
    cross_out = bell_draw(streams_of[14], (D, D), (max(1, D * 4 // TXT)) ** -0.5, 1.25, ((0, 16),))
    mlp_up = bell_draw(streams_of[15], (D, FF), D ** -0.5, 0.15625, ((0, 16),))
    mlp_down = bell_draw(streams_of[16], (FF, D), FF ** -0.5, 0.078125, ((0, 16),))
    thresholds = jnp.clip(jnp.exp(jax.random.uniform(streams_of[17], (2, HEADS), jnp.float32, math.log(1.0), math.log(3.0))), 1.0, 3.0)
    return dict(latent=latent, skip_input=skip_input, condition=condition, text_encoder_states=text_encoder_states, text_lengths=text_lengths, out_grad=out_grad, skip_gain=skip_gain, norm_gains=norm_gains, skip_linear=skip_linear, shift_linear=shift_linear, self_qkv=self_qkv, self_out=self_out, cross_query=cross_query, cross_keyval=cross_keyval, cross_out=cross_out, mlp_up=mlp_up, mlp_down=mlp_down, thresholds=thresholds)


@jax.custom_vjp
def low(v):
    return lax.optimization_barrier(v.astype(jnp.bfloat16)).astype(jnp.float32)

@jax.custom_vjp
def low_back(v):
    return v

def low_keep(v):
    return (low(v), None)

def low_pass(kept, grad):
    return (grad,)

def back_keep(v):
    return (v, None)

def back_low(kept, grad):
    return (low(grad),)
low.defvjp(low_keep, low_pass)
low_back.defvjp(back_keep, back_low)
norm_eps = 1e-06
masked_value = -1e+30
highest = lax.Precision.HIGHEST

def to_float(array):
    return array.astype(jnp.float32)

def matmul_high(left, right):
    return jnp.dot(left, right, precision=highest, preferred_element_type=jnp.float32)

def layer_norm(values):
    center = values - lax.optimization_barrier(jnp.mean(values, axis=-1, keepdims=True))
    spread = lax.optimization_barrier(jnp.mean(center * center, axis=-1, keepdims=True))
    return center * lax.rsqrt(spread + norm_eps)

def rotary_tables(row_pos, col_pos, head_dim):
    quarter = head_dim // 4
    freqs = 10000.0 ** (-jnp.arange(quarter, dtype=jnp.float32) / quarter)
    row_angle = row_pos.astype(jnp.float32)[:, None] * freqs[None, :]
    col_angle = col_pos.astype(jnp.float32)[:, None] * freqs[None, :]
    angles = jnp.stack([row_angle, col_angle], axis=1)
    return (jnp.cos(angles), jnp.sin(angles))

def rotate(values, cosine_table, sine_table):
    tokens, heads, head_dim = values.shape
    quarter = head_dim // 4
    pieces = values.reshape(tokens, heads, 2, 2, quarter)
    former = pieces[:, :, :, 0, :]
    latter = pieces[:, :, :, 1, :]
    cos_wide = cosine_table[:, None, :, :]
    sin_wide = sine_table[:, None, :, :]
    turned = jnp.stack([former * cos_wide - latter * sin_wide, latter * cos_wide + former * sin_wide], axis=3)
    return turned.reshape(tokens, heads, head_dim)

def diffusion_transformer_block(block_parameters, latent, skip_input, condition, text_encoder_states, text_valid_mask, cosine_table, sine_table):
    skip_gain, norm_gains, skip_linear, shift_linear, self_qkv, self_out, cross_query, cross_keyval, cross_out, mlp_up, mlp_down = block_parameters
    length = latent.shape[0]
    text_rows = text_encoder_states.shape[0]
    scaling = HD ** (-0.5)
    joined = jnp.concatenate([latent, skip_input], axis=1)
    normed = low(layer_norm(joined) * skip_gain)
    hidden = low_back(matmul_high(normed, skip_linear))
    shift = low_back(matmul_high(low(jax.nn.silu(condition))[None, :], shift_linear))
    attn_in = low(layer_norm(hidden) * norm_gains[0] + shift)
    qkv_proj = low_back(matmul_high(attn_in, self_qkv)).reshape(length, 3, HEADS, HD)
    queries = low(rotate(layer_norm(qkv_proj[:, 0]), cosine_table, sine_table))
    keys_all = low(rotate(layer_norm(qkv_proj[:, 1]), cosine_table, sine_table))
    values_all = low(qkv_proj[:, 2])
    scores = low_back(jnp.einsum('qhd,khd->hqk', queries, keys_all, precision=highest) * scaling)
    self_peak = lax.optimization_barrier(jnp.max(scores, axis=(1, 2)))
    probs = jax.nn.softmax(scores, axis=-1)
    mixed = low_back(jnp.einsum('hqk,khd->qhd', low(probs), values_all, precision=highest))
    attn_cat = low(mixed.reshape(length, HEADS * HD))
    after_self = hidden + low_back(matmul_high(attn_cat, self_out))
    cross_in = low(layer_norm(after_self) * norm_gains[1])
    cq_proj = low_back(matmul_high(cross_in, cross_query)).reshape(length, HEADS, HD)
    cross_queries = low(layer_norm(cq_proj))
    ckv_proj = low_back(matmul_high(text_encoder_states, cross_keyval)).reshape(text_rows, 2, HEADS, HD)
    cross_keys = low(layer_norm(ckv_proj[:, 0]))
    cross_values = low(ckv_proj[:, 1])
    raw_cross = low_back(jnp.einsum('qhd,khd->hqk', cross_queries, cross_keys, precision=highest) * scaling)
    cross_scores = jnp.where(text_valid_mask[None, None, :], raw_cross, masked_value)
    cross_peak = lax.optimization_barrier(jnp.max(cross_scores, axis=(1, 2)))
    cross_probs = jax.nn.softmax(cross_scores, axis=-1)
    cross_mixed = low_back(jnp.einsum('hqk,khd->qhd', low(cross_probs), cross_values, precision=highest))
    cross_cat = low(cross_mixed.reshape(length, HEADS * HD))
    after_cross = after_self + low_back(matmul_high(cross_cat, cross_out))
    mlp_in = low(layer_norm(after_cross) * norm_gains[2])
    upper = low_back(matmul_high(mlp_in, mlp_up))
    activated = low(jax.nn.gelu(upper, approximate=True))
    result = after_cross + low_back(matmul_high(activated, mlp_down))
    return (result, jnp.stack([self_peak, cross_peak]))

def reference(latent, skip_input, condition, text_encoder_states, text_lengths, out_grad, skip_gain, norm_gains, skip_linear, shift_linear, self_qkv, self_out, cross_query, cross_keyval, cross_out, mlp_up, mlp_down, thresholds):
    block_parameters = tuple((to_float(weight) for weight in (skip_gain, norm_gains, skip_linear, shift_linear, self_qkv, self_out, cross_query, cross_keyval, cross_out, mlp_up, mlp_down)))
    positions = jnp.arange(LEN)
    cosine_table, sine_table = rotary_tables(positions // GRID_W, positions % GRID_W, HD)

    def one_sample(carry, item):
        running, peaks = carry
        lat_rows, skip_rows, cond_row, text_rows, text_count, cot_rows = item
        text_valid_mask = jnp.arange(TXT) < text_count

        def forward(block_weights, latent_input, skip_tokens_local, condition_input, text_input):
            return diffusion_transformer_block(block_weights, latent_input, skip_tokens_local, condition_input, text_input, text_valid_mask, cosine_table, sine_table)
        result, pull, maxima = jax.vjp(forward, block_parameters, to_float(lat_rows), to_float(skip_rows), to_float(cond_row), to_float(text_rows), has_aux=True)
        grads = pull(to_float(cot_rows))
        running = jax.tree.map(jnp.add, running, grads[0])
        peaks = jnp.maximum(peaks, maxima)
        return ((running, peaks), (result.astype(jnp.bfloat16), grads[1], grads[2], grads[3], grads[4]))
    start_grads = jax.tree.map(jnp.zeros_like, block_parameters)
    start_peaks = jnp.full((2, HEADS), masked_value, jnp.float32)
    (running, peaks), stacked = lax.scan(one_sample, (start_grads, start_peaks), (latent, skip_input, condition, text_encoder_states, text_lengths, out_grad))
    block_out, lat_grad, skip_grad, cond_grad, text_grad = stacked
    factors = thresholds / jnp.maximum(peaks, thresholds)
    roots = jnp.sqrt(factors)
    self_cols = jnp.repeat(roots[0], HD)
    cross_cols = jnp.repeat(roots[1], HD)
    unit_cols = jnp.ones((D,), jnp.float32)
    clipped_qkv = (to_float(self_qkv) * jnp.concatenate([self_cols, self_cols, unit_cols])[None, :]).astype(jnp.bfloat16)
    clipped_query = (to_float(cross_query) * cross_cols[None, :]).astype(jnp.bfloat16)
    clipped_keyval = (to_float(cross_keyval) * jnp.concatenate([cross_cols, unit_cols])[None, :]).astype(jnp.bfloat16)
    return (block_out, lat_grad, skip_grad, cond_grad, text_grad, running[0], running[1], running[2], running[3], running[4], running[5], running[6], running[7], running[8], running[9], running[10], clipped_qkv, clipped_query, clipped_keyval, peaks)
```

```python
import jax
import jax.numpy as jnp
from jax import lax
from jax.sharding import PartitionSpec as P

HEADS = 16
HD = 88
GRID_W = 32

norm_eps = 1e-06
masked_value = -1e30
bf16 = jnp.bfloat16
f32 = jnp.float32


def layer_norm(values):
    center = values - jnp.mean(values, axis=-1, keepdims=True)
    spread = jnp.mean(center * center, axis=-1, keepdims=True)
    return center * lax.rsqrt(spread + norm_eps)


def rotary_tables(row_pos, col_pos, head_dim):
    quarter = head_dim // 4
    freqs = 10000.0 ** (-jnp.arange(quarter, dtype=f32) / quarter)
    row_angle = row_pos.astype(f32)[:, None] * freqs[None, :]
    col_angle = col_pos.astype(f32)[:, None] * freqs[None, :]
    angles = jnp.stack([row_angle, col_angle], axis=1)
    return (jnp.cos(angles), jnp.sin(angles))


def rotate(values, cosine_table, sine_table):
    rows, tokens, heads, head_dim = values.shape
    quarter = head_dim // 4
    pieces = values.reshape(rows, tokens, heads, 2, 2, quarter)
    former = pieces[..., 0, :]
    latter = pieces[..., 1, :]
    cos_wide = cosine_table[None, :, None, :, :]
    sin_wide = sine_table[None, :, None, :, :]
    turned = jnp.stack(
        [former * cos_wide - latter * sin_wide, latter * cos_wide + former * sin_wide], axis=4
    )
    return turned.reshape(rows, tokens, heads, head_dim)


def gained_norm(values, gain):
    return layer_norm(values) * gain


def gelu_tanh(values):
    return jax.nn.gelu(values, approximate=True)


def dot_plain(left, right):
    return jnp.dot(left, right, preferred_element_type=f32)


def dot_left_t(left, right):
    return lax.dot_general(
        left, right, (((0,), (0,)), ((), ())), preferred_element_type=f32
    )


def dot_right_t(left, right):
    return lax.dot_general(
        left, right, (((1,), (1,)), ((), ())), preferred_element_type=f32
    )


def softmax_back(probs, prob_grad):
    return probs * (prob_grad - jnp.sum(prob_grad * probs, axis=-1, keepdims=True))


class Links:
    def __init__(self, fsdp_count):
        self.count = fsdp_count
        self.inner = fsdp_count // 4
        self.bits = self.inner.bit_length() - 1
        self.low_count = self.inner
        self.me = lax.axis_index("fsdp")
        self.core = lax.axis_index("seq")

    def swap(self, value, mask_first, mask_second):
        pairs = []
        for index in range(self.count):
            pairs.append((2 * index, 2 * (index ^ mask_first)))
            pairs.append((2 * index + 1, 2 * (index ^ mask_second) + 1))
        return lax.ppermute(value, ("fsdp", "seq"), pairs)

    def sibling(self, value):
        return lax.ppermute(value, "seq", [(0, 1), (1, 0)])

    def pick(self, first, second):
        return jnp.where(self.core == 0, first, second)

    def reverse(self, index):
        out = 0
        for bit in range(self.bits):
            out |= ((index >> bit) & 1) << (self.bits - 1 - bit)
        return out

    def masks(self, step):
        return 1 << step, 1 << (self.bits - 1 - step)

    def offset(self, block):
        return (block % 4) * self.inner + block // 4

    def place(self, offset):
        return (offset % self.inner) * 4 + offset // self.inner

    def gather(self, shard):
        half = shard.shape[1] // 2
        mine = self.pick(shard[:, :half], shard[:, half:])
        stack = [mine]
        for k in range(1, 4):
            stack.append(self.swap(mine, k * self.inner, k * self.inner))
        blocks = [jnp.concatenate(stack, axis=0)]
        for step in range(self.bits):
            got = [self.swap(block, *self.masks(step)) for block in blocks]
            blocks = blocks + got
        ordered = []
        for index in range(self.low_count):
            back = self.reverse(index)
            ordered.append(
                blocks[index] if back == index else self.pick(blocks[index], blocks[back])
            )
        own = jnp.concatenate(ordered, axis=0)
        return own, self.sibling(own)

    def scatter(self, own, other):
        rows = own.shape[0]
        whole = (own.astype(f32) + self.sibling(other).astype(f32)).astype(bf16)
        size = rows // self.low_count
        cuts = [whole[index * size : (index + 1) * size] for index in range(self.low_count)]
        blocks = []
        for index in range(self.low_count):
            back = self.reverse(index)
            blocks.append(cuts[index] if back == index else self.pick(cuts[index], cuts[back]))
        for step in reversed(range(self.bits)):
            keep = blocks[: 1 << step]
            send = jnp.concatenate(blocks[1 << step :], axis=0)
            got = self.swap(send, *self.masks(step))
            blocks = [
                (block.astype(f32) + got[at * size : (at + 1) * size].astype(f32)).astype(bf16)
                for at, block in enumerate(keep)
            ]
        last = blocks[0]
        part = size // 4
        total = last[:part].astype(f32)
        for k in range(1, 4):
            got = self.swap(last[k * part : (k + 1) * part], k * self.inner, k * self.inner)
            total = total + got.astype(f32)
        return self.columns(total, self.sibling(total))

    def columns(self, own, other):
        return self.pick(
            jnp.concatenate([own, other], axis=-1), jnp.concatenate([other, own], axis=-1)
        )

    def halves(self, value):
        half = value.shape[-1] // 2
        first, second = value[..., :half], value[..., half:]
        return self.pick(first, second), self.pick(second, first)

    def order_matrix(self, size):
        block = size // self.count
        at = lax.broadcasted_iota(jnp.int32, (size, size), 0)
        to = lax.broadcasted_iota(jnp.int32, (size, size), 1)
        place = to // block
        source = jnp.bitwise_xor(self.me, (place % 4) * self.inner + place // 4)
        return (at == source * block + to % block).astype(bf16)

    def order_blocks(self, value):
        size = value.shape[1] // self.count
        parts = []
        for block in range(self.count):
            source = jnp.bitwise_xor(self.me, self.offset(block))
            parts.append(lax.dynamic_slice_in_dim(value, source * size, size, 1))
        return jnp.concatenate(parts, axis=1)

    def restore_blocks(self, value):
        size = value.shape[1] // self.count
        parts = []
        for shard in range(self.count):
            source = self.place(jnp.bitwise_xor(self.me, shard))
            parts.append(lax.dynamic_slice_in_dim(value, source * size, size, 1))
        return jnp.concatenate(parts, axis=1)

    def small_gather(self, value):
        for bit in range(self.count.bit_length() - 1):
            got = self.swap(value, 1 << bit, 1 << bit)
            upper = (self.me >> bit) & 1
            value = jnp.where(
                upper == 1,
                jnp.concatenate([got, value], axis=0),
                jnp.concatenate([value, got], axis=0),
            )
        return value

    def small_scatter(self, value):
        for bit in reversed(range(self.count.bit_length() - 1)):
            size = value.shape[0] // 2
            upper = (self.me >> bit) & 1
            keep = jnp.where(upper == 1, value[size:], value[:size])
            send = jnp.where(upper == 1, value[:size], value[size:])
            value = keep + self.swap(send, 1 << bit, 1 << bit)
        return value

    def largest(self, value):
        value = jnp.maximum(value, self.sibling(value))
        for bit in range(self.count.bit_length() - 1):
            value = jnp.maximum(value, self.swap(value, 1 << bit, 1 << bit))
        return value


def exact_restore(matrix, value):
    high = value.astype(bf16)
    low = (value - high.astype(f32)).astype(bf16)
    return dot_right_t(high, matrix) + dot_right_t(low, matrix)


def attend(queries, keys, scaling):
    return jnp.einsum("bqhd,bkhd->bhqk", queries, keys, preferred_element_type=f32) * scaling


def mix(probs, values):
    return jnp.einsum("bhqk,bkhd->bqhd", probs, values, preferred_element_type=f32)


def mix_back(probs, grads):
    return jnp.einsum("bhqk,bqhd->bkhd", probs, grads, preferred_element_type=f32)


def local(
    latent,
    skip_input,
    condition,
    text_encoder_states,
    text_lengths,
    out_grad,
    skip_gain,
    norm_gains,
    skip_linear,
    shift_linear,
    self_qkv,
    self_out,
    cross_query,
    cross_keyval,
    cross_out,
    mlp_up,
    mlp_down,
    thresholds,
):
    batch, tokens, width = latent.shape
    rows = batch * tokens
    text_rows = text_encoder_states.shape[1]
    text_width = text_encoder_states.shape[2]
    scaling = HD ** (-0.5)
    links = Links(lax.axis_size("fsdp"))
    me, core = links.me, links.core
    count = links.count

    positions = core * tokens + jnp.arange(tokens)
    cosine_table, sine_table = rotary_tables(positions // GRID_W, positions % GRID_W, HD)

    gain_rows = skip_gain.shape[0]
    third = norm_gains.shape[1]
    packed = links.small_gather(
        jnp.concatenate([skip_gain, norm_gains.reshape(-1)])[None, :]
    )
    skip_gain_all = packed[:, :gain_rows].reshape(-1).astype(f32)
    gains = (
        packed[:, gain_rows:].reshape(count, 3, third).transpose(1, 0, 2).reshape(3, width)
    ).astype(f32)
    cond_act = jax.nn.silu(condition.astype(f32)).astype(bf16)
    cond_all = links.small_gather(cond_act)
    shift_rows = shift_linear.shape[0]
    cond_cut = lax.dynamic_slice_in_dim(cond_all, me * shift_rows, shift_rows, 1)
    shift = links.small_scatter(dot_plain(cond_cut, shift_linear))

    w_skip = links.gather(skip_linear)
    w_qkv = links.gather(self_qkv)
    w_self_out = links.gather(self_out)
    w_query = links.gather(cross_query)
    w_keyval = links.gather(cross_keyval)
    w_cross_out = links.gather(cross_out)
    w_up = links.gather(mlp_up)
    w_down = links.gather(mlp_down)

    order = links.order_matrix(width)
    order_wide = links.order_matrix(2 * width)
    order_text = links.order_matrix(text_width)

    def product(value, weight):
        return links.columns(dot_plain(value, weight[0]), dot_plain(value, weight[1]))

    def product_back(grad_halves, weight):
        return dot_right_t(grad_halves[0], weight[0]) + dot_right_t(grad_halves[1], weight[1])

    def weight_grad(value, grad_halves):
        return links.scatter(
            dot_left_t(value, grad_halves[0]).astype(bf16),
            dot_left_t(value, grad_halves[1]).astype(bf16),
        )

    def reorder(value):
        return dot_plain(value, order).astype(bf16)

    def restore(value):
        return dot_right_t(value.astype(bf16), order).astype(bf16)

    def heads_of(value):
        return value.reshape(batch, -1, HEADS, HD)

    joined = jnp.concatenate(
        [latent.reshape(rows, width), skip_input.reshape(rows, width)], axis=1
    ).astype(f32)
    normed = gained_norm(joined, skip_gain_all).astype(bf16)
    normed = dot_plain(normed, order_wide).astype(bf16)
    hidden = product(normed, w_skip)

    def shifted(values, gain, moved):
        wide = jnp.broadcast_to(moved[:, None, :], (batch, tokens, width)).reshape(rows, width)
        return layer_norm(values) * gain + wide

    attn_in = reorder(shifted(hidden, gains[0], shift).astype(bf16))
    qkv_proj = product(attn_in, w_qkv)
    query_proj = heads_of(qkv_proj[:, :width])
    key_proj = heads_of(qkv_proj[:, width : 2 * width])

    def norm_rotate(values):
        return rotate(layer_norm(values), cosine_table, sine_table)

    queries = norm_rotate(query_proj).astype(bf16)
    keys_here = norm_rotate(key_proj).astype(bf16)
    values_here = heads_of(qkv_proj[:, 2 * width :].astype(bf16))
    keyval_here = jnp.concatenate(
        [keys_here.reshape(rows, width), values_here.reshape(rows, width)], axis=1
    )
    keyval_there = links.sibling(keyval_here)
    keys_all = jnp.concatenate([keys_here, heads_of(keyval_there[:, :width])], axis=1)
    values_all = jnp.concatenate([values_here, heads_of(keyval_there[:, width:])], axis=1)
    scores = attend(queries, keys_all, scaling)
    self_peak = jnp.max(scores, axis=(0, 2, 3))
    probs = jax.nn.softmax(scores, axis=-1)
    mixed = mix(probs.astype(bf16), values_all)
    attn_cat = reorder(mixed.reshape(rows, width).astype(bf16))
    after_self = hidden + product(attn_cat, w_self_out)
    cross_in = reorder(gained_norm(after_self, gains[1]).astype(bf16))
    cq_proj = heads_of(product(cross_in, w_query))
    cross_queries = layer_norm(cq_proj).astype(bf16)

    text = text_encoder_states.reshape(batch * text_rows, text_width)
    text_ordered = dot_plain(text, order_text).astype(bf16)
    ckv_proj = product(text_ordered, w_keyval)
    ckey_proj = heads_of(ckv_proj[:, :width])
    cross_keys = layer_norm(ckey_proj).astype(bf16)
    cross_values = heads_of(ckv_proj[:, width:].astype(bf16))
    text_valid = jnp.arange(text_rows)[None, :] < text_lengths[:, None]
    cross_scores = jnp.where(
        text_valid[:, None, None, :], attend(cross_queries, cross_keys, scaling), masked_value
    )
    cross_peak = jnp.max(cross_scores, axis=(0, 2, 3))
    cross_probs = jax.nn.softmax(cross_scores, axis=-1)
    cross_mixed = mix(cross_probs.astype(bf16), cross_values)
    cross_cat = reorder(cross_mixed.reshape(rows, width).astype(bf16))
    after_cross = after_self + product(cross_cat, w_cross_out)
    mlp_in = reorder(gained_norm(after_cross, gains[2]).astype(bf16))
    upper = product(mlp_in, w_up)
    activated = links.order_blocks(gelu_tanh(upper).astype(bf16))

    down_in = out_grad.reshape(rows, width)
    result_grad = down_in.astype(f32)
    down_halves = links.halves(down_in)
    grad_down = weight_grad(activated, down_halves)
    block_out = (after_cross + product(activated, w_down)).astype(bf16)
    act_grad = links.restore_blocks(product_back(down_halves, w_down))
    upper_grad = jax.vjp(gelu_tanh, upper)[1](act_grad)[0].astype(bf16)
    upper_halves = links.halves(upper_grad)
    grad_up = weight_grad(mlp_in, upper_halves)
    mlp_in_grad = exact_restore(order, product_back(upper_halves, w_up))
    cross_part, gain_third = jax.vjp(gained_norm, after_cross, gains[2])[1](mlp_in_grad)
    cross_grad = result_grad + cross_part
    cross_halves = links.halves(cross_grad.astype(bf16))
    grad_cross_out = weight_grad(cross_cat, cross_halves)
    cmix_grad = heads_of(restore(product_back(cross_halves, w_cross_out)))
    cval_grad = mix_back(cross_probs.astype(bf16), cmix_grad)
    cprob_grad = jnp.einsum("bqhd,bkhd->bhqk", cmix_grad, cross_values, preferred_element_type=f32)
    cscore_grad = softmax_back(cross_probs, cprob_grad).astype(bf16)
    cquery_grad = mix(cscore_grad, cross_keys) * scaling
    ckey_grad = mix_back(cscore_grad, cross_queries) * scaling
    cq_grad = jax.vjp(layer_norm, cq_proj)[1](cquery_grad)[0].reshape(rows, width).astype(bf16)
    cq_halves = links.halves(cq_grad)
    grad_cross_query = weight_grad(cross_in, cq_halves)
    cross_in_grad = exact_restore(order, product_back(cq_halves, w_query))
    self_part, gain_second = jax.vjp(gained_norm, after_self, gains[1])[1](cross_in_grad)
    self_grad = cross_grad + self_part

    text_half = text_rows // 2
    ckeyval = jnp.concatenate(
        [
            ckey_grad.reshape(batch, text_rows, width),
            cval_grad.reshape(batch, text_rows, width),
        ],
        axis=2,
    ).astype(bf16)
    ckeyval_mine = lax.dynamic_slice_in_dim(ckeyval, core * text_half, text_half, 1)
    ckeyval_theirs = lax.dynamic_slice_in_dim(ckeyval, (1 - core) * text_half, text_half, 1)
    ckeyval_sum = ckeyval_mine.astype(f32) + links.sibling(ckeyval_theirs).astype(f32)
    ckey_mine = lax.dynamic_slice_in_dim(ckey_proj, core * text_half, text_half, 1)
    ckey_pre = jax.vjp(layer_norm, ckey_mine)[1](heads_of(ckeyval_sum[..., :width]))[0]
    keyval_grad = jnp.concatenate(
        [ckey_pre.reshape(batch * text_half, width), ckeyval_sum[..., width:].reshape(-1, width)],
        axis=1,
    ).astype(bf16)
    text_mine = lax.dynamic_slice_in_dim(
        text_ordered.reshape(batch, text_rows, text_width), core * text_half, text_half, 1
    ).reshape(-1, text_width)
    keyval_halves = links.halves(keyval_grad)
    grad_keyval = weight_grad(text_mine, keyval_halves)
    grad_text = exact_restore(order_text, product_back(keyval_halves, w_keyval))
    grad_text = grad_text.reshape(batch, text_half, text_width)

    self_halves = links.halves(self_grad.astype(bf16))
    grad_self_out = weight_grad(attn_cat, self_halves)
    mix_grad = heads_of(restore(product_back(self_halves, w_self_out)))
    value_grad = mix_back(probs.astype(bf16), mix_grad)
    prob_grad = jnp.einsum("bqhd,bkhd->bhqk", mix_grad, values_all, preferred_element_type=f32)
    score_grad = softmax_back(probs, prob_grad).astype(bf16)
    query_grad = mix(score_grad, keys_all) * scaling
    key_grad = mix_back(score_grad, queries) * scaling
    there = jnp.concatenate(
        [key_grad[:, tokens:].reshape(rows, width), value_grad[:, tokens:].reshape(rows, width)],
        axis=1,
    ).astype(bf16)
    from_there = links.sibling(there).astype(f32)
    key_here = key_grad[:, :tokens] + heads_of(from_there[:, :width])
    value_here = value_grad[:, :tokens].reshape(rows, width) + from_there[:, width:]
    query_pre = jax.vjp(norm_rotate, query_proj)[1](query_grad)[0]
    key_pre = jax.vjp(norm_rotate, key_proj)[1](key_here)[0]
    qkv_grad = jnp.concatenate(
        [query_pre.reshape(rows, width), key_pre.reshape(rows, width), value_here], axis=1
    ).astype(bf16)
    qkv_halves = links.halves(qkv_grad)
    grad_qkv = weight_grad(attn_in, qkv_halves)
    attn_in_grad = exact_restore(order, product_back(qkv_halves, w_qkv))
    hidden_part, gain_first, shift_grad = jax.vjp(shifted, hidden, gains[0], shift)[1](
        attn_in_grad
    )
    hidden_grad = self_grad + hidden_part
    hidden_halves = links.halves(hidden_grad.astype(bf16))
    grad_skip_linear = weight_grad(normed, hidden_halves)
    normed_grad = exact_restore(order_wide, product_back(hidden_halves, w_skip))
    joined_grad, skip_gain_grad = jax.vjp(gained_norm, joined, skip_gain_all)[1](normed_grad)

    shift_sum = shift_grad + links.sibling(shift_grad)
    shift_all = links.small_gather(shift_sum.astype(bf16))
    grad_shift = dot_left_t(cond_cut, shift_all)
    cond_back = links.small_gather(dot_right_t(shift_all, shift_linear)[None])
    cond_mine = lax.dynamic_slice_in_dim(cond_back, me * batch, batch, 1)
    cond_mine = cond_mine.transpose(1, 0, 2).reshape(batch, width)
    grad_cond = jax.vjp(jax.nn.silu, condition.astype(f32))[1](cond_mine)[0]

    gains_grad = jnp.stack([gain_first, gain_second, gain_third])
    gains_grad = gains_grad.reshape(3, count, third).transpose(1, 0, 2).reshape(count, 3 * third)
    packed_grad = jnp.concatenate([skip_gain_grad.reshape(count, gain_rows), gains_grad], axis=1)
    packed_grad = links.small_scatter(packed_grad)
    packed_grad = (packed_grad + links.sibling(packed_grad))[0]
    grad_skip_gain = packed_grad[:gain_rows]
    grad_gains = packed_grad[gain_rows:].reshape(3, third)

    peaks = links.largest(jnp.stack([self_peak, cross_peak]))
    roots = jnp.sqrt(thresholds / jnp.maximum(peaks, thresholds))
    self_cols = jnp.repeat(roots[0], HD)
    cross_cols = jnp.repeat(roots[1], HD)
    unit_cols = jnp.ones((width,), f32)
    clipped_qkv = (
        self_qkv.astype(f32) * jnp.concatenate([self_cols, self_cols, unit_cols])[None, :]
    ).astype(bf16)
    clipped_query = (cross_query.astype(f32) * cross_cols[None, :]).astype(bf16)
    clipped_keyval = (
        cross_keyval.astype(f32) * jnp.concatenate([cross_cols, unit_cols])[None, :]
    ).astype(bf16)
    return (
        block_out.reshape(batch, tokens, width),
        joined_grad[:, :width].reshape(batch, tokens, width),
        joined_grad[:, width:].reshape(batch, tokens, width),
        grad_cond,
        grad_text,
        grad_skip_gain,
        grad_gains,
        grad_skip_linear,
        grad_shift,
        grad_qkv,
        grad_self_out,
        grad_cross_query,
        grad_keyval,
        grad_cross_out,
        grad_up,
        grad_down,
        clipped_qkv,
        clipped_query,
        clipped_keyval,
        peaks,
    )


def solution(mesh):
    rows = P("fsdp", None)
    tokens = P("fsdp", "seq", None)
    in_specs = (
        tokens,
        tokens,
        rows,
        P("fsdp", None, None),
        P("fsdp"),
        tokens,
        P("fsdp"),
        P(None, "fsdp"),
        *([rows] * 9),
        P(),
    )
    out_specs = (
        *([tokens] * 3),
        rows,
        tokens,
        P("fsdp"),
        P(None, "fsdp"),
        *([rows] * 12),
        P(),
    )
    return jax.shard_map(local, mesh=mesh, in_specs=in_specs, out_specs=out_specs, check_vma=False)
```

```python
import functools

import jax
import jax.numpy as jnp
from jax import lax
from jax.experimental import pallas as pl
from jax.experimental.pallas import tpu as pltpu
from jax.sharding import PartitionSpec as P

HEADS = 16
HD = 88
GRID_W = 32

norm_eps = 1e-06
masked_value = -1e30
bf16 = jnp.bfloat16
f32 = jnp.float32
MESH = pl.DeviceIdType.MESH
ANYWHERE = pl.BlockSpec(memory_space=pl.ANY)
IN_VMEM = pl.BlockSpec(memory_space=pltpu.VMEM)


def layer_norm(values):
    center = values - jnp.mean(values, axis=-1, keepdims=True)
    spread = jnp.mean(center * center, axis=-1, keepdims=True)
    return center * lax.rsqrt(spread + norm_eps)


def rotary_tables(row_pos, col_pos, head_dim):
    quarter = head_dim // 4
    freqs = 10000.0 ** (-jnp.arange(quarter, dtype=f32) / quarter)
    row_angle = row_pos.astype(f32)[:, None] * freqs[None, :]
    col_angle = col_pos.astype(f32)[:, None] * freqs[None, :]
    angles = jnp.stack([row_angle, col_angle], axis=1)
    return (jnp.cos(angles), jnp.sin(angles))


def rotate(values, cosine_table, sine_table):
    rows, tokens, heads, head_dim = values.shape
    quarter = head_dim // 4
    pieces = values.reshape(rows, tokens, heads, 2, 2, quarter)
    former = pieces[..., 0, :]
    latter = pieces[..., 1, :]
    cos_wide = cosine_table[None, :, None, :, :]
    sin_wide = sine_table[None, :, None, :, :]
    turned = jnp.stack(
        [former * cos_wide - latter * sin_wide, latter * cos_wide + former * sin_wide], axis=4
    )
    return turned.reshape(rows, tokens, heads, head_dim)


def gained_norm(values, gain):
    return layer_norm(values) * gain


def gelu_tanh(values):
    return jax.nn.gelu(values, approximate=True)


def dot_plain(left, right):
    return jnp.dot(left, right, preferred_element_type=f32)


def dot_left_t(left, right):
    return lax.dot_general(
        left, right, (((0,), (0,)), ((), ())), preferred_element_type=f32
    )


def dot_right_t(left, right):
    return lax.dot_general(
        left, right, (((1,), (1,)), ((), ())), preferred_element_type=f32
    )


def softmax_back(probs, prob_grad):
    return probs * (prob_grad - jnp.sum(prob_grad * probs, axis=-1, keepdims=True))


def greet(peers):
    barrier = pltpu.get_barrier_semaphore()
    for peer in peers:
        pl.semaphore_signal(barrier, inc=1, device_id=peer, device_id_type=MESH)
    pl.semaphore_wait(barrier, len(peers))


def trade_body(count, same, source, out, send, recv, local):
    me = lax.axis_index("fsdp")
    core = lax.axis_index("seq")
    greet([(jnp.bitwise_xor(me, j), core) for j in range(1, count)])

    def part(index):
        return source if same else source.at[index]

    def copy(j):
        peer = jnp.bitwise_xor(me, j)
        return pltpu.make_async_remote_copy(
            src_ref=part(peer),
            dst_ref=out.at[me],
            send_sem=send.at[j],
            recv_sem=recv.at[j],
            device_id=(peer, core),
            device_id_type=MESH,
        )

    for j in range(1, count):
        copy(j).start()
    here = pltpu.make_async_copy(part(me), out.at[me], local.at[0])
    here.start()
    here.wait()
    for j in range(1, count):
        copy(j).wait_send()
        copy(j).wait_recv()


def trade(value, count, same, identity):
    shape = value.shape if same else value.shape[1:]
    return pl.pallas_call(
        functools.partial(trade_body, count, same),
        out_shape=jax.ShapeDtypeStruct((count, *shape), value.dtype),
        in_specs=[IN_VMEM],
        out_specs=IN_VMEM,
        scratch_shapes=[
            pltpu.SemaphoreType.DMA((count,)),
            pltpu.SemaphoreType.DMA((count,)),
            pltpu.SemaphoreType.DMA((1,)),
        ],
        compiler_params=pltpu.CompilerParams(collective_id=identity, has_side_effects=True),
    )(value)


def neighbours(quad):
    me = lax.axis_index("fsdp")
    core = lax.axis_index("seq")
    first, second = 1 + core, 2 - core

    def at(mask):
        return (jnp.bitwise_xor(me, mask), core)

    return core, first, second, at, (me, 1 - core)


def gather_body(count, quad, *refs):
    mine, out = refs[:count], refs[count : 2 * count]
    send, recv, local = refs[2 * count :]
    core, first_mask, second_mask, at, sibling = neighbours(quad)
    far_peers = [at(k * quad) for k in range(1, 4)]
    greet([*far_peers, at(first_mask), at(second_mask), sibling])

    def copy(w, slot, source, target, peer):
        return pltpu.make_async_remote_copy(
            src_ref=source,
            dst_ref=target,
            send_sem=send.at[w, slot],
            recv_sem=recv.at[w, slot],
            device_id=peer,
            device_id_type=MESH,
        )

    def block(w, q):
        return out[w].at[core, pl.ds(4 * q, 4)]

    def far(w, k):
        return copy(w, k - 1, mine[w], out[w].at[core, k], far_peers[k - 1])

    def keep(w):
        return pltpu.make_async_copy(mine[w], out[w].at[core, 0], local.at[w])

    def first(w):
        return copy(w, 3, block(w, 0), block(w, first_mask), at(first_mask))

    def second(w):
        return copy(w, 4, block(w, 0), block(w, second_mask), at(second_mask))

    def both(w):
        return copy(w, 5, block(w, first_mask), block(w, 3), at(second_mask))

    def twin(w, n):
        q = (0, first_mask, second_mask, 3)[n]
        return copy(w, 6 + n, block(w, q), block(w, q), sibling)

    for w in range(count):
        keep(w).start()
        for k in range(1, 4):
            far(w, k).start()
    for step in range(count + 2):
        w = step
        if w < count:
            keep(w).wait()
            for k in range(1, 4):
                far(w, k).wait_recv()
            first(w).start()
            second(w).start()
            twin(w, 0).start()
        w = step - 1
        if 0 <= w < count:
            first(w).wait_recv()
            both(w).start()
            twin(w, 1).start()
            second(w).wait_recv()
            twin(w, 2).start()
        w = step - 2
        if 0 <= w < count:
            both(w).wait_recv()
            twin(w, 3).start()
    for w in range(count):
        for k in range(1, 4):
            far(w, k).wait_send()
        first(w).wait_send()
        second(w).wait_send()
        both(w).wait_send()
        for n in range(4):
            twin(w, n).wait_send()
            twin(w, n).wait_recv()


def gather(shards, quad, identity):
    count = len(shards)
    return pl.pallas_call(
        functools.partial(gather_body, count, quad),
        out_shape=[jax.ShapeDtypeStruct((2, 16, *s.shape), bf16) for s in shards],
        in_specs=[ANYWHERE] * count,
        out_specs=[ANYWHERE] * count,
        scratch_shapes=[
            pltpu.SemaphoreType.DMA((count, 10)),
            pltpu.SemaphoreType.DMA((count, 10)),
            pltpu.SemaphoreType.DMA((count,)),
        ],
        compiler_params=pltpu.CompilerParams(collective_id=identity, has_side_effects=True),
    )(*shards)


def scatter_body(count, quad, *refs):
    source, out = refs[:count], refs[count : 2 * count]
    kept, half, quarter, last, total = (
        refs[(2 + n) * count : (3 + n) * count] for n in range(5)
    )
    send, recv, local = refs[7 * count :]
    core, first_mask, second_mask, at, sibling = neighbours(quad)
    far_peers = [at(k * quad) for k in range(1, 4)]
    greet([*far_peers, at(first_mask), at(second_mask), sibling])

    def copy(w, slot, origin, target, peer):
        return pltpu.make_async_remote_copy(
            src_ref=origin,
            dst_ref=target,
            send_sem=send.at[w, slot],
            recv_sem=recv.at[w, slot],
            device_id=peer,
            device_id_type=MESH,
        )

    def block(w, q):
        return source[w].at[pl.ds(4 * q, 4)]

    def give(w, n):
        q = 3 if n == 0 else second_mask
        return copy(w, n, block(w, q), half[w].at[n], at(second_mask))

    def load(w, n):
        q = first_mask if n == 0 else 0
        return pltpu.make_async_copy(block(w, q), kept[w].at[n], local.at[w, n])

    def pass_on(w):
        return copy(w, 2, half[w].at[0], quarter[w], at(first_mask))

    def far(w, k):
        return copy(w, 2 + k, half[w].at[1, k], last[w].at[k - 1], far_peers[k - 1])

    def twin(w):
        return copy(w, 6, total[w], out[w].at[core], sibling)

    def store(w):
        return pltpu.make_async_copy(total[w], out[w].at[core], local.at[w, 2])

    def lanes(w, body):
        width = total[w].shape[1]
        step = 256 if width % 256 == 0 else 128 if width % 128 == 0 else width
        if step == width:
            body(slice(None))
        else:

            @pl.loop(0, width // step)
            def _(i):
                body(pl.ds(pl.multiple_of(i * step, step), step))

    for w in range(count):
        for n in range(2):
            give(w, n).start()
            load(w, n).start()
    for step in range(count + 2):
        w = step
        if w < count:
            give(w, 0).wait_recv()
            load(w, 0).wait()

            def body(c):
                for k in range(4):
                    half[w][0, k, :, c] = (
                        half[w][0, k, :, c].astype(f32) + kept[w][0, k, :, c].astype(f32)
                    ).astype(bf16)

            lanes(w, body)
            pass_on(w).start()
        w = step - 1
        if 0 <= w < count:
            give(w, 1).wait_recv()
            load(w, 1).wait()
            pass_on(w).wait_recv()

            def body(c):
                for k in range(4):
                    value = half[w][1, k, :, c].astype(f32) + kept[w][1, k, :, c].astype(f32)
                    value = value + quarter[w][k, :, c].astype(f32)
                    if k == 0:
                        total[w][:, c] = value
                    else:
                        half[w][1, k, :, c] = value.astype(bf16)

            lanes(w, body)
            for k in range(1, 4):
                far(w, k).start()
        w = step - 2
        if 0 <= w < count:
            for k in range(1, 4):
                far(w, k).wait_recv()

            def body(c):
                value = total[w][:, c]
                for k in range(3):
                    value = value + last[w][k, :, c].astype(f32)
                total[w][:, c] = value

            lanes(w, body)
            twin(w).start()
            store(w).start()
    for w in range(count):
        give(w, 0).wait_send()
        give(w, 1).wait_send()
        pass_on(w).wait_send()
        for k in range(1, 4):
            far(w, k).wait_send()
        twin(w).wait_send()
        twin(w).wait_recv()
        store(w).wait()


def scatter(sums, quad, identity):
    count = len(sums)
    shapes = [s.shape[1:] for s in sums]

    def buffers(*lead):
        return [pltpu.VMEM((*lead, *s), bf16) for s in shapes]

    return pl.pallas_call(
        functools.partial(scatter_body, count, quad),
        out_shape=[jax.ShapeDtypeStruct((2, *s), f32) for s in shapes],
        in_specs=[ANYWHERE] * count,
        out_specs=[ANYWHERE] * count,
        scratch_shapes=[
            *buffers(2, 4),
            *buffers(2, 4),
            *buffers(4),
            *buffers(3),
            *[pltpu.VMEM(s, f32) for s in shapes],
            pltpu.SemaphoreType.DMA((count, 7)),
            pltpu.SemaphoreType.DMA((count, 7)),
            pltpu.SemaphoreType.DMA((count, 3)),
        ],
        compiler_params=pltpu.CompilerParams(
            collective_id=identity, has_side_effects=True, vmem_limit_bytes=56 * 2**20
        ),
    )(*sums)


class Links:
    def __init__(self, fsdp_count):
        self.count = fsdp_count
        self.me = lax.axis_index("fsdp")
        self.core = lax.axis_index("seq")
        self.high_bits = fsdp_count.bit_length() - 3
        self.quad = 4 << (self.high_bits - 2)
        offsets = [0]
        for bit in range(self.high_bits - 2):
            offsets = offsets + [offset | (4 << bit) for offset in offsets]
        self.high_offsets = [k * self.quad | offset for k in range(4) for offset in offsets]

    def swap(self, value, mask_first, mask_second):
        pairs = []
        for index in range(self.count):
            pairs.append((2 * index, 2 * (index ^ mask_first)))
            pairs.append((2 * index + 1, 2 * (index ^ mask_second) + 1))
        return lax.ppermute(value, ("fsdp", "seq"), pairs)

    def sibling(self, value):
        return lax.ppermute(value, "seq", [(0, 1), (1, 0)])

    def pick(self, first, second):
        return jnp.where(self.core == 0, first, second)

    def offset(self, block):
        return self.high_offsets[block % (self.count // 4)] | (block // (self.count // 4))

    def place(self, offset):
        table = [0] * self.count
        for block in range(self.count):
            table[self.offset(block)] = block
        return jnp.array(table, jnp.int32)[offset]

    def columns(self, own, other):
        return self.pick(
            jnp.concatenate([own, other], axis=-1), jnp.concatenate([other, own], axis=-1)
        )

    def halves(self, value):
        half = value.shape[-1] // 2
        first, second = value[..., :half], value[..., half:]
        return self.pick(first, second), self.pick(second, first)

    def order_matrix(self, size):
        block = size // self.count
        at = lax.broadcasted_iota(jnp.int32, (size, size), 0)
        table = jnp.array([self.offset(b) for b in range(self.count)], jnp.int32)
        starts = jnp.bitwise_xor(self.me, table) * block
        wanted = (starts[:, None] + jnp.arange(block, dtype=jnp.int32)[None, :]).reshape(1, size)
        return (at == wanted).astype(bf16)

    def order_skip(self, width):
        block = width // self.count
        offsets = [
            offset & (self.count // 2 - 1) for offset in self.high_offsets[: self.count // 2 // 4 * 1]
        ]
        offsets = [offset | q for q in range(4) for offset in offsets]
        lower = jnp.bitwise_and(self.me, self.count // 2 - 1)
        starts = jnp.bitwise_xor(lower, jnp.array(offsets, jnp.int32)) * (2 * block)
        starts = jnp.stack([starts, starts + block])
        wanted = (starts[:, :, None] + jnp.arange(block, dtype=jnp.int32)).reshape(1, width)
        return (lax.broadcasted_iota(jnp.int32, (width, width), 0) == wanted).astype(bf16)

    def order_blocks(self, value):
        size = value.shape[1] // self.count
        parts = []
        for block in range(self.count):
            source = jnp.bitwise_xor(self.me, self.offset(block))
            parts.append(lax.dynamic_slice_in_dim(value, source * size, size, 1))
        return jnp.concatenate(parts, axis=1)

    def restore_blocks(self, value):
        size = value.shape[1] // self.count
        parts = []
        for shard in range(self.count):
            source = self.place(jnp.bitwise_xor(self.me, shard))
            parts.append(lax.dynamic_slice_in_dim(value, source * size, size, 1))
        return jnp.concatenate(parts, axis=1)

    def extra_gather(self, mine):
        blocks = mine
        for bit in range(self.high_bits - 2):
            blocks = jnp.concatenate([blocks, self.swap(blocks, 4 << bit, 4 << bit)], axis=0)
        return blocks

    def extra_scatter(self, value):
        for bit in reversed(range(self.high_bits - 2)):
            size = value.shape[-2] // 2
            value = value[..., :size, :] + self.swap(value[..., size:, :], 4 << bit, 4 << bit)
        return value


class Gather:
    def __init__(self, links, shards):
        self.links = links
        half = shards[0].shape[1] // 2
        self.rows = shards[0].shape[0]
        self.weights = len(shards)
        self.shards = jnp.concatenate(
            [links.pick(shard[:, :half], shard[:, half:]) for shard in shards], axis=0
        )
        self.pending = [self.shards]
        self.stage = 0

    def advance(self):
        links = self.links
        self.stage += 1
        if self.stage == 1:
            blocks = [self.pending[0]]
            for bit in range(links.high_bits - 2):
                got = links.swap(jnp.concatenate(blocks, axis=0), 4 << bit, 4 << bit)
                size = self.rows * self.weights
                blocks = blocks + [got[at * size : (at + 1) * size] for at in range(len(blocks))]
            self.low_blocks = len(blocks)
            mine = jnp.concatenate(blocks, axis=0) if len(blocks) > 1 else blocks[0]
            self.pending = [mine] + [
                links.swap(mine, k * links.quad, k * links.quad) for k in range(1, 4)
            ]
        elif self.stage == 2:
            size = self.rows * self.weights
            cuts = [
                got[at * size + w * self.rows : at * size + (w + 1) * self.rows]
                for w in range(self.weights)
                for got in self.pending
                for at in range(self.low_blocks)
            ]
            base = jnp.concatenate(cuts, axis=0)
            self.pending = [
                base, links.swap(base, 1, 2), links.swap(base, 2, 1), links.sibling(base)
            ]
        elif self.stage == 3:
            base, first, second, base_there = self.pending
            self.kept = [base, second, base_there]
            self.pending = [
                links.swap(first, 2, 1), links.sibling(first), links.sibling(second), *self.pending
            ]
        elif self.stage == 4:
            self.pending[0:1] = [links.sibling(self.pending[0]), self.pending[0]]
        elif self.stage == 5:
            both_there, both, first_there, second_there, base, first, second, base_there = self.pending
            size = base.shape[0] // self.weights
            self.result = []
            for w in range(self.weights):
                cut = slice(w * size, (w + 1) * size)
                pick = links.pick
                own = jnp.concatenate(
                    [base[cut], pick(first[cut], second[cut]), pick(second[cut], first[cut]), both[cut]],
                    axis=0,
                )
                other = jnp.concatenate(
                    [
                        base_there[cut],
                        pick(second_there[cut], first_there[cut]),
                        pick(first_there[cut], second_there[cut]),
                        both_there[cut],
                    ],
                    axis=0,
                )
                self.result.append((own, other))
            self.pending = []

    def finish(self):
        while self.stage < 5:
            self.advance()
        return self.result


class Scatter:
    def __init__(self, links, pairs):
        self.links = links
        self.pairs = pairs
        self.pending = [other for _, other in pairs]
        self.stage = 0

    def advance(self):
        links = self.links
        pick = links.pick
        self.stage += 1
        if self.stage == 1:
            self.pending = [own for own, _ in self.pairs] + [
                links.sibling(other) for other in self.pending
            ]
        elif self.stage == 2:
            count = len(self.pairs)
            send, keep = [[], []], [[], []]
            for own, got in zip(self.pending[:count], self.pending[count:]):
                size = own.shape[0] // 4
                cuts = [
                    own[q * size : (q + 1) * size].astype(f32) + got[q * size : (q + 1) * size].astype(f32)
                    for q in range(4)
                ]
                send[0].append(pick(cuts[2], cuts[1]).astype(bf16))
                send[1].append(cuts[3].astype(bf16))
                keep[0].append(cuts[0])
                keep[1].append(pick(cuts[1], cuts[2]))
            self.sizes = [part.shape[0] for part in keep[0]]
            self.keep = [jnp.concatenate(part, axis=0) for part in keep]
            self.pending = [links.swap(jnp.concatenate(send[0] + send[1], axis=0), 2, 1)]
        elif self.stage == 3:
            total = sum(self.sizes)
            got = self.pending[0].astype(f32)
            self.keep, send = self.keep[0] + got[:total], (self.keep[1] + got[total:]).astype(bf16)
            self.pending = [links.swap(send, 1, 2)]
        elif self.stage == 4:
            summed = self.keep + self.pending[0].astype(f32)
            keep, send = [], [[], [], []]
            start = 0
            for size in self.sizes:
                part = size // 4
                keep.append(summed[start : start + part])
                for k in range(1, 4):
                    send[k - 1].append(summed[start + k * part : start + (k + 1) * part].astype(bf16))
                start += size
            self.keep = jnp.concatenate(keep, axis=0)
            self.pending = [
                links.swap(jnp.concatenate(send[k - 1], axis=0), k * links.quad, k * links.quad)
                for k in range(1, 4)
            ]
        elif self.stage == 5:
            total = self.keep
            for got in self.pending:
                total = total + got.astype(f32)
            rows = [size // 4 for size in self.sizes]
            for bit in reversed(range(links.high_bits - 2)):
                keep, send, start = [], [], 0
                for at, size in enumerate(rows):
                    keep.append(total[start : start + size // 2])
                    send.append(total[start + size // 2 : start + size])
                    start += size
                    rows[at] = size // 2
                got = links.swap(jnp.concatenate(send, axis=0), 4 << bit, 4 << bit)
                total = jnp.concatenate(keep, axis=0) + got
            self.rows = rows
            self.pending = [total, links.sibling(total)]
        elif self.stage == 6:
            whole = links.columns(*self.pending)
            self.result, start = [], 0
            for size in self.rows:
                self.result.append(whole[start : start + size])
                start += size
            self.pending = []

    def finish(self):
        while self.stage < 6:
            self.advance()
        return self.result


def tie(value, *jobs):
    leaves, tree = jax.tree.flatten(value)
    flat = list(leaves)
    for job in jobs:
        flat.extend(job.pending)
    flat = list(lax.optimization_barrier(tuple(flat)))
    at = len(leaves)
    value = jax.tree.unflatten(tree, flat[:at])
    for job in jobs:
        job.pending = flat[at : at + len(job.pending)]
        at += len(job.pending)
        job.advance()
    return value


def lanes_of(value, multiple):
    size = 128 * multiple
    spare = -value.shape[-1] % size
    value = jnp.pad(value, [(0, 0)] * (value.ndim - 1) + [(0, spare)])
    return value.reshape(*value.shape[:-1], -1, 128)


def exact_restore(matrix, value):
    high = value.astype(bf16)
    low = (value - high.astype(f32)).astype(bf16)
    return dot_right_t(high, matrix) + dot_right_t(low, matrix)


def attend(queries, keys, scaling):
    return jnp.einsum("bqhd,bkhd->bhqk", queries, keys, preferred_element_type=f32) * scaling


def mix(probs, values):
    return jnp.einsum("bhqk,bkhd->bqhd", probs, values, preferred_element_type=f32)


def mix_back(probs, grads):
    return jnp.einsum("bhqk,bqhd->bkhd", probs, grads, preferred_element_type=f32)


def local(
    latent,
    skip_input,
    condition,
    text_encoder_states,
    text_lengths,
    out_grad,
    skip_gain,
    norm_gains,
    skip_linear,
    shift_linear,
    self_qkv,
    self_out,
    cross_query,
    cross_keyval,
    cross_out,
    mlp_up,
    mlp_down,
    thresholds,
):
    batch, tokens, width = latent.shape
    rows = batch * tokens
    text_rows = text_encoder_states.shape[1]
    text_width = text_encoder_states.shape[2]
    scaling = HD ** (-0.5)
    links = Links(lax.axis_size("fsdp"))
    me, core = links.me, links.core
    count = links.count

    positions = core * tokens + jnp.arange(tokens)
    cosine_table, sine_table = rotary_tables(positions // GRID_W, positions % GRID_W, HD)

    gain_rows = skip_gain.shape[0]
    third = norm_gains.shape[1]
    cond_act = jax.nn.silu(condition.astype(f32)).astype(bf16)
    small = jnp.concatenate([skip_gain, norm_gains.reshape(-1), cond_act.reshape(-1)])
    small = trade(lanes_of(small, 16), count, True, 1).reshape(count, -1)
    skip_gain_all = small[:, :gain_rows].reshape(-1).astype(f32)
    cond_start = gain_rows + 3 * third
    gains = small[:, gain_rows:cond_start].reshape(count, 3, third)
    gains = gains.transpose(1, 0, 2).reshape(3, width).astype(f32)
    cond_all = small[:, cond_start : cond_start + batch * width].reshape(count * batch, width)
    shift_rows = shift_linear.shape[0]
    cond_cut = lax.dynamic_slice_in_dim(cond_all, me * shift_rows, shift_rows, 1)
    shift_parts = dot_plain(cond_cut, shift_linear).reshape(count, batch * width)
    shift_parts = trade(lanes_of(shift_parts, 8), count, False, 2)
    shift = jnp.sum(shift_parts.reshape(count, -1), axis=0)[: batch * width].reshape(batch, width)

    def columns_mine(weight):
        half = weight.shape[1] // 2
        return links.pick(weight[:, :half], weight[:, half:])

    skip_half = skip_linear.shape[0] // 2
    shards = [
        links.pick(skip_linear[:skip_half], skip_linear[skip_half:]),
        columns_mine(self_qkv),
        links.pick(self_out, cross_out),
        columns_mine(cross_query),
        columns_mine(cross_keyval),
    ]
    shards = [links.extra_gather(shard) for shard in shards]
    shards = lax.optimization_barrier((shift, *shards))
    shift = shards[0]
    gathered = gather(shards[1:], links.quad, 3)
    w_skip, w_qkv, w_pair, w_query, w_keyval = (
        g.reshape(2, 16 * g.shape[2], g.shape[3]) for g in gathered
    )
    w_self_out, w_cross_out = w_pair[0], w_pair[1]
    get_up = Gather(links, [mlp_up])
    get_down = Gather(links, [mlp_down])
    w_skip = tie(w_skip, get_up, get_down)

    order = links.order_matrix(width)
    order_skip = links.order_skip(width)
    order_text = links.order_matrix(text_width)

    def product(value, weight):
        return jnp.concatenate([dot_plain(value, weight[0]), dot_plain(value, weight[1])], axis=1)

    def product_back(grad, weight):
        half = grad.shape[1] // 2
        return dot_right_t(grad[:, :half], weight[0]) + dot_right_t(grad[:, half:], weight[1])

    def sum_twins(own, other):
        there = links.sibling(dot_left_t(*other).astype(bf16))
        return own, there

    def finish_twins(own, there):
        value = (dot_left_t(*own) + there.astype(f32)).astype(bf16)
        return value.reshape(16, value.shape[0] // 16, value.shape[1])

    def column_grad(value, grad):
        own, other = links.halves(grad)
        return sum_twins((value, own), (value, other))

    def weight_grad(value, grad_halves):
        return (
            dot_left_t(value, grad_halves[0]).astype(bf16),
            dot_left_t(value, grad_halves[1]).astype(bf16),
        )

    def relative_product(value, weight):
        return links.columns(dot_plain(value, weight[0]), dot_plain(value, weight[1]))

    def relative_back(grad_halves, weight):
        return dot_right_t(grad_halves[0], weight[0]) + dot_right_t(grad_halves[1], weight[1])

    def reorder(value):
        return dot_plain(value, order).astype(bf16)

    def restore(value):
        return dot_right_t(value.astype(bf16), order).astype(bf16)

    def heads_of(value):
        return value.reshape(batch, -1, HEADS, HD)

    joined = jnp.concatenate(
        [latent.reshape(rows, width), skip_input.reshape(rows, width)], axis=1
    ).astype(f32)
    normed = gained_norm(joined, skip_gain_all).astype(bf16)
    upper_half = (me >= count // 2).astype(jnp.int32)
    near = jnp.where(upper_half == 0, normed[:, :width], normed[:, width:])
    away = jnp.where(upper_half == 0, normed[:, width:], normed[:, :width])
    near = dot_plain(near, order_skip).astype(bf16).reshape(rows, 2, 4, 1, -1)
    away = dot_plain(away, order_skip).astype(bf16).reshape(rows, 2, 4, 1, -1)
    normed = jnp.concatenate([near, away], axis=3).reshape(rows, 2, width)
    normed = (normed[:, 0], normed[:, 1])
    hidden = dot_plain(normed[0], w_skip[0]) + dot_plain(normed[1], w_skip[1])

    def shifted(values, gain, moved):
        wide = jnp.broadcast_to(moved[:, None, :], (batch, tokens, width)).reshape(rows, width)
        return layer_norm(values) * gain + wide

    attn_in = reorder(shifted(hidden, gains[0], shift).astype(bf16))
    qkv_proj = product(attn_in, w_qkv)
    query_proj = heads_of(qkv_proj[:, :width])
    key_proj = heads_of(qkv_proj[:, width : 2 * width])

    def norm_rotate(values):
        return rotate(layer_norm(values), cosine_table, sine_table)

    queries = norm_rotate(query_proj).astype(bf16)
    keys_here = norm_rotate(key_proj).astype(bf16)
    values_here = heads_of(qkv_proj[:, 2 * width :].astype(bf16))
    keyval_here = jnp.concatenate(
        [keys_here.reshape(rows, width), values_here.reshape(rows, width)], axis=1
    )
    keyval_there = links.sibling(keyval_here)
    keys_all = jnp.concatenate([keys_here, heads_of(keyval_there[:, :width])], axis=1)
    values_all = jnp.concatenate([values_here, heads_of(keyval_there[:, width:])], axis=1)
    queries = tie(queries, get_up)
    scores = attend(queries, keys_all, scaling)
    self_peak = jnp.max(scores, axis=(0, 2, 3))
    probs = jax.nn.softmax(scores, axis=-1)
    mixed = mix(probs.astype(bf16), values_all)
    attn_cat = reorder(mixed.reshape(rows, width).astype(bf16))
    attn_cat = tie(attn_cat, get_down)
    after_self = hidden + dot_plain(attn_cat, w_self_out)
    cross_in = reorder(gained_norm(after_self, gains[1]).astype(bf16))
    cq_proj = heads_of(product(cross_in, w_query))
    cross_queries = layer_norm(cq_proj).astype(bf16)

    text = text_encoder_states.reshape(batch * text_rows, text_width)
    text_ordered = dot_plain(text, order_text).astype(bf16)
    ckv_proj = product(text_ordered, w_keyval)
    ckey_proj = heads_of(ckv_proj[:, :width])
    cross_keys = layer_norm(ckey_proj).astype(bf16)
    cross_values = heads_of(ckv_proj[:, width:].astype(bf16))
    text_valid = jnp.arange(text_rows)[None, :] < text_lengths[:, None]
    cross_queries = tie(cross_queries, get_up)
    cross_scores = jnp.where(
        text_valid[:, None, None, :], attend(cross_queries, cross_keys, scaling), masked_value
    )
    cross_peak = jnp.max(cross_scores, axis=(0, 2, 3))
    cross_probs = jax.nn.softmax(cross_scores, axis=-1)
    cross_mixed = mix(cross_probs.astype(bf16), cross_values)
    cross_cat = reorder(cross_mixed.reshape(rows, width).astype(bf16))
    after_cross = after_self + dot_plain(cross_cat, w_cross_out)
    mlp_in = reorder(gained_norm(after_cross, gains[2]).astype(bf16))
    mlp_in = tie(mlp_in, get_up, get_down)
    (w_up,) = get_up.finish()
    upper = relative_product(mlp_in, w_up)
    activated = links.order_blocks(gelu_tanh(upper).astype(bf16))

    down_in = out_grad.reshape(rows, width)
    result_grad = down_in.astype(f32)
    down_halves = links.halves(down_in)
    put_down = Scatter(links, [weight_grad(activated, down_halves)])
    put_down.advance()
    activated = tie(activated, put_down)
    (w_down,) = get_down.finish()
    block_out = (after_cross + relative_product(activated, w_down)).astype(bf16)
    act_grad = links.restore_blocks(relative_back(down_halves, w_down))
    upper_grad = jax.vjp(gelu_tanh, upper)[1](act_grad)[0].astype(bf16)
    upper_halves = links.halves(upper_grad)
    put_up = Scatter(links, [weight_grad(mlp_in, upper_halves)])
    put_up.advance()
    mlp_in_grad = exact_restore(order, relative_back(upper_halves, w_up))
    cross_part, gain_third = jax.vjp(gained_norm, after_cross, gains[2])[1](mlp_in_grad)
    cross_grad = result_grad + cross_part
    cross_bf = tie(cross_grad.astype(bf16), put_up)
    cmix_grad = heads_of(restore(dot_right_t(cross_bf, w_cross_out)))
    cval_grad = mix_back(cross_probs.astype(bf16), cmix_grad)
    cmix_grad = tie(cmix_grad, put_down)
    cprob_grad = jnp.einsum("bqhd,bkhd->bhqk", cmix_grad, cross_values, preferred_element_type=f32)
    cscore_grad = softmax_back(cross_probs, cprob_grad).astype(bf16)
    cquery_grad = mix(cscore_grad, cross_keys) * scaling
    ckey_grad = mix_back(cscore_grad, cross_queries) * scaling
    cq_grad = jax.vjp(layer_norm, cq_proj)[1](cquery_grad)[0].reshape(rows, width).astype(bf16)
    put_query = column_grad(cross_in, cq_grad)
    cq_grad = tie(cq_grad, put_up, put_down)
    cross_in_grad = exact_restore(order, product_back(cq_grad, w_query))
    self_part, gain_second = jax.vjp(gained_norm, after_self, gains[1])[1](cross_in_grad)
    self_grad = cross_grad + self_part

    text_half = text_rows // 2
    ckeyval = jnp.concatenate(
        [
            ckey_grad.reshape(batch, text_rows, width),
            cval_grad.reshape(batch, text_rows, width),
        ],
        axis=2,
    ).astype(bf16)
    ckeyval_mine = lax.dynamic_slice_in_dim(ckeyval, core * text_half, text_half, 1)
    ckeyval_theirs = lax.dynamic_slice_in_dim(ckeyval, (1 - core) * text_half, text_half, 1)
    ckeyval_sum = ckeyval_mine.astype(f32) + links.sibling(ckeyval_theirs).astype(f32)
    ckey_mine = lax.dynamic_slice_in_dim(ckey_proj, core * text_half, text_half, 1)
    ckey_pre = jax.vjp(layer_norm, ckey_mine)[1](heads_of(ckeyval_sum[..., :width]))[0]
    keyval_grad = jnp.concatenate(
        [ckey_pre.reshape(batch * text_half, width), ckeyval_sum[..., width:].reshape(-1, width)],
        axis=1,
    ).astype(bf16)
    text_mine = lax.dynamic_slice_in_dim(
        text_ordered.reshape(batch, text_rows, text_width), core * text_half, text_half, 1
    ).reshape(-1, text_width)
    put_keyval = column_grad(text_mine, keyval_grad)
    grad_text = exact_restore(order_text, product_back(keyval_grad, w_keyval))
    grad_text = grad_text.reshape(batch, text_half, text_width)

    self_bf = self_grad.astype(bf16)
    put_pair = sum_twins(
        (links.pick(attn_cat, cross_cat), links.pick(self_bf, cross_bf)),
        (links.pick(cross_cat, attn_cat), links.pick(cross_bf, self_bf)),
    )
    self_bf = tie(self_bf, put_down)
    mix_grad = heads_of(restore(dot_right_t(self_bf, w_self_out)))
    mix_grad = tie(mix_grad, put_up)
    value_grad = mix_back(probs.astype(bf16), mix_grad)
    prob_grad = jnp.einsum("bqhd,bkhd->bhqk", mix_grad, values_all, preferred_element_type=f32)
    score_grad = softmax_back(probs, prob_grad).astype(bf16)
    score_grad = tie(score_grad, put_up)
    query_grad = mix(score_grad, keys_all) * scaling
    key_grad = mix_back(score_grad, queries) * scaling
    there = jnp.concatenate(
        [key_grad[:, tokens:].reshape(rows, width), value_grad[:, tokens:].reshape(rows, width)],
        axis=1,
    ).astype(bf16)
    from_there = links.sibling(there).astype(f32)
    key_here = key_grad[:, :tokens] + heads_of(from_there[:, :width])
    value_here = value_grad[:, :tokens].reshape(rows, width) + from_there[:, width:]
    query_pre = jax.vjp(norm_rotate, query_proj)[1](query_grad)[0]
    key_pre = jax.vjp(norm_rotate, key_proj)[1](key_here)[0]
    qkv_grad = jnp.concatenate(
        [query_pre.reshape(rows, width), key_pre.reshape(rows, width), value_here], axis=1
    ).astype(bf16)
    put_qkv = column_grad(attn_in, qkv_grad)
    attn_in_grad = exact_restore(order, product_back(qkv_grad, w_qkv))
    hidden_part, gain_first, shift_grad = jax.vjp(shifted, hidden, gains[0], shift)[1](
        attn_in_grad
    )
    hidden_grad = self_grad + hidden_part
    hidden_bf = hidden_grad.astype(bf16)
    put_skip = sum_twins(
        (links.pick(*normed), hidden_bf), (links.pick(normed[1], normed[0]), hidden_bf)
    )
    normed_grad = jnp.concatenate(
        [dot_right_t(hidden_bf, w_skip[0]), dot_right_t(hidden_bf, w_skip[1])], axis=1
    ).reshape(rows, 2, 4, 2, -1)
    near_grad = exact_restore(order_skip, normed_grad[:, :, :, 0].reshape(rows, width))
    away_grad = exact_restore(order_skip, normed_grad[:, :, :, 1].reshape(rows, width))
    normed_grad = jnp.concatenate(
        [
            jnp.where(upper_half == 0, near_grad, away_grad),
            jnp.where(upper_half == 0, away_grad, near_grad),
        ],
        axis=1,
    )
    joined_grad, skip_gain_grad = jax.vjp(gained_norm, joined, skip_gain_all)[1](normed_grad)

    sums = [
        finish_twins(*put) for put in (put_pair, put_query, put_keyval, put_qkv, put_skip)
    ]
    (grad_down,) = put_down.finish()
    (grad_up,) = put_up.finish()
    scattered = [links.extra_scatter(part) for part in scatter(sums, links.quad, 4)]
    grad_self_out, grad_cross_out = scattered[0][0], scattered[0][1]
    grad_cross_query, grad_keyval, grad_qkv = (
        jnp.concatenate([part[0], part[1]], axis=1) for part in scattered[1:4]
    )
    grad_skip_linear = scattered[4].reshape(skip_linear.shape)

    gains_grad = jnp.stack([gain_first, gain_second, gain_third])
    gains_grad = gains_grad.reshape(3, count, third).transpose(1, 0, 2).reshape(count, 3 * third)
    gains_grad = jnp.concatenate([skip_gain_grad.reshape(count, gain_rows), gains_grad], axis=1)
    peaks = jnp.stack([self_peak, cross_peak])
    cores = jnp.concatenate([shift_grad.reshape(-1), gains_grad.reshape(-1), peaks.reshape(-1)])
    there = links.sibling(cores)
    peaks = jnp.maximum(cores, there)[-2 * HEADS :]
    cores = cores + there
    ends = (batch * width, batch * width + count * cond_start)
    gains_grad = cores[ends[0] : ends[1]].reshape(count, cond_start)
    shift_bf = cores[: ends[0]].astype(bf16).astype(f32)
    shared = trade(lanes_of(jnp.concatenate([shift_bf, peaks]), 8), count, True, 5)
    shared = shared.reshape(count, -1)
    shift_all = shared[:, : ends[0]].reshape(count * batch, width).astype(bf16)
    peaks = jnp.max(shared[:, ends[0] : ends[0] + 2 * HEADS], axis=0).reshape(2, HEADS)
    grad_shift = dot_left_t(cond_cut, shift_all)
    cond_back = dot_right_t(shift_all, shift_linear).reshape(count, batch * shift_rows)
    owned = trade(lanes_of(jnp.concatenate([cond_back, gains_grad], axis=1), 8), count, False, 6)
    owned = owned.reshape(count, -1)
    cond_mine = owned[:, : batch * shift_rows].reshape(count, batch, shift_rows)
    cond_mine = cond_mine.transpose(1, 0, 2).reshape(batch, width)
    grad_cond = jax.vjp(jax.nn.silu, condition.astype(f32))[1](cond_mine)[0]
    own_gains = jnp.sum(owned[:, batch * shift_rows : batch * shift_rows + cond_start], axis=0)
    grad_skip_gain = own_gains[:gain_rows]
    grad_gains = own_gains[gain_rows:].reshape(3, third)

    roots = jnp.sqrt(thresholds / jnp.maximum(peaks, thresholds))
    self_cols = jnp.repeat(roots[0], HD)
    cross_cols = jnp.repeat(roots[1], HD)
    unit_cols = jnp.ones((width,), f32)
    clipped_qkv = (
        self_qkv.astype(f32) * jnp.concatenate([self_cols, self_cols, unit_cols])[None, :]
    ).astype(bf16)
    clipped_query = (cross_query.astype(f32) * cross_cols[None, :]).astype(bf16)
    clipped_keyval = (
        cross_keyval.astype(f32) * jnp.concatenate([cross_cols, unit_cols])[None, :]
    ).astype(bf16)
    return (
        block_out.reshape(batch, tokens, width),
        joined_grad[:, :width].reshape(batch, tokens, width),
        joined_grad[:, width:].reshape(batch, tokens, width),
        grad_cond,
        grad_text,
        grad_skip_gain,
        grad_gains,
        grad_skip_linear,
        grad_shift,
        grad_qkv,
        grad_self_out,
        grad_cross_query,
        grad_keyval,
        grad_cross_out,
        grad_up,
        grad_down,
        clipped_qkv,
        clipped_query,
        clipped_keyval,
        peaks,
    )


def solution(mesh):
    rows = P("fsdp", None)
    tokens = P("fsdp", "seq", None)
    in_specs = (
        tokens,
        tokens,
        rows,
        P("fsdp", None, None),
        P("fsdp"),
        tokens,
        P("fsdp"),
        P(None, "fsdp"),
        *([rows] * 9),
        P(),
    )
    out_specs = (
        *([tokens] * 3),
        rows,
        tokens,
        P("fsdp"),
        P(None, "fsdp"),
        *([rows] * 12),
        P(),
    )
    return jax.shard_map(local, mesh=mesh, in_specs=in_specs, out_specs=out_specs, check_vma=False)
```

```python
import functools

import jax
import jax.numpy as jnp
from jax import lax
from jax.experimental import pallas as pl
from jax.experimental.pallas import tpu as pltpu
from jax.sharding import PartitionSpec as P

HEADS = 16
HD = 88
GRID_W = 32

norm_eps = 1e-06
masked_value = -1e30
bf16 = jnp.bfloat16
f32 = jnp.float32
MESH = pl.DeviceIdType.MESH
ANYWHERE = pl.BlockSpec(memory_space=pl.ANY)
IN_VMEM = pl.BlockSpec(memory_space=pltpu.VMEM)


def layer_norm(values):
    center = values - jnp.mean(values, axis=-1, keepdims=True)
    spread = jnp.mean(center * center, axis=-1, keepdims=True)
    return center * lax.rsqrt(spread + norm_eps)


def gained_norm(values, gain):
    return layer_norm(values) * gain


def gelu_tanh(values):
    return jax.nn.gelu(values, approximate=True)


def dot_plain(left, right):
    return jnp.dot(left, right, preferred_element_type=f32)


def dot_left_t(left, right):
    return lax.dot_general(
        left, right, (((0,), (0,)), ((), ())), preferred_element_type=f32
    )


def dot_right_t(left, right):
    return lax.dot_general(
        left, right, (((1,), (1,)), ((), ())), preferred_element_type=f32
    )


def softmax_back(probs, prob_grad):
    return probs * (prob_grad - jnp.sum(prob_grad * probs, axis=-1, keepdims=True))


def greet(peers):
    barrier = pltpu.get_barrier_semaphore()
    for peer in peers:
        pl.semaphore_signal(barrier, inc=1, device_id=peer, device_id_type=MESH)
    pl.semaphore_wait(barrier, len(peers))


def trade_body(count, same, source, out, send, recv, local):
    me = lax.axis_index("fsdp")
    core = lax.axis_index("seq")
    greet([(jnp.bitwise_xor(me, j), core) for j in range(1, count)])

    def part(index):
        return source if same else source.at[index]

    def copy(j):
        peer = jnp.bitwise_xor(me, j)
        return pltpu.make_async_remote_copy(
            src_ref=part(peer),
            dst_ref=out.at[me],
            send_sem=send.at[j],
            recv_sem=recv.at[j],
            device_id=(peer, core),
            device_id_type=MESH,
        )

    for j in range(1, count):
        copy(j).start()
    here = pltpu.make_async_copy(part(me), out.at[me], local.at[0])
    here.start()
    here.wait()
    for j in range(1, count):
        copy(j).wait_send()
        copy(j).wait_recv()


def trade(value, count, same, identity):
    shape = value.shape if same else value.shape[1:]
    return pl.pallas_call(
        functools.partial(trade_body, count, same),
        out_shape=jax.ShapeDtypeStruct((count, *shape), value.dtype),
        in_specs=[IN_VMEM],
        out_specs=IN_VMEM,
        scratch_shapes=[
            pltpu.SemaphoreType.DMA((count,)),
            pltpu.SemaphoreType.DMA((count,)),
            pltpu.SemaphoreType.DMA((1,)),
        ],
        compiler_params=pltpu.CompilerParams(collective_id=identity, has_side_effects=True),
    )(value)


def neighbours(quad):
    me = lax.axis_index("fsdp")
    core = lax.axis_index("seq")
    first, second = 1 + core, 2 - core

    def at(mask):
        return (jnp.bitwise_xor(me, mask), core)

    return core, first, second, at, (me, 1 - core)


def gather_body(count, quad, *refs):
    mine, out = refs[:count], refs[count : 2 * count]
    send, recv, local = refs[2 * count :]
    core, first_mask, second_mask, at, sibling = neighbours(quad)
    far_peers = [at(k * quad) for k in range(1, 4)]
    greet([*far_peers, at(first_mask), at(second_mask), sibling])

    def copy(w, slot, source, target, peer):
        return pltpu.make_async_remote_copy(
            src_ref=source,
            dst_ref=target,
            send_sem=send.at[w, slot],
            recv_sem=recv.at[w, slot],
            device_id=peer,
            device_id_type=MESH,
        )

    def block(w, q):
        return out[w].at[core, pl.ds(4 * q, 4)]

    def far(w, k):
        return copy(w, k - 1, mine[w], out[w].at[core, k], far_peers[k - 1])

    def keep(w):
        return pltpu.make_async_copy(mine[w], out[w].at[core, 0], local.at[w])

    def first(w):
        return copy(w, 3, block(w, 0), block(w, first_mask), at(first_mask))

    def second(w):
        return copy(w, 4, block(w, 0), block(w, second_mask), at(second_mask))

    def both(w):
        return copy(w, 5, block(w, first_mask), block(w, 3), at(second_mask))

    def twin(w, n):
        q = (0, first_mask, second_mask, 3)[n]
        return copy(w, 6 + n, block(w, q), block(w, q), sibling)

    for w in range(count):
        keep(w).start()
        for k in range(1, 4):
            far(w, k).start()
    for step in range(count + 2):
        w = step
        if w < count:
            keep(w).wait()
            for k in range(1, 4):
                far(w, k).wait_recv()
            first(w).start()
            second(w).start()
            twin(w, 0).start()
        w = step - 1
        if 0 <= w < count:
            first(w).wait_recv()
            both(w).start()
            twin(w, 1).start()
            second(w).wait_recv()
            twin(w, 2).start()
        w = step - 2
        if 0 <= w < count:
            both(w).wait_recv()
            twin(w, 3).start()
    for w in range(count):
        for k in range(1, 4):
            far(w, k).wait_send()
        first(w).wait_send()
        second(w).wait_send()
        both(w).wait_send()
        for n in range(4):
            twin(w, n).wait_send()
            twin(w, n).wait_recv()


def gather(shards, quad, identity):
    count = len(shards)
    return pl.pallas_call(
        functools.partial(gather_body, count, quad),
        out_shape=[jax.ShapeDtypeStruct((2, 16, *s.shape), bf16) for s in shards],
        in_specs=[ANYWHERE] * count,
        out_specs=[ANYWHERE] * count,
        scratch_shapes=[
            pltpu.SemaphoreType.DMA((count, 10)),
            pltpu.SemaphoreType.DMA((count, 10)),
            pltpu.SemaphoreType.DMA((count,)),
        ],
        compiler_params=pltpu.CompilerParams(collective_id=identity, has_side_effects=True),
    )(*shards)


def scatter_body(count, quad, *refs):
    source, out = refs[:count], refs[count : 2 * count]
    kept, half, quarter, last, total = (
        refs[(2 + n) * count : (3 + n) * count] for n in range(5)
    )
    send, recv, local = refs[7 * count :]
    core, first_mask, second_mask, at, sibling = neighbours(quad)
    far_peers = [at(k * quad) for k in range(1, 4)]
    greet([*far_peers, at(first_mask), at(second_mask), sibling])

    def copy(w, slot, origin, target, peer):
        return pltpu.make_async_remote_copy(
            src_ref=origin,
            dst_ref=target,
            send_sem=send.at[w, slot],
            recv_sem=recv.at[w, slot],
            device_id=peer,
            device_id_type=MESH,
        )

    def block(w, q):
        if len(source[w].shape) == 4:
            return source[w].at[:, q]
        return source[w].at[pl.ds(4 * q, 4)]

    def give(w, n):
        q = 3 if n == 0 else second_mask
        return copy(w, n, block(w, q), half[w].at[n], at(second_mask))

    def load(w, n):
        q = first_mask if n == 0 else 0
        return pltpu.make_async_copy(block(w, q), kept[w].at[n], local.at[w, n])

    def pass_on(w):
        return copy(w, 2, half[w].at[0], quarter[w], at(first_mask))

    def far(w, k):
        return copy(w, 2 + k, half[w].at[1, k], last[w].at[k - 1], far_peers[k - 1])

    def twin(w):
        return copy(w, 6, total[w], out[w].at[core], sibling)

    def store(w):
        return pltpu.make_async_copy(total[w], out[w].at[core], local.at[w, 2])

    def lanes(w, body):
        width = total[w].shape[1]
        step = 256 if width % 256 == 0 else 128 if width % 128 == 0 else width
        if step == width:
            body(slice(None))
        else:

            @pl.loop(0, width // step)
            def _(i):
                body(pl.ds(pl.multiple_of(i * step, step), step))

    for w in range(count):
        for n in range(2):
            give(w, n).start()
            load(w, n).start()
    for step in range(count + 2):
        w = step
        if w < count:
            give(w, 0).wait_recv()
            load(w, 0).wait()

            def body(c):
                for k in range(4):
                    half[w][0, k, :, c] = (
                        half[w][0, k, :, c].astype(f32) + kept[w][0, k, :, c].astype(f32)
                    ).astype(bf16)

            lanes(w, body)
            pass_on(w).start()
        w = step - 1
        if 0 <= w < count:
            give(w, 1).wait_recv()
            load(w, 1).wait()
            pass_on(w).wait_recv()

            def body(c):
                for k in range(4):
                    value = half[w][1, k, :, c].astype(f32) + kept[w][1, k, :, c].astype(f32)
                    value = value + quarter[w][k, :, c].astype(f32)
                    if k == 0:
                        total[w][:, c] = value
                    else:
                        half[w][1, k, :, c] = value.astype(bf16)

            lanes(w, body)
            for k in range(1, 4):
                far(w, k).start()
        w = step - 2
        if 0 <= w < count:
            for k in range(1, 4):
                far(w, k).wait_recv()

            def body(c):
                value = total[w][:, c]
                for k in range(3):
                    value = value + last[w][k, :, c].astype(f32)
                total[w][:, c] = value

            lanes(w, body)
            twin(w).start()
            store(w).start()
    for w in range(count):
        give(w, 0).wait_send()
        give(w, 1).wait_send()
        pass_on(w).wait_send()
        for k in range(1, 4):
            far(w, k).wait_send()
        twin(w).wait_send()
        twin(w).wait_recv()
        store(w).wait()


def scatter(sums, quad, identity):
    count = len(sums)
    shapes = [s.shape[-2:] for s in sums]

    def buffers(*lead):
        return [pltpu.VMEM((*lead, *s), bf16) for s in shapes]

    return pl.pallas_call(
        functools.partial(scatter_body, count, quad),
        out_shape=[jax.ShapeDtypeStruct((2, *s), f32) for s in shapes],
        in_specs=[ANYWHERE] * count,
        out_specs=[ANYWHERE] * count,
        scratch_shapes=[
            *buffers(2, 4),
            *buffers(2, 4),
            *buffers(4),
            *buffers(3),
            *[pltpu.VMEM(s, f32) for s in shapes],
            pltpu.SemaphoreType.DMA((count, 7)),
            pltpu.SemaphoreType.DMA((count, 7)),
            pltpu.SemaphoreType.DMA((count, 3)),
        ],
        compiler_params=pltpu.CompilerParams(
            collective_id=identity, has_side_effects=True, vmem_limit_bytes=56 * 2**20
        ),
    )(*sums)


def gelu_parts(value):
    inner = 0.7978845608028654 * (value + 0.044715 * value * value * value)
    return jnp.tanh(inner)


def gelu_of(value):
    return 0.5 * value * (1.0 + gelu_parts(value))


class GatherPlan:
    def __init__(self, mine, out, send, recv, local):
        self.mine, self.out = mine, out
        self.send, self.recv, self.local = send, recv, local
        self.core, self.first_mask, self.second_mask, self.at, self.sibling = neighbours(4)
        self.far_peers = [self.at(4 * k) for k in range(1, 4)]

    def peers(self):
        return [*self.far_peers, self.at(self.first_mask), self.at(self.second_mask), self.sibling]

    def copy(self, w, slot, source, target, peer):
        return pltpu.make_async_remote_copy(
            src_ref=source,
            dst_ref=target,
            send_sem=self.send.at[w, slot],
            recv_sem=self.recv.at[w, slot],
            device_id=peer,
            device_id_type=MESH,
        )

    def block(self, w, q):
        return self.out[w].at[self.core, :, q]

    def far(self, w, k):
        return self.copy(
            w, k - 1, self.mine[w], self.out[w].at[self.core, k, 0], self.far_peers[k - 1]
        )

    def keep(self, w):
        return pltpu.make_async_copy(
            self.mine[w], self.out[w].at[self.core, 0, 0], self.local.at[w]
        )

    def first(self, w):
        mask = self.first_mask
        return self.copy(w, 3, self.block(w, 0), self.block(w, mask), self.at(mask))

    def second(self, w):
        mask = self.second_mask
        return self.copy(w, 4, self.block(w, 0), self.block(w, mask), self.at(mask))

    def both(self, w):
        return self.copy(
            w, 5, self.block(w, self.first_mask), self.block(w, 3), self.at(self.second_mask)
        )

    def twin(self, w, n):
        q = (0, self.first_mask, self.second_mask, 3)[n]
        return self.copy(w, 6 + n, self.block(w, q), self.block(w, q), self.sibling)

    def begin(self, w):
        self.keep(w).start()
        for k in range(1, 4):
            self.far(w, k).start()

    def spread(self, w):
        self.keep(w).wait()
        for k in range(1, 4):
            self.far(w, k).wait_recv()
        self.first(w).start()
        self.second(w).start()
        self.twin(w, 0).start()

    def cross(self, w):
        self.first(w).wait_recv()
        self.both(w).start()
        self.twin(w, 1).start()
        self.second(w).wait_recv()
        self.twin(w, 2).start()

    def close(self, w):
        self.both(w).wait_recv()
        self.twin(w, 3).start()

    def ready(self, w):
        for n in range(4):
            self.twin(w, n).wait_recv()

    def finish(self, w):
        for k in range(1, 4):
            self.far(w, k).wait_send()
        self.first(w).wait_send()
        self.second(w).wait_send()
        self.both(w).wait_send()
        for n in range(4):
            self.twin(w, n).wait_send()


def stream(weight, tiles, buffer, semaphore, body):
    depth = buffer.shape[0]
    height = weight.shape[3]

    def copy(index):
        half, start, size = tiles[index]
        slot = index % depth
        return pltpu.make_async_copy(
            weight.at[half, :, :, :, pl.ds(start, size)],
            buffer.at[slot, :, :, pl.ds(0, height), pl.ds(0, size)],
            semaphore.at[slot],
        )

    for index in range(min(depth - 1, len(tiles))):
        copy(index).start()
    for index, (_, _, size) in enumerate(tiles):
        if index + depth - 1 < len(tiles):
            copy(index + depth - 1).start()
        copy(index).wait()
        body(index, buffer[index % depth, :, :, :height, :size].reshape(16 * height, size))


def tiles_of(width, size, halves=(0, 1)):
    return [
        (half, start, min(size, width - start)) for half in halves for start in range(0, width, size)
    ]


def forward_body(batch, scaling, *refs):
    refs = list(refs)
    take = refs.pop
    latent, skip, skip_gain, gains, shift = (take(0) for _ in range(5))
    order, order_skip, heads_ref = (take(0) for _ in range(3))
    tables = [take(0) for _ in range(3)]
    text, valid = take(0), take(0)
    mine = [take(0) for _ in range(7)]
    out = [take(0) for _ in range(7)]
    normed, hidden, attn_in, qkv, keyval_here, keyval_there = (take(0) for _ in range(6))
    attn_cat, after_self, cross_in, cq_proj, ckey_mine, cross_keyval = (take(0) for _ in range(6))
    cross_cat, after_cross, mlp_in, upper, activated = (take(0) for _ in range(5))
    self_peak, cross_peak = take(0), take(0)
    wide, narrow, buffer, semaphore, send, recv, local, twin_send, twin_recv = refs
    rows, width = hidden.shape
    size = rows // batch
    me = lax.axis_index("fsdp")
    core = lax.axis_index("seq")
    plan = GatherPlan(mine, out, send, recv, local)
    skip_w, qkv_w, pair_w, query_w, keyval_w, up_w, down_w = range(7)

    greet(plan.peers())
    for w in range(7):
        plan.begin(w)

    def each(body):
        for b in range(batch):
            body(b, pl.ds(b * size, size))

    def reorder(value):
        return dot_plain(value, order[...]).astype(bf16)

    upper_half = me >= 8

    def normed_part(b, rows_b):
        left = latent[rows_b, :].astype(f32)
        right = skip[rows_b, :].astype(f32)
        mean = (
            jnp.sum(left, axis=1, keepdims=True) + jnp.sum(right, axis=1, keepdims=True)
        ) / (2 * width)
        left, right = left - mean, right - mean
        spread = (
            jnp.sum(left * left, axis=1, keepdims=True)
            + jnp.sum(right * right, axis=1, keepdims=True)
        ) / (2 * width)
        factor = lax.rsqrt(spread + norm_eps)
        left = (left * factor * skip_gain[:, :width]).astype(bf16)
        right = (right * factor * skip_gain[:, width:]).astype(bf16)
        near = jnp.where(upper_half, right, left)
        away = jnp.where(upper_half, left, right)
        for half in range(2):
            normed[half, 0, rows_b, :] = dot_plain(near, order_skip[half]).astype(bf16)
            normed[half, 1, rows_b, :] = dot_plain(away, order_skip[half]).astype(bf16)

    each(normed_part)
    plan.spread(skip_w)
    plan.spread(qkv_w)
    plan.cross(skip_w)
    plan.spread(pair_w)
    plan.cross(qkv_w)
    plan.close(skip_w)
    plan.ready(skip_w)

    skip_tiles = tiles_of(width, 512)

    def skip_product(index, tile):
        half, start, extent = skip_tiles[index]
        cut = tile.shape[0] // 2
        value = dot_plain(normed[half, 0], tile[:cut]) + dot_plain(normed[half, 1], tile[cut:])
        lanes = pl.ds(start, extent)
        if half == 0:
            hidden[:, lanes] = value
        else:
            hidden[:, lanes] += value

    stream(out[skip_w], skip_tiles, buffer, semaphore, skip_product)

    def attn_in_part(b, rows_b):
        value = layer_norm(hidden[rows_b, :]) * gains[0:1, :] + shift[b : b + 1, :]
        attn_in[rows_b, :] = reorder(value.astype(bf16))

    each(attn_in_part)
    plan.spread(query_w)
    plan.cross(pair_w)
    plan.close(qkv_w)
    plan.ready(qkv_w)

    qkv_tiles = tiles_of(out[qkv_w].shape[4], 512)

    def qkv_product(index, tile):
        half, start, extent = qkv_tiles[index]
        value = dot_plain(attn_in[...], tile)
        for at in range(0, extent, 128):
            lane = start + at
            piece = value[:, at : at + 128]
            if lane < width:
                qkv[:, pl.ds(half * width + lane, 128)] = piece
            else:
                place = lane - width + half * 768
                if place < width:
                    keyval_here[:, pl.ds(width + place, 128)] = piece.astype(bf16)

    stream(out[qkv_w], qkv_tiles, buffer, semaphore, qkv_product)

    def key_part(b, rows_b):
        value, _ = head_norm(qkv[rows_b, pl.ds(width, width)], heads_ref)
        keyval_here[rows_b, pl.ds(0, width)] = turn(value, tables).astype(bf16)

    each(key_part)
    exchange = pltpu.make_async_remote_copy(
        src_ref=keyval_here,
        dst_ref=keyval_there,
        send_sem=twin_send,
        recv_sem=twin_recv,
        device_id=plan.sibling,
        device_id_type=MESH,
    )
    exchange.start()

    def query_part(b, rows_b):
        value, _ = head_norm(qkv[rows_b, pl.ds(0, width)], heads_ref)
        narrow[rows_b, :] = turn(value, tables).astype(bf16)

    each(query_part)
    plan.spread(keyval_w)
    plan.cross(query_w)
    plan.close(pair_w)
    exchange.wait()

    def attend(sources, peak, target, masked):
        peak[...] = jnp.full_like(peak, masked_value)
        wide[...] = jnp.zeros_like(wide)

        @pl.loop(0, batch)
        def _(b):
            rows_b = pl.ds(pl.multiple_of(b * size, size), size)
            for head in range(HEADS):
                lanes, inside = window_of(head, width)
                query = narrow[rows_b, lanes] * inside.astype(bf16)
                scores = dot_right_t(query, pair_rows(sources, b, size, lanes)) * scaling
                if masked:
                    scores = jnp.where(valid[pl.ds(b, 1), :] > 0.5, scores, masked_value)
                probs, largest = softmax_of(scores)
                largest = jnp.max(largest, axis=0, keepdims=True)
                peak[head : head + 1, :] = jnp.maximum(
                    peak[head : head + 1, :], jnp.broadcast_to(largest, (1, 128))
                )
                value = pair_rows(sources, b, size, shift_lanes(lanes, width))
                wide[rows_b, lanes] += dot_plain(probs.astype(bf16), value) * inside

        target[...] = reorder(wide[...].astype(bf16))

    attend([keyval_here, keyval_there], self_peak, attn_cat, False)
    plan.ready(pair_w)
    pair_tiles = tiles_of(width, 512)

    def out_product(source, before, after):
        def body(index, tile):
            lanes = pl.ds(pair_tiles[index][1], pair_tiles[index][2])
            after[:, lanes] = before[:, lanes] + dot_plain(source[...], tile)

        return body

    pair_body = out_product(attn_cat, hidden, after_self)
    stream(out[pair_w], tiles_of(width, 512, (0,)), buffer, semaphore, pair_body)

    def cross_in_part(b, rows_b):
        value = layer_norm(after_self[rows_b, :]) * gains[1:2, :]
        cross_in[rows_b, :] = reorder(value.astype(bf16))

    each(cross_in_part)
    plan.spread(up_w)
    plan.cross(keyval_w)
    plan.close(query_w)
    plan.ready(query_w)
    query_tiles = tiles_of(out[query_w].shape[4], 512)

    def query_product(index, tile):
        half, start, extent = query_tiles[index]
        place = half * out[query_w].shape[4] + start
        extent = min(extent, width - place)
        cq_proj[:, pl.ds(place, extent)] = dot_plain(cross_in[...], tile)[:, :extent]

    stream(out[query_w], query_tiles, buffer, semaphore, query_product)

    def cross_query_part(b, rows_b):
        narrow[rows_b, :] = head_norm(cq_proj[rows_b, :], heads_ref)[0].astype(bf16)

    each(cross_query_part)
    plan.spread(down_w)
    plan.close(keyval_w)
    plan.ready(keyval_w)
    keyval_tiles = tiles_of(width, 512)

    def keyval_product(index, tile):
        half, start, extent = keyval_tiles[index]
        value = dot_plain(text[...], tile)
        if half == 0:
            upper[:, pl.ds(start, extent)] = value[:rows]
            upper[:, pl.ds(width + start, extent)] = value[rows:]
        else:
            cross_keyval[:, pl.ds(width + start, extent)] = value.astype(bf16)

    stream(out[keyval_w], keyval_tiles, buffer, semaphore, keyval_product)
    for b in range(batch):
        for at in range(2):
            part = pl.ds(at * size, size)
            lanes = pl.ds(b * width, width)
            cross_keyval[pl.ds(b * 2 * size + at * size, size), pl.ds(0, width)] = head_norm(
                upper[part, lanes], heads_ref
            )[0].astype(bf16)
        ckey_mine[pl.ds(b * size, size), :] = upper[
            pl.ds(pl.multiple_of(core * size, size), size), pl.ds(b * width, width)
        ]
    attend([cross_keyval], cross_peak, cross_cat, True)
    pair_body = out_product(cross_cat, after_self, after_cross)
    stream(out[pair_w], tiles_of(width, 512, (1,)), buffer, semaphore, pair_body)

    def mlp_in_part(b, rows_b):
        value = layer_norm(after_cross[rows_b, :]) * gains[2:3, :]
        mlp_in[rows_b, :] = reorder(value.astype(bf16))

    each(mlp_in_part)
    plan.cross(up_w)
    plan.close(up_w)
    plan.ready(up_w)
    block = activated.shape[1] // 16
    up_tiles = tiles_of(out[up_w].shape[4], block)

    def up_product(index, tile):
        value = dot_plain(mlp_in[...], tile)
        upper[:, pl.ds(index * block, block)] = value
        slot = jnp.bitwise_xor(me, index)
        activated[:, pl.ds(pl.multiple_of(slot * block, block), block)] = gelu_of(value).astype(bf16)

    stream(out[up_w], up_tiles, buffer, semaphore, up_product)
    plan.cross(down_w)
    plan.close(down_w)
    plan.ready(down_w)
    for w in range(7):
        plan.finish(w)


class Links:
    def __init__(self, fsdp_count):
        self.count = fsdp_count
        self.me = lax.axis_index("fsdp")
        self.core = lax.axis_index("seq")
        self.high_bits = fsdp_count.bit_length() - 3
        self.quad = 4 << (self.high_bits - 2)
        offsets = [0]
        for bit in range(self.high_bits - 2):
            offsets = offsets + [offset | (4 << bit) for offset in offsets]
        self.high_offsets = [k * self.quad | offset for k in range(4) for offset in offsets]

    def swap(self, value, mask_first, mask_second):
        pairs = []
        for index in range(self.count):
            pairs.append((2 * index, 2 * (index ^ mask_first)))
            pairs.append((2 * index + 1, 2 * (index ^ mask_second) + 1))
        return lax.ppermute(value, ("fsdp", "seq"), pairs)

    def sibling(self, value):
        return lax.ppermute(value, "seq", [(0, 1), (1, 0)])

    def pick(self, first, second):
        return jnp.where(self.core == 0, first, second)

    def offset(self, block):
        return self.high_offsets[block % (self.count // 4)] | (block // (self.count // 4))

    def place(self, offset):
        table = [0] * self.count
        for block in range(self.count):
            table[self.offset(block)] = block
        return jnp.array(table, jnp.int32)[offset]

    def columns(self, own, other):
        return self.pick(
            jnp.concatenate([own, other], axis=-1), jnp.concatenate([other, own], axis=-1)
        )

    def halves(self, value):
        half = value.shape[-1] // 2
        first, second = value[..., :half], value[..., half:]
        return self.pick(first, second), self.pick(second, first)

    def order_matrix(self, size):
        block = size // self.count
        at = lax.broadcasted_iota(jnp.int32, (size, size), 0)
        table = jnp.array([self.offset(b) for b in range(self.count)], jnp.int32)
        starts = jnp.bitwise_xor(self.me, table) * block
        wanted = (starts[:, None] + jnp.arange(block, dtype=jnp.int32)[None, :]).reshape(1, size)
        return (at == wanted).astype(bf16)

    def order_skip(self, width):
        block = width // self.count
        offsets = [
            offset & (self.count // 2 - 1) for offset in self.high_offsets[: self.count // 2 // 4 * 1]
        ]
        offsets = [offset | q for q in range(4) for offset in offsets]
        lower = jnp.bitwise_and(self.me, self.count // 2 - 1)
        starts = jnp.bitwise_xor(lower, jnp.array(offsets, jnp.int32)) * (2 * block)
        starts = jnp.stack([starts, starts + block])
        wanted = (starts[:, :, None] + jnp.arange(block, dtype=jnp.int32)).reshape(1, width)
        return (lax.broadcasted_iota(jnp.int32, (width, width), 0) == wanted).astype(bf16)

    def order_blocks(self, value):
        size = value.shape[1] // self.count
        parts = []
        for block in range(self.count):
            source = jnp.bitwise_xor(self.me, self.offset(block))
            parts.append(lax.dynamic_slice_in_dim(value, source * size, size, 1))
        return jnp.concatenate(parts, axis=1)

    def restore_blocks(self, value):
        size = value.shape[1] // self.count
        parts = []
        for shard in range(self.count):
            source = self.place(jnp.bitwise_xor(self.me, shard))
            parts.append(lax.dynamic_slice_in_dim(value, source * size, size, 1))
        return jnp.concatenate(parts, axis=1)

    def extra_gather(self, mine):
        blocks = mine
        for bit in range(self.high_bits - 2):
            blocks = jnp.concatenate([blocks, self.swap(blocks, 4 << bit, 4 << bit)], axis=0)
        return blocks

    def extra_scatter(self, value):
        for bit in reversed(range(self.high_bits - 2)):
            size = value.shape[-2] // 2
            value = value[..., :size, :] + self.swap(value[..., size:, :], 4 << bit, 4 << bit)
        return value


class Gather:
    def __init__(self, links, shards):
        self.links = links
        half = shards[0].shape[1] // 2
        self.rows = shards[0].shape[0]
        self.weights = len(shards)
        self.shards = jnp.concatenate(
            [links.pick(shard[:, :half], shard[:, half:]) for shard in shards], axis=0
        )
        self.pending = [self.shards]
        self.stage = 0

    def advance(self):
        links = self.links
        self.stage += 1
        if self.stage == 1:
            blocks = [self.pending[0]]
            for bit in range(links.high_bits - 2):
                got = links.swap(jnp.concatenate(blocks, axis=0), 4 << bit, 4 << bit)
                size = self.rows * self.weights
                blocks = blocks + [got[at * size : (at + 1) * size] for at in range(len(blocks))]
            self.low_blocks = len(blocks)
            mine = jnp.concatenate(blocks, axis=0) if len(blocks) > 1 else blocks[0]
            self.pending = [mine] + [
                links.swap(mine, k * links.quad, k * links.quad) for k in range(1, 4)
            ]
        elif self.stage == 2:
            size = self.rows * self.weights
            cuts = [
                got[at * size + w * self.rows : at * size + (w + 1) * self.rows]
                for w in range(self.weights)
                for got in self.pending
                for at in range(self.low_blocks)
            ]
            base = jnp.concatenate(cuts, axis=0)
            self.pending = [
                base, links.swap(base, 1, 2), links.swap(base, 2, 1), links.sibling(base)
            ]
        elif self.stage == 3:
            base, first, second, base_there = self.pending
            self.kept = [base, second, base_there]
            self.pending = [
                links.swap(first, 2, 1), links.sibling(first), links.sibling(second), *self.pending
            ]
        elif self.stage == 4:
            self.pending[0:1] = [links.sibling(self.pending[0]), self.pending[0]]
        elif self.stage == 5:
            both_there, both, first_there, second_there, base, first, second, base_there = self.pending
            size = base.shape[0] // self.weights
            self.result = []
            for w in range(self.weights):
                cut = slice(w * size, (w + 1) * size)
                pick = links.pick
                own = jnp.concatenate(
                    [base[cut], pick(first[cut], second[cut]), pick(second[cut], first[cut]), both[cut]],
                    axis=0,
                )
                other = jnp.concatenate(
                    [
                        base_there[cut],
                        pick(second_there[cut], first_there[cut]),
                        pick(first_there[cut], second_there[cut]),
                        both_there[cut],
                    ],
                    axis=0,
                )
                self.result.append((own, other))
            self.pending = []

    def finish(self):
        while self.stage < 5:
            self.advance()
        return self.result


class Scatter:
    def __init__(self, links, pairs):
        self.links = links
        self.pairs = pairs
        self.pending = [other for _, other in pairs]
        self.stage = 0

    def advance(self):
        links = self.links
        pick = links.pick
        self.stage += 1
        if self.stage == 1:
            self.pending = [own for own, _ in self.pairs] + [
                links.sibling(other) for other in self.pending
            ]
        elif self.stage == 2:
            count = len(self.pairs)
            send, keep = [[], []], [[], []]
            for own, got in zip(self.pending[:count], self.pending[count:]):
                size = own.shape[0] // 4
                cuts = [
                    own[q * size : (q + 1) * size].astype(f32) + got[q * size : (q + 1) * size].astype(f32)
                    for q in range(4)
                ]
                send[0].append(pick(cuts[2], cuts[1]).astype(bf16))
                send[1].append(cuts[3].astype(bf16))
                keep[0].append(cuts[0])
                keep[1].append(pick(cuts[1], cuts[2]))
            self.sizes = [part.shape[0] for part in keep[0]]
            self.keep = [jnp.concatenate(part, axis=0) for part in keep]
            self.pending = [links.swap(jnp.concatenate(send[0] + send[1], axis=0), 2, 1)]
        elif self.stage == 3:
            total = sum(self.sizes)
            got = self.pending[0].astype(f32)
            self.keep, send = self.keep[0] + got[:total], (self.keep[1] + got[total:]).astype(bf16)
            self.pending = [links.swap(send, 1, 2)]
        elif self.stage == 4:
            summed = self.keep + self.pending[0].astype(f32)
            keep, send = [], [[], [], []]
            start = 0
            for size in self.sizes:
                part = size // 4
                keep.append(summed[start : start + part])
                for k in range(1, 4):
                    send[k - 1].append(summed[start + k * part : start + (k + 1) * part].astype(bf16))
                start += size
            self.keep = jnp.concatenate(keep, axis=0)
            self.pending = [
                links.swap(jnp.concatenate(send[k - 1], axis=0), k * links.quad, k * links.quad)
                for k in range(1, 4)
            ]
        elif self.stage == 5:
            total = self.keep
            for got in self.pending:
                total = total + got.astype(f32)
            rows = [size // 4 for size in self.sizes]
            for bit in reversed(range(links.high_bits - 2)):
                keep, send, start = [], [], 0
                for at, size in enumerate(rows):
                    keep.append(total[start : start + size // 2])
                    send.append(total[start + size // 2 : start + size])
                    start += size
                    rows[at] = size // 2
                got = links.swap(jnp.concatenate(send, axis=0), 4 << bit, 4 << bit)
                total = jnp.concatenate(keep, axis=0) + got
            self.rows = rows
            self.pending = [total, links.sibling(total)]
        elif self.stage == 6:
            whole = links.columns(*self.pending)
            self.result, start = [], 0
            for size in self.rows:
                self.result.append(whole[start : start + size])
                start += size
            self.pending = []

    def finish(self):
        while self.stage < 6:
            self.advance()
        return self.result


def tie(value, *jobs):
    leaves, tree = jax.tree.flatten(value)
    flat = list(leaves)
    for job in jobs:
        flat.extend(job.pending)
    flat = list(lax.optimization_barrier(tuple(flat)))
    at = len(leaves)
    value = jax.tree.unflatten(tree, flat[:at])
    for job in jobs:
        job.pending = flat[at : at + len(job.pending)]
        at += len(job.pending)
        job.advance()
    return value


def parts_of(value):
    high = value.astype(bf16)
    return high, (value - high.astype(f32)).astype(bf16)


def sum_heads(value, heads_ref):
    high, low = parts_of(value)
    return dot_plain(high, heads_ref[...]) + dot_plain(low, heads_ref[...])


def spread_heads(value, heads_ref):
    high, low = parts_of(value)
    return dot_right_t(high, heads_ref[...]) + dot_right_t(low, heads_ref[...])


def head_norm(value, heads_ref):
    center = value - spread_heads(sum_heads(value, heads_ref) * (1.0 / HD), heads_ref)
    spread = sum_heads(center * center, heads_ref) * (1.0 / HD)
    factor = spread_heads(lax.rsqrt(spread + norm_eps), heads_ref)
    return center * factor, factor


def head_norm_back(grad, normed, factor, heads_ref):
    first = sum_heads(grad, heads_ref) * (1.0 / HD)
    second = sum_heads(grad * normed, heads_ref) * (1.0 / HD)
    return factor * (
        grad - spread_heads(first, heads_ref) - normed * spread_heads(second, heads_ref)
    )


def partner(value, former):
    quarter = HD // 4
    width = value.shape[1]
    up = pltpu.roll(value, width - quarter, 1)
    down = pltpu.roll(value, quarter, 1)
    return jnp.where(former > 0.5, up, down)


def turn(value, table_refs):
    cosine, sine, former = table_refs
    return value * cosine[...] + partner(value, former[...]) * sine[...]


def turn_back(value, table_refs):
    cosine, sine, former = table_refs
    return value * cosine[...] - partner(value, former[...]) * sine[...]


def window_of(head, width):
    start = min(head * HD // 128 * 128, width - 256)
    lane = lax.broadcasted_iota(jnp.int32, (1, 256), 1) + start
    inside = jnp.logical_and(lane >= head * HD, lane < (head + 1) * HD)
    return pl.ds(start, 256), inside.astype(f32)


def normed_rows(proj_ref, heads_ref, table_refs, rows):
    value, factor = head_norm(proj_ref[rows, :], heads_ref)
    turned = turn(value, table_refs) if table_refs else value
    return value, factor, turned


def keys_body(batch, turned, *refs):
    key_ref, value_ref, heads_ref = refs[:3]
    table_refs, out_ref = refs[3:-1], refs[-1]
    width = key_ref.shape[1]
    size = key_ref.shape[0] // batch
    for b in range(batch):
        rows = pl.ds(b * size, size)
        out_ref[rows, :width] = normed_rows(key_ref, heads_ref, table_refs, rows)[2].astype(bf16)
        out_ref[rows, width:] = value_ref[rows, :].astype(bf16)


def pair_rows(refs, b, size, lanes):
    if len(refs) == 2:
        return jnp.concatenate([ref[pl.ds(b * size, size), lanes] for ref in refs], axis=0)
    return refs[0][pl.ds(b * 2 * size, 2 * size), lanes]


def shift_lanes(lanes, width):
    return pl.ds(lanes.start + width, lanes.size)


def scores_of(query, key, lengths_ref, b, scaling):
    scores = dot_right_t(query, key) * scaling
    if lengths_ref is not None:
        column = lax.broadcasted_iota(jnp.int32, scores.shape, 1)
        scores = jnp.where(column < lengths_ref[b], scores, masked_value)
    return scores


def softmax_of(scores):
    largest = jnp.max(scores, axis=1, keepdims=True)
    raised = jnp.exp(scores - largest)
    return raised / jnp.sum(raised, axis=1, keepdims=True), largest


def attention_body(batch, masked, turned, sources, scaling, *refs):
    refs = list(refs)
    lengths_ref = refs.pop(0) if masked else None
    proj_ref, heads_ref = refs.pop(0), refs.pop(0)
    table_refs = [refs.pop(0) for _ in range(3)] if turned else []
    keyval_refs = [refs.pop(0) for _ in range(sources)]
    out_ref, peak_ref, query_ref, mixed_ref = refs
    size, width = proj_ref.shape[0] // batch, proj_ref.shape[1]
    peak_ref[...] = jnp.full_like(peak_ref, masked_value)
    mixed_ref[...] = jnp.zeros_like(mixed_ref)
    for b in range(batch):
        rows = pl.ds(b * size, size)
        query_ref[rows, :] = normed_rows(proj_ref, heads_ref, table_refs, rows)[2].astype(bf16)

    @pl.loop(0, batch)
    def _(b):
        rows = pl.ds(pl.multiple_of(b * size, size), size)
        for head in range(HEADS):
            lanes, inside = window_of(head, width)
            query = query_ref[rows, lanes] * inside.astype(bf16)
            key = pair_rows(keyval_refs, b, size, lanes)
            scores = scores_of(query, key, lengths_ref, b, scaling)
            probs, largest = softmax_of(scores)
            largest = jnp.max(largest, axis=0, keepdims=True)
            peak_ref[head : head + 1, :] = jnp.maximum(
                peak_ref[head : head + 1, :], jnp.broadcast_to(largest, (1, 128))
            )
            value = pair_rows(keyval_refs, b, size, shift_lanes(lanes, width))
            mixed_ref[rows, lanes] += dot_plain(probs.astype(bf16), value) * inside

    out_ref[...] = mixed_ref[...].astype(bf16)


def attention_back_body(batch, masked, turned, sources, scaling, *refs):
    refs = list(refs)
    lengths_ref = refs.pop(0) if masked else None
    proj_ref, grad_ref, heads_ref = refs.pop(0), refs.pop(0), refs.pop(0)
    table_refs = [refs.pop(0) for _ in range(3)] if turned else []
    keyval_refs = [refs.pop(0) for _ in range(sources)]
    out_ref, here_ref, there_ref, normed_ref, factor_ref, query_ref, back_ref, total_ref = refs
    size, width = proj_ref.shape[0] // batch, proj_ref.shape[1]
    back_ref[...] = jnp.zeros_like(back_ref)
    total_ref[...] = jnp.zeros_like(total_ref)
    for b in range(batch):
        rows = pl.ds(b * size, size)
        normed, factor, query = normed_rows(proj_ref, heads_ref, table_refs, rows)
        normed_ref[rows, :] = normed
        factor_ref[rows, :] = factor
        query_ref[rows, :] = query.astype(bf16)

    @pl.loop(0, batch)
    def _(b):
        rows = pl.ds(pl.multiple_of(b * size, size), size)
        for head in range(HEADS):
            lanes, inside = window_of(head, width)
            behind = shift_lanes(lanes, width)
            query = query_ref[rows, lanes] * inside.astype(bf16)
            key = pair_rows(keyval_refs, b, size, lanes)
            probs, _ = softmax_of(scores_of(query, key, lengths_ref, b, scaling))
            grad = grad_ref[rows, lanes] * inside.astype(bf16)
            value = pair_rows(keyval_refs, b, size, behind)
            prob_grad = dot_right_t(grad, value)
            score_grad = softmax_back(probs, prob_grad).astype(bf16)
            value_grad = dot_left_t(probs.astype(bf16), grad)
            key_grad = dot_left_t(score_grad, query) * scaling
            back_ref[rows, lanes] += dot_plain(score_grad, key) * (inside * scaling)
            for at in range(2):
                part = slice(at * size, (at + 1) * size)
                total_ref[at, rows, lanes] += key_grad[part]
                total_ref[at, rows, behind] += value_grad[part]

    for b in range(batch):
        rows = pl.ds(b * size, size)
        grad = back_ref[rows, :]
        if table_refs:
            grad = turn_back(grad, table_refs)
        out_ref[rows, :] = head_norm_back(
            grad, normed_ref[rows, :], factor_ref[rows, :], heads_ref
        ).astype(bf16)
    mine = lax.axis_index("seq") if masked else 0
    here_ref[...] = total_ref[mine]
    there_ref[...] = total_ref[1 - mine].astype(bf16)


def keys_back_body(batch, turned, *refs):
    key_ref, here_ref, from_there_ref, heads_ref = refs[:4]
    table_refs, out_ref = refs[4:-1], refs[-1]
    width = key_ref.shape[1]
    size = key_ref.shape[0] // batch
    for b in range(batch):
        rows = pl.ds(b * size, size)
        normed, factor, _ = normed_rows(key_ref, heads_ref, (), rows)
        grad = here_ref[rows, :width] + from_there_ref[rows, :width].astype(f32)
        if table_refs:
            grad = turn_back(grad, table_refs)
        out_ref[rows, :width] = head_norm_back(grad, normed, factor, heads_ref).astype(bf16)
        out_ref[rows, width:] = (
            here_ref[rows, width:] + from_there_ref[rows, width:].astype(f32)
        ).astype(bf16)


def plain_call(body, outs, blocks, scratch=(), lengths=None):
    def spec(array, column):
        if column is None:
            return pl.BlockSpec(array.shape, lambda i, *_: (0,) * array.ndim)
        return pl.BlockSpec((array.shape[0], column[1]), lambda i, *_: (0, column[0]))

    def out_spec(shape):
        return pl.BlockSpec(shape.shape, lambda i, *_: (0,) * len(shape.shape))

    grid_spec = pltpu.PrefetchScalarGridSpec(
        num_scalar_prefetch=0 if lengths is None else 1,
        grid=(1,),
        in_specs=[spec(*block) for block in blocks],
        out_specs=[out_spec(shape) for shape in outs],
        scratch_shapes=list(scratch),
    )
    given = [] if lengths is None else [lengths]
    return pl.pallas_call(
        body,
        grid_spec=grid_spec,
        out_shape=list(outs),
        compiler_params=pltpu.CompilerParams(vmem_limit_bytes=50 * 2**20),
    )(*given, *[array for array, _ in blocks])


def lanes_of(value, multiple):
    size = 128 * multiple
    spare = -value.shape[-1] % size
    value = jnp.pad(value, [(0, 0)] * (value.ndim - 1) + [(0, spare)])
    return value.reshape(*value.shape[:-1], -1, 128)


def exact_restore(matrix, value):
    high = value.astype(bf16)
    low = (value - high.astype(f32)).astype(bf16)
    return dot_right_t(high, matrix) + dot_right_t(low, matrix)


def local(
    latent,
    skip_input,
    condition,
    text_encoder_states,
    text_lengths,
    out_grad,
    skip_gain,
    norm_gains,
    skip_linear,
    shift_linear,
    self_qkv,
    self_out,
    cross_query,
    cross_keyval,
    cross_out,
    mlp_up,
    mlp_down,
    thresholds,
):
    batch, tokens, width = latent.shape
    rows = batch * tokens
    text_rows = text_encoder_states.shape[1]
    text_width = text_encoder_states.shape[2]
    scaling = HD ** (-0.5)
    links = Links(lax.axis_size("fsdp"))
    me, core = links.me, links.core
    count = links.count

    positions = core * tokens + jnp.arange(tokens)
    feature = jnp.arange(width) % HD
    freqs = 10000.0 ** (-(feature % (HD // 4)).astype(f32) / (HD // 4))
    place = jnp.where(
        feature[None, :] < HD // 2, (positions // GRID_W)[:, None], (positions % GRID_W)[:, None]
    )
    angles = place.astype(f32) * freqs[None, :]
    former = (feature % (HD // 2) < HD // 4)[None, :]
    cosine = jnp.cos(angles)
    sine = jnp.where(former, -jnp.sin(angles), jnp.sin(angles))
    tables = [(cosine, None), (sine, None), (former.astype(f32), None)]
    head_at = jnp.arange(width)[:, None] // HD == jnp.arange(128)[None, :]
    head_at = (head_at.astype(bf16), None)

    gain_rows = skip_gain.shape[0]
    third = norm_gains.shape[1]
    cond_act = jax.nn.silu(condition.astype(f32)).astype(bf16)
    small = jnp.concatenate([skip_gain, norm_gains.reshape(-1), cond_act.reshape(-1)])
    small = trade(lanes_of(small, 16), count, True, 1).reshape(count, -1)
    skip_gain_all = small[:, :gain_rows].reshape(-1).astype(f32)
    cond_start = gain_rows + 3 * third
    gains = small[:, gain_rows:cond_start].reshape(count, 3, third)
    gains = gains.transpose(1, 0, 2).reshape(3, width).astype(f32)
    cond_all = small[:, cond_start : cond_start + batch * width].reshape(count * batch, width)
    shift_rows = shift_linear.shape[0]
    cond_cut = lax.dynamic_slice_in_dim(cond_all, me * shift_rows, shift_rows, 1)
    shift_parts = dot_plain(cond_cut, shift_linear).reshape(count, batch * width)
    shift_parts = trade(lanes_of(shift_parts, 8), count, False, 2)
    shift = jnp.sum(shift_parts.reshape(count, -1), axis=0)[: batch * width].reshape(batch, width)

    def columns_mine(weight):
        half = weight.shape[1] // 2
        return links.pick(weight[:, :half], weight[:, half:])

    skip_half = skip_linear.shape[0] // 2
    shards = [
        links.pick(skip_linear[:skip_half], skip_linear[skip_half:]),
        columns_mine(self_qkv),
        links.pick(self_out, cross_out),
        columns_mine(cross_query),
        columns_mine(cross_keyval),
    ]
    shards = [links.extra_gather(shard) for shard in shards]
    shards = lax.optimization_barrier((shift, *shards))
    shift = shards[0]
    gathered = gather(shards[1:], links.quad, 3)
    w_skip, w_qkv, w_pair, w_query, w_keyval = (
        g.reshape(2, 16 * g.shape[2], g.shape[3]) for g in gathered
    )
    w_self_out, w_cross_out = w_pair[0], w_pair[1]
    get_up = Gather(links, [mlp_up])
    get_down = Gather(links, [mlp_down])
    w_skip = tie(w_skip, get_up, get_down)

    order = links.order_matrix(width)
    order_skip = links.order_skip(width)
    order_text = links.order_matrix(text_width)

    def product(value, weight):
        return jnp.concatenate([dot_plain(value, weight[0]), dot_plain(value, weight[1])], axis=1)

    def product_back(grad, weight):
        half = grad.shape[1] // 2
        return dot_right_t(grad[:, :half], weight[0]) + dot_right_t(grad[:, half:], weight[1])

    def sum_twins(own, other):
        there = links.sibling(dot_left_t(*other).astype(bf16))
        return own, there

    def finish_twins(own, there):
        value = (dot_left_t(*own) + there.astype(f32)).astype(bf16)
        return value.reshape(16, value.shape[0] // 16, value.shape[1])

    def column_grad(value, grad):
        own, other = links.halves(grad)
        return sum_twins((value, own), (value, other))

    def weight_grad(value, grad_halves):
        return (
            dot_left_t(value, grad_halves[0]).astype(bf16),
            dot_left_t(value, grad_halves[1]).astype(bf16),
        )

    def relative_product(value, weight):
        return links.columns(dot_plain(value, weight[0]), dot_plain(value, weight[1]))

    def relative_back(grad_halves, weight):
        return dot_right_t(grad_halves[0], weight[0]) + dot_right_t(grad_halves[1], weight[1])

    def reorder(value):
        return dot_plain(value, order).astype(bf16)

    def restore(value):
        return dot_right_t(value.astype(bf16), order).astype(bf16)

    joined = jnp.concatenate(
        [latent.reshape(rows, width), skip_input.reshape(rows, width)], axis=1
    ).astype(f32)
    normed = gained_norm(joined, skip_gain_all).astype(bf16)
    upper_half = (me >= count // 2).astype(jnp.int32)
    near = jnp.where(upper_half == 0, normed[:, :width], normed[:, width:])
    away = jnp.where(upper_half == 0, normed[:, width:], normed[:, :width])
    near = dot_plain(near, order_skip).astype(bf16).reshape(rows, 2, 4, 1, -1)
    away = dot_plain(away, order_skip).astype(bf16).reshape(rows, 2, 4, 1, -1)
    normed = jnp.concatenate([near, away], axis=3).reshape(rows, 2, width)
    normed = (normed[:, 0], normed[:, 1])
    hidden = dot_plain(normed[0], w_skip[0]) + dot_plain(normed[1], w_skip[1])

    def shifted(values, gain, moved):
        wide = jnp.broadcast_to(moved[:, None, :], (batch, tokens, width)).reshape(rows, width)
        return layer_norm(values) * gain + wide

    attn_in = reorder(shifted(hidden, gains[0], shift).astype(bf16))
    qkv_proj = product(attn_in, w_qkv)
    query_block, key_block, value_block = ((qkv_proj, (at, width)) for at in range(3))

    def shaped(height, breadth, dtype):
        return jax.ShapeDtypeStruct((height, breadth), dtype)

    (keyval_here,) = plain_call(
        functools.partial(keys_body, batch, True),
        [shaped(rows, 2 * width, bf16)],
        [key_block, value_block, head_at, *tables],
    )
    keyval_there = links.sibling(keyval_here)
    qkv_proj = tie(qkv_proj, get_up)
    keyvals = [(keyval_here, None), (keyval_there, None)]
    attention_scratch = [pltpu.VMEM((rows, width), bf16), pltpu.VMEM((rows, width), f32)]
    attn_cat, self_peak = plain_call(
        functools.partial(attention_body, batch, False, True, 2, scaling),
        [shaped(rows, width, bf16), shaped(HEADS, 128, f32)],
        [query_block, head_at, *tables, *keyvals],
        attention_scratch,
    )
    attn_cat = reorder(attn_cat)
    attn_cat = tie(attn_cat, get_down)
    after_self = hidden + dot_plain(attn_cat, w_self_out)
    cross_in = reorder(gained_norm(after_self, gains[1]).astype(bf16))
    cq_proj = product(cross_in, w_query)

    text = text_encoder_states.reshape(batch * text_rows, text_width)
    text_ordered = dot_plain(text, order_text).astype(bf16)
    ckv_proj = product(text_ordered, w_keyval)
    (cross_keyval_all,) = plain_call(
        functools.partial(keys_body, batch, False),
        [shaped(batch * text_rows, 2 * width, bf16)],
        [(ckv_proj, (0, width)), (ckv_proj, (1, width)), head_at],
    )
    cq_proj = tie(cq_proj, get_up)
    cross_cat, cross_peak = plain_call(
        functools.partial(attention_body, batch, True, False, 1, scaling),
        [shaped(rows, width, bf16), shaped(HEADS, 128, f32)],
        [(cq_proj, None), head_at, (cross_keyval_all, None)],
        attention_scratch,
        text_lengths,
    )
    cross_cat = reorder(cross_cat)
    after_cross = after_self + dot_plain(cross_cat, w_cross_out)
    mlp_in = reorder(gained_norm(after_cross, gains[2]).astype(bf16))
    mlp_in = tie(mlp_in, get_up, get_down)
    (w_up,) = get_up.finish()
    upper = relative_product(mlp_in, w_up)
    activated = links.order_blocks(gelu_tanh(upper).astype(bf16))

    down_in = out_grad.reshape(rows, width)
    result_grad = down_in.astype(f32)
    down_halves = links.halves(down_in)
    put_down = Scatter(links, [weight_grad(activated, down_halves)])
    put_down.advance()
    activated = tie(activated, put_down)
    (w_down,) = get_down.finish()
    block_out = (after_cross + relative_product(activated, w_down)).astype(bf16)
    act_grad = links.restore_blocks(relative_back(down_halves, w_down))
    upper_grad = jax.vjp(gelu_tanh, upper)[1](act_grad)[0].astype(bf16)
    upper_halves = links.halves(upper_grad)
    put_up = Scatter(links, [weight_grad(mlp_in, upper_halves)])
    put_up.advance()
    mlp_in_grad = exact_restore(order, relative_back(upper_halves, w_up))
    cross_part, gain_third = jax.vjp(gained_norm, after_cross, gains[2])[1](mlp_in_grad)
    cross_grad = result_grad + cross_part
    cross_bf = tie(cross_grad.astype(bf16), put_up)
    cmix_grad = restore(dot_right_t(cross_bf, w_cross_out))
    cmix_grad = tie(cmix_grad, put_down)
    back_scratch = [
        pltpu.VMEM((rows, width), f32),
        pltpu.VMEM((rows, width), f32),
        pltpu.VMEM((rows, width), bf16),
        pltpu.VMEM((rows, width), f32),
        pltpu.VMEM((2, rows, 2 * width), f32),
    ]
    back_outs = [
        shaped(rows, width, bf16), shaped(rows, 2 * width, f32), shaped(rows, 2 * width, bf16)
    ]
    cq_grad, ckeyval_mine, ckeyval_theirs = plain_call(
        functools.partial(attention_back_body, batch, True, False, 1, scaling),
        back_outs,
        [(cq_proj, None), (cmix_grad, None), head_at, (cross_keyval_all, None)],
        back_scratch,
        text_lengths,
    )
    put_query = column_grad(cross_in, cq_grad)
    cq_grad = tie(cq_grad, put_up, put_down)
    cross_in_grad = exact_restore(order, product_back(cq_grad, w_query))
    self_part, gain_second = jax.vjp(gained_norm, after_self, gains[1])[1](cross_in_grad)
    self_grad = cross_grad + self_part

    text_half = text_rows // 2
    ckey_mine = lax.dynamic_slice_in_dim(
        ckv_proj.reshape(batch, text_rows, 2 * width)[:, :, :width], core * text_half, text_half, 1
    ).reshape(batch * text_half, width)
    (keyval_grad,) = plain_call(
        functools.partial(keys_back_body, batch, False),
        [shaped(batch * text_half, 2 * width, bf16)],
        [
            (ckey_mine, None),
            (ckeyval_mine, None),
            (links.sibling(ckeyval_theirs), None),
            head_at,
        ],
    )
    text_mine = lax.dynamic_slice_in_dim(
        text_ordered.reshape(batch, text_rows, text_width), core * text_half, text_half, 1
    ).reshape(-1, text_width)
    put_keyval = column_grad(text_mine, keyval_grad)
    grad_text = exact_restore(order_text, product_back(keyval_grad, w_keyval))
    grad_text = grad_text.reshape(batch, text_half, text_width)

    self_bf = self_grad.astype(bf16)
    put_pair = sum_twins(
        (links.pick(attn_cat, cross_cat), links.pick(self_bf, cross_bf)),
        (links.pick(cross_cat, attn_cat), links.pick(cross_bf, self_bf)),
    )
    self_bf = tie(self_bf, put_down)
    mix_grad = restore(dot_right_t(self_bf, w_self_out))
    mix_grad = tie(mix_grad, put_up)
    query_grad, here, there = plain_call(
        functools.partial(attention_back_body, batch, False, True, 2, scaling),
        back_outs,
        [query_block, (mix_grad, None), head_at, *tables, *keyvals],
        back_scratch,
    )
    here = tie(here, put_up)
    (key_value_grad,) = plain_call(
        functools.partial(keys_back_body, batch, True),
        [shaped(rows, 2 * width, bf16)],
        [key_block, (here, None), (links.sibling(there), None), head_at, *tables],
    )
    qkv_grad = jnp.concatenate([query_grad, key_value_grad], axis=1)
    put_qkv = column_grad(attn_in, qkv_grad)
    attn_in_grad = exact_restore(order, product_back(qkv_grad, w_qkv))
    hidden_part, gain_first, shift_grad = jax.vjp(shifted, hidden, gains[0], shift)[1](
        attn_in_grad
    )
    hidden_grad = self_grad + hidden_part
    hidden_bf = hidden_grad.astype(bf16)
    put_skip = sum_twins(
        (links.pick(*normed), hidden_bf), (links.pick(normed[1], normed[0]), hidden_bf)
    )
    normed_grad = jnp.concatenate(
        [dot_right_t(hidden_bf, w_skip[0]), dot_right_t(hidden_bf, w_skip[1])], axis=1
    ).reshape(rows, 2, 4, 2, -1)
    near_grad = exact_restore(order_skip, normed_grad[:, :, :, 0].reshape(rows, width))
    away_grad = exact_restore(order_skip, normed_grad[:, :, :, 1].reshape(rows, width))
    normed_grad = jnp.concatenate(
        [
            jnp.where(upper_half == 0, near_grad, away_grad),
            jnp.where(upper_half == 0, away_grad, near_grad),
        ],
        axis=1,
    )
    joined_grad, skip_gain_grad = jax.vjp(gained_norm, joined, skip_gain_all)[1](normed_grad)

    sums = [
        finish_twins(*put) for put in (put_pair, put_query, put_keyval, put_qkv, put_skip)
    ]
    (grad_down,) = put_down.finish()
    (grad_up,) = put_up.finish()
    scattered = [links.extra_scatter(part) for part in scatter(sums, links.quad, 4)]
    grad_self_out, grad_cross_out = scattered[0][0], scattered[0][1]
    grad_cross_query, grad_keyval, grad_qkv = (
        jnp.concatenate([part[0], part[1]], axis=1) for part in scattered[1:4]
    )
    grad_skip_linear = scattered[4].reshape(skip_linear.shape)

    gains_grad = jnp.stack([gain_first, gain_second, gain_third])
    gains_grad = gains_grad.reshape(3, count, third).transpose(1, 0, 2).reshape(count, 3 * third)
    gains_grad = jnp.concatenate([skip_gain_grad.reshape(count, gain_rows), gains_grad], axis=1)
    peaks = jnp.stack([self_peak[:, 0], cross_peak[:, 0]])
    cores = jnp.concatenate([shift_grad.reshape(-1), gains_grad.reshape(-1), peaks.reshape(-1)])
    there = links.sibling(cores)
    peaks = jnp.maximum(cores, there)[-2 * HEADS :]
    cores = cores + there
    ends = (batch * width, batch * width + count * cond_start)
    gains_grad = cores[ends[0] : ends[1]].reshape(count, cond_start)
    shift_bf = cores[: ends[0]].astype(bf16).astype(f32)
    shared = trade(lanes_of(jnp.concatenate([shift_bf, peaks]), 8), count, True, 5)
    shared = shared.reshape(count, -1)
    shift_all = shared[:, : ends[0]].reshape(count * batch, width).astype(bf16)
    peaks = jnp.max(shared[:, ends[0] : ends[0] + 2 * HEADS], axis=0).reshape(2, HEADS)
    grad_shift = dot_left_t(cond_cut, shift_all)
    cond_back = dot_right_t(shift_all, shift_linear).reshape(count, batch * shift_rows)
    owned = trade(lanes_of(jnp.concatenate([cond_back, gains_grad], axis=1), 8), count, False, 6)
    owned = owned.reshape(count, -1)
    cond_mine = owned[:, : batch * shift_rows].reshape(count, batch, shift_rows)
    cond_mine = cond_mine.transpose(1, 0, 2).reshape(batch, width)
    grad_cond = jax.vjp(jax.nn.silu, condition.astype(f32))[1](cond_mine)[0]
    own_gains = jnp.sum(owned[:, batch * shift_rows : batch * shift_rows + cond_start], axis=0)
    grad_skip_gain = own_gains[:gain_rows]
    grad_gains = own_gains[gain_rows:].reshape(3, third)

    roots = jnp.sqrt(thresholds / jnp.maximum(peaks, thresholds))
    self_cols = jnp.repeat(roots[0], HD)
    cross_cols = jnp.repeat(roots[1], HD)
    unit_cols = jnp.ones((width,), f32)
    clipped_qkv = (
        self_qkv.astype(f32) * jnp.concatenate([self_cols, self_cols, unit_cols])[None, :]
    ).astype(bf16)
    clipped_query = (cross_query.astype(f32) * cross_cols[None, :]).astype(bf16)
    clipped_keyval = (
        cross_keyval.astype(f32) * jnp.concatenate([cross_cols, unit_cols])[None, :]
    ).astype(bf16)
    return (
        block_out.reshape(batch, tokens, width),
        joined_grad[:, :width].reshape(batch, tokens, width),
        joined_grad[:, width:].reshape(batch, tokens, width),
        grad_cond,
        grad_text,
        grad_skip_gain,
        grad_gains,
        grad_skip_linear,
        grad_shift,
        grad_qkv,
        grad_self_out,
        grad_cross_query,
        grad_keyval,
        grad_cross_out,
        grad_up,
        grad_down,
        clipped_qkv,
        clipped_query,
        clipped_keyval,
        peaks,
    )


def local_sixteen(
    latent,
    skip_input,
    condition,
    text_encoder_states,
    text_lengths,
    out_grad,
    skip_gain,
    norm_gains,
    skip_linear,
    shift_linear,
    self_qkv,
    self_out,
    cross_query,
    cross_keyval,
    cross_out,
    mlp_up,
    mlp_down,
    thresholds,
):
    batch, tokens, width = latent.shape
    rows = batch * tokens
    text_rows = text_encoder_states.shape[1]
    text_width = text_encoder_states.shape[2]
    scaling = HD ** (-0.5)
    links = Links(lax.axis_size("fsdp"))
    me, core = links.me, links.core
    count = links.count

    positions = core * tokens + jnp.arange(tokens)
    feature = jnp.arange(width) % HD
    freqs = 10000.0 ** (-(feature % (HD // 4)).astype(f32) / (HD // 4))
    place = jnp.where(
        feature[None, :] < HD // 2, (positions // GRID_W)[:, None], (positions % GRID_W)[:, None]
    )
    angles = place.astype(f32) * freqs[None, :]
    former = (feature % (HD // 2) < HD // 4)[None, :]
    cosine = jnp.cos(angles)
    sine = jnp.where(former, -jnp.sin(angles), jnp.sin(angles))
    tables = [(cosine, None), (sine, None), (former.astype(f32), None)]
    head_at = jnp.arange(width)[:, None] // HD == jnp.arange(128)[None, :]
    head_at = (head_at.astype(bf16), None)

    gain_rows = skip_gain.shape[0]
    third = norm_gains.shape[1]
    cond_act = jax.nn.silu(condition.astype(f32)).astype(bf16)
    small = jnp.concatenate([skip_gain, norm_gains.reshape(-1), cond_act.reshape(-1)])
    small = trade(lanes_of(small, 16), count, True, 1).reshape(count, -1)
    skip_gain_all = small[:, :gain_rows].reshape(-1).astype(f32)
    cond_start = gain_rows + 3 * third
    gains = small[:, gain_rows:cond_start].reshape(count, 3, third)
    gains = gains.transpose(1, 0, 2).reshape(3, width).astype(f32)
    cond_all = small[:, cond_start : cond_start + batch * width].reshape(count * batch, width)
    shift_rows = shift_linear.shape[0]
    cond_cut = lax.dynamic_slice_in_dim(cond_all, me * shift_rows, shift_rows, 1)
    shift_parts = dot_plain(cond_cut, shift_linear).reshape(count, batch * width)
    shift_parts = trade(lanes_of(shift_parts, 8), count, False, 2)
    shift = jnp.sum(shift_parts.reshape(count, -1), axis=0)[: batch * width].reshape(batch, width)

    def halves_of(weight):
        cut = (weight.shape[1] // 2 + 127) // 128 * 128
        first, second = weight[:, :cut], weight[:, cut:]
        return first, jnp.pad(second, ((0, 0), (0, cut - second.shape[1])))

    def qkv_halves(value):
        edge = 2 * width + 768
        first = jnp.concatenate([value[:, :width], value[:, 2 * width : edge]], axis=1)
        rest = jnp.pad(value[:, edge:], ((0, 0), (0, 2 * 768 - width)))
        return first, jnp.concatenate([value[:, width : 2 * width], rest], axis=1)

    def qkv_whole(first, second):
        last = second[:, width : 2 * width - 768]
        return jnp.concatenate(
            [first[:, :width], second[:, :width], first[:, width:], last], axis=1
        )

    skip_half = skip_linear.shape[0] // 2
    shards = [
        links.pick(skip_linear[:skip_half], skip_linear[skip_half:]),
        links.pick(*qkv_halves(self_qkv)),
        links.pick(self_out, cross_out),
        links.pick(*halves_of(cross_query)),
        links.pick(*halves_of(cross_keyval)),
        links.pick(*halves_of(mlp_up)),
        links.pick(*halves_of(mlp_down)),
    ]
    block = width // 16

    def one_hot(starts, size, height):
        wanted = (starts[:, None] + jnp.arange(size, dtype=jnp.int32)).reshape(1, -1)
        rows_at = lax.broadcasted_iota(jnp.int32, (height, wanted.shape[1]), 0)
        return (rows_at == wanted).astype(bf16)

    slots = jnp.arange(16, dtype=jnp.int32)
    order = one_hot(jnp.bitwise_xor(me, slots) * block, block, width)
    text_block = text_width // 16
    order_text = one_hot(jnp.bitwise_xor(me, slots) * text_block, text_block, text_width)
    lower = jnp.bitwise_xor(jnp.bitwise_and(me, 7), slots[:8]) * (2 * block)
    order_skip = jnp.stack([one_hot(lower + at * block, block, width) for at in range(2)])
    text = text_encoder_states.reshape(batch * text_rows, text_width)
    text_ordered = dot_plain(text, order_text).astype(bf16)
    valid = (jnp.arange(text_rows)[None, :] < text_lengths[:, None]).astype(f32)
    head_at = (jnp.arange(width)[:, None] // HD == jnp.arange(128)[None, :]).astype(bf16)
    table_arrays = [table for table, _ in tables]

    def shaped(*shape, dtype=f32):
        return jax.ShapeDtypeStruct(shape, dtype)

    flat, flat_low = shaped(rows, width), shaped(rows, width, dtype=bf16)
    double_low = shaped(rows, 2 * width, dtype=bf16)
    inner = mlp_down.shape[0] * 16
    given = [
        latent.reshape(rows, width),
        skip_input.reshape(rows, width),
        skip_gain_all[None, :],
        gains,
        shift,
        order,
        order_skip,
        head_at,
        *table_arrays,
        text_ordered,
        valid,
    ]
    saved = [
        shaped(2, 2, rows, width // 2, dtype=bf16),
        flat,
        flat_low,
        shaped(rows, 2 * width),
        double_low,
        double_low,
        flat_low,
        flat,
        flat_low,
        flat,
        flat,
        shaped(batch * text_rows, 2 * width, dtype=bf16),
        flat_low,
        flat,
        flat_low,
        shaped(rows, inner),
        shaped(rows, inner, dtype=bf16),
        shaped(HEADS, 128),
        shaped(HEADS, 128),
    ]
    (
        *gathered,
        normed,
        hidden,
        attn_in,
        qkv_proj,
        keyval_here,
        keyval_there,
        attn_cat,
        after_self,
        cross_in,
        cq_proj,
        ckey_mine,
        cross_keyval_all,
        cross_cat,
        after_cross,
        mlp_in,
        upper,
        activated,
        self_peak,
        cross_peak,
    ) = pl.pallas_call(
        functools.partial(forward_body, batch, scaling),
        out_shape=[shaped(2, 4, 4, *shard.shape, dtype=bf16) for shard in shards] + saved,
        in_specs=[IN_VMEM] * len(given) + [ANYWHERE] * 7,
        out_specs=[ANYWHERE] * 7 + [IN_VMEM] * len(saved),
        scratch_shapes=[
            pltpu.VMEM((rows, width), f32),
            pltpu.VMEM((rows, width), bf16),
            pltpu.VMEM((3, 4, 4, block, 512), bf16),
            pltpu.SemaphoreType.DMA((3,)),
            pltpu.SemaphoreType.DMA((7, 10)),
            pltpu.SemaphoreType.DMA((7, 10)),
            pltpu.SemaphoreType.DMA((7,)),
            pltpu.SemaphoreType.DMA,
            pltpu.SemaphoreType.DMA,
        ],
        compiler_params=pltpu.CompilerParams(
            collective_id=7, has_side_effects=True, vmem_limit_bytes=62 * 2**20
        ),
    )(*given, *shards)
    w_skip, w_qkv, w_pair, w_query, w_keyval, w_up, w_down = (
        g.reshape(2, 16 * g.shape[3], g.shape[4]) for g in gathered
    )

    def cut_halves(value):
        cut = (value.shape[1] // 2 + 127) // 128 * 128
        second = value[:, cut:]
        return value[:, :cut], jnp.pad(second, ((0, 0), (0, cut - second.shape[1])))

    def product(halves, weight):
        return dot_plain(halves[0], weight[0]) + dot_plain(halves[1], weight[1])

    def product_back(halves, weight):
        return dot_right_t(halves[0], weight[0]) + dot_right_t(halves[1], weight[1])

    def sum_twins(*pairs):
        (left, right), (left_two, right_two) = pairs
        there = dot_left_t(links.pick(left_two, left), links.pick(right_two, right)).astype(bf16)
        mine = dot_left_t(links.pick(left, left_two), links.pick(right, right_two))
        value = (mine + links.sibling(there).astype(f32)).astype(bf16)
        return value.reshape(4, 4, value.shape[0] // 16, value.shape[1])

    def column_grad(value, halves):
        return sum_twins((value, halves[0]), (value, halves[1]))

    def restore(value):
        return dot_right_t(value.astype(bf16), order).astype(bf16)

    def blocks_moved(value):
        size = value.shape[1] // 16
        return jnp.concatenate(
            [
                lax.dynamic_slice_in_dim(value, jnp.bitwise_xor(me, at) * size, size, 1)
                for at in range(16)
            ],
            axis=1,
        )

    down_in = out_grad.reshape(rows, width)
    result_grad = down_in.astype(f32)
    down_halves = cut_halves(down_in)
    put_down = column_grad(activated, down_halves)
    result = [dot_plain(activated, w_down[0]), dot_plain(activated, w_down[1])]
    result = jnp.concatenate([result[0], result[1][:, : width - result[0].shape[1]]], axis=1)
    block_out = (after_cross + result).astype(bf16)
    act_grad = blocks_moved(product_back(down_halves, w_down))
    upper_grad = jax.vjp(gelu_tanh, upper)[1](act_grad)[0].astype(bf16)
    upper_halves = cut_halves(upper_grad)
    put_up = column_grad(mlp_in, upper_halves)
    mlp_in_grad = exact_restore(order, product_back(upper_halves, w_up))
    cross_part, gain_third = jax.vjp(gained_norm, after_cross, gains[2])[1](mlp_in_grad)
    cross_grad = result_grad + cross_part
    cross_bf = cross_grad.astype(bf16)
    cmix_grad = restore(dot_right_t(cross_bf, w_pair[1]))
    back_scratch = [
        pltpu.VMEM((rows, width), f32),
        pltpu.VMEM((rows, width), f32),
        pltpu.VMEM((rows, width), bf16),
        pltpu.VMEM((rows, width), f32),
        pltpu.VMEM((2, rows, 2 * width), f32),
    ]
    back_outs = [flat_low, shaped(rows, 2 * width), double_low]
    heads_block = (head_at, None)
    cq_grad, ckeyval_mine, ckeyval_theirs = plain_call(
        functools.partial(attention_back_body, batch, True, False, 1, scaling),
        back_outs,
        [(cq_proj, None), (cmix_grad, None), heads_block, (cross_keyval_all, None)],
        back_scratch,
        text_lengths,
    )
    cq_halves = cut_halves(cq_grad)
    put_query = column_grad(cross_in, cq_halves)
    cross_in_grad = exact_restore(order, product_back(cq_halves, w_query))
    self_part, gain_second = jax.vjp(gained_norm, after_self, gains[1])[1](cross_in_grad)
    self_grad = cross_grad + self_part

    text_half = text_rows // 2
    (keyval_grad,) = plain_call(
        functools.partial(keys_back_body, batch, False),
        [double_low],
        [
            (ckey_mine, None),
            (ckeyval_mine, None),
            (links.sibling(ckeyval_theirs), None),
            heads_block,
        ],
    )
    text_mine = lax.dynamic_slice_in_dim(
        text_ordered.reshape(batch, text_rows, text_width), core * text_half, text_half, 1
    ).reshape(-1, text_width)
    keyval_halves = cut_halves(keyval_grad)
    put_keyval = column_grad(text_mine, keyval_halves)
    grad_text = exact_restore(order_text, product_back(keyval_halves, w_keyval))
    grad_text = grad_text.reshape(batch, text_half, text_width)

    self_bf = self_grad.astype(bf16)
    put_pair = sum_twins((attn_cat, self_bf), (cross_cat, cross_bf))
    mix_grad = restore(dot_right_t(self_bf, w_pair[0]))
    query_grad, here, there = plain_call(
        functools.partial(attention_back_body, batch, False, True, 2, scaling),
        back_outs,
        [
            (qkv_proj, (0, width)),
            (mix_grad, None),
            heads_block,
            *tables,
            (keyval_here, None),
            (keyval_there, None),
        ],
        back_scratch,
    )
    (key_value_grad,) = plain_call(
        functools.partial(keys_back_body, batch, True),
        [double_low],
        [(qkv_proj, (1, width)), (here, None), (links.sibling(there), None), heads_block, *tables],
    )
    qkv_grad = qkv_halves(jnp.concatenate([query_grad, key_value_grad], axis=1))
    put_qkv = column_grad(attn_in, qkv_grad)
    attn_in_grad = exact_restore(order, product_back(qkv_grad, w_qkv))

    def shifted(values, gain, moved):
        wide = jnp.broadcast_to(moved[:, None, :], (batch, tokens, width)).reshape(rows, width)
        return layer_norm(values) * gain + wide

    hidden_part, gain_first, shift_grad = jax.vjp(shifted, hidden, gains[0], shift)[1](
        attn_in_grad
    )
    hidden_grad = self_grad + hidden_part
    hidden_bf = hidden_grad.astype(bf16)
    normed_halves = [jnp.concatenate([normed[c, 0], normed[c, 1]], axis=1) for c in range(2)]
    put_skip = sum_twins((normed_halves[0], hidden_bf), (normed_halves[1], hidden_bf))
    near_grad, away_grad = 0.0, 0.0
    for at in range(2):
        part = dot_right_t(hidden_bf, w_skip[at])
        near_grad = near_grad + exact_restore(order_skip[at], part[:, : width // 2])
        away_grad = away_grad + exact_restore(order_skip[at], part[:, width // 2 :])
    normed_grad = jnp.concatenate(
        [jnp.where(me < 8, near_grad, away_grad), jnp.where(me < 8, away_grad, near_grad)], axis=1
    )
    joined = jnp.concatenate(
        [latent.reshape(rows, width), skip_input.reshape(rows, width)], axis=1
    ).astype(f32)
    joined_grad, skip_gain_grad = jax.vjp(gained_norm, joined, skip_gain_all)[1](normed_grad)
    grads_down, grads_up = scatter([put_down, put_up], 4, 8)
    grads = scatter([put_pair, put_query, put_keyval, put_qkv, put_skip], 4, 4)
    grad_down = jnp.concatenate([grads_down[0], grads_down[1]], axis=1)[:, :width]
    grad_up = jnp.concatenate([grads_up[0], grads_up[1]], axis=1)
    grad_self_out, grad_cross_out = grads[0][0], grads[0][1]
    grad_cross_query = jnp.concatenate([grads[1][0], grads[1][1]], axis=1)[:, :width]
    grad_keyval = jnp.concatenate([grads[2][0], grads[2][1]], axis=1)
    grad_qkv = qkv_whole(grads[3][0], grads[3][1])
    grad_skip_linear = grads[4].reshape(skip_linear.shape)

    gains_grad = jnp.stack([gain_first, gain_second, gain_third])
    gains_grad = gains_grad.reshape(3, count, third).transpose(1, 0, 2).reshape(count, 3 * third)
    gains_grad = jnp.concatenate([skip_gain_grad.reshape(count, gain_rows), gains_grad], axis=1)
    peaks = jnp.stack([self_peak[:, 0], cross_peak[:, 0]])
    cores = jnp.concatenate([shift_grad.reshape(-1), gains_grad.reshape(-1), peaks.reshape(-1)])
    there = links.sibling(cores)
    peaks = jnp.maximum(cores, there)[-2 * HEADS :]
    cores = cores + there
    ends = (batch * width, batch * width + count * cond_start)
    gains_grad = cores[ends[0] : ends[1]].reshape(count, cond_start)
    shift_bf = cores[: ends[0]].astype(bf16).astype(f32)
    shared = trade(lanes_of(jnp.concatenate([shift_bf, peaks]), 8), count, True, 5)
    shared = shared.reshape(count, -1)
    shift_all = shared[:, : ends[0]].reshape(count * batch, width).astype(bf16)
    peaks = jnp.max(shared[:, ends[0] : ends[0] + 2 * HEADS], axis=0).reshape(2, HEADS)
    grad_shift = dot_left_t(cond_cut, shift_all)
    cond_back = dot_right_t(shift_all, shift_linear).reshape(count, batch * shift_rows)
    owned = trade(lanes_of(jnp.concatenate([cond_back, gains_grad], axis=1), 8), count, False, 6)
    owned = owned.reshape(count, -1)
    cond_mine = owned[:, : batch * shift_rows].reshape(count, batch, shift_rows)
    cond_mine = cond_mine.transpose(1, 0, 2).reshape(batch, width)
    grad_cond = jax.vjp(jax.nn.silu, condition.astype(f32))[1](cond_mine)[0]
    own_gains = jnp.sum(owned[:, batch * shift_rows : batch * shift_rows + cond_start], axis=0)
    grad_skip_gain = own_gains[:gain_rows]
    grad_gains = own_gains[gain_rows:].reshape(3, third)

    roots = jnp.sqrt(thresholds / jnp.maximum(peaks, thresholds))
    self_cols = jnp.repeat(roots[0], HD)
    cross_cols = jnp.repeat(roots[1], HD)
    unit_cols = jnp.ones((width,), f32)
    clipped_qkv = (
        self_qkv.astype(f32) * jnp.concatenate([self_cols, self_cols, unit_cols])[None, :]
    ).astype(bf16)
    clipped_query = (cross_query.astype(f32) * cross_cols[None, :]).astype(bf16)
    clipped_keyval = (
        cross_keyval.astype(f32) * jnp.concatenate([cross_cols, unit_cols])[None, :]
    ).astype(bf16)
    return (
        block_out.reshape(batch, tokens, width),
        joined_grad[:, :width].reshape(batch, tokens, width),
        joined_grad[:, width:].reshape(batch, tokens, width),
        grad_cond,
        grad_text,
        grad_skip_gain,
        grad_gains,
        grad_skip_linear,
        grad_shift,
        grad_qkv,
        grad_self_out,
        grad_cross_query,
        grad_keyval,
        grad_cross_out,
        grad_up,
        grad_down,
        clipped_qkv,
        clipped_query,
        clipped_keyval,
        peaks,
    )


def solution(mesh):
    rows = P("fsdp", None)
    tokens = P("fsdp", "seq", None)
    in_specs = (
        tokens,
        tokens,
        rows,
        P("fsdp", None, None),
        P("fsdp"),
        tokens,
        P("fsdp"),
        P(None, "fsdp"),
        *([rows] * 9),
        P(),
    )
    out_specs = (
        *([tokens] * 3),
        rows,
        tokens,
        P("fsdp"),
        P(None, "fsdp"),
        *([rows] * 12),
        P(),
    )
    step = local_sixteen if mesh.shape["fsdp"] == 16 else local
    return jax.shard_map(step, mesh=mesh, in_specs=in_specs, out_specs=out_specs, check_vma=False)
```

```python
import functools

import jax
import jax.numpy as jnp
from jax import lax
from jax.experimental import pallas as pl
from jax.experimental.pallas import tpu as pltpu
from jax.sharding import PartitionSpec as P

HEADS = 16
HD = 88
GRID_W = 32

norm_eps = 1e-06
masked_value = -1e30
bf16 = jnp.bfloat16
f32 = jnp.float32
MESH = pl.DeviceIdType.MESH
ANYWHERE = pl.BlockSpec(memory_space=pl.ANY)
IN_VMEM = pl.BlockSpec(memory_space=pltpu.VMEM)


def layer_norm(values):
    center = values - jnp.mean(values, axis=-1, keepdims=True)
    spread = jnp.mean(center * center, axis=-1, keepdims=True)
    return center * lax.rsqrt(spread + norm_eps)


def gained_norm(values, gain):
    return layer_norm(values) * gain


def gelu_tanh(values):
    return jax.nn.gelu(values, approximate=True)


def dot_plain(left, right):
    return jnp.dot(left, right, preferred_element_type=f32)


def dot_left_t(left, right):
    return lax.dot_general(
        left, right, (((0,), (0,)), ((), ())), preferred_element_type=f32
    )


def dot_right_t(left, right):
    return lax.dot_general(
        left, right, (((1,), (1,)), ((), ())), preferred_element_type=f32
    )


def softmax_back(probs, prob_grad):
    return probs * (prob_grad - jnp.sum(prob_grad * probs, axis=-1, keepdims=True))


def greet(peers):
    barrier = pltpu.get_barrier_semaphore()
    for peer in peers:
        pl.semaphore_signal(barrier, inc=1, device_id=peer, device_id_type=MESH)
    pl.semaphore_wait(barrier, len(peers))


def trade_body(count, same, source, out, send, recv, local):
    me = lax.axis_index("fsdp")
    core = lax.axis_index("seq")
    greet([(jnp.bitwise_xor(me, j), core) for j in range(1, count)])

    def part(index):
        return source if same else source.at[index]

    def copy(j):
        peer = jnp.bitwise_xor(me, j)
        return pltpu.make_async_remote_copy(
            src_ref=part(peer),
            dst_ref=out.at[me],
            send_sem=send.at[j],
            recv_sem=recv.at[j],
            device_id=(peer, core),
            device_id_type=MESH,
        )

    for j in range(1, count):
        copy(j).start()
    here = pltpu.make_async_copy(part(me), out.at[me], local.at[0])
    here.start()
    here.wait()
    for j in range(1, count):
        copy(j).wait_send()
        copy(j).wait_recv()


def trade(value, count, same, identity):
    shape = value.shape if same else value.shape[1:]
    return pl.pallas_call(
        functools.partial(trade_body, count, same),
        out_shape=jax.ShapeDtypeStruct((count, *shape), value.dtype),
        in_specs=[IN_VMEM],
        out_specs=IN_VMEM,
        scratch_shapes=[
            pltpu.SemaphoreType.DMA((count,)),
            pltpu.SemaphoreType.DMA((count,)),
            pltpu.SemaphoreType.DMA((1,)),
        ],
        compiler_params=pltpu.CompilerParams(collective_id=identity, has_side_effects=True),
    )(value)


def neighbours(quad):
    me = lax.axis_index("fsdp")
    core = lax.axis_index("seq")
    first, second = 1 + core, 2 - core

    def at(mask):
        return (jnp.bitwise_xor(me, mask), core)

    return core, first, second, at, (me, 1 - core)


def gather_body(count, quad, *refs):
    mine, out = refs[:count], refs[count : 2 * count]
    send, recv, local = refs[2 * count :]
    core, first_mask, second_mask, at, sibling = neighbours(quad)
    far_peers = [at(k * quad) for k in range(1, 4)]
    greet([*far_peers, at(first_mask), at(second_mask), sibling])

    def copy(w, slot, source, target, peer):
        return pltpu.make_async_remote_copy(
            src_ref=source,
            dst_ref=target,
            send_sem=send.at[w, slot],
            recv_sem=recv.at[w, slot],
            device_id=peer,
            device_id_type=MESH,
        )

    def block(w, q):
        return out[w].at[core, pl.ds(4 * q, 4)]

    def far(w, k):
        return copy(w, k - 1, mine[w], out[w].at[core, k], far_peers[k - 1])

    def keep(w):
        return pltpu.make_async_copy(mine[w], out[w].at[core, 0], local.at[w])

    def first(w):
        return copy(w, 3, block(w, 0), block(w, first_mask), at(first_mask))

    def second(w):
        return copy(w, 4, block(w, 0), block(w, second_mask), at(second_mask))

    def both(w):
        return copy(w, 5, block(w, first_mask), block(w, 3), at(second_mask))

    def twin(w, n):
        q = (0, first_mask, second_mask, 3)[n]
        return copy(w, 6 + n, block(w, q), block(w, q), sibling)

    for w in range(count):
        keep(w).start()
        for k in range(1, 4):
            far(w, k).start()
    for step in range(count + 2):
        w = step
        if w < count:
            keep(w).wait()
            for k in range(1, 4):
                far(w, k).wait_recv()
            first(w).start()
            second(w).start()
            twin(w, 0).start()
        w = step - 1
        if 0 <= w < count:
            first(w).wait_recv()
            both(w).start()
            twin(w, 1).start()
            second(w).wait_recv()
            twin(w, 2).start()
        w = step - 2
        if 0 <= w < count:
            both(w).wait_recv()
            twin(w, 3).start()
    for w in range(count):
        for k in range(1, 4):
            far(w, k).wait_send()
        first(w).wait_send()
        second(w).wait_send()
        both(w).wait_send()
        for n in range(4):
            twin(w, n).wait_send()
            twin(w, n).wait_recv()


def gather(shards, quad, identity):
    count = len(shards)
    return pl.pallas_call(
        functools.partial(gather_body, count, quad),
        out_shape=[jax.ShapeDtypeStruct((2, 16, *s.shape), bf16) for s in shards],
        in_specs=[ANYWHERE] * count,
        out_specs=[ANYWHERE] * count,
        scratch_shapes=[
            pltpu.SemaphoreType.DMA((count, 10)),
            pltpu.SemaphoreType.DMA((count, 10)),
            pltpu.SemaphoreType.DMA((count,)),
        ],
        compiler_params=pltpu.CompilerParams(collective_id=identity, has_side_effects=True),
    )(*shards)


def scatter_body(count, quad, *refs):
    source, out = refs[:count], refs[count : 2 * count]
    kept, half, quarter, last, total = (
        refs[(2 + n) * count : (3 + n) * count] for n in range(5)
    )
    send, recv, local = refs[7 * count :]
    core, first_mask, second_mask, at, sibling = neighbours(quad)
    far_peers = [at(k * quad) for k in range(1, 4)]
    greet([*far_peers, at(first_mask), at(second_mask), sibling])

    def copy(w, slot, origin, target, peer):
        return pltpu.make_async_remote_copy(
            src_ref=origin,
            dst_ref=target,
            send_sem=send.at[w, slot],
            recv_sem=recv.at[w, slot],
            device_id=peer,
            device_id_type=MESH,
        )

    def block(w, q):
        if len(source[w].shape) == 4:
            return source[w].at[:, q]
        return source[w].at[pl.ds(4 * q, 4)]

    def give(w, n):
        q = 3 if n == 0 else second_mask
        return copy(w, n, block(w, q), half[w].at[n], at(second_mask))

    def load(w, n):
        q = first_mask if n == 0 else 0
        return pltpu.make_async_copy(block(w, q), kept[w].at[n], local.at[w, n])

    def pass_on(w):
        return copy(w, 2, half[w].at[0], quarter[w], at(first_mask))

    def far(w, k):
        return copy(w, 2 + k, half[w].at[1, k], last[w].at[k - 1], far_peers[k - 1])

    def twin(w):
        return copy(w, 6, total[w], out[w].at[core], sibling)

    def store(w):
        return pltpu.make_async_copy(total[w], out[w].at[core], local.at[w, 2])

    def lanes(w, body):
        width = total[w].shape[1]
        step = 256 if width % 256 == 0 else 128 if width % 128 == 0 else width
        if step == width:
            body(slice(None))
        else:

            @pl.loop(0, width // step)
            def _(i):
                body(pl.ds(pl.multiple_of(i * step, step), step))

    for w in range(count):
        for n in range(2):
            give(w, n).start()
            load(w, n).start()
    for step in range(count + 2):
        w = step
        if w < count:
            give(w, 0).wait_recv()
            load(w, 0).wait()

            def body(c):
                for k in range(4):
                    half[w][0, k, :, c] = (
                        half[w][0, k, :, c].astype(f32) + kept[w][0, k, :, c].astype(f32)
                    ).astype(bf16)

            lanes(w, body)
            pass_on(w).start()
        w = step - 1
        if 0 <= w < count:
            give(w, 1).wait_recv()
            load(w, 1).wait()
            pass_on(w).wait_recv()

            def body(c):
                for k in range(4):
                    value = half[w][1, k, :, c].astype(f32) + kept[w][1, k, :, c].astype(f32)
                    value = value + quarter[w][k, :, c].astype(f32)
                    if k == 0:
                        total[w][:, c] = value
                    else:
                        half[w][1, k, :, c] = value.astype(bf16)

            lanes(w, body)
            for k in range(1, 4):
                far(w, k).start()
        w = step - 2
        if 0 <= w < count:
            for k in range(1, 4):
                far(w, k).wait_recv()

            def body(c):
                value = total[w][:, c]
                for k in range(3):
                    value = value + last[w][k, :, c].astype(f32)
                total[w][:, c] = value

            lanes(w, body)
            twin(w).start()
            store(w).start()
    for w in range(count):
        give(w, 0).wait_send()
        give(w, 1).wait_send()
        pass_on(w).wait_send()
        for k in range(1, 4):
            far(w, k).wait_send()
        twin(w).wait_send()
        twin(w).wait_recv()
        store(w).wait()


def scatter(sums, quad, identity):
    count = len(sums)
    shapes = [s.shape[-2:] for s in sums]

    def buffers(*lead):
        return [pltpu.VMEM((*lead, *s), bf16) for s in shapes]

    return pl.pallas_call(
        functools.partial(scatter_body, count, quad),
        out_shape=[jax.ShapeDtypeStruct((2, *s), f32) for s in shapes],
        in_specs=[ANYWHERE] * count,
        out_specs=[ANYWHERE] * count,
        scratch_shapes=[
            *buffers(2, 4),
            *buffers(2, 4),
            *buffers(4),
            *buffers(3),
            *[pltpu.VMEM(s, f32) for s in shapes],
            pltpu.SemaphoreType.DMA((count, 7)),
            pltpu.SemaphoreType.DMA((count, 7)),
            pltpu.SemaphoreType.DMA((count, 3)),
        ],
        compiler_params=pltpu.CompilerParams(
            collective_id=identity, has_side_effects=True, vmem_limit_bytes=56 * 2**20
        ),
    )(*sums)


def gelu_parts(value):
    inner = 0.7978845608028654 * (value + 0.044715 * value * value * value)
    return jnp.tanh(inner)


def gelu_of(value):
    return 0.5 * value * (1.0 + gelu_parts(value))


class GatherPlan:
    def __init__(self, mine, out, send, recv, local):
        self.mine, self.out = mine, out
        self.send, self.recv, self.local = send, recv, local
        self.core, self.first_mask, self.second_mask, self.at, self.sibling = neighbours(4)
        self.far_peers = [self.at(4 * k) for k in range(1, 4)]

    def peers(self):
        return [*self.far_peers, self.at(self.first_mask), self.at(self.second_mask), self.sibling]

    def copy(self, w, slot, source, target, peer):
        return pltpu.make_async_remote_copy(
            src_ref=source,
            dst_ref=target,
            send_sem=self.send.at[w, slot],
            recv_sem=self.recv.at[w, slot],
            device_id=peer,
            device_id_type=MESH,
        )

    def block(self, w, q):
        return self.out[w].at[self.core, :, q]

    def far(self, w, k):
        return self.copy(
            w, k - 1, self.mine[w], self.out[w].at[self.core, k, 0], self.far_peers[k - 1]
        )

    def keep(self, w):
        return pltpu.make_async_copy(
            self.mine[w], self.out[w].at[self.core, 0, 0], self.local.at[w]
        )

    def first(self, w):
        mask = self.first_mask
        return self.copy(w, 3, self.block(w, 0), self.block(w, mask), self.at(mask))

    def second(self, w):
        mask = self.second_mask
        return self.copy(w, 4, self.block(w, 0), self.block(w, mask), self.at(mask))

    def both(self, w):
        return self.copy(
            w, 5, self.block(w, self.first_mask), self.block(w, 3), self.at(self.second_mask)
        )

    def twin(self, w, n):
        q = (0, self.first_mask, self.second_mask, 3)[n]
        return self.copy(w, 6 + n, self.block(w, q), self.block(w, q), self.sibling)

    def begin(self, w):
        self.keep(w).start()
        for k in range(1, 4):
            self.far(w, k).start()

    def spread(self, w):
        self.keep(w).wait()
        for k in range(1, 4):
            self.far(w, k).wait_recv()
        self.first(w).start()
        self.second(w).start()
        self.twin(w, 0).start()

    def cross(self, w):
        self.first(w).wait_recv()
        self.both(w).start()
        self.twin(w, 1).start()
        self.second(w).wait_recv()
        self.twin(w, 2).start()

    def close(self, w):
        self.both(w).wait_recv()
        self.twin(w, 3).start()

    def ready(self, w):
        for n in range(4):
            self.twin(w, n).wait_recv()

    def finish(self, w):
        for k in range(1, 4):
            self.far(w, k).wait_send()
        self.first(w).wait_send()
        self.second(w).wait_send()
        self.both(w).wait_send()
        for n in range(4):
            self.twin(w, n).wait_send()


def stream(weight, tiles, buffer, semaphore, body):
    depth = buffer.shape[0]
    height = weight.shape[3]

    def copy(index):
        half, start, size = tiles[index]
        slot = index % depth
        return pltpu.make_async_copy(
            weight.at[half, :, :, :, pl.ds(start, size)],
            buffer.at[slot, :, :, pl.ds(0, height), pl.ds(0, size)],
            semaphore.at[slot],
        )

    for index in range(min(depth - 1, len(tiles))):
        copy(index).start()
    for index, (_, _, size) in enumerate(tiles):
        if index + depth - 1 < len(tiles):
            copy(index + depth - 1).start()
        copy(index).wait()
        body(index, buffer[index % depth, :, :, :height, :size].reshape(16 * height, size))


def tiles_of(width, size, halves=(0, 1)):
    return [
        (half, start, min(size, width - start)) for half in halves for start in range(0, width, size)
    ]


def forward_body(batch, scaling, *refs):
    refs = list(refs)
    take = refs.pop
    latent, skip, skip_gain, gains, shift = (take(0) for _ in range(5))
    order, order_skip, heads_ref = (take(0) for _ in range(3))
    tables = [take(0) for _ in range(3)]
    text, valid = take(0), take(0)
    mine = [take(0) for _ in range(7)]
    out = [take(0) for _ in range(7)]
    normed, hidden, attn_in, qkv, keyval_here, keyval_there = (take(0) for _ in range(6))
    attn_cat, after_self, cross_in, cq_proj, ckey_mine, cross_keyval = (take(0) for _ in range(6))
    cross_cat, after_cross, mlp_in, upper, activated = (take(0) for _ in range(5))
    self_peak, cross_peak = take(0), take(0)
    wide, narrow, buffer, semaphore, send, recv, local, twin_send, twin_recv = refs
    rows, width = hidden.shape
    size = rows // batch
    me = lax.axis_index("fsdp")
    core = lax.axis_index("seq")
    plan = GatherPlan(mine, out, send, recv, local)
    skip_w, qkv_w, pair_w, query_w, keyval_w, up_w, down_w = range(7)

    greet(plan.peers())
    for w in range(7):
        plan.begin(w)

    def each(body):
        for b in range(batch):
            body(b, pl.ds(b * size, size))

    def reorder(value):
        return dot_plain(value, order[...]).astype(bf16)

    upper_half = me >= 8

    def normed_part(b, rows_b):
        left = latent[rows_b, :].astype(f32)
        right = skip[rows_b, :].astype(f32)
        mean = (
            jnp.sum(left, axis=1, keepdims=True) + jnp.sum(right, axis=1, keepdims=True)
        ) / (2 * width)
        left, right = left - mean, right - mean
        spread = (
            jnp.sum(left * left, axis=1, keepdims=True)
            + jnp.sum(right * right, axis=1, keepdims=True)
        ) / (2 * width)
        factor = lax.rsqrt(spread + norm_eps)
        left = (left * factor * skip_gain[:, :width]).astype(bf16)
        right = (right * factor * skip_gain[:, width:]).astype(bf16)
        near = jnp.where(upper_half, right, left)
        away = jnp.where(upper_half, left, right)
        for half in range(2):
            normed[half, 0, rows_b, :] = dot_plain(near, order_skip[half]).astype(bf16)
            normed[half, 1, rows_b, :] = dot_plain(away, order_skip[half]).astype(bf16)

    each(normed_part)
    plan.spread(skip_w)
    plan.spread(qkv_w)
    plan.cross(skip_w)
    plan.spread(pair_w)
    plan.cross(qkv_w)
    plan.close(skip_w)
    plan.ready(skip_w)

    skip_tiles = tiles_of(width, 512)

    def skip_product(index, tile):
        half, start, extent = skip_tiles[index]
        cut = tile.shape[0] // 2
        value = dot_plain(normed[half, 0], tile[:cut]) + dot_plain(normed[half, 1], tile[cut:])
        lanes = pl.ds(start, extent)
        if half == 0:
            hidden[:, lanes] = value
        else:
            hidden[:, lanes] += value

    stream(out[skip_w], skip_tiles, buffer, semaphore, skip_product)

    def attn_in_part(b, rows_b):
        value = layer_norm(hidden[rows_b, :]) * gains[0:1, :] + shift[b : b + 1, :]
        attn_in[rows_b, :] = reorder(value.astype(bf16))

    each(attn_in_part)
    plan.spread(query_w)
    plan.cross(pair_w)
    plan.close(qkv_w)
    plan.ready(qkv_w)

    qkv_tiles = tiles_of(out[qkv_w].shape[4], 512)

    def qkv_product(index, tile):
        half, start, extent = qkv_tiles[index]
        value = dot_plain(attn_in[...], tile)
        for at in range(0, extent, 128):
            lane = start + at
            piece = value[:, at : at + 128]
            if lane < width:
                qkv[:, pl.ds(half * width + lane, 128)] = piece
            else:
                place = lane - width + half * 768
                if place < width:
                    keyval_here[:, pl.ds(width + place, 128)] = piece.astype(bf16)

    stream(out[qkv_w], qkv_tiles, buffer, semaphore, qkv_product)

    def key_part(b, rows_b):
        value, _ = head_norm(qkv[rows_b, pl.ds(width, width)], heads_ref)
        keyval_here[rows_b, pl.ds(0, width)] = turn(value, tables).astype(bf16)

    each(key_part)
    exchange = pltpu.make_async_remote_copy(
        src_ref=keyval_here,
        dst_ref=keyval_there,
        send_sem=twin_send,
        recv_sem=twin_recv,
        device_id=plan.sibling,
        device_id_type=MESH,
    )
    exchange.start()

    def query_part(b, rows_b):
        value, _ = head_norm(qkv[rows_b, pl.ds(0, width)], heads_ref)
        narrow[rows_b, :] = turn(value, tables).astype(bf16)

    each(query_part)
    plan.spread(keyval_w)
    plan.cross(query_w)
    plan.close(pair_w)
    exchange.wait()

    def attend(sources, peak, target, masked):
        peak[...] = jnp.full_like(peak, masked_value)
        wide[...] = jnp.zeros_like(wide)

        @pl.loop(0, batch)
        def _(b):
            rows_b = pl.ds(pl.multiple_of(b * size, size), size)
            for head in range(HEADS):
                lanes, inside = window_of(head, width)
                query = narrow[rows_b, lanes] * inside.astype(bf16)
                scores = dot_right_t(query, pair_rows(sources, b, size, lanes)) * scaling
                if masked:
                    scores = jnp.where(valid[pl.ds(b, 1), :] > 0.5, scores, masked_value)
                probs, largest = softmax_of(scores)
                largest = jnp.max(largest, axis=0, keepdims=True)
                peak[head : head + 1, :] = jnp.maximum(
                    peak[head : head + 1, :], jnp.broadcast_to(largest, (1, 128))
                )
                value = pair_rows(sources, b, size, shift_lanes(lanes, width))
                wide[rows_b, lanes] += dot_plain(probs.astype(bf16), value) * inside

        target[...] = reorder(wide[...].astype(bf16))

    attend([keyval_here, keyval_there], self_peak, attn_cat, False)
    plan.ready(pair_w)
    pair_tiles = tiles_of(width, 512)

    def out_product(source, before, after):
        def body(index, tile):
            lanes = pl.ds(pair_tiles[index][1], pair_tiles[index][2])
            after[:, lanes] = before[:, lanes] + dot_plain(source[...], tile)

        return body

    pair_body = out_product(attn_cat, hidden, after_self)
    stream(out[pair_w], tiles_of(width, 512, (0,)), buffer, semaphore, pair_body)

    def cross_in_part(b, rows_b):
        value = layer_norm(after_self[rows_b, :]) * gains[1:2, :]
        cross_in[rows_b, :] = reorder(value.astype(bf16))

    each(cross_in_part)
    plan.spread(up_w)
    plan.cross(keyval_w)
    plan.close(query_w)
    plan.ready(query_w)
    query_tiles = tiles_of(out[query_w].shape[4], 512)

    def query_product(index, tile):
        half, start, extent = query_tiles[index]
        place = half * out[query_w].shape[4] + start
        extent = min(extent, width - place)
        cq_proj[:, pl.ds(place, extent)] = dot_plain(cross_in[...], tile)[:, :extent]

    stream(out[query_w], query_tiles, buffer, semaphore, query_product)

    def cross_query_part(b, rows_b):
        narrow[rows_b, :] = head_norm(cq_proj[rows_b, :], heads_ref)[0].astype(bf16)

    each(cross_query_part)
    plan.spread(down_w)
    plan.close(keyval_w)
    plan.ready(keyval_w)
    keyval_tiles = tiles_of(width, 512)

    def keyval_product(index, tile):
        half, start, extent = keyval_tiles[index]
        value = dot_plain(text[...], tile)
        if half == 0:
            upper[:, pl.ds(start, extent)] = value[:rows]
            upper[:, pl.ds(width + start, extent)] = value[rows:]
        else:
            cross_keyval[:, pl.ds(width + start, extent)] = value.astype(bf16)

    stream(out[keyval_w], keyval_tiles, buffer, semaphore, keyval_product)
    for b in range(batch):
        for at in range(2):
            part = pl.ds(at * size, size)
            lanes = pl.ds(b * width, width)
            cross_keyval[pl.ds(b * 2 * size + at * size, size), pl.ds(0, width)] = head_norm(
                upper[part, lanes], heads_ref
            )[0].astype(bf16)
        ckey_mine[pl.ds(b * size, size), :] = upper[
            pl.ds(pl.multiple_of(core * size, size), size), pl.ds(b * width, width)
        ]
    attend([cross_keyval], cross_peak, cross_cat, True)
    pair_body = out_product(cross_cat, after_self, after_cross)
    stream(out[pair_w], tiles_of(width, 512, (1,)), buffer, semaphore, pair_body)

    def mlp_in_part(b, rows_b):
        value = layer_norm(after_cross[rows_b, :]) * gains[2:3, :]
        mlp_in[rows_b, :] = reorder(value.astype(bf16))

    each(mlp_in_part)
    plan.cross(up_w)
    plan.close(up_w)
    plan.ready(up_w)
    block = activated.shape[1] // 16
    up_tiles = tiles_of(out[up_w].shape[4], block)

    def up_product(index, tile):
        value = dot_plain(mlp_in[...], tile)
        upper[:, pl.ds(index * block, block)] = value
        slot = jnp.bitwise_xor(me, index)
        activated[:, pl.ds(pl.multiple_of(slot * block, block), block)] = gelu_of(value).astype(bf16)

    stream(out[up_w], up_tiles, buffer, semaphore, up_product)
    plan.cross(down_w)
    plan.close(down_w)
    plan.ready(down_w)
    for w in range(7):
        plan.finish(w)


def gelu_slope(value):
    bent = gelu_parts(value)
    inner = 0.7978845608028654 * (1.0 + 3 * 0.044715 * value * value)
    return 0.5 * (1.0 + bent) + 0.5 * value * (1.0 - bent * bent) * inner


def norm_back(value, gain, grad):
    center = value - jnp.mean(value, axis=-1, keepdims=True)
    factor = lax.rsqrt(jnp.mean(center * center, axis=-1, keepdims=True) + norm_eps)
    normed = center * factor
    gain_grad = jnp.sum(grad * normed, axis=0, keepdims=True)
    grad = grad * gain
    first = jnp.mean(grad, axis=-1, keepdims=True)
    second = jnp.mean(grad * normed, axis=-1, keepdims=True)
    return factor * (grad - first - normed * second), gain_grad


class TwinSum:
    def __init__(self, there, sums, send, recv, local, out_buffer, in_buffer, sibling):
        self.there, self.sums = there, sums
        self.send, self.recv, self.local = send, recv, local
        self.out_buffer, self.in_buffer, self.sibling = out_buffer, in_buffer, sibling

    def away(self, w, index, place, source):
        return pltpu.make_async_remote_copy(
            src_ref=source,
            dst_ref=place(self.there[w]),
            send_sem=self.send.at[w, index],
            recv_sem=self.recv.at[w, index],
            device_id=self.sibling,
            device_id_type=MESH,
        )

    def run(self, w, places, shape, other, own, between=None):
        depth = self.out_buffer.shape[0]

        def slot(buffer, index):
            views = [pl.ds(0, n) for n in shape(index)]
            return buffer.at[(index % depth, *views)]

        for index, place in enumerate(places):
            if index >= depth:
                before = index - depth
                self.away(w, before, places[before], slot(self.out_buffer, before)).wait_send()
            target = slot(self.out_buffer, index)
            target[...] = other(index).astype(bf16)
            self.away(w, index, place, target).start()
        for index in range(max(0, len(places) - depth), len(places)):
            self.away(w, index, places[index], slot(self.out_buffer, index)).wait_send()
        if between is not None:
            between()

        def fetch(index):
            return pltpu.make_async_copy(
                places[index](self.there[w]),
                slot(self.in_buffer, index),
                self.local.at[index % depth],
            )

        def store(index):
            return pltpu.make_async_copy(
                slot(self.out_buffer, index),
                places[index](self.sums[w]),
                self.local.at[depth + index % depth],
            )

        def begin(index):
            self.away(w, index, places[index], slot(self.out_buffer, index)).wait_recv()
            fetch(index).start()

        begin(0)
        for index in range(len(places)):
            if index + 1 < len(places):
                begin(index + 1)
            value = own(index)
            fetch(index).wait()
            if index >= depth:
                store(index - depth).wait()
            target = slot(self.out_buffer, index)
            target[...] = (value + slot(self.in_buffer, index)[...].astype(f32)).astype(bf16)
            store(index).start()
        for index in range(max(0, len(places) - depth), len(places)):
            store(index).wait()


def lane_places(height, width, size):
    starts = [(start, min(size, width - start)) for start in range(0, width, size)]
    places = [
        lambda ref, start=start, extent=extent: ref.at[:, :, :, pl.ds(start, extent)]
        for start, extent in starts
    ]
    return starts, places, lambda index: (4, 4, height, starts[index][1])


def mlp_back_body(batch, *refs):
    refs = list(refs)
    take = refs.pop
    out_grad, activated, upper, mlp_in, after_cross, order, gains = (take(0) for _ in range(7))
    up_w, down_w = take(0), take(0)
    block_out, cross_grad, gain_grad = (take(0) for _ in range(3))
    sums = [take(0), take(0)]
    there = [take(0), take(0)]
    upper_grad, turned, total, down_buffer, up_buffer = (take(0) for _ in range(5))
    out_down, in_down, out_up, in_up = (take(0) for _ in range(4))
    semaphore, send, recv, local = refs
    rows, width = after_cross.shape
    size = rows // batch
    block = activated.shape[1] // 16
    half_width = out_grad.shape[2]
    me = lax.axis_index("fsdp")
    core = lax.axis_index("seq")
    sibling = (me, 1 - core)
    greet([sibling])

    planes = [
        lambda ref, k=k, q=q: ref.at[k, q] for k in range(4) for q in range(4)
    ]
    down = TwinSum(there, sums, send, recv, local, out_down, in_down, sibling)

    def down_part(half):
        def part(index):
            return dot_left_t(activated[:, index * block : (index + 1) * block], out_grad[half])

        return part

    def down_back():
        depth = down_buffer.shape[0]

        def copy(index):
            k, q = divmod(index, 4)
            return pltpu.make_async_copy(
                down_w.at[:, k, q], down_buffer.at[index % depth], semaphore.at[index % depth]
            )

        for index in range(depth - 1):
            copy(index).start()
        total[...] = jnp.zeros_like(total)
        for index in range(16):
            if index + depth - 1 < 16:
                copy(index + depth - 1).start()
            copy(index).wait()
            first, second = down_buffer[index % depth, 0], down_buffer[index % depth, 1]
            shard = jnp.bitwise_xor(me, index)
            lanes = pl.ds(pl.multiple_of(shard * block, block), block)
            grad = dot_right_t(out_grad[0], first) + dot_right_t(out_grad[1], second)
            grad = (grad * gelu_slope(upper[:, lanes])).astype(bf16)
            in_half = pl.multiple_of((shard % 8) * block, block)
            upper_grad[shard // 8, :, pl.ds(in_half, block)] = grad
            active = activated[:, index * block : (index + 1) * block]
            total[0] += dot_plain(active, first)
            total[1] += dot_plain(active, second)
        cut = width - half_width
        block_out[:, pl.ds(0, half_width)] = (
            after_cross[:, pl.ds(0, half_width)] + total[0]
        ).astype(bf16)
        block_out[:, pl.ds(half_width, cut)] = (
            after_cross[:, pl.ds(half_width, cut)] + total[1][:, :cut]
        ).astype(bf16)

    down.run(
        0, planes, lambda index: (block, half_width), down_part(1 - core), down_part(core), down_back
    )

    turned[...] = jnp.transpose(mlp_in[...])
    starts, places, shape = lane_places(width // 16, upper_grad.shape[2], out_up.shape[4])
    up = TwinSum(there, sums, send, recv, local, out_up, in_up, sibling)

    def up_part(half):
        def part(index):
            start, extent = starts[index]
            value = dot_plain(turned[...], upper_grad[half, :, pl.ds(start, extent)])
            return value.reshape(4, 4, width // 16, extent)

        return part

    def up_back():
        tiles = tiles_of(upper_grad.shape[2], 512)

        def body(index, tile):
            half, start, extent = tiles[index]
            value = dot_right_t(upper_grad[half, :, pl.ds(start, extent)], tile)
            if index == 0:
                cross_grad[...] = value
            else:
                cross_grad[...] += value

        stream(up_w, tiles, up_buffer, semaphore, body)
        gain_grad[...] = jnp.zeros_like(gain_grad)
        for b in range(batch):
            rows_b = pl.ds(b * size, size)
            grad = exact_restore(order[...], cross_grad[rows_b, :])
            value, gain_part = norm_back(after_cross[rows_b, :], gains[2:3, :], grad)
            gain_grad[0:1, :] += gain_part
            result = jnp.concatenate(
                [out_grad[0, rows_b, :], out_grad[1, rows_b, : width - half_width]], axis=1
            )
            cross_grad[rows_b, :] = result.astype(f32) + value

    up.run(1, places, shape, up_part(1 - core), up_part(core), up_back)


class ScatterPlan:
    def __init__(self, sums, out, half, passing, quarter, leaving, last, slots, totals, sems):
        self.sums, self.out, self.half = sums, out, half
        self.passing, self.quarter, self.leaving, self.last = passing, quarter, leaving, last
        self.slots, self.totals = slots, totals
        self.send, self.recv, self.load, self.store = sems
        self.core, self.first_mask, self.second_mask, self.at, self.sibling = neighbours(4)
        self.far_peers = [self.at(4 * k) for k in range(1, 4)]

    def peers(self):
        return [*self.far_peers, self.at(self.first_mask), self.at(self.second_mask), self.sibling]

    def copy(self, w, slot, source, target, peer):
        return pltpu.make_async_remote_copy(
            src_ref=source,
            dst_ref=target,
            send_sem=self.send.at[w, slot],
            recv_sem=self.recv.at[w, slot],
            device_id=peer,
            device_id_type=MESH,
        )

    def give(self, w, n):
        q = 3 if n == 0 else self.second_mask
        return self.copy(
            w, n, self.sums[w].at[:, q], self.half[w].at[n], self.at(self.second_mask)
        )

    def hand(self, w):
        return self.copy(w, 2, self.passing[w], self.quarter[w], self.at(self.first_mask))

    def far(self, w, k):
        return self.copy(
            w, 2 + k, self.leaving[w].at[k - 1], self.last[w].at[k - 1], self.far_peers[k - 1]
        )

    def chunks(self, w):
        height, width = self.out[w].shape[1:]
        which = 0 if height <= self.slots[0].shape[1] else 1
        size = self.slots[which].shape[2]
        return which, height, [(s, min(size, width - s)) for s in range(0, width, size)]

    def add(self, w, groups, finish):
        which, height, chunks = self.chunks(w)
        slots = self.slots[which]
        for start, extent in chunks:
            lanes = pl.ds(start, extent)
            views = []
            for planes in groups:
                for plane in planes:
                    at = len(views)
                    view = slots.at[at, pl.ds(0, height), pl.ds(0, extent)]
                    copy = pltpu.make_async_copy(plane.at[:, lanes], view, self.load.at[at])
                    copy.start()
                    views.append((view, copy))
            at = 0
            pending = []
            for index, planes in enumerate(groups):
                mine = views[at : at + len(planes)]
                at += len(planes)
                for _, copy in mine:
                    copy.wait()
                pending.extend(finish(index, lanes, extent, [view for view, _ in mine]))
            for copy in pending:
                copy.wait()

    def added(self, views, extent, put):
        step = 256 if extent % 256 == 0 else 128

        @pl.loop(0, extent // step)
        def _(i):
            lanes = pl.ds(pl.multiple_of(i * step, step), step)
            value = views[0][:, lanes].astype(f32)
            for view in views[1:]:
                value = value + view[:, lanes].astype(f32)
            put(lanes, value)

    def rounded(self, targets):
        def finish(index, lanes, extent, views):
            def put(at, value):
                views[0][:, at] = value.astype(bf16)

            self.added(views, extent, put)
            copy = pltpu.make_async_copy(
                views[0], targets[index].at[:, lanes], self.store.at[index]
            )
            copy.start()
            return [copy]

        return finish

    def begin(self, w):
        self.give(w, 0).start()
        self.give(w, 1).start()

    def middle(self, w):
        self.give(w, 0).wait_recv()
        mask = self.first_mask
        groups = [[self.half[w].at[0, k], self.sums[w].at[k, mask]] for k in range(4)]
        self.add(w, groups, self.rounded([self.passing[w].at[k] for k in range(4)]))
        self.hand(w).start()

    def leave(self, w):
        self.give(w, 1).wait_recv()
        self.hand(w).wait_recv()
        groups = [
            [self.half[w].at[1, k], self.sums[w].at[k, 0], self.quarter[w].at[k]]
            for k in range(1, 4)
        ]
        self.add(w, groups, self.rounded([self.leaving[w].at[k] for k in range(3)]))
        for k in range(1, 4):
            self.far(w, k).start()

    def close(self, w):
        for k in range(1, 4):
            self.far(w, k).wait_recv()
        group = [self.half[w].at[1, 0], self.sums[w].at[0, 0], self.quarter[w].at[0]]
        group += [self.last[w].at[k] for k in range(3)]
        which, height, _ = self.chunks(w)
        totals = self.totals[which]

        def finish(index, lanes, extent, views):
            total = totals.at[pl.ds(0, height), pl.ds(0, extent)]

            def put(at, value):
                total[:, at] = value

            self.added(views, extent, put)
            target = self.out[w].at[self.core, :, lanes]
            here = pltpu.make_async_copy(total, target, self.store.at[0])
            there = self.copy(w, 6 + (0 if lanes.start == 0 else 1), total, target, self.sibling)
            here.start()
            there.start()
            here.wait()
            there.wait_send()
            there.wait_recv()
            return []

        self.add(w, [group], finish)

    def finish(self, w):
        self.give(w, 0).wait_send()
        self.give(w, 1).wait_send()
        self.hand(w).wait_send()
        for k in range(1, 4):
            self.far(w, k).wait_send()


def rest_back_body(batch, scaling, *refs):
    refs = list(refs)
    take = refs.pop

    def several(count):
        return [take(0) for _ in range(count)]

    cross_cat, attn_cat, cross_in, attn_in, text, after_self, hidden, normed = several(8)
    gains, order, heads_ref = several(3)
    tables = several(3)
    valid = take(0)
    skip_w, qkv_w, pair_w, query_w, keyval_w = several(5)
    cross_keyval, cq_proj, ckey_mine, qkv, keyval_here, keyval_there, cross_grad = several(7)
    summed = several(2)
    text_grad, gain_grads, shift_grad, normed_grad = several(4)
    out = several(7)
    own_sums, there = several(5), several(5)
    half, passing, quarter, leaving, last = (several(7) for _ in range(5))
    grad, wide, factor, back = several(4)
    query, mix_grad, total, keyval, proj, turned, halves = several(7)
    buffer, out_buffer, in_buffer = several(3)
    slots, totals = several(2), several(2)
    landed = take(0)
    semaphore, loads, twin_send, twin_recv, twin_local = several(5)
    exchange_send, exchange_recv, send, recv, add_load, add_store = several(6)
    rows, width = hidden.shape
    size = rows // batch
    block = width // 16
    core = lax.axis_index("seq")
    down, up, query_s, keyval_s, pair_s, qkv_s, skip_s = range(7)
    plan = ScatterPlan(
        summed + own_sums, out, half, passing, quarter, leaving, last, slots, totals,
        (send, recv, add_load, add_store),
    )
    twin = TwinSum(
        there, own_sums, twin_send, twin_recv, twin_local, out_buffer, in_buffer, plan.sibling
    )
    greet(plan.peers())
    plan.begin(down)
    plan.begin(up)

    first_lanes, last_lanes = pl.ds(0, width), pl.ds(width, width)

    def load(*pairs):
        copies = [
            pltpu.make_async_copy(source, target, loads.at[at])
            for at, (source, target) in enumerate(pairs)
        ]
        for copy in copies:
            copy.start()
        for copy in copies:
            copy.wait()

    load(
        (cross_grad, grad),
        (cross_keyval, keyval),
        (cq_proj, proj.at[:, first_lanes]),
        (ckey_mine, proj.at[:, last_lanes]),
    )
    gain_grads[...] = jnp.zeros_like(gain_grads)
    shift_grad[...] = jnp.zeros_like(shift_grad)

    def each(body):
        for b in range(batch):
            body(b, pl.ds(b * size, size))

    def back_through(weight, tiles, factor_of, target):
        def body(index, tile):
            value = dot_right_t(factor_of(*tiles[index]), tile)
            if index == 0:
                target[...] = value
            else:
                target[...] += value

        stream(weight, tiles, buffer, semaphore, body)

    def restored(target):
        def part(b, rows_b):
            target[rows_b, :] = dot_right_t(wide[rows_b, :].astype(bf16), order[...]).astype(bf16)

        each(part)

    def split_lanes(value, rows_b, start):
        halves[0, rows_b, pl.ds(start, 768)] = value[:, :768]
        halves[1, rows_b, pl.ds(start, width - 768)] = value[:, 768:]
        halves[1, rows_b, pl.ds(start + width - 768, 2 * 768 - width)] = jnp.zeros(
            (value.shape[0], 2 * 768 - width), bf16
        )

    def attention_back(sources, table_refs, masked, put):
        back[...] = jnp.zeros_like(back)
        total[...] = jnp.zeros_like(total)

        def prepare(b, rows_b):
            value, scale = head_norm(proj[rows_b, first_lanes], heads_ref)
            wide[rows_b, :] = value
            factor[rows_b, :] = scale
            turned_value = turn(value, table_refs) if table_refs else value
            query[rows_b, :] = turned_value.astype(bf16)

        each(prepare)

        @pl.loop(0, batch)
        def _(b):
            rows_b = pl.ds(pl.multiple_of(b * size, size), size)
            for head in range(HEADS):
                lanes, inside = window_of(head, width)
                behind = shift_lanes(lanes, width)
                queries = query[rows_b, lanes] * inside.astype(bf16)
                keys = pair_rows(sources, b, size, lanes)
                scores = dot_right_t(queries, keys) * scaling
                if masked:
                    scores = jnp.where(valid[pl.ds(b, 1), :] > 0.5, scores, masked_value)
                probs, _ = softmax_of(scores)
                grads = mix_grad[rows_b, lanes] * inside.astype(bf16)
                prob_grad = dot_right_t(grads, pair_rows(sources, b, size, behind))
                score_grad = softmax_back(probs, prob_grad).astype(bf16)
                value_grad = dot_left_t(probs.astype(bf16), grads)
                key_grad = dot_left_t(score_grad, queries) * scaling
                back[rows_b, lanes] += dot_plain(score_grad, keys) * (inside * scaling)
                for at in range(2):
                    part = slice(at * size, (at + 1) * size)
                    total[at, rows_b, lanes] += key_grad[part]
                    total[at, rows_b, behind] += value_grad[part]

        def finish(b, rows_b):
            value = back[rows_b, :]
            if table_refs:
                value = turn_back(value, table_refs)
            value = head_norm_back(value, wide[rows_b, :], factor[rows_b, :], heads_ref)
            put(value.astype(bf16), rows_b)

        each(finish)

    def exchange(index):
        return pltpu.make_async_remote_copy(
            src_ref=keyval.at[pl.ds(0, rows), :],
            dst_ref=landed.at[index],
            send_sem=exchange_send.at[index],
            recv_sem=exchange_recv.at[index],
            device_id=plan.sibling,
            device_id_type=MESH,
        )

    def keys_back(index, mine, table_refs, put):
        def part(b, rows_b):
            normed_keys, scale = head_norm(proj[rows_b, last_lanes], heads_ref)
            value = total[mine, rows_b, first_lanes] + landed[index, rows_b, first_lanes].astype(f32)
            if table_refs:
                value = turn_back(value, table_refs)
            key_grad = head_norm_back(value, normed_keys, scale, heads_ref).astype(bf16)
            value = total[mine, rows_b, last_lanes] + landed[index, rows_b, last_lanes].astype(f32)
            put(key_grad, value.astype(bf16), rows_b)

        each(part)

    def twin_product(w, extent, height, left, right):
        starts, places, shape = lane_places(height, extent, out_buffer.shape[4])

        def part(which):
            def value(index):
                start, lanes = starts[index]
                product = dot_plain(left(which), right(which, start, lanes))
                return product.reshape(4, 4, height, lanes)

            return value

        twin.run(w, places, shape, part(1 - core), part(core))

    halves[1, :, first_lanes] = grad[...].astype(bf16)
    pair_tiles = tiles_of(width, 384, (1,))
    back_through(
        pair_w, pair_tiles, lambda at, start, extent: halves[at, :, pl.ds(start, extent)], wide
    )
    restored(mix_grad)
    attention_back([keyval], (), True, lambda value, rows_b: split_lanes(value, rows_b, width))
    keyval[pl.ds(0, rows), :] = total[1 - core].astype(bf16)
    exchange(0).start()
    plan.middle(down)
    query_tiles = tiles_of(768, 384)
    back_through(
        query_w,
        query_tiles,
        lambda at, start, extent: halves[at, :, pl.ds(width + start, extent)],
        wide,
    )

    def self_part(b, rows_b):
        value = exact_restore(order[...], wide[rows_b, :])
        value, gain_part = norm_back(after_self[rows_b, :], gains[1:2, :], value)
        gain_grads[1:2, :] += gain_part
        value = grad[rows_b, :] + value
        grad[rows_b, :] = value
        halves[0, rows_b, first_lanes] = value.astype(bf16)

    each(self_part)
    pair_tiles_two = tiles_of(width, 384, (0,))
    back_through(
        pair_w, pair_tiles_two, lambda at, start, extent: halves[at, :, pl.ds(start, extent)], wide
    )
    restored(mix_grad)
    turned[0] = jnp.transpose(attn_cat[...])
    turned[1] = jnp.transpose(cross_cat[...])
    twin_product(
        2,
        width,
        block,
        lambda at: turned[at],
        lambda at, start, extent: halves[at, :, pl.ds(start, extent)],
    )
    plan.begin(pair_s)
    turned[0] = jnp.transpose(cross_in[...])
    twin_product(
        0,
        768,
        block,
        lambda at: turned[0],
        lambda at, start, extent: halves[at, :, pl.ds(width + start, extent)],
    )
    plan.begin(query_s)
    plan.middle(up)
    plan.leave(down)

    exchange(0).wait()

    def text_part(key_grad, value_grad, rows_b):
        halves[0, rows_b, first_lanes] = key_grad
        halves[1, rows_b, first_lanes] = value_grad

    keys_back(0, core, (), text_part)
    text_width = text.shape[1]
    turned[0, pl.ds(0, text_width), :] = jnp.transpose(text[...])
    twin_product(
        1,
        width,
        text_width // 16,
        lambda at: turned[0, pl.ds(0, text_width), :],
        lambda at, start, extent: halves[at, :, pl.ds(start, extent)],
    )
    plan.begin(keyval_s)
    keyval_tiles = tiles_of(width, 384)
    back_through(
        keyval_w,
        keyval_tiles,
        lambda at, start, extent: halves[at, :, pl.ds(start, extent)],
        text_grad,
    )

    load(
        (qkv, proj),
        (keyval_here, keyval.at[pl.ds(0, rows), :]),
        (keyval_there, keyval.at[pl.ds(rows, rows), :]),
    )

    def query_part(value, rows_b):
        halves[0, rows_b, first_lanes] = value

    sources = [keyval.at[pl.ds(0, rows), :], keyval.at[pl.ds(rows, rows), :]]
    attention_back(sources, tables, False, query_part)
    keyval[pl.ds(0, rows), :] = total[1].astype(bf16)
    exchange(1).start()
    plan.leave(up)
    plan.close(down)
    plan.middle(pair_s)
    plan.middle(query_s)
    exchange(1).wait()

    def key_part(key_grad, value_grad, rows_b):
        halves[1, rows_b, first_lanes] = key_grad
        split_lanes(value_grad, rows_b, width)

    keys_back(1, 0, tables, key_part)
    turned[0] = jnp.transpose(attn_in[...])
    wide_half = halves.shape[2]
    twin_product(
        3,
        wide_half,
        block,
        lambda at: turned[0],
        lambda at, start, extent: halves[at, :, pl.ds(start, extent)],
    )
    plan.begin(qkv_s)
    qkv_tiles = tiles_of(wide_half, 384)
    back_through(
        qkv_w, qkv_tiles, lambda at, start, extent: halves[at, :, pl.ds(start, extent)], wide
    )

    def hidden_part(b, rows_b):
        value = exact_restore(order[...], wide[rows_b, :])
        shift_grad[b : b + 1, :] = jnp.sum(value, axis=0, keepdims=True)
        value, gain_part = norm_back(hidden[rows_b, :], gains[0:1, :], value)
        gain_grads[0:1, :] += gain_part
        halves[0, rows_b, first_lanes] = (grad[rows_b, :] + value).astype(bf16)

    each(hidden_part)
    plan.close(up)
    plan.middle(keyval_s)
    plan.leave(pair_s)
    plan.leave(query_s)

    for at in range(2):
        for part in range(2):
            turned[at, pl.ds(part * (width // 2), width // 2), :] = jnp.transpose(
                normed[at, part]
            )
    twin_product(
        4,
        width,
        block,
        lambda at: turned[at],
        lambda at, start, extent: halves[0, :, pl.ds(start, extent)],
    )
    plan.begin(skip_s)
    plan.leave(keyval_s)
    plan.middle(qkv_s)
    skip_tiles = tiles_of(width, 384)

    def skip_body(index, tile):
        at, start, extent = skip_tiles[index]
        value = dot_right_t(halves[0, :, pl.ds(start, extent)], tile)
        lanes = pl.ds(at * width, width)
        if start == 0:
            total[0, :, lanes] = value
        else:
            total[0, :, lanes] += value

    stream(skip_w, skip_tiles, buffer, semaphore, skip_body)
    keep = pltpu.make_async_copy(total.at[0], normed_grad, loads.at[0])
    keep.start()
    plan.close(pair_s)
    plan.close(query_s)
    plan.close(keyval_s)
    plan.leave(qkv_s)
    plan.middle(skip_s)
    plan.close(qkv_s)
    plan.leave(skip_s)
    plan.close(skip_s)
    keep.wait()
    for w in range(7):
        plan.finish(w)


def joined_back_body(batch, normed_grad, latent, skip, skip_gain, order_skip, joined, gain_grad):
    width = latent.shape[1]
    size = latent.shape[0] // batch
    upper_half = lax.axis_index("fsdp") >= 8
    gain_grad[...] = jnp.zeros_like(gain_grad)
    for b in range(batch):
        rows_b = pl.ds(b * size, size)
        near, away = 0.0, 0.0
        for at in range(2):
            part = normed_grad[rows_b, at * width : (at + 1) * width]
            near = near + exact_restore(order_skip[at], part[:, : width // 2])
            away = away + exact_restore(order_skip[at], part[:, width // 2 :])
        left = latent[rows_b, :].astype(f32)
        right = skip[rows_b, :].astype(f32)
        left_grad = jnp.where(upper_half, away, near)
        right_grad = jnp.where(upper_half, near, away)

        def mean(first, second):
            total = jnp.sum(first, axis=1, keepdims=True) + jnp.sum(second, axis=1, keepdims=True)
            return total / (2 * width)

        middle = mean(left, right)
        left, right = left - middle, right - middle
        factor = lax.rsqrt(mean(left * left, right * right) + norm_eps)
        left, right = left * factor, right * factor
        gain_grad[0:1, :width] += jnp.sum(left_grad * left, axis=0, keepdims=True)
        gain_grad[0:1, width:] += jnp.sum(right_grad * right, axis=0, keepdims=True)
        left_grad = left_grad * skip_gain[:, :width]
        right_grad = right_grad * skip_gain[:, width:]
        first = mean(left_grad, right_grad)
        second = mean(left_grad * left, right_grad * right)
        joined[0, rows_b, :] = factor * (left_grad - first - left * second)
        joined[1, rows_b, :] = factor * (right_grad - first - right * second)


class Links:
    def __init__(self, fsdp_count):
        self.count = fsdp_count
        self.me = lax.axis_index("fsdp")
        self.core = lax.axis_index("seq")
        self.high_bits = fsdp_count.bit_length() - 3
        self.quad = 4 << (self.high_bits - 2)
        offsets = [0]
        for bit in range(self.high_bits - 2):
            offsets = offsets + [offset | (4 << bit) for offset in offsets]
        self.high_offsets = [k * self.quad | offset for k in range(4) for offset in offsets]

    def swap(self, value, mask_first, mask_second):
        pairs = []
        for index in range(self.count):
            pairs.append((2 * index, 2 * (index ^ mask_first)))
            pairs.append((2 * index + 1, 2 * (index ^ mask_second) + 1))
        return lax.ppermute(value, ("fsdp", "seq"), pairs)

    def sibling(self, value):
        return lax.ppermute(value, "seq", [(0, 1), (1, 0)])

    def pick(self, first, second):
        return jnp.where(self.core == 0, first, second)

    def offset(self, block):
        return self.high_offsets[block % (self.count // 4)] | (block // (self.count // 4))

    def place(self, offset):
        table = [0] * self.count
        for block in range(self.count):
            table[self.offset(block)] = block
        return jnp.array(table, jnp.int32)[offset]

    def columns(self, own, other):
        return self.pick(
            jnp.concatenate([own, other], axis=-1), jnp.concatenate([other, own], axis=-1)
        )

    def halves(self, value):
        half = value.shape[-1] // 2
        first, second = value[..., :half], value[..., half:]
        return self.pick(first, second), self.pick(second, first)

    def order_matrix(self, size):
        block = size // self.count
        at = lax.broadcasted_iota(jnp.int32, (size, size), 0)
        table = jnp.array([self.offset(b) for b in range(self.count)], jnp.int32)
        starts = jnp.bitwise_xor(self.me, table) * block
        wanted = (starts[:, None] + jnp.arange(block, dtype=jnp.int32)[None, :]).reshape(1, size)
        return (at == wanted).astype(bf16)

    def order_skip(self, width):
        block = width // self.count
        offsets = [
            offset & (self.count // 2 - 1) for offset in self.high_offsets[: self.count // 2 // 4 * 1]
        ]
        offsets = [offset | q for q in range(4) for offset in offsets]
        lower = jnp.bitwise_and(self.me, self.count // 2 - 1)
        starts = jnp.bitwise_xor(lower, jnp.array(offsets, jnp.int32)) * (2 * block)
        starts = jnp.stack([starts, starts + block])
        wanted = (starts[:, :, None] + jnp.arange(block, dtype=jnp.int32)).reshape(1, width)
        return (lax.broadcasted_iota(jnp.int32, (width, width), 0) == wanted).astype(bf16)

    def order_blocks(self, value):
        size = value.shape[1] // self.count
        parts = []
        for block in range(self.count):
            source = jnp.bitwise_xor(self.me, self.offset(block))
            parts.append(lax.dynamic_slice_in_dim(value, source * size, size, 1))
        return jnp.concatenate(parts, axis=1)

    def restore_blocks(self, value):
        size = value.shape[1] // self.count
        parts = []
        for shard in range(self.count):
            source = self.place(jnp.bitwise_xor(self.me, shard))
            parts.append(lax.dynamic_slice_in_dim(value, source * size, size, 1))
        return jnp.concatenate(parts, axis=1)

    def extra_gather(self, mine):
        blocks = mine
        for bit in range(self.high_bits - 2):
            blocks = jnp.concatenate([blocks, self.swap(blocks, 4 << bit, 4 << bit)], axis=0)
        return blocks

    def extra_scatter(self, value):
        for bit in reversed(range(self.high_bits - 2)):
            size = value.shape[-2] // 2
            value = value[..., :size, :] + self.swap(value[..., size:, :], 4 << bit, 4 << bit)
        return value


class Gather:
    def __init__(self, links, shards):
        self.links = links
        half = shards[0].shape[1] // 2
        self.rows = shards[0].shape[0]
        self.weights = len(shards)
        self.shards = jnp.concatenate(
            [links.pick(shard[:, :half], shard[:, half:]) for shard in shards], axis=0
        )
        self.pending = [self.shards]
        self.stage = 0

    def advance(self):
        links = self.links
        self.stage += 1
        if self.stage == 1:
            blocks = [self.pending[0]]
            for bit in range(links.high_bits - 2):
                got = links.swap(jnp.concatenate(blocks, axis=0), 4 << bit, 4 << bit)
                size = self.rows * self.weights
                blocks = blocks + [got[at * size : (at + 1) * size] for at in range(len(blocks))]
            self.low_blocks = len(blocks)
            mine = jnp.concatenate(blocks, axis=0) if len(blocks) > 1 else blocks[0]
            self.pending = [mine] + [
                links.swap(mine, k * links.quad, k * links.quad) for k in range(1, 4)
            ]
        elif self.stage == 2:
            size = self.rows * self.weights
            cuts = [
                got[at * size + w * self.rows : at * size + (w + 1) * self.rows]
                for w in range(self.weights)
                for got in self.pending
                for at in range(self.low_blocks)
            ]
            base = jnp.concatenate(cuts, axis=0)
            self.pending = [
                base, links.swap(base, 1, 2), links.swap(base, 2, 1), links.sibling(base)
            ]
        elif self.stage == 3:
            base, first, second, base_there = self.pending
            self.kept = [base, second, base_there]
            self.pending = [
                links.swap(first, 2, 1), links.sibling(first), links.sibling(second), *self.pending
            ]
        elif self.stage == 4:
            self.pending[0:1] = [links.sibling(self.pending[0]), self.pending[0]]
        elif self.stage == 5:
            both_there, both, first_there, second_there, base, first, second, base_there = self.pending
            size = base.shape[0] // self.weights
            self.result = []
            for w in range(self.weights):
                cut = slice(w * size, (w + 1) * size)
                pick = links.pick
                own = jnp.concatenate(
                    [base[cut], pick(first[cut], second[cut]), pick(second[cut], first[cut]), both[cut]],
                    axis=0,
                )
                other = jnp.concatenate(
                    [
                        base_there[cut],
                        pick(second_there[cut], first_there[cut]),
                        pick(first_there[cut], second_there[cut]),
                        both_there[cut],
                    ],
                    axis=0,
                )
                self.result.append((own, other))
            self.pending = []

    def finish(self):
        while self.stage < 5:
            self.advance()
        return self.result


class Scatter:
    def __init__(self, links, pairs):
        self.links = links
        self.pairs = pairs
        self.pending = [other for _, other in pairs]
        self.stage = 0

    def advance(self):
        links = self.links
        pick = links.pick
        self.stage += 1
        if self.stage == 1:
            self.pending = [own for own, _ in self.pairs] + [
                links.sibling(other) for other in self.pending
            ]
        elif self.stage == 2:
            count = len(self.pairs)
            send, keep = [[], []], [[], []]
            for own, got in zip(self.pending[:count], self.pending[count:]):
                size = own.shape[0] // 4
                cuts = [
                    own[q * size : (q + 1) * size].astype(f32) + got[q * size : (q + 1) * size].astype(f32)
                    for q in range(4)
                ]
                send[0].append(pick(cuts[2], cuts[1]).astype(bf16))
                send[1].append(cuts[3].astype(bf16))
                keep[0].append(cuts[0])
                keep[1].append(pick(cuts[1], cuts[2]))
            self.sizes = [part.shape[0] for part in keep[0]]
            self.keep = [jnp.concatenate(part, axis=0) for part in keep]
            self.pending = [links.swap(jnp.concatenate(send[0] + send[1], axis=0), 2, 1)]
        elif self.stage == 3:
            total = sum(self.sizes)
            got = self.pending[0].astype(f32)
            self.keep, send = self.keep[0] + got[:total], (self.keep[1] + got[total:]).astype(bf16)
            self.pending = [links.swap(send, 1, 2)]
        elif self.stage == 4:
            summed = self.keep + self.pending[0].astype(f32)
            keep, send = [], [[], [], []]
            start = 0
            for size in self.sizes:
                part = size // 4
                keep.append(summed[start : start + part])
                for k in range(1, 4):
                    send[k - 1].append(summed[start + k * part : start + (k + 1) * part].astype(bf16))
                start += size
            self.keep = jnp.concatenate(keep, axis=0)
            self.pending = [
                links.swap(jnp.concatenate(send[k - 1], axis=0), k * links.quad, k * links.quad)
                for k in range(1, 4)
            ]
        elif self.stage == 5:
            total = self.keep
            for got in self.pending:
                total = total + got.astype(f32)
            rows = [size // 4 for size in self.sizes]
            for bit in reversed(range(links.high_bits - 2)):
                keep, send, start = [], [], 0
                for at, size in enumerate(rows):
                    keep.append(total[start : start + size // 2])
                    send.append(total[start + size // 2 : start + size])
                    start += size
                    rows[at] = size // 2
                got = links.swap(jnp.concatenate(send, axis=0), 4 << bit, 4 << bit)
                total = jnp.concatenate(keep, axis=0) + got
            self.rows = rows
            self.pending = [total, links.sibling(total)]
        elif self.stage == 6:
            whole = links.columns(*self.pending)
            self.result, start = [], 0
            for size in self.rows:
                self.result.append(whole[start : start + size])
                start += size
            self.pending = []

    def finish(self):
        while self.stage < 6:
            self.advance()
        return self.result


def tie(value, *jobs):
    leaves, tree = jax.tree.flatten(value)
    flat = list(leaves)
    for job in jobs:
        flat.extend(job.pending)
    flat = list(lax.optimization_barrier(tuple(flat)))
    at = len(leaves)
    value = jax.tree.unflatten(tree, flat[:at])
    for job in jobs:
        job.pending = flat[at : at + len(job.pending)]
        at += len(job.pending)
        job.advance()
    return value


def parts_of(value):
    high = value.astype(bf16)
    return high, (value - high.astype(f32)).astype(bf16)


def sum_heads(value, heads_ref):
    high, low = parts_of(value)
    return dot_plain(high, heads_ref[...]) + dot_plain(low, heads_ref[...])


def spread_heads(value, heads_ref):
    high, low = parts_of(value)
    return dot_right_t(high, heads_ref[...]) + dot_right_t(low, heads_ref[...])


def head_norm(value, heads_ref):
    center = value - spread_heads(sum_heads(value, heads_ref) * (1.0 / HD), heads_ref)
    spread = sum_heads(center * center, heads_ref) * (1.0 / HD)
    factor = spread_heads(lax.rsqrt(spread + norm_eps), heads_ref)
    return center * factor, factor


def head_norm_back(grad, normed, factor, heads_ref):
    first = sum_heads(grad, heads_ref) * (1.0 / HD)
    second = sum_heads(grad * normed, heads_ref) * (1.0 / HD)
    return factor * (
        grad - spread_heads(first, heads_ref) - normed * spread_heads(second, heads_ref)
    )


def partner(value, former):
    quarter = HD // 4
    width = value.shape[1]
    up = pltpu.roll(value, width - quarter, 1)
    down = pltpu.roll(value, quarter, 1)
    return jnp.where(former > 0.5, up, down)


def turn(value, table_refs):
    cosine, sine, former = table_refs
    return value * cosine[...] + partner(value, former[...]) * sine[...]


def turn_back(value, table_refs):
    cosine, sine, former = table_refs
    return value * cosine[...] - partner(value, former[...]) * sine[...]


def window_of(head, width):
    start = min(head * HD // 128 * 128, width - 256)
    lane = lax.broadcasted_iota(jnp.int32, (1, 256), 1) + start
    inside = jnp.logical_and(lane >= head * HD, lane < (head + 1) * HD)
    return pl.ds(start, 256), inside.astype(f32)


def normed_rows(proj_ref, heads_ref, table_refs, rows):
    value, factor = head_norm(proj_ref[rows, :], heads_ref)
    turned = turn(value, table_refs) if table_refs else value
    return value, factor, turned


def keys_body(batch, turned, *refs):
    key_ref, value_ref, heads_ref = refs[:3]
    table_refs, out_ref = refs[3:-1], refs[-1]
    width = key_ref.shape[1]
    size = key_ref.shape[0] // batch
    for b in range(batch):
        rows = pl.ds(b * size, size)
        out_ref[rows, :width] = normed_rows(key_ref, heads_ref, table_refs, rows)[2].astype(bf16)
        out_ref[rows, width:] = value_ref[rows, :].astype(bf16)


def pair_rows(refs, b, size, lanes):
    if len(refs) == 2:
        return jnp.concatenate([ref[pl.ds(b * size, size), lanes] for ref in refs], axis=0)
    return refs[0][pl.ds(b * 2 * size, 2 * size), lanes]


def shift_lanes(lanes, width):
    return pl.ds(lanes.start + width, lanes.size)


def scores_of(query, key, lengths_ref, b, scaling):
    scores = dot_right_t(query, key) * scaling
    if lengths_ref is not None:
        column = lax.broadcasted_iota(jnp.int32, scores.shape, 1)
        scores = jnp.where(column < lengths_ref[b], scores, masked_value)
    return scores


def softmax_of(scores):
    largest = jnp.max(scores, axis=1, keepdims=True)
    raised = jnp.exp(scores - largest)
    return raised / jnp.sum(raised, axis=1, keepdims=True), largest


def attention_body(batch, masked, turned, sources, scaling, *refs):
    refs = list(refs)
    lengths_ref = refs.pop(0) if masked else None
    proj_ref, heads_ref = refs.pop(0), refs.pop(0)
    table_refs = [refs.pop(0) for _ in range(3)] if turned else []
    keyval_refs = [refs.pop(0) for _ in range(sources)]
    out_ref, peak_ref, query_ref, mixed_ref = refs
    size, width = proj_ref.shape[0] // batch, proj_ref.shape[1]
    peak_ref[...] = jnp.full_like(peak_ref, masked_value)
    mixed_ref[...] = jnp.zeros_like(mixed_ref)
    for b in range(batch):
        rows = pl.ds(b * size, size)
        query_ref[rows, :] = normed_rows(proj_ref, heads_ref, table_refs, rows)[2].astype(bf16)

    @pl.loop(0, batch)
    def _(b):
        rows = pl.ds(pl.multiple_of(b * size, size), size)
        for head in range(HEADS):
            lanes, inside = window_of(head, width)
            query = query_ref[rows, lanes] * inside.astype(bf16)
            key = pair_rows(keyval_refs, b, size, lanes)
            scores = scores_of(query, key, lengths_ref, b, scaling)
            probs, largest = softmax_of(scores)
            largest = jnp.max(largest, axis=0, keepdims=True)
            peak_ref[head : head + 1, :] = jnp.maximum(
                peak_ref[head : head + 1, :], jnp.broadcast_to(largest, (1, 128))
            )
            value = pair_rows(keyval_refs, b, size, shift_lanes(lanes, width))
            mixed_ref[rows, lanes] += dot_plain(probs.astype(bf16), value) * inside

    out_ref[...] = mixed_ref[...].astype(bf16)


def attention_back_body(batch, masked, turned, sources, scaling, *refs):
    refs = list(refs)
    lengths_ref = refs.pop(0) if masked else None
    proj_ref, grad_ref, heads_ref = refs.pop(0), refs.pop(0), refs.pop(0)
    table_refs = [refs.pop(0) for _ in range(3)] if turned else []
    keyval_refs = [refs.pop(0) for _ in range(sources)]
    out_ref, here_ref, there_ref, normed_ref, factor_ref, query_ref, back_ref, total_ref = refs
    size, width = proj_ref.shape[0] // batch, proj_ref.shape[1]
    back_ref[...] = jnp.zeros_like(back_ref)
    total_ref[...] = jnp.zeros_like(total_ref)
    for b in range(batch):
        rows = pl.ds(b * size, size)
        normed, factor, query = normed_rows(proj_ref, heads_ref, table_refs, rows)
        normed_ref[rows, :] = normed
        factor_ref[rows, :] = factor
        query_ref[rows, :] = query.astype(bf16)

    @pl.loop(0, batch)
    def _(b):
        rows = pl.ds(pl.multiple_of(b * size, size), size)
        for head in range(HEADS):
            lanes, inside = window_of(head, width)
            behind = shift_lanes(lanes, width)
            query = query_ref[rows, lanes] * inside.astype(bf16)
            key = pair_rows(keyval_refs, b, size, lanes)
            probs, _ = softmax_of(scores_of(query, key, lengths_ref, b, scaling))
            grad = grad_ref[rows, lanes] * inside.astype(bf16)
            value = pair_rows(keyval_refs, b, size, behind)
            prob_grad = dot_right_t(grad, value)
            score_grad = softmax_back(probs, prob_grad).astype(bf16)
            value_grad = dot_left_t(probs.astype(bf16), grad)
            key_grad = dot_left_t(score_grad, query) * scaling
            back_ref[rows, lanes] += dot_plain(score_grad, key) * (inside * scaling)
            for at in range(2):
                part = slice(at * size, (at + 1) * size)
                total_ref[at, rows, lanes] += key_grad[part]
                total_ref[at, rows, behind] += value_grad[part]

    for b in range(batch):
        rows = pl.ds(b * size, size)
        grad = back_ref[rows, :]
        if table_refs:
            grad = turn_back(grad, table_refs)
        out_ref[rows, :] = head_norm_back(
            grad, normed_ref[rows, :], factor_ref[rows, :], heads_ref
        ).astype(bf16)
    mine = lax.axis_index("seq") if masked else 0
    here_ref[...] = total_ref[mine]
    there_ref[...] = total_ref[1 - mine].astype(bf16)


def keys_back_body(batch, turned, *refs):
    key_ref, here_ref, from_there_ref, heads_ref = refs[:4]
    table_refs, out_ref = refs[4:-1], refs[-1]
    width = key_ref.shape[1]
    size = key_ref.shape[0] // batch
    for b in range(batch):
        rows = pl.ds(b * size, size)
        normed, factor, _ = normed_rows(key_ref, heads_ref, (), rows)
        grad = here_ref[rows, :width] + from_there_ref[rows, :width].astype(f32)
        if table_refs:
            grad = turn_back(grad, table_refs)
        out_ref[rows, :width] = head_norm_back(grad, normed, factor, heads_ref).astype(bf16)
        out_ref[rows, width:] = (
            here_ref[rows, width:] + from_there_ref[rows, width:].astype(f32)
        ).astype(bf16)


def plain_call(body, outs, blocks, scratch=(), lengths=None):
    def spec(array, column):
        if column is None:
            return pl.BlockSpec(array.shape, lambda i, *_: (0,) * array.ndim)
        return pl.BlockSpec((array.shape[0], column[1]), lambda i, *_: (0, column[0]))

    def out_spec(shape):
        return pl.BlockSpec(shape.shape, lambda i, *_: (0,) * len(shape.shape))

    grid_spec = pltpu.PrefetchScalarGridSpec(
        num_scalar_prefetch=0 if lengths is None else 1,
        grid=(1,),
        in_specs=[spec(*block) for block in blocks],
        out_specs=[out_spec(shape) for shape in outs],
        scratch_shapes=list(scratch),
    )
    given = [] if lengths is None else [lengths]
    return pl.pallas_call(
        body,
        grid_spec=grid_spec,
        out_shape=list(outs),
        compiler_params=pltpu.CompilerParams(vmem_limit_bytes=50 * 2**20),
    )(*given, *[array for array, _ in blocks])


def lanes_of(value, multiple):
    size = 128 * multiple
    spare = -value.shape[-1] % size
    value = jnp.pad(value, [(0, 0)] * (value.ndim - 1) + [(0, spare)])
    return value.reshape(*value.shape[:-1], -1, 128)


def exact_restore(matrix, value):
    high = value.astype(bf16)
    low = (value - high.astype(f32)).astype(bf16)
    return dot_right_t(high, matrix) + dot_right_t(low, matrix)


def local(
    latent,
    skip_input,
    condition,
    text_encoder_states,
    text_lengths,
    out_grad,
    skip_gain,
    norm_gains,
    skip_linear,
    shift_linear,
    self_qkv,
    self_out,
    cross_query,
    cross_keyval,
    cross_out,
    mlp_up,
    mlp_down,
    thresholds,
):
    batch, tokens, width = latent.shape
    rows = batch * tokens
    text_rows = text_encoder_states.shape[1]
    text_width = text_encoder_states.shape[2]
    scaling = HD ** (-0.5)
    links = Links(lax.axis_size("fsdp"))
    me, core = links.me, links.core
    count = links.count

    positions = core * tokens + jnp.arange(tokens)
    feature = jnp.arange(width) % HD
    freqs = 10000.0 ** (-(feature % (HD // 4)).astype(f32) / (HD // 4))
    place = jnp.where(
        feature[None, :] < HD // 2, (positions // GRID_W)[:, None], (positions % GRID_W)[:, None]
    )
    angles = place.astype(f32) * freqs[None, :]
    former = (feature % (HD // 2) < HD // 4)[None, :]
    cosine = jnp.cos(angles)
    sine = jnp.where(former, -jnp.sin(angles), jnp.sin(angles))
    tables = [(cosine, None), (sine, None), (former.astype(f32), None)]
    head_at = jnp.arange(width)[:, None] // HD == jnp.arange(128)[None, :]
    head_at = (head_at.astype(bf16), None)

    gain_rows = skip_gain.shape[0]
    third = norm_gains.shape[1]
    cond_act = jax.nn.silu(condition.astype(f32)).astype(bf16)
    small = jnp.concatenate([skip_gain, norm_gains.reshape(-1), cond_act.reshape(-1)])
    small = trade(lanes_of(small, 16), count, True, 1).reshape(count, -1)
    skip_gain_all = small[:, :gain_rows].reshape(-1).astype(f32)
    cond_start = gain_rows + 3 * third
    gains = small[:, gain_rows:cond_start].reshape(count, 3, third)
    gains = gains.transpose(1, 0, 2).reshape(3, width).astype(f32)
    cond_all = small[:, cond_start : cond_start + batch * width].reshape(count * batch, width)
    shift_rows = shift_linear.shape[0]
    cond_cut = lax.dynamic_slice_in_dim(cond_all, me * shift_rows, shift_rows, 1)
    shift_parts = dot_plain(cond_cut, shift_linear).reshape(count, batch * width)
    shift_parts = trade(lanes_of(shift_parts, 8), count, False, 2)
    shift = jnp.sum(shift_parts.reshape(count, -1), axis=0)[: batch * width].reshape(batch, width)

    def columns_mine(weight):
        half = weight.shape[1] // 2
        return links.pick(weight[:, :half], weight[:, half:])

    skip_half = skip_linear.shape[0] // 2
    shards = [
        links.pick(skip_linear[:skip_half], skip_linear[skip_half:]),
        columns_mine(self_qkv),
        links.pick(self_out, cross_out),
        columns_mine(cross_query),
        columns_mine(cross_keyval),
    ]
    shards = [links.extra_gather(shard) for shard in shards]
    shards = lax.optimization_barrier((shift, *shards))
    shift = shards[0]
    gathered = gather(shards[1:], links.quad, 3)
    w_skip, w_qkv, w_pair, w_query, w_keyval = (
        g.reshape(2, 16 * g.shape[2], g.shape[3]) for g in gathered
    )
    w_self_out, w_cross_out = w_pair[0], w_pair[1]
    get_up = Gather(links, [mlp_up])
    get_down = Gather(links, [mlp_down])
    w_skip = tie(w_skip, get_up, get_down)

    order = links.order_matrix(width)
    order_skip = links.order_skip(width)
    order_text = links.order_matrix(text_width)

    def product(value, weight):
        return jnp.concatenate([dot_plain(value, weight[0]), dot_plain(value, weight[1])], axis=1)

    def product_back(grad, weight):
        half = grad.shape[1] // 2
        return dot_right_t(grad[:, :half], weight[0]) + dot_right_t(grad[:, half:], weight[1])

    def sum_twins(own, other):
        there = links.sibling(dot_left_t(*other).astype(bf16))
        return own, there

    def finish_twins(own, there):
        value = (dot_left_t(*own) + there.astype(f32)).astype(bf16)
        return value.reshape(16, value.shape[0] // 16, value.shape[1])

    def column_grad(value, grad):
        own, other = links.halves(grad)
        return sum_twins((value, own), (value, other))

    def weight_grad(value, grad_halves):
        return (
            dot_left_t(value, grad_halves[0]).astype(bf16),
            dot_left_t(value, grad_halves[1]).astype(bf16),
        )

    def relative_product(value, weight):
        return links.columns(dot_plain(value, weight[0]), dot_plain(value, weight[1]))

    def relative_back(grad_halves, weight):
        return dot_right_t(grad_halves[0], weight[0]) + dot_right_t(grad_halves[1], weight[1])

    def reorder(value):
        return dot_plain(value, order).astype(bf16)

    def restore(value):
        return dot_right_t(value.astype(bf16), order).astype(bf16)

    joined = jnp.concatenate(
        [latent.reshape(rows, width), skip_input.reshape(rows, width)], axis=1
    ).astype(f32)
    normed = gained_norm(joined, skip_gain_all).astype(bf16)
    upper_half = (me >= count // 2).astype(jnp.int32)
    near = jnp.where(upper_half == 0, normed[:, :width], normed[:, width:])
    away = jnp.where(upper_half == 0, normed[:, width:], normed[:, :width])
    near = dot_plain(near, order_skip).astype(bf16).reshape(rows, 2, 4, 1, -1)
    away = dot_plain(away, order_skip).astype(bf16).reshape(rows, 2, 4, 1, -1)
    normed = jnp.concatenate([near, away], axis=3).reshape(rows, 2, width)
    normed = (normed[:, 0], normed[:, 1])
    hidden = dot_plain(normed[0], w_skip[0]) + dot_plain(normed[1], w_skip[1])

    def shifted(values, gain, moved):
        wide = jnp.broadcast_to(moved[:, None, :], (batch, tokens, width)).reshape(rows, width)
        return layer_norm(values) * gain + wide

    attn_in = reorder(shifted(hidden, gains[0], shift).astype(bf16))
    qkv_proj = product(attn_in, w_qkv)
    query_block, key_block, value_block = ((qkv_proj, (at, width)) for at in range(3))

    def shaped(height, breadth, dtype):
        return jax.ShapeDtypeStruct((height, breadth), dtype)

    (keyval_here,) = plain_call(
        functools.partial(keys_body, batch, True),
        [shaped(rows, 2 * width, bf16)],
        [key_block, value_block, head_at, *tables],
    )
    keyval_there = links.sibling(keyval_here)
    qkv_proj = tie(qkv_proj, get_up)
    keyvals = [(keyval_here, None), (keyval_there, None)]
    attention_scratch = [pltpu.VMEM((rows, width), bf16), pltpu.VMEM((rows, width), f32)]
    attn_cat, self_peak = plain_call(
        functools.partial(attention_body, batch, False, True, 2, scaling),
        [shaped(rows, width, bf16), shaped(HEADS, 128, f32)],
        [query_block, head_at, *tables, *keyvals],
        attention_scratch,
    )
    attn_cat = reorder(attn_cat)
    attn_cat = tie(attn_cat, get_down)
    after_self = hidden + dot_plain(attn_cat, w_self_out)
    cross_in = reorder(gained_norm(after_self, gains[1]).astype(bf16))
    cq_proj = product(cross_in, w_query)

    text = text_encoder_states.reshape(batch * text_rows, text_width)
    text_ordered = dot_plain(text, order_text).astype(bf16)
    ckv_proj = product(text_ordered, w_keyval)
    (cross_keyval_all,) = plain_call(
        functools.partial(keys_body, batch, False),
        [shaped(batch * text_rows, 2 * width, bf16)],
        [(ckv_proj, (0, width)), (ckv_proj, (1, width)), head_at],
    )
    cq_proj = tie(cq_proj, get_up)
    cross_cat, cross_peak = plain_call(
        functools.partial(attention_body, batch, True, False, 1, scaling),
        [shaped(rows, width, bf16), shaped(HEADS, 128, f32)],
        [(cq_proj, None), head_at, (cross_keyval_all, None)],
        attention_scratch,
        text_lengths,
    )
    cross_cat = reorder(cross_cat)
    after_cross = after_self + dot_plain(cross_cat, w_cross_out)
    mlp_in = reorder(gained_norm(after_cross, gains[2]).astype(bf16))
    mlp_in = tie(mlp_in, get_up, get_down)
    (w_up,) = get_up.finish()
    upper = relative_product(mlp_in, w_up)
    activated = links.order_blocks(gelu_tanh(upper).astype(bf16))

    down_in = out_grad.reshape(rows, width)
    result_grad = down_in.astype(f32)
    down_halves = links.halves(down_in)
    put_down = Scatter(links, [weight_grad(activated, down_halves)])
    put_down.advance()
    activated = tie(activated, put_down)
    (w_down,) = get_down.finish()
    block_out = (after_cross + relative_product(activated, w_down)).astype(bf16)
    act_grad = links.restore_blocks(relative_back(down_halves, w_down))
    upper_grad = jax.vjp(gelu_tanh, upper)[1](act_grad)[0].astype(bf16)
    upper_halves = links.halves(upper_grad)
    put_up = Scatter(links, [weight_grad(mlp_in, upper_halves)])
    put_up.advance()
    mlp_in_grad = exact_restore(order, relative_back(upper_halves, w_up))
    cross_part, gain_third = jax.vjp(gained_norm, after_cross, gains[2])[1](mlp_in_grad)
    cross_grad = result_grad + cross_part
    cross_bf = tie(cross_grad.astype(bf16), put_up)
    cmix_grad = restore(dot_right_t(cross_bf, w_cross_out))
    cmix_grad = tie(cmix_grad, put_down)
    back_scratch = [
        pltpu.VMEM((rows, width), f32),
        pltpu.VMEM((rows, width), f32),
        pltpu.VMEM((rows, width), bf16),
        pltpu.VMEM((rows, width), f32),
        pltpu.VMEM((2, rows, 2 * width), f32),
    ]
    back_outs = [
        shaped(rows, width, bf16), shaped(rows, 2 * width, f32), shaped(rows, 2 * width, bf16)
    ]
    cq_grad, ckeyval_mine, ckeyval_theirs = plain_call(
        functools.partial(attention_back_body, batch, True, False, 1, scaling),
        back_outs,
        [(cq_proj, None), (cmix_grad, None), head_at, (cross_keyval_all, None)],
        back_scratch,
        text_lengths,
    )
    put_query = column_grad(cross_in, cq_grad)
    cq_grad = tie(cq_grad, put_up, put_down)
    cross_in_grad = exact_restore(order, product_back(cq_grad, w_query))
    self_part, gain_second = jax.vjp(gained_norm, after_self, gains[1])[1](cross_in_grad)
    self_grad = cross_grad + self_part

    text_half = text_rows // 2
    ckey_mine = lax.dynamic_slice_in_dim(
        ckv_proj.reshape(batch, text_rows, 2 * width)[:, :, :width], core * text_half, text_half, 1
    ).reshape(batch * text_half, width)
    (keyval_grad,) = plain_call(
        functools.partial(keys_back_body, batch, False),
        [shaped(batch * text_half, 2 * width, bf16)],
        [
            (ckey_mine, None),
            (ckeyval_mine, None),
            (links.sibling(ckeyval_theirs), None),
            head_at,
        ],
    )
    text_mine = lax.dynamic_slice_in_dim(
        text_ordered.reshape(batch, text_rows, text_width), core * text_half, text_half, 1
    ).reshape(-1, text_width)
    put_keyval = column_grad(text_mine, keyval_grad)
    grad_text = exact_restore(order_text, product_back(keyval_grad, w_keyval))
    grad_text = grad_text.reshape(batch, text_half, text_width)

    self_bf = self_grad.astype(bf16)
    put_pair = sum_twins(
        (links.pick(attn_cat, cross_cat), links.pick(self_bf, cross_bf)),
        (links.pick(cross_cat, attn_cat), links.pick(cross_bf, self_bf)),
    )
    self_bf = tie(self_bf, put_down)
    mix_grad = restore(dot_right_t(self_bf, w_self_out))
    mix_grad = tie(mix_grad, put_up)
    query_grad, here, there = plain_call(
        functools.partial(attention_back_body, batch, False, True, 2, scaling),
        back_outs,
        [query_block, (mix_grad, None), head_at, *tables, *keyvals],
        back_scratch,
    )
    here = tie(here, put_up)
    (key_value_grad,) = plain_call(
        functools.partial(keys_back_body, batch, True),
        [shaped(rows, 2 * width, bf16)],
        [key_block, (here, None), (links.sibling(there), None), head_at, *tables],
    )
    qkv_grad = jnp.concatenate([query_grad, key_value_grad], axis=1)
    put_qkv = column_grad(attn_in, qkv_grad)
    attn_in_grad = exact_restore(order, product_back(qkv_grad, w_qkv))
    hidden_part, gain_first, shift_grad = jax.vjp(shifted, hidden, gains[0], shift)[1](
        attn_in_grad
    )
    hidden_grad = self_grad + hidden_part
    hidden_bf = hidden_grad.astype(bf16)
    put_skip = sum_twins(
        (links.pick(*normed), hidden_bf), (links.pick(normed[1], normed[0]), hidden_bf)
    )
    normed_grad = jnp.concatenate(
        [dot_right_t(hidden_bf, w_skip[0]), dot_right_t(hidden_bf, w_skip[1])], axis=1
    ).reshape(rows, 2, 4, 2, -1)
    near_grad = exact_restore(order_skip, normed_grad[:, :, :, 0].reshape(rows, width))
    away_grad = exact_restore(order_skip, normed_grad[:, :, :, 1].reshape(rows, width))
    normed_grad = jnp.concatenate(
        [
            jnp.where(upper_half == 0, near_grad, away_grad),
            jnp.where(upper_half == 0, away_grad, near_grad),
        ],
        axis=1,
    )
    joined_grad, skip_gain_grad = jax.vjp(gained_norm, joined, skip_gain_all)[1](normed_grad)

    sums = [
        finish_twins(*put) for put in (put_pair, put_query, put_keyval, put_qkv, put_skip)
    ]
    (grad_down,) = put_down.finish()
    (grad_up,) = put_up.finish()
    scattered = [links.extra_scatter(part) for part in scatter(sums, links.quad, 4)]
    grad_self_out, grad_cross_out = scattered[0][0], scattered[0][1]
    grad_cross_query, grad_keyval, grad_qkv = (
        jnp.concatenate([part[0], part[1]], axis=1) for part in scattered[1:4]
    )
    grad_skip_linear = scattered[4].reshape(skip_linear.shape)

    gains_grad = jnp.stack([gain_first, gain_second, gain_third])
    gains_grad = gains_grad.reshape(3, count, third).transpose(1, 0, 2).reshape(count, 3 * third)
    gains_grad = jnp.concatenate([skip_gain_grad.reshape(count, gain_rows), gains_grad], axis=1)
    peaks = jnp.stack([self_peak[:, 0], cross_peak[:, 0]])
    cores = jnp.concatenate([shift_grad.reshape(-1), gains_grad.reshape(-1), peaks.reshape(-1)])
    there = links.sibling(cores)
    peaks = jnp.maximum(cores, there)[-2 * HEADS :]
    cores = cores + there
    ends = (batch * width, batch * width + count * cond_start)
    gains_grad = cores[ends[0] : ends[1]].reshape(count, cond_start)
    shift_bf = cores[: ends[0]].astype(bf16).astype(f32)
    shared = trade(lanes_of(jnp.concatenate([shift_bf, peaks]), 8), count, True, 5)
    shared = shared.reshape(count, -1)
    shift_all = shared[:, : ends[0]].reshape(count * batch, width).astype(bf16)
    peaks = jnp.max(shared[:, ends[0] : ends[0] + 2 * HEADS], axis=0).reshape(2, HEADS)
    grad_shift = dot_left_t(cond_cut, shift_all)
    cond_back = dot_right_t(shift_all, shift_linear).reshape(count, batch * shift_rows)
    owned = trade(lanes_of(jnp.concatenate([cond_back, gains_grad], axis=1), 8), count, False, 6)
    owned = owned.reshape(count, -1)
    cond_mine = owned[:, : batch * shift_rows].reshape(count, batch, shift_rows)
    cond_mine = cond_mine.transpose(1, 0, 2).reshape(batch, width)
    grad_cond = jax.vjp(jax.nn.silu, condition.astype(f32))[1](cond_mine)[0]
    own_gains = jnp.sum(owned[:, batch * shift_rows : batch * shift_rows + cond_start], axis=0)
    grad_skip_gain = own_gains[:gain_rows]
    grad_gains = own_gains[gain_rows:].reshape(3, third)

    roots = jnp.sqrt(thresholds / jnp.maximum(peaks, thresholds))
    self_cols = jnp.repeat(roots[0], HD)
    cross_cols = jnp.repeat(roots[1], HD)
    unit_cols = jnp.ones((width,), f32)
    clipped_qkv = (
        self_qkv.astype(f32) * jnp.concatenate([self_cols, self_cols, unit_cols])[None, :]
    ).astype(bf16)
    clipped_query = (cross_query.astype(f32) * cross_cols[None, :]).astype(bf16)
    clipped_keyval = (
        cross_keyval.astype(f32) * jnp.concatenate([cross_cols, unit_cols])[None, :]
    ).astype(bf16)
    return (
        block_out.reshape(batch, tokens, width),
        joined_grad[:, :width].reshape(batch, tokens, width),
        joined_grad[:, width:].reshape(batch, tokens, width),
        grad_cond,
        grad_text,
        grad_skip_gain,
        grad_gains,
        grad_skip_linear,
        grad_shift,
        grad_qkv,
        grad_self_out,
        grad_cross_query,
        grad_keyval,
        grad_cross_out,
        grad_up,
        grad_down,
        clipped_qkv,
        clipped_query,
        clipped_keyval,
        peaks,
    )


def local_sixteen(
    latent,
    skip_input,
    condition,
    text_encoder_states,
    text_lengths,
    out_grad,
    skip_gain,
    norm_gains,
    skip_linear,
    shift_linear,
    self_qkv,
    self_out,
    cross_query,
    cross_keyval,
    cross_out,
    mlp_up,
    mlp_down,
    thresholds,
):
    batch, tokens, width = latent.shape
    rows = batch * tokens
    text_rows = text_encoder_states.shape[1]
    text_width = text_encoder_states.shape[2]
    scaling = HD ** (-0.5)
    links = Links(lax.axis_size("fsdp"))
    me, core = links.me, links.core
    count = links.count

    positions = core * tokens + jnp.arange(tokens)
    feature = jnp.arange(width) % HD
    freqs = 10000.0 ** (-(feature % (HD // 4)).astype(f32) / (HD // 4))
    place = jnp.where(
        feature[None, :] < HD // 2, (positions // GRID_W)[:, None], (positions % GRID_W)[:, None]
    )
    angles = place.astype(f32) * freqs[None, :]
    former = (feature % (HD // 2) < HD // 4)[None, :]
    cosine = jnp.cos(angles)
    sine = jnp.where(former, -jnp.sin(angles), jnp.sin(angles))
    tables = [(cosine, None), (sine, None), (former.astype(f32), None)]
    head_at = jnp.arange(width)[:, None] // HD == jnp.arange(128)[None, :]
    head_at = (head_at.astype(bf16), None)

    gain_rows = skip_gain.shape[0]
    third = norm_gains.shape[1]
    cond_act = jax.nn.silu(condition.astype(f32)).astype(bf16)
    small = jnp.concatenate([skip_gain, norm_gains.reshape(-1), cond_act.reshape(-1)])
    small = trade(lanes_of(small, 16), count, True, 1).reshape(count, -1)
    skip_gain_all = small[:, :gain_rows].reshape(-1).astype(f32)
    cond_start = gain_rows + 3 * third
    gains = small[:, gain_rows:cond_start].reshape(count, 3, third)
    gains = gains.transpose(1, 0, 2).reshape(3, width).astype(f32)
    cond_all = small[:, cond_start : cond_start + batch * width].reshape(count * batch, width)
    shift_rows = shift_linear.shape[0]
    cond_cut = lax.dynamic_slice_in_dim(cond_all, me * shift_rows, shift_rows, 1)
    shift_parts = dot_plain(cond_cut, shift_linear).reshape(count, batch * width)
    shift_parts = trade(lanes_of(shift_parts, 8), count, False, 2)
    shift = jnp.sum(shift_parts.reshape(count, -1), axis=0)[: batch * width].reshape(batch, width)

    def halves_of(weight):
        cut = (weight.shape[1] // 2 + 127) // 128 * 128
        first, second = weight[:, :cut], weight[:, cut:]
        return first, jnp.pad(second, ((0, 0), (0, cut - second.shape[1])))

    def qkv_halves(value):
        edge = 2 * width + 768
        first = jnp.concatenate([value[:, :width], value[:, 2 * width : edge]], axis=1)
        rest = jnp.pad(value[:, edge:], ((0, 0), (0, 2 * 768 - width)))
        return first, jnp.concatenate([value[:, width : 2 * width], rest], axis=1)

    def qkv_whole(first, second):
        last = second[:, width : 2 * width - 768]
        return jnp.concatenate(
            [first[:, :width], second[:, :width], first[:, width:], last], axis=1
        )

    skip_half = skip_linear.shape[0] // 2
    shards = [
        links.pick(skip_linear[:skip_half], skip_linear[skip_half:]),
        links.pick(*qkv_halves(self_qkv)),
        links.pick(self_out, cross_out),
        links.pick(*halves_of(cross_query)),
        links.pick(*halves_of(cross_keyval)),
        links.pick(*halves_of(mlp_up)),
        links.pick(*halves_of(mlp_down)),
    ]
    block = width // 16

    def one_hot(starts, size, height):
        wanted = (starts[:, None] + jnp.arange(size, dtype=jnp.int32)).reshape(1, -1)
        rows_at = lax.broadcasted_iota(jnp.int32, (height, wanted.shape[1]), 0)
        return (rows_at == wanted).astype(bf16)

    slots = jnp.arange(16, dtype=jnp.int32)
    order = one_hot(jnp.bitwise_xor(me, slots) * block, block, width)
    text_block = text_width // 16
    order_text = one_hot(jnp.bitwise_xor(me, slots) * text_block, text_block, text_width)
    lower = jnp.bitwise_xor(jnp.bitwise_and(me, 7), slots[:8]) * (2 * block)
    order_skip = jnp.stack([one_hot(lower + at * block, block, width) for at in range(2)])
    text = text_encoder_states.reshape(batch * text_rows, text_width)
    text_ordered = dot_plain(text, order_text).astype(bf16)
    valid = (jnp.arange(text_rows)[None, :] < text_lengths[:, None]).astype(f32)
    head_at = (jnp.arange(width)[:, None] // HD == jnp.arange(128)[None, :]).astype(bf16)
    table_arrays = [table for table, _ in tables]

    def shaped(*shape, dtype=f32):
        return jax.ShapeDtypeStruct(shape, dtype)

    flat, flat_low = shaped(rows, width), shaped(rows, width, dtype=bf16)
    double_low = shaped(rows, 2 * width, dtype=bf16)
    inner = mlp_down.shape[0] * 16
    given = [
        latent.reshape(rows, width),
        skip_input.reshape(rows, width),
        skip_gain_all[None, :],
        gains,
        shift,
        order,
        order_skip,
        head_at,
        *table_arrays,
        text_ordered,
        valid,
    ]
    saved = [
        shaped(2, 2, rows, width // 2, dtype=bf16),
        flat,
        flat_low,
        shaped(rows, 2 * width),
        double_low,
        double_low,
        flat_low,
        flat,
        flat_low,
        flat,
        flat,
        shaped(batch * text_rows, 2 * width, dtype=bf16),
        flat_low,
        flat,
        flat_low,
        shaped(rows, inner),
        shaped(rows, inner, dtype=bf16),
        shaped(HEADS, 128),
        shaped(HEADS, 128),
    ]
    (
        *gathered,
        normed,
        hidden,
        attn_in,
        qkv_proj,
        keyval_here,
        keyval_there,
        attn_cat,
        after_self,
        cross_in,
        cq_proj,
        ckey_mine,
        cross_keyval_all,
        cross_cat,
        after_cross,
        mlp_in,
        upper,
        activated,
        self_peak,
        cross_peak,
    ) = pl.pallas_call(
        functools.partial(forward_body, batch, scaling),
        out_shape=[shaped(2, 4, 4, *shard.shape, dtype=bf16) for shard in shards] + saved,
        in_specs=[IN_VMEM] * len(given) + [ANYWHERE] * 7,
        out_specs=[ANYWHERE] * 7 + [IN_VMEM] * len(saved),
        scratch_shapes=[
            pltpu.VMEM((rows, width), f32),
            pltpu.VMEM((rows, width), bf16),
            pltpu.VMEM((3, 4, 4, block, 512), bf16),
            pltpu.SemaphoreType.DMA((3,)),
            pltpu.SemaphoreType.DMA((7, 10)),
            pltpu.SemaphoreType.DMA((7, 10)),
            pltpu.SemaphoreType.DMA((7,)),
            pltpu.SemaphoreType.DMA,
            pltpu.SemaphoreType.DMA,
        ],
        compiler_params=pltpu.CompilerParams(
            collective_id=7, has_side_effects=True, vmem_limit_bytes=62 * 2**20
        ),
    )(*given, *shards)
    down_in = out_grad.reshape(rows, width)
    cut = shards[6].shape[1]
    out_halves = jnp.stack(
        [down_in[:, :cut], jnp.pad(down_in[:, cut:], ((0, 0), (0, 2 * cut - width)))]
    )
    up_shape, down_shape = shards[5].shape, shards[6].shape
    whole = [shaped(4, 4, *shape, dtype=bf16) for shape in (down_shape, up_shape)]
    tile = 384
    block_out, cross_grad, gain_third, *rest = pl.pallas_call(
        functools.partial(mlp_back_body, batch),
        out_shape=[flat_low, flat, shaped(8, width), *whole, *whole],
        in_specs=[IN_VMEM] * 7 + [ANYWHERE] * 2,
        out_specs=[IN_VMEM] * 3 + [ANYWHERE] * 4,
        scratch_shapes=[
            pltpu.VMEM((2, rows, inner // 2), bf16),
            pltpu.VMEM((width, rows), bf16),
            pltpu.VMEM((2, rows, cut), f32),
            pltpu.VMEM((3, 2, *down_shape), bf16),
            pltpu.VMEM((3, 4, 4, block, 512), bf16),
            pltpu.VMEM((2, *down_shape), bf16),
            pltpu.VMEM((2, *down_shape), bf16),
            pltpu.VMEM((2, 4, 4, block, tile), bf16),
            pltpu.VMEM((2, 4, 4, block, tile), bf16),
            pltpu.SemaphoreType.DMA((3,)),
            pltpu.SemaphoreType.DMA((2, 16)),
            pltpu.SemaphoreType.DMA((2, 16)),
            pltpu.SemaphoreType.DMA((4,)),
        ],
        compiler_params=pltpu.CompilerParams(
            collective_id=8, has_side_effects=True, vmem_limit_bytes=60 * 2**20
        ),
    )(out_halves, activated, upper, mlp_in, after_cross, order, gains, gathered[5], gathered[6])
    sums_down, sums_up = rest[0], rest[1]

    text_half = text_rows // 2
    text_mine = lax.dynamic_slice_in_dim(
        text_ordered.reshape(batch, text_rows, text_width), core * text_half, text_half, 1
    ).reshape(-1, text_width)
    parts = [shards[at].shape for at in (6, 5, 3, 4, 2, 1, 0)]
    moved = [
        *[shaped(2, *shape) for shape in parts],
        *[shaped(4, 4, *shape, dtype=bf16) for shape in parts[2:]],
        *[shaped(4, 4, *shape, dtype=bf16) for shape in parts[2:]],
        *[shaped(2, 4, *shape, dtype=bf16) for shape in parts],
        *[shaped(4, *shape, dtype=bf16) for shape in parts],
        *[shaped(4, *shape, dtype=bf16) for shape in parts],
        *[shaped(3, *shape, dtype=bf16) for shape in parts],
        *[shaped(3, *shape, dtype=bf16) for shape in parts],
    ]
    placed = [
        cross_cat, attn_cat, cross_in, attn_in, text_mine, after_self, hidden, normed,
        gains, order, head_at, *table_arrays, valid,
    ]
    apart = [
        *gathered[:5],
        cross_keyval_all, cq_proj, ckey_mine, qkv_proj, keyval_here, keyval_there, cross_grad,
        sums_down, sums_up,
    ]
    small_outs = [shaped(rows, text_width), shaped(8, width), shaped(8, width)]
    text_grad, gain_grads, shift_grad, normed_grad, *rest = pl.pallas_call(
        functools.partial(rest_back_body, batch, scaling),
        out_shape=[*small_outs, shaped(rows, 2 * width), *moved],
        in_specs=[IN_VMEM] * len(placed) + [ANYWHERE] * len(apart),
        out_specs=[IN_VMEM] * 3 + [ANYWHERE] * (1 + len(moved)),
        scratch_shapes=[
            *[pltpu.VMEM((rows, width), f32)] * 4,
            pltpu.VMEM((rows, width), bf16),
            pltpu.VMEM((rows, width), bf16),
            pltpu.VMEM((2, rows, 2 * width), f32),
            pltpu.VMEM((2 * rows, 2 * width), bf16),
            pltpu.VMEM((rows, 2 * width), f32),
            pltpu.VMEM((2, width, rows), bf16),
            pltpu.VMEM((2, rows, shards[1].shape[1]), bf16),
            pltpu.VMEM((3, 4, 4, block, tile), bf16),
            pltpu.VMEM((2, 4, 4, block, tile), bf16),
            pltpu.VMEM((2, 4, 4, block, tile), bf16),
            pltpu.VMEM((9, block, 1536), bf16),
            pltpu.VMEM((9, down_shape[0], tile), bf16),
            pltpu.VMEM((block, 1536), f32),
            pltpu.VMEM((down_shape[0], tile), f32),
            pltpu.VMEM((2, rows, 2 * width), bf16),
            pltpu.SemaphoreType.DMA((3,)),
            pltpu.SemaphoreType.DMA((4,)),
            pltpu.SemaphoreType.DMA((5, 8)),
            pltpu.SemaphoreType.DMA((5, 8)),
            pltpu.SemaphoreType.DMA((4,)),
            pltpu.SemaphoreType.DMA((2,)),
            pltpu.SemaphoreType.DMA((2,)),
            pltpu.SemaphoreType.DMA((7, 8)),
            pltpu.SemaphoreType.DMA((7, 8)),
            pltpu.SemaphoreType.DMA((9,)),
            pltpu.SemaphoreType.DMA((4,)),
        ],
        compiler_params=pltpu.CompilerParams(
            collective_id=9, has_side_effects=True, vmem_limit_bytes=62 * 2**20
        ),
    )(*placed, *apart)
    grads = rest[:7]
    joined_grad, skip_gain_grad = pl.pallas_call(
        functools.partial(joined_back_body, batch),
        out_shape=[shaped(2, rows, width), shaped(8, 2 * width)],
        in_specs=[IN_VMEM] * 5,
        out_specs=[IN_VMEM] * 2,
        compiler_params=pltpu.CompilerParams(vmem_limit_bytes=60 * 2**20),
    )(normed_grad, latent.reshape(rows, width), skip_input.reshape(rows, width), skip_gain_all[None, :], order_skip)
    skip_gain_grad = skip_gain_grad[0]
    gain_first, gain_second, gain_third = gain_grads[0], gain_grads[1], gain_third[0]
    shift_grad = shift_grad[:batch]
    grad_text = exact_restore(order_text, text_grad).reshape(batch, text_half, text_width)

    def wide_of(part):
        return jnp.concatenate([part[0], part[1]], axis=1)

    grad_down = wide_of(grads[0])[:, :width]
    grad_up = wide_of(grads[1])
    grad_cross_query = wide_of(grads[2])[:, :width]
    grad_keyval = wide_of(grads[3])
    grad_self_out, grad_cross_out = grads[4][0], grads[4][1]
    grad_qkv = qkv_whole(grads[5][0], grads[5][1])
    grad_skip_linear = grads[6].reshape(skip_linear.shape)

    gains_grad = jnp.stack([gain_first, gain_second, gain_third])
    gains_grad = gains_grad.reshape(3, count, third).transpose(1, 0, 2).reshape(count, 3 * third)
    gains_grad = jnp.concatenate([skip_gain_grad.reshape(count, gain_rows), gains_grad], axis=1)
    peaks = jnp.stack([self_peak[:, 0], cross_peak[:, 0]])
    cores = jnp.concatenate([shift_grad.reshape(-1), gains_grad.reshape(-1), peaks.reshape(-1)])
    there = links.sibling(cores)
    peaks = jnp.maximum(cores, there)[-2 * HEADS :]
    cores = cores + there
    ends = (batch * width, batch * width + count * cond_start)
    gains_grad = cores[ends[0] : ends[1]].reshape(count, cond_start)
    shift_bf = cores[: ends[0]].astype(bf16).astype(f32)
    shared = trade(lanes_of(jnp.concatenate([shift_bf, peaks]), 8), count, True, 5)
    shared = shared.reshape(count, -1)
    shift_all = shared[:, : ends[0]].reshape(count * batch, width).astype(bf16)
    peaks = jnp.max(shared[:, ends[0] : ends[0] + 2 * HEADS], axis=0).reshape(2, HEADS)
    grad_shift = dot_left_t(cond_cut, shift_all)
    cond_back = dot_right_t(shift_all, shift_linear).reshape(count, batch * shift_rows)
    owned = trade(lanes_of(jnp.concatenate([cond_back, gains_grad], axis=1), 8), count, False, 6)
    owned = owned.reshape(count, -1)
    cond_mine = owned[:, : batch * shift_rows].reshape(count, batch, shift_rows)
    cond_mine = cond_mine.transpose(1, 0, 2).reshape(batch, width)
    grad_cond = jax.vjp(jax.nn.silu, condition.astype(f32))[1](cond_mine)[0]
    own_gains = jnp.sum(owned[:, batch * shift_rows : batch * shift_rows + cond_start], axis=0)
    grad_skip_gain = own_gains[:gain_rows]
    grad_gains = own_gains[gain_rows:].reshape(3, third)

    roots = jnp.sqrt(thresholds / jnp.maximum(peaks, thresholds))
    self_cols = jnp.repeat(roots[0], HD)
    cross_cols = jnp.repeat(roots[1], HD)
    unit_cols = jnp.ones((width,), f32)
    clipped_qkv = (
        self_qkv.astype(f32) * jnp.concatenate([self_cols, self_cols, unit_cols])[None, :]
    ).astype(bf16)
    clipped_query = (cross_query.astype(f32) * cross_cols[None, :]).astype(bf16)
    clipped_keyval = (
        cross_keyval.astype(f32) * jnp.concatenate([cross_cols, unit_cols])[None, :]
    ).astype(bf16)
    return (
        block_out.reshape(batch, tokens, width),
        joined_grad[0].reshape(batch, tokens, width),
        joined_grad[1].reshape(batch, tokens, width),
        grad_cond,
        grad_text,
        grad_skip_gain,
        grad_gains,
        grad_skip_linear,
        grad_shift,
        grad_qkv,
        grad_self_out,
        grad_cross_query,
        grad_keyval,
        grad_cross_out,
        grad_up,
        grad_down,
        clipped_qkv,
        clipped_query,
        clipped_keyval,
        peaks,
    )


def solution(mesh):
    rows = P("fsdp", None)
    tokens = P("fsdp", "seq", None)
    in_specs = (
        tokens,
        tokens,
        rows,
        P("fsdp", None, None),
        P("fsdp"),
        tokens,
        P("fsdp"),
        P(None, "fsdp"),
        *([rows] * 9),
        P(),
    )
    out_specs = (
        *([tokens] * 3),
        rows,
        tokens,
        P("fsdp"),
        P(None, "fsdp"),
        *([rows] * 12),
        P(),
    )
    step = local_sixteen if mesh.shape["fsdp"] == 16 else local
    return jax.shard_map(step, mesh=mesh, in_specs=in_specs, out_specs=out_specs, check_vma=False)
```

```python
import functools

import jax
import jax.numpy as jnp
from jax import lax
from jax.experimental import pallas as pl
from jax.experimental.pallas import tpu as pltpu
from jax.sharding import PartitionSpec as P

HEADS = 16
HD = 88
GRID_W = 32

norm_eps = 1e-06
masked_value = -1e30
bf16 = jnp.bfloat16
f32 = jnp.float32
MESH = pl.DeviceIdType.MESH
ANYWHERE = pl.BlockSpec(memory_space=pl.ANY)
IN_VMEM = pl.BlockSpec(memory_space=pltpu.VMEM)


def layer_norm(values):
    center = values - jnp.mean(values, axis=-1, keepdims=True)
    spread = jnp.mean(center * center, axis=-1, keepdims=True)
    return center * lax.rsqrt(spread + norm_eps)


def gained_norm(values, gain):
    return layer_norm(values) * gain


def gelu_tanh(values):
    return jax.nn.gelu(values, approximate=True)


def dot_plain(left, right):
    return jnp.dot(left, right, preferred_element_type=f32)


def dot_left_t(left, right):
    return lax.dot_general(
        left, right, (((0,), (0,)), ((), ())), preferred_element_type=f32
    )


def dot_right_t(left, right):
    return lax.dot_general(
        left, right, (((1,), (1,)), ((), ())), preferred_element_type=f32
    )


def softmax_back(probs, prob_grad):
    return probs * (prob_grad - jnp.sum(prob_grad * probs, axis=-1, keepdims=True))


def greet(peers):
    barrier = pltpu.get_barrier_semaphore()
    for peer in peers:
        pl.semaphore_signal(barrier, inc=1, device_id=peer, device_id_type=MESH)
    pl.semaphore_wait(barrier, len(peers))


def trade_body(count, same, source, out, send, recv, local):
    me = lax.axis_index("fsdp")
    core = lax.axis_index("seq")
    greet([(jnp.bitwise_xor(me, j), core) for j in range(1, count)])

    def part(index):
        return source if same else source.at[index]

    def copy(j):
        peer = jnp.bitwise_xor(me, j)
        return pltpu.make_async_remote_copy(
            src_ref=part(peer),
            dst_ref=out.at[me],
            send_sem=send.at[j],
            recv_sem=recv.at[j],
            device_id=(peer, core),
            device_id_type=MESH,
        )

    for j in range(1, count):
        copy(j).start()
    here = pltpu.make_async_copy(part(me), out.at[me], local.at[0])
    here.start()
    here.wait()
    for j in range(1, count):
        copy(j).wait_send()
        copy(j).wait_recv()


def trade(value, count, same, identity):
    shape = value.shape if same else value.shape[1:]
    return pl.pallas_call(
        functools.partial(trade_body, count, same),
        out_shape=jax.ShapeDtypeStruct((count, *shape), value.dtype),
        in_specs=[IN_VMEM],
        out_specs=IN_VMEM,
        scratch_shapes=[
            pltpu.SemaphoreType.DMA((count,)),
            pltpu.SemaphoreType.DMA((count,)),
            pltpu.SemaphoreType.DMA((1,)),
        ],
        compiler_params=pltpu.CompilerParams(collective_id=identity, has_side_effects=True),
    )(value)


def neighbours(quad):
    me = lax.axis_index("fsdp")
    core = lax.axis_index("seq")
    first, second = 1 + core, 2 - core

    def at(mask):
        return (jnp.bitwise_xor(me, mask), core)

    return core, first, second, at, (me, 1 - core)


def gather_body(count, quad, *refs):
    mine, out = refs[:count], refs[count : 2 * count]
    send, recv, local = refs[2 * count :]
    core, first_mask, second_mask, at, sibling = neighbours(quad)
    far_peers = [at(k * quad) for k in range(1, 4)]
    greet([*far_peers, at(first_mask), at(second_mask), sibling])

    def copy(w, slot, source, target, peer):
        return pltpu.make_async_remote_copy(
            src_ref=source,
            dst_ref=target,
            send_sem=send.at[w, slot],
            recv_sem=recv.at[w, slot],
            device_id=peer,
            device_id_type=MESH,
        )

    def block(w, q):
        return out[w].at[core, pl.ds(4 * q, 4)]

    def far(w, k):
        return copy(w, k - 1, mine[w], out[w].at[core, k], far_peers[k - 1])

    def keep(w):
        return pltpu.make_async_copy(mine[w], out[w].at[core, 0], local.at[w])

    def first(w):
        return copy(w, 3, block(w, 0), block(w, first_mask), at(first_mask))

    def second(w):
        return copy(w, 4, block(w, 0), block(w, second_mask), at(second_mask))

    def both(w):
        return copy(w, 5, block(w, first_mask), block(w, 3), at(second_mask))

    def twin(w, n):
        q = (0, first_mask, second_mask, 3)[n]
        return copy(w, 6 + n, block(w, q), block(w, q), sibling)

    for w in range(count):
        keep(w).start()
        for k in range(1, 4):
            far(w, k).start()
    for step in range(count + 2):
        w = step
        if w < count:
            keep(w).wait()
            for k in range(1, 4):
                far(w, k).wait_recv()
            first(w).start()
            second(w).start()
            twin(w, 0).start()
        w = step - 1
        if 0 <= w < count:
            first(w).wait_recv()
            both(w).start()
            twin(w, 1).start()
            second(w).wait_recv()
            twin(w, 2).start()
        w = step - 2
        if 0 <= w < count:
            both(w).wait_recv()
            twin(w, 3).start()
    for w in range(count):
        for k in range(1, 4):
            far(w, k).wait_send()
        first(w).wait_send()
        second(w).wait_send()
        both(w).wait_send()
        for n in range(4):
            twin(w, n).wait_send()
            twin(w, n).wait_recv()


def gather(shards, quad, identity):
    count = len(shards)
    return pl.pallas_call(
        functools.partial(gather_body, count, quad),
        out_shape=[jax.ShapeDtypeStruct((2, 16, *s.shape), bf16) for s in shards],
        in_specs=[ANYWHERE] * count,
        out_specs=[ANYWHERE] * count,
        scratch_shapes=[
            pltpu.SemaphoreType.DMA((count, 10)),
            pltpu.SemaphoreType.DMA((count, 10)),
            pltpu.SemaphoreType.DMA((count,)),
        ],
        compiler_params=pltpu.CompilerParams(collective_id=identity, has_side_effects=True),
    )(*shards)


def scatter_body(count, quad, *refs):
    source, out = refs[:count], refs[count : 2 * count]
    kept, half, quarter, last, total = (
        refs[(2 + n) * count : (3 + n) * count] for n in range(5)
    )
    send, recv, local = refs[7 * count :]
    core, first_mask, second_mask, at, sibling = neighbours(quad)
    far_peers = [at(k * quad) for k in range(1, 4)]
    greet([*far_peers, at(first_mask), at(second_mask), sibling])

    def copy(w, slot, origin, target, peer):
        return pltpu.make_async_remote_copy(
            src_ref=origin,
            dst_ref=target,
            send_sem=send.at[w, slot],
            recv_sem=recv.at[w, slot],
            device_id=peer,
            device_id_type=MESH,
        )

    def block(w, q):
        if len(source[w].shape) == 4:
            return source[w].at[:, q]
        return source[w].at[pl.ds(4 * q, 4)]

    def give(w, n):
        q = 3 if n == 0 else second_mask
        return copy(w, n, block(w, q), half[w].at[n], at(second_mask))

    def load(w, n):
        q = first_mask if n == 0 else 0
        return pltpu.make_async_copy(block(w, q), kept[w].at[n], local.at[w, n])

    def pass_on(w):
        return copy(w, 2, half[w].at[0], quarter[w], at(first_mask))

    def far(w, k):
        return copy(w, 2 + k, half[w].at[1, k], last[w].at[k - 1], far_peers[k - 1])

    def twin(w):
        return copy(w, 6, total[w], out[w].at[core], sibling)

    def store(w):
        return pltpu.make_async_copy(total[w], out[w].at[core], local.at[w, 2])

    def lanes(w, body):
        width = total[w].shape[1]
        step = 256 if width % 256 == 0 else 128 if width % 128 == 0 else width
        if step == width:
            body(slice(None))
        else:

            @pl.loop(0, width // step)
            def _(i):
                body(pl.ds(pl.multiple_of(i * step, step), step))

    for w in range(count):
        for n in range(2):
            give(w, n).start()
            load(w, n).start()
    for step in range(count + 2):
        w = step
        if w < count:
            give(w, 0).wait_recv()
            load(w, 0).wait()

            def body(c):
                for k in range(4):
                    half[w][0, k, :, c] = (
                        half[w][0, k, :, c].astype(f32) + kept[w][0, k, :, c].astype(f32)
                    ).astype(bf16)

            lanes(w, body)
            pass_on(w).start()
        w = step - 1
        if 0 <= w < count:
            give(w, 1).wait_recv()
            load(w, 1).wait()
            pass_on(w).wait_recv()

            def body(c):
                for k in range(4):
                    value = half[w][1, k, :, c].astype(f32) + kept[w][1, k, :, c].astype(f32)
                    value = value + quarter[w][k, :, c].astype(f32)
                    if k == 0:
                        total[w][:, c] = value
                    else:
                        half[w][1, k, :, c] = value.astype(bf16)

            lanes(w, body)
            for k in range(1, 4):
                far(w, k).start()
        w = step - 2
        if 0 <= w < count:
            for k in range(1, 4):
                far(w, k).wait_recv()

            def body(c):
                value = total[w][:, c]
                for k in range(3):
                    value = value + last[w][k, :, c].astype(f32)
                total[w][:, c] = value

            lanes(w, body)
            twin(w).start()
            store(w).start()
    for w in range(count):
        give(w, 0).wait_send()
        give(w, 1).wait_send()
        pass_on(w).wait_send()
        for k in range(1, 4):
            far(w, k).wait_send()
        twin(w).wait_send()
        twin(w).wait_recv()
        store(w).wait()


def scatter(sums, quad, identity):
    count = len(sums)
    shapes = [s.shape[-2:] for s in sums]

    def buffers(*lead):
        return [pltpu.VMEM((*lead, *s), bf16) for s in shapes]

    return pl.pallas_call(
        functools.partial(scatter_body, count, quad),
        out_shape=[jax.ShapeDtypeStruct((2, *s), f32) for s in shapes],
        in_specs=[ANYWHERE] * count,
        out_specs=[ANYWHERE] * count,
        scratch_shapes=[
            *buffers(2, 4),
            *buffers(2, 4),
            *buffers(4),
            *buffers(3),
            *[pltpu.VMEM(s, f32) for s in shapes],
            pltpu.SemaphoreType.DMA((count, 7)),
            pltpu.SemaphoreType.DMA((count, 7)),
            pltpu.SemaphoreType.DMA((count, 3)),
        ],
        compiler_params=pltpu.CompilerParams(
            collective_id=identity, has_side_effects=True, vmem_limit_bytes=56 * 2**20
        ),
    )(*sums)


def gelu_parts(value):
    inner = 0.7978845608028654 * (value + 0.044715 * value * value * value)
    return jnp.tanh(inner)


def gelu_of(value):
    return 0.5 * value * (1.0 + gelu_parts(value))


class GatherPlan:
    def __init__(self, pieces, send, recv, local):
        self.pieces = pieces
        self.send, self.recv, self.local = send, recv, local
        self.core, self.first_mask, self.second_mask, self.at, self.sibling = neighbours(4)
        self.far_peers = [self.at(4 * k) for k in range(1, 4)]

    def peers(self):
        return [*self.far_peers, self.at(self.first_mask), self.at(self.second_mask), self.sibling]

    def copy(self, w, slot, source, target, peer):
        return pltpu.make_async_remote_copy(
            src_ref=source,
            dst_ref=target,
            send_sem=self.send.at[w, slot],
            recv_sem=self.recv.at[w, slot],
            device_id=peer,
            device_id_type=MESH,
        )

    def mine(self, w):
        shard, _, lanes = self.pieces[w]
        return shard.at[:, lanes]

    def block(self, w, q):
        _, out, lanes = self.pieces[w]
        return out.at[self.core, :, q, :, lanes]

    def plane(self, w, k, q):
        _, out, lanes = self.pieces[w]
        return out.at[self.core, k, q, :, lanes]

    def layer(self, w, k):
        _, out, lanes = self.pieces[w]
        return out.at[self.core, k, :, :, lanes]

    def far(self, w, k):
        return self.copy(w, k - 1, self.mine(w), self.plane(w, k, 0), self.far_peers[k - 1])

    def keep(self, w):
        return pltpu.make_async_copy(self.mine(w), self.plane(w, 0, 0), self.local.at[w])

    def first(self, w):
        mask = self.first_mask
        return self.copy(w, 3, self.block(w, 0), self.block(w, mask), self.at(mask))

    def second(self, w):
        mask = self.second_mask
        return self.copy(w, 4, self.block(w, 0), self.block(w, mask), self.at(mask))

    def both(self, w):
        return self.copy(
            w, 5, self.block(w, self.first_mask), self.block(w, 3), self.at(self.second_mask)
        )

    def twin(self, w, n):
        q = (0, self.first_mask, self.second_mask, 3)[n]
        return self.copy(w, 6 + n, self.block(w, q), self.block(w, q), self.sibling)


    def low_first(self, w):
        mask = self.first_mask
        return self.copy(w, 3, self.mine(w), self.plane(w, 0, mask), self.at(mask))

    def low_second(self, w):
        mask = self.second_mask
        return self.copy(w, 4, self.mine(w), self.plane(w, 0, mask), self.at(mask))

    def low_both(self, w):
        mask = self.second_mask
        return self.copy(
            w, 5, self.plane(w, 0, self.first_mask), self.plane(w, 0, 3), self.at(mask)
        )

    def low_far(self, w, k):
        return self.copy(w, k - 1, self.layer(w, 0), self.layer(w, k), self.far_peers[k - 1])

    def low_twin(self, w, k):
        return self.copy(w, 6 + k, self.layer(w, k), self.layer(w, k), self.sibling)

    def low_begin(self, w):
        self.keep(w).start()
        self.low_first(w).start()
        self.low_second(w).start()

    def low_cross(self, w):
        self.low_first(w).wait_recv()
        self.low_both(w).start()
        self.low_second(w).wait_recv()

    def low_spread(self, w):
        self.keep(w).wait()
        self.low_both(w).wait_recv()
        for k in range(1, 4):
            self.low_far(w, k).start()
        self.low_twin(w, 0).start()

    def low_close(self, w):
        for k in range(1, 4):
            self.low_far(w, k).wait_recv()
            self.low_twin(w, k).start()

    def low_finish(self, w):
        self.low_first(w).wait_send()
        self.low_second(w).wait_send()
        self.low_both(w).wait_send()
        for k in range(1, 4):
            self.low_far(w, k).wait_send()
        for k in range(4):
            self.low_twin(w, k).wait_send()

    def low_ready(self, w):
        for k in range(4):
            self.low_twin(w, k).wait_recv()

    def begin(self, w):
        self.keep(w).start()
        for k in range(1, 4):
            self.far(w, k).start()

    def spread(self, w):
        self.keep(w).wait()
        for k in range(1, 4):
            self.far(w, k).wait_recv()
        self.first(w).start()
        self.second(w).start()
        self.twin(w, 0).start()

    def cross(self, w):
        self.first(w).wait_recv()
        self.both(w).start()
        self.twin(w, 1).start()
        self.second(w).wait_recv()
        self.twin(w, 2).start()

    def close(self, w):
        self.both(w).wait_recv()
        self.twin(w, 3).start()

    def ready(self, w):
        for n in range(4):
            self.twin(w, n).wait_recv()

    def finish(self, w):
        for k in range(1, 4):
            self.far(w, k).wait_send()
        self.first(w).wait_send()
        self.second(w).wait_send()
        self.both(w).wait_send()
        for n in range(4):
            self.twin(w, n).wait_send()


def stream(weight, tiles, buffer, semaphore, body):
    depth = buffer.shape[0]
    height = weight.shape[3]

    def copy(index):
        half, start, size = tiles[index]
        slot = index % depth
        return pltpu.make_async_copy(
            weight.at[half, :, :, :, pl.ds(start, size)],
            buffer.at[slot, :, :, pl.ds(0, height), pl.ds(0, size)],
            semaphore.at[slot],
        )

    for index in range(min(depth - 1, len(tiles))):
        copy(index).start()
    for index, (_, _, size) in enumerate(tiles):
        if index + depth - 1 < len(tiles):
            copy(index + depth - 1).start()
        copy(index).wait()
        body(index, buffer[index % depth, :, :, :height, :size].reshape(16 * height, size))


def tiles_of(width, size, halves=(0, 1)):
    return [
        (half, start, min(size, width - start)) for half in halves for start in range(0, width, size)
    ]


def forward_body(batch, scaling, *refs):
    refs = list(refs)
    take = refs.pop
    latent, skip, skip_gain, gains, shift, out_grad, valid = (take(0) for _ in range(7))
    loaded = [take(0) for _ in range(7)]
    mine = [take(0) for _ in range(7)]
    out = [take(0) for _ in range(7)]
    saved_out = [take(0) for _ in range(19)]
    sums_down, there_down = take(0), take(0)
    saved = [take(0) for _ in range(19)]
    order, order_skip, heads_ref, *tables, text = placed = [take(0) for _ in range(7)]
    wide, narrow, buffer, out_down, in_down, semaphore, send, recv, local = (
        take(0) for _ in range(9)
    )
    twin_send, twin_recv, sum_send, sum_recv, sum_local, load_sem, save_sem = refs
    normed, hidden, attn_in, qkv, keyval_here, keyval_there = saved[:6]
    attn_cat, after_self, cross_in, cq_proj, ckey_mine, cross_keyval = saved[6:12]
    cross_cat, after_cross, mlp_in, upper, activated, self_peak, cross_peak = saved[12:]
    rows, width = hidden.shape
    size = rows // batch
    me = lax.axis_index("fsdp")
    core = lax.axis_index("seq")
    pieces = [(mine[w], out[w], pl.ds(0, mine[w].shape[1])) for w in range(6)]
    cut = mine[6].shape[1] // 2
    pieces += [(mine[6], out[6], pl.ds(at * cut, cut)) for at in range(2)]
    plan = GatherPlan(pieces, send, recv, local)
    skip_w, qkv_w, pair_w, query_w, keyval_w, up_w, down_w, last_w = range(8)

    greet(plan.peers())
    plan.low_begin(last_w)
    plan.begin(skip_w)
    plan.begin(qkv_w)
    loads = [
        pltpu.make_async_copy(source, target, load_sem.at[at])
        for at, (source, target) in enumerate(zip(loaded, placed))
    ]
    saves = [
        pltpu.make_async_copy(source, target, save_sem.at[at])
        for at, (source, target) in enumerate(zip(saved, saved_out))
    ]
    for copy in loads:
        copy.start()
    for copy in loads:
        copy.wait()

    def save(*places):
        for at in places:
            saves[at].start()

    def each(body):
        for b in range(batch):
            body(b, pl.ds(b * size, size))

    def reorder(value):
        return dot_plain(value, order[...]).astype(bf16)

    upper_half = me >= 8

    def normed_part(b, rows_b):
        left = latent[rows_b, :].astype(f32)
        right = skip[rows_b, :].astype(f32)
        mean = (
            jnp.sum(left, axis=1, keepdims=True) + jnp.sum(right, axis=1, keepdims=True)
        ) / (2 * width)
        left, right = left - mean, right - mean
        spread = (
            jnp.sum(left * left, axis=1, keepdims=True)
            + jnp.sum(right * right, axis=1, keepdims=True)
        ) / (2 * width)
        factor = lax.rsqrt(spread + norm_eps)
        left = (left * factor * skip_gain[:, :width]).astype(bf16)
        right = (right * factor * skip_gain[:, width:]).astype(bf16)
        near = jnp.where(upper_half, right, left)
        away = jnp.where(upper_half, left, right)
        for half in range(2):
            normed[half, 0, rows_b, :] = dot_plain(near, order_skip[half]).astype(bf16)
            normed[half, 1, rows_b, :] = dot_plain(away, order_skip[half]).astype(bf16)

    each(normed_part)
    save(0)
    plan.low_cross(last_w)
    plan.spread(skip_w)
    plan.begin(pair_w)
    plan.cross(skip_w)
    plan.spread(qkv_w)
    plan.begin(query_w)
    plan.close(skip_w)
    plan.ready(skip_w)

    skip_tiles = tiles_of(width, 512)

    def skip_product(index, tile):
        half, start, extent = skip_tiles[index]
        cut = tile.shape[0] // 2
        value = dot_plain(normed[half, 0], tile[:cut]) + dot_plain(normed[half, 1], tile[cut:])
        lanes = pl.ds(start, extent)
        if half == 0:
            hidden[:, lanes] = value
        else:
            hidden[:, lanes] += value

    stream(out[skip_w], skip_tiles, buffer, semaphore, skip_product)
    save(1)

    def attn_in_part(b, rows_b):
        value = layer_norm(hidden[rows_b, :]) * gains[0:1, :] + shift[b : b + 1, :]
        attn_in[rows_b, :] = reorder(value.astype(bf16))

    each(attn_in_part)
    save(2)
    plan.cross(qkv_w)
    plan.spread(pair_w)
    plan.begin(keyval_w)
    plan.spread(query_w)
    plan.begin(up_w)
    plan.close(qkv_w)
    plan.ready(qkv_w)

    qkv_tiles = tiles_of(out[qkv_w].shape[4], 512)

    def qkv_product(index, tile):
        half, start, extent = qkv_tiles[index]
        value = dot_plain(attn_in[...], tile)
        for at in range(0, extent, 128):
            lane = start + at
            piece = value[:, at : at + 128]
            if lane < width:
                qkv[:, pl.ds(half * width + lane, 128)] = piece
            else:
                place = lane - width + half * 768
                if place < width:
                    keyval_here[:, pl.ds(width + place, 128)] = piece.astype(bf16)

    stream(out[qkv_w], qkv_tiles, buffer, semaphore, qkv_product)

    def key_part(b, rows_b):
        value, _ = head_norm(qkv[rows_b, pl.ds(width, width)], heads_ref)
        keyval_here[rows_b, pl.ds(0, width)] = turn(value, tables).astype(bf16)

    each(key_part)
    save(3, 4)
    exchange = pltpu.make_async_remote_copy(
        src_ref=keyval_here,
        dst_ref=keyval_there,
        send_sem=twin_send,
        recv_sem=twin_recv,
        device_id=plan.sibling,
        device_id_type=MESH,
    )
    exchange.start()

    def query_part(b, rows_b):
        value, _ = head_norm(qkv[rows_b, pl.ds(0, width)], heads_ref)
        narrow[rows_b, :] = turn(value, tables).astype(bf16)

    each(query_part)
    plan.cross(pair_w)
    plan.spread(keyval_w)
    plan.begin(down_w)
    plan.close(pair_w)
    exchange.wait()
    save(5)

    def attend(sources, peak, target, masked):
        peak[...] = jnp.full_like(peak, masked_value)
        wide[...] = jnp.zeros_like(wide)

        @pl.loop(0, batch)
        def _(b):
            rows_b = pl.ds(pl.multiple_of(b * size, size), size)
            for head in range(HEADS):
                lanes, inside = window_of(head, width)
                query = narrow[rows_b, lanes] * inside.astype(bf16)
                scores = dot_right_t(query, pair_rows(sources, b, size, lanes)) * scaling
                if masked:
                    scores = jnp.where(valid[pl.ds(b, 1), :] > 0.5, scores, masked_value)
                probs, largest = softmax_of(scores)
                largest = jnp.max(largest, axis=0, keepdims=True)
                peak[head : head + 1, :] = jnp.maximum(
                    peak[head : head + 1, :], jnp.broadcast_to(largest, (1, 128))
                )
                value = pair_rows(sources, b, size, shift_lanes(lanes, width))
                wide[rows_b, lanes] += dot_plain(probs.astype(bf16), value) * inside

        target[...] = reorder(wide[...].astype(bf16))

    attend([keyval_here, keyval_there], self_peak, attn_cat, False)
    save(6, 17)
    plan.cross(query_w)
    plan.spread(up_w)
    plan.low_spread(last_w)
    plan.ready(pair_w)
    pair_tiles = tiles_of(width, 512)

    def out_product(source, before, after):
        def body(index, tile):
            lanes = pl.ds(pair_tiles[index][1], pair_tiles[index][2])
            after[:, lanes] = before[:, lanes] + dot_plain(source[...], tile)

        return body

    pair_body = out_product(attn_cat, hidden, after_self)
    stream(out[pair_w], tiles_of(width, 512, (0,)), buffer, semaphore, pair_body)
    save(7)

    def cross_in_part(b, rows_b):
        value = layer_norm(after_self[rows_b, :]) * gains[1:2, :]
        cross_in[rows_b, :] = reorder(value.astype(bf16))

    each(cross_in_part)
    save(8)
    plan.close(query_w)
    plan.ready(query_w)
    query_tiles = tiles_of(out[query_w].shape[4], 512)

    def query_product(index, tile):
        half, start, extent = query_tiles[index]
        place = half * out[query_w].shape[4] + start
        extent = min(extent, width - place)
        cq_proj[:, pl.ds(place, extent)] = dot_plain(cross_in[...], tile)[:, :extent]

    stream(out[query_w], query_tiles, buffer, semaphore, query_product)
    save(9)

    def cross_query_part(b, rows_b):
        narrow[rows_b, :] = head_norm(cq_proj[rows_b, :], heads_ref)[0].astype(bf16)

    each(cross_query_part)
    plan.cross(keyval_w)
    plan.spread(down_w)
    plan.close(keyval_w)
    plan.ready(keyval_w)
    keyval_tiles = tiles_of(width, 512)

    def keyval_product(index, tile):
        half, start, extent = keyval_tiles[index]
        value = dot_plain(text[...], tile)
        if half == 0:
            upper[:, pl.ds(start, extent)] = value[:rows]
            upper[:, pl.ds(width + start, extent)] = value[rows:]
        else:
            cross_keyval[:, pl.ds(width + start, extent)] = value.astype(bf16)

    stream(out[keyval_w], keyval_tiles, buffer, semaphore, keyval_product)
    for b in range(batch):
        for at in range(2):
            part = pl.ds(at * size, size)
            lanes = pl.ds(b * width, width)
            cross_keyval[pl.ds(b * 2 * size + at * size, size), pl.ds(0, width)] = head_norm(
                upper[part, lanes], heads_ref
            )[0].astype(bf16)
        ckey_mine[pl.ds(b * size, size), :] = upper[
            pl.ds(pl.multiple_of(core * size, size), size), pl.ds(b * width, width)
        ]
    attend([cross_keyval], cross_peak, cross_cat, True)
    save(10, 11, 12, 18)
    pair_body = out_product(cross_cat, after_self, after_cross)
    stream(out[pair_w], tiles_of(width, 512, (1,)), buffer, semaphore, pair_body)
    save(13)

    def mlp_in_part(b, rows_b):
        value = layer_norm(after_cross[rows_b, :]) * gains[2:3, :]
        mlp_in[rows_b, :] = reorder(value.astype(bf16))

    each(mlp_in_part)
    save(14)
    plan.cross(up_w)
    plan.cross(down_w)
    plan.close(up_w)
    plan.ready(up_w)
    block = activated.shape[1] // 16
    up_tiles = tiles_of(out[up_w].shape[4], block)

    def up_product(index, tile):
        value = dot_plain(mlp_in[...], tile)
        upper[:, pl.ds(index * block, block)] = value
        slot = jnp.bitwise_xor(me, index)
        activated[:, pl.ds(pl.multiple_of(slot * block, block), block)] = gelu_of(value).astype(bf16)

    stream(out[up_w], up_tiles, buffer, semaphore, up_product)
    save(15, 16)
    def down_part(half):
        def part(index):
            return dot_left_t(activated[:, index * block : (index + 1) * block], out_grad[half])

        return part

    planes = [lambda ref, k=k, q=q: ref.at[k, q] for k in range(4) for q in range(4)]
    down_sum = TwinSum(
        [there_down], [sums_down], sum_send, sum_recv, sum_local, out_down, in_down, plan.sibling
    )
    down_sum.run(
        0, planes, lambda index: mine[6].shape, down_part(1 - core), down_part(core)
    )
    plan.close(down_w)
    plan.low_close(last_w)
    plan.ready(down_w)
    plan.low_ready(last_w)
    for w in range(7):
        plan.finish(w)
    plan.low_finish(last_w)
    for copy in saves:
        copy.wait()


def gelu_slope(value):
    bent = gelu_parts(value)
    inner = 0.7978845608028654 * (1.0 + 3 * 0.044715 * value * value)
    return 0.5 * (1.0 + bent) + 0.5 * value * (1.0 - bent * bent) * inner


def norm_back(value, gain, grad):
    center = value - jnp.mean(value, axis=-1, keepdims=True)
    factor = lax.rsqrt(jnp.mean(center * center, axis=-1, keepdims=True) + norm_eps)
    normed = center * factor
    gain_grad = jnp.sum(grad * normed, axis=0, keepdims=True)
    grad = grad * gain
    first = jnp.mean(grad, axis=-1, keepdims=True)
    second = jnp.mean(grad * normed, axis=-1, keepdims=True)
    return factor * (grad - first - normed * second), gain_grad


class TwinSum:
    def __init__(self, there, sums, send, recv, local, out_buffer, in_buffer, sibling):
        self.there, self.sums = there, sums
        self.send, self.recv, self.local = send, recv, local
        self.out_buffer, self.in_buffer, self.sibling = out_buffer, in_buffer, sibling

    def away(self, w, index, place, source):
        return pltpu.make_async_remote_copy(
            src_ref=source,
            dst_ref=place(self.there[w]),
            send_sem=self.send.at[w, index],
            recv_sem=self.recv.at[w, index],
            device_id=self.sibling,
            device_id_type=MESH,
        )

    def run(self, w, places, shape, other, own, between=None):
        depth = self.out_buffer.shape[0]

        def slot(buffer, index):
            views = [pl.ds(0, n) for n in shape(index)]
            return buffer.at[(index % depth, *views)]

        for index, place in enumerate(places):
            if index >= depth:
                before = index - depth
                self.away(w, before, places[before], slot(self.out_buffer, before)).wait_send()
            target = slot(self.out_buffer, index)
            target[...] = other(index).astype(bf16)
            self.away(w, index, place, target).start()
        for index in range(max(0, len(places) - depth), len(places)):
            self.away(w, index, places[index], slot(self.out_buffer, index)).wait_send()
        if between is not None:
            between()

        def fetch(index):
            return pltpu.make_async_copy(
                places[index](self.there[w]),
                slot(self.in_buffer, index),
                self.local.at[index % depth],
            )

        def store(index):
            return pltpu.make_async_copy(
                slot(self.out_buffer, index),
                places[index](self.sums[w]),
                self.local.at[depth + index % depth],
            )

        def begin(index):
            self.away(w, index, places[index], slot(self.out_buffer, index)).wait_recv()
            fetch(index).start()

        begin(0)
        for index in range(len(places)):
            if index + 1 < len(places):
                begin(index + 1)
            value = own(index)
            fetch(index).wait()
            if index >= depth:
                store(index - depth).wait()
            target = slot(self.out_buffer, index)
            target[...] = (value + slot(self.in_buffer, index)[...].astype(f32)).astype(bf16)
            store(index).start()
        for index in range(max(0, len(places) - depth), len(places)):
            store(index).wait()


def lane_places(height, width, size):
    starts = [(start, min(size, width - start)) for start in range(0, width, size)]
    places = [
        lambda ref, start=start, extent=extent: ref.at[:, :, :, pl.ds(start, extent)]
        for start, extent in starts
    ]
    return starts, places, lambda index: (4, 4, height, starts[index][1])


def mlp_back_body(batch, *refs):
    refs = list(refs)
    take = refs.pop
    out_grad, activated, upper, mlp_in, after_cross, order, gains = (take(0) for _ in range(7))
    up_w, down_w, sums_down = (take(0) for _ in range(3))
    block_out, cross_grad, gain_grad = (take(0) for _ in range(3))
    sums_up, there_up, half_down = (take(0) for _ in range(3))
    upper_grad, turned, total, down_buffer, up_buffer = (take(0) for _ in range(5))
    out_up, in_up = take(0), take(0)
    semaphore, send, recv, local, give_send, give_recv = refs
    rows, width = after_cross.shape
    size = rows // batch
    block = activated.shape[1] // 16
    half_width = out_grad.shape[2]
    me = lax.axis_index("fsdp")
    core = lax.axis_index("seq")
    plan = ScatterPlan(
        [sums_down], None, [half_down], None, None, None, None, None, None,
        (give_send, give_recv, None, None),
    )
    sibling = plan.sibling
    greet([plan.at(plan.second_mask), sibling])
    plan.begin(0)

    def down_back():
        depth = down_buffer.shape[0]

        def copy(index):
            k, q = divmod(index, 4)
            return pltpu.make_async_copy(
                down_w.at[:, k, q], down_buffer.at[index % depth], semaphore.at[index % depth]
            )

        for index in range(depth - 1):
            copy(index).start()
        total[...] = jnp.zeros_like(total)
        for index in range(16):
            if index + depth - 1 < 16:
                copy(index + depth - 1).start()
            copy(index).wait()
            first, second = down_buffer[index % depth, 0], down_buffer[index % depth, 1]
            shard = jnp.bitwise_xor(me, index)
            lanes = pl.ds(pl.multiple_of(shard * block, block), block)
            grad = dot_right_t(out_grad[0], first) + dot_right_t(out_grad[1], second)
            grad = (grad * gelu_slope(upper[:, lanes])).astype(bf16)
            in_half = pl.multiple_of((shard % 8) * block, block)
            upper_grad[shard // 8, :, pl.ds(in_half, block)] = grad
            active = activated[:, index * block : (index + 1) * block]
            total[0] += dot_plain(active, first)
            total[1] += dot_plain(active, second)
        cut = width - half_width
        block_out[:, pl.ds(0, half_width)] = (
            after_cross[:, pl.ds(0, half_width)] + total[0]
        ).astype(bf16)
        block_out[:, pl.ds(half_width, cut)] = (
            after_cross[:, pl.ds(half_width, cut)] + total[1][:, :cut]
        ).astype(bf16)

    down_back()

    turned[...] = jnp.transpose(mlp_in[...])
    starts, places, shape = lane_places(width // 16, upper_grad.shape[2], out_up.shape[4])
    up = TwinSum([there_up], [sums_up], send, recv, local, out_up, in_up, sibling)

    def up_part(half):
        def part(index):
            start, extent = starts[index]
            value = dot_plain(turned[...], upper_grad[half, :, pl.ds(start, extent)])
            return value.reshape(4, 4, width // 16, extent)

        return part

    def up_back():
        tiles = tiles_of(upper_grad.shape[2], 512)

        def body(index, tile):
            half, start, extent = tiles[index]
            value = dot_right_t(upper_grad[half, :, pl.ds(start, extent)], tile)
            if index == 0:
                cross_grad[...] = value
            else:
                cross_grad[...] += value

        stream(up_w, tiles, up_buffer, semaphore, body)
        gain_grad[...] = jnp.zeros_like(gain_grad)
        for b in range(batch):
            rows_b = pl.ds(b * size, size)
            grad = restore_order(order[...], cross_grad[rows_b, :])
            value, gain_part = norm_back(after_cross[rows_b, :], gains[2:3, :], grad)
            gain_grad[0:1, :] += gain_part
            result = jnp.concatenate(
                [out_grad[0, rows_b, :], out_grad[1, rows_b, : width - half_width]], axis=1
            )
            cross_grad[rows_b, :] = result.astype(f32) + value

    up.run(0, places, shape, up_part(1 - core), up_part(core), up_back)
    for n in range(2):
        plan.give(0, n).wait_send()
        plan.give(0, n).wait_recv()


class ScatterPlan:
    def __init__(
        self, sums, out, half, passing, quarter, leaving, last, slots, totals, sems, given=()
    ):
        self.given = given
        self.sums, self.out, self.half = sums, out, half
        self.passing, self.quarter, self.leaving, self.last = passing, quarter, leaving, last
        self.slots, self.totals = slots, totals
        self.send, self.recv, self.load, self.store = sems
        self.core, self.first_mask, self.second_mask, self.at, self.sibling = neighbours(4)
        self.far_peers = [self.at(4 * k) for k in range(1, 4)]

    def peers(self):
        return [*self.far_peers, self.at(self.first_mask), self.at(self.second_mask), self.sibling]

    def copy(self, w, slot, source, target, peer):
        return pltpu.make_async_remote_copy(
            src_ref=source,
            dst_ref=target,
            send_sem=self.send.at[w, slot],
            recv_sem=self.recv.at[w, slot],
            device_id=peer,
            device_id_type=MESH,
        )

    def give(self, w, n):
        q = 3 if n == 0 else self.second_mask
        return self.copy(
            w, n, self.sums[w].at[:, q], self.half[w].at[n], self.at(self.second_mask)
        )

    def hand(self, w):
        return self.copy(w, 2, self.passing[w], self.quarter[w], self.at(self.first_mask))

    def far(self, w, k):
        return self.copy(
            w, 2 + k, self.leaving[w].at[k - 1], self.last[w].at[k - 1], self.far_peers[k - 1]
        )

    def add(self, w, groups, finish, settle):
        height, width = self.sums[w].shape[2:]
        which = 0 if height <= self.slots[0].shape[2] else 1
        slots = self.slots[which]
        size = slots.shape[3]
        chunks = [(start, min(size, width - start)) for start in range(0, width, size)]

        def loads(chunk):
            start, extent = chunks[chunk]
            bank = chunk % 2
            copies, views = [], []
            for planes in groups:
                for plane in planes:
                    at = len(copies)
                    view = slots.at[bank, at, pl.ds(0, height), pl.ds(0, extent)]
                    views.append(view)
                    copies.append(
                        pltpu.make_async_copy(
                            plane.at[:, pl.ds(start, extent)], view, self.load.at[bank, at]
                        )
                    )
            return copies, views

        def lanes_of_chunk(chunk):
            start, extent = chunks[chunk]
            return pl.ds(start, extent), extent

        for copy in loads(0)[0]:
            copy.start()
        for chunk in range(len(chunks)):
            bank = chunk % 2
            if chunk >= 1:
                settle(1 - bank, chunk - 1, *lanes_of_chunk(chunk - 1))
            if chunk + 1 < len(chunks):
                for copy in loads(chunk + 1)[0]:
                    copy.start()
            copies, views = loads(chunk)
            at = 0
            for index, planes in enumerate(groups):
                for copy in copies[at : at + len(planes)]:
                    copy.wait()
                finish(bank, chunk, index, *lanes_of_chunk(chunk), views[at : at + len(planes)])
                at += len(planes)
        last = len(chunks) - 1
        settle(last % 2, last, *lanes_of_chunk(last))

    def added(self, views, extent, kind, put):
        step = 256 if extent % 256 == 0 else 128

        @pl.loop(0, extent // step)
        def _(i):
            lanes = pl.ds(pl.multiple_of(i * step, step), step)
            value = views[0][:, lanes].astype(kind)
            for view in views[1:]:
                value = value + view[:, lanes].astype(kind)
            put(lanes, value)

    def rounded(self, w, groups, targets):
        height = self.sums[w].shape[2]
        which = 0 if height <= self.slots[0].shape[2] else 1
        starts = [sum(len(planes) for planes in groups[:at]) for at in range(len(groups))]

        def store(bank, index, lanes, extent):
            view = self.slots[which].at[bank, starts[index], pl.ds(0, height), pl.ds(0, extent)]
            return pltpu.make_async_copy(
                view, targets[index].at[:, lanes], self.store.at[bank, index]
            )

        def finish(bank, chunk, index, lanes, extent, views):
            def put(at, value):
                views[0][:, at] = value.astype(bf16)

            self.added(views, extent, bf16 if len(views) == 2 else f32, put)
            store(bank, index, lanes, extent).start()

        def settle(bank, chunk, lanes, extent):
            for index in range(len(groups)):
                store(bank, index, lanes, extent).wait()

        self.add(w, groups, finish, settle)

    def begin(self, w):
        self.give(w, 0).start()
        self.give(w, 1).start()

    def middle(self, w):
        if w not in self.given:
            self.give(w, 0).wait_recv()
        mask = self.first_mask
        groups = [[self.half[w].at[0, k], self.sums[w].at[k, mask]] for k in range(4)]
        self.rounded(w, groups, [self.passing[w].at[k] for k in range(4)])
        self.hand(w).start()

    def leave(self, w):
        if w not in self.given:
            self.give(w, 1).wait_recv()
        self.hand(w).wait_recv()
        groups = [
            [self.half[w].at[1, k], self.sums[w].at[k, 0], self.quarter[w].at[k]]
            for k in range(1, 4)
        ]
        self.rounded(w, groups, [self.leaving[w].at[k] for k in range(3)])
        for k in range(1, 4):
            self.far(w, k).start()

    def close(self, w):
        for k in range(1, 4):
            self.far(w, k).wait_recv()
        group = [self.half[w].at[1, 0], self.sums[w].at[0, 0], self.quarter[w].at[0]]
        group += [self.last[w].at[k] for k in range(3)]
        height = self.sums[w].shape[2]
        which = 0 if height <= self.slots[0].shape[2] else 1

        def moves(bank, chunk, lanes, extent):
            total = self.totals[which].at[bank, pl.ds(0, height), pl.ds(0, extent)]
            target = self.out[w].at[self.core, :, lanes]
            here = pltpu.make_async_copy(total, target, self.store.at[bank, 0])
            return total, here, self.copy(w, 6 + chunk, total, target, self.sibling)

        def finish(bank, chunk, index, lanes, extent, views):
            total, here, there = moves(bank, chunk, lanes, extent)

            def put(at, value):
                total[:, at] = value

            self.added(views, extent, f32, put)
            here.start()
            there.start()

        def settle(bank, chunk, lanes, extent):
            _, here, there = moves(bank, chunk, lanes, extent)
            here.wait()
            there.wait_send()
            there.wait_recv()

        self.add(w, [group], finish, settle)

    def finish(self, w):
        if w not in self.given:
            self.give(w, 0).wait_send()
            self.give(w, 1).wait_send()
        self.hand(w).wait_send()
        for k in range(1, 4):
            self.far(w, k).wait_send()


def rest_back_body(batch, scaling, *refs):
    refs = list(refs)
    take = refs.pop

    def several(count):
        return [take(0) for _ in range(count)]

    gains, valid = several(2)
    loaded = several(13)
    skip_w, qkv_w, pair_w, query_w, keyval_w = several(5)
    cross_keyval, cq_proj, ckey_mine, qkv, keyval_here, keyval_there, cross_grad = several(7)
    summed, half_down = several(2), take(0)
    text_grad, gain_grads, shift_grad, normed_grad = several(4)
    out = several(7)
    own_sums, there = several(5), several(5)
    half = [half_down, *several(6)]
    passing, quarter, leaving, last = (several(7) for _ in range(4))
    grad, wide, factor, back = several(4)
    query, mix_grad, total, keyval, proj, turned, halves = several(7)
    placed = several(13)
    cross_cat, attn_cat, cross_in, attn_in, text, after_self, hidden, normed = placed[:8]
    order, heads_ref, *tables = placed[8:]
    buffer, out_buffer, in_buffer = several(3)
    slots, totals = several(2), several(2)
    landed = take(0)
    semaphore, loads, twin_send, twin_recv, twin_local = several(5)
    exchange_send, exchange_recv, send, recv, add_load, add_store = several(6)
    rows, width = hidden.shape
    size = rows // batch
    block = width // 16
    core = lax.axis_index("seq")
    down, up, query_s, keyval_s, pair_s, qkv_s, skip_s = range(7)
    plan = ScatterPlan(
        summed + own_sums, out, half, passing, quarter, leaving, last, slots, totals,
        (send, recv, add_load, add_store), (0,),
    )
    twin = TwinSum(
        there, own_sums, twin_send, twin_recv, twin_local, out_buffer, in_buffer, plan.sibling
    )
    greet(plan.peers())
    plan.begin(up)

    first_lanes, last_lanes = pl.ds(0, width), pl.ds(width, width)

    def load(*pairs):
        copies = [
            pltpu.make_async_copy(source, target, loads.at[at])
            for at, (source, target) in enumerate(pairs)
        ]
        for copy in copies:
            copy.start()
        for copy in copies:
            copy.wait()

    load(
        (cross_grad, grad),
        (cross_keyval, keyval),
        (cq_proj, proj.at[:, first_lanes]),
        (ckey_mine, proj.at[:, last_lanes]),
        *zip(loaded, placed),
    )
    plan.middle(down)
    gain_grads[...] = jnp.zeros_like(gain_grads)
    shift_grad[...] = jnp.zeros_like(shift_grad)

    def each(body):
        for b in range(batch):
            body(b, pl.ds(b * size, size))

    def back_through(weight, tiles, factor_of, target):
        def body(index, tile):
            value = dot_right_t(factor_of(*tiles[index]), tile)
            if index == 0:
                target[...] = value
            else:
                target[...] += value

        stream(weight, tiles, buffer, semaphore, body)

    def restored(target):
        def part(b, rows_b):
            target[rows_b, :] = dot_right_t(wide[rows_b, :].astype(bf16), order[...]).astype(bf16)

        each(part)

    def split_lanes(value, rows_b, start):
        halves[0, rows_b, pl.ds(start, 768)] = value[:, :768]
        halves[1, rows_b, pl.ds(start, width - 768)] = value[:, 768:]
        halves[1, rows_b, pl.ds(start + width - 768, 2 * 768 - width)] = jnp.zeros(
            (value.shape[0], 2 * 768 - width), bf16
        )

    def attention_back(sources, table_refs, masked, put):
        back[...] = jnp.zeros_like(back)
        total[...] = jnp.zeros_like(total)

        def prepare(b, rows_b):
            value, scale = head_norm(proj[rows_b, first_lanes], heads_ref)
            wide[rows_b, :] = value
            factor[rows_b, :] = scale
            turned_value = turn(value, table_refs) if table_refs else value
            query[rows_b, :] = turned_value.astype(bf16)

        each(prepare)

        @pl.loop(0, batch)
        def _(b):
            rows_b = pl.ds(pl.multiple_of(b * size, size), size)
            for head in range(HEADS):
                lanes, inside = window_of(head, width)
                behind = shift_lanes(lanes, width)
                queries = query[rows_b, lanes] * inside.astype(bf16)
                keys = pair_rows(sources, b, size, lanes)
                scores = dot_right_t(queries, keys) * scaling
                if masked:
                    scores = jnp.where(valid[pl.ds(b, 1), :] > 0.5, scores, masked_value)
                probs, _ = softmax_of(scores)
                grads = mix_grad[rows_b, lanes] * inside.astype(bf16)
                prob_grad = dot_right_t(grads, pair_rows(sources, b, size, behind))
                score_grad = softmax_back(probs, prob_grad).astype(bf16)
                value_grad = dot_left_t(probs.astype(bf16), grads)
                key_grad = dot_left_t(score_grad, queries) * scaling
                back[rows_b, lanes] += dot_plain(score_grad, keys) * (inside * scaling)
                for at in range(2):
                    part = slice(at * size, (at + 1) * size)
                    total[at, rows_b, lanes] += key_grad[part]
                    total[at, rows_b, behind] += value_grad[part]

        def finish(b, rows_b):
            value = back[rows_b, :]
            if table_refs:
                value = turn_back(value, table_refs)
            value = head_norm_back(value, wide[rows_b, :], factor[rows_b, :], heads_ref)
            put(value.astype(bf16), rows_b)

        each(finish)

    def exchange(index):
        return pltpu.make_async_remote_copy(
            src_ref=keyval.at[pl.ds(0, rows), :],
            dst_ref=landed.at[index],
            send_sem=exchange_send.at[index],
            recv_sem=exchange_recv.at[index],
            device_id=plan.sibling,
            device_id_type=MESH,
        )

    def keys_back(index, mine, table_refs, put):
        def part(b, rows_b):
            normed_keys, scale = head_norm(proj[rows_b, last_lanes], heads_ref)
            value = total[mine, rows_b, first_lanes] + landed[index, rows_b, first_lanes].astype(f32)
            if table_refs:
                value = turn_back(value, table_refs)
            key_grad = head_norm_back(value, normed_keys, scale, heads_ref).astype(bf16)
            value = total[mine, rows_b, last_lanes] + landed[index, rows_b, last_lanes].astype(f32)
            put(key_grad, value.astype(bf16), rows_b)

        each(part)

    def twin_product(w, extent, height, left, right):
        starts, places, shape = lane_places(height, extent, out_buffer.shape[4])

        def part(which):
            def value(index):
                start, lanes = starts[index]
                product = dot_plain(left(which), right(which, start, lanes))
                return product.reshape(4, 4, height, lanes)

            return value

        twin.run(w, places, shape, part(1 - core), part(core))

    halves[1, :, first_lanes] = grad[...].astype(bf16)
    pair_tiles = tiles_of(width, 384, (1,))
    back_through(
        pair_w, pair_tiles, lambda at, start, extent: halves[at, :, pl.ds(start, extent)], wide
    )
    restored(mix_grad)
    attention_back([keyval], (), True, lambda value, rows_b: split_lanes(value, rows_b, width))
    keyval[pl.ds(0, rows), :] = total[1 - core].astype(bf16)
    exchange(0).start()
    plan.leave(down)
    query_tiles = tiles_of(768, 384)
    back_through(
        query_w,
        query_tiles,
        lambda at, start, extent: halves[at, :, pl.ds(width + start, extent)],
        wide,
    )

    def self_part(b, rows_b):
        value = restore_order(order[...], wide[rows_b, :])
        value, gain_part = norm_back(after_self[rows_b, :], gains[1:2, :], value)
        gain_grads[1:2, :] += gain_part
        value = grad[rows_b, :] + value
        grad[rows_b, :] = value
        halves[0, rows_b, first_lanes] = value.astype(bf16)

    each(self_part)
    pair_tiles_two = tiles_of(width, 384, (0,))
    back_through(
        pair_w, pair_tiles_two, lambda at, start, extent: halves[at, :, pl.ds(start, extent)], wide
    )
    restored(mix_grad)
    turned[0] = jnp.transpose(attn_cat[...])
    turned[1] = jnp.transpose(cross_cat[...])
    twin_product(
        2,
        width,
        block,
        lambda at: turned[at],
        lambda at, start, extent: halves[at, :, pl.ds(start, extent)],
    )
    plan.begin(pair_s)
    turned[0] = jnp.transpose(cross_in[...])
    twin_product(
        0,
        768,
        block,
        lambda at: turned[0],
        lambda at, start, extent: halves[at, :, pl.ds(width + start, extent)],
    )
    plan.begin(query_s)
    plan.middle(up)
    exchange(0).wait()

    def text_part(key_grad, value_grad, rows_b):
        landed[0, rows_b, first_lanes] = key_grad
        landed[0, rows_b, last_lanes] = value_grad

    keys_back(0, core, (), text_part)

    load(
        (qkv, proj),
        (keyval_here, keyval.at[pl.ds(0, rows), :]),
        (keyval_there, keyval.at[pl.ds(rows, rows), :]),
    )

    def query_part(value, rows_b):
        halves[0, rows_b, first_lanes] = value

    sources = [keyval.at[pl.ds(0, rows), :], keyval.at[pl.ds(rows, rows), :]]
    attention_back(sources, tables, False, query_part)
    keyval[pl.ds(0, rows), :] = total[1].astype(bf16)
    exchange(1).start()
    plan.middle(pair_s)
    plan.middle(query_s)
    exchange(1).wait()

    def key_part(key_grad, value_grad, rows_b):
        halves[1, rows_b, first_lanes] = key_grad
        split_lanes(value_grad, rows_b, width)

    keys_back(1, 0, tables, key_part)
    turned[0] = jnp.transpose(attn_in[...])
    wide_half = halves.shape[2]
    twin_product(
        3,
        wide_half,
        block,
        lambda at: turned[0],
        lambda at, start, extent: halves[at, :, pl.ds(start, extent)],
    )
    plan.begin(qkv_s)
    qkv_tiles = tiles_of(wide_half, 384)
    back_through(
        qkv_w, qkv_tiles, lambda at, start, extent: halves[at, :, pl.ds(start, extent)], wide
    )

    def hidden_part(b, rows_b):
        value = restore_order(order[...], wide[rows_b, :])
        shift_grad[b : b + 1, :] = jnp.sum(value, axis=0, keepdims=True)
        value, gain_part = norm_back(hidden[rows_b, :], gains[0:1, :], value)
        gain_grads[0:1, :] += gain_part
        halves[0, rows_b, first_lanes] = (grad[rows_b, :] + value).astype(bf16)

    each(hidden_part)
    plan.leave(up)

    for at in range(2):
        for part in range(2):
            turned[at, pl.ds(part * (width // 2), width // 2), :] = jnp.transpose(
                normed[at, part]
            )
    twin_product(
        4,
        width,
        block,
        lambda at: turned[at],
        lambda at, start, extent: halves[0, :, pl.ds(start, extent)],
    )
    plan.begin(skip_s)
    plan.leave(pair_s)
    plan.leave(query_s)

    text_width = text.shape[1]
    turned[0, pl.ds(0, text_width), :] = jnp.transpose(text[...])
    twin_product(
        1,
        width,
        text_width // 16,
        lambda at: turned[0, pl.ds(0, text_width), :],
        lambda at, start, extent: landed[0, :, pl.ds(at * width + start, extent)]
        if isinstance(at, int)
        else landed[0, :, pl.ds(pl.multiple_of(at * width + start, 128), extent)],
    )
    plan.begin(keyval_s)
    plan.middle(qkv_s)
    back_through(
        keyval_w,
        tiles_of(width, 384),
        lambda at, start, extent: landed[0, :, pl.ds(at * width + start, extent)],
        text_grad,
    )
    skip_tiles = tiles_of(width, 384)

    def skip_body(index, tile):
        at, start, extent = skip_tiles[index]
        value = dot_right_t(halves[0, :, pl.ds(start, extent)], tile)
        lanes = pl.ds(at * width, width)
        if start == 0:
            total[0, :, lanes] = value
        else:
            total[0, :, lanes] += value

    stream(skip_w, skip_tiles, buffer, semaphore, skip_body)
    keep = pltpu.make_async_copy(total.at[0], normed_grad, loads.at[0])
    keep.start()
    plan.close(down)
    plan.middle(skip_s)
    plan.leave(qkv_s)
    plan.middle(keyval_s)
    plan.close(up)
    plan.leave(skip_s)
    plan.leave(keyval_s)
    plan.close(pair_s)
    plan.close(query_s)
    plan.close(qkv_s)
    plan.close(skip_s)
    plan.close(keyval_s)
    keep.wait()
    for w in range(7):
        plan.finish(w)


def joined_back_body(batch, normed_grad, latent, skip, skip_gain, order_skip, joined, gain_grad):
    width = latent.shape[1]
    size = latent.shape[0] // batch
    upper_half = lax.axis_index("fsdp") >= 8
    gain_grad[...] = jnp.zeros_like(gain_grad)
    for b in range(batch):
        rows_b = pl.ds(b * size, size)
        near, away = 0.0, 0.0
        for at in range(2):
            part = normed_grad[rows_b, at * width : (at + 1) * width]
            near = near + restore_order(order_skip[at], part[:, : width // 2])
            away = away + restore_order(order_skip[at], part[:, width // 2 :])
        left = latent[rows_b, :].astype(f32)
        right = skip[rows_b, :].astype(f32)
        left_grad = jnp.where(upper_half, away, near)
        right_grad = jnp.where(upper_half, near, away)

        def mean(first, second):
            total = jnp.sum(first, axis=1, keepdims=True) + jnp.sum(second, axis=1, keepdims=True)
            return total / (2 * width)

        middle = mean(left, right)
        left, right = left - middle, right - middle
        factor = lax.rsqrt(mean(left * left, right * right) + norm_eps)
        left, right = left * factor, right * factor
        gain_grad[0:1, :width] += jnp.sum(left_grad * left, axis=0, keepdims=True)
        gain_grad[0:1, width:] += jnp.sum(right_grad * right, axis=0, keepdims=True)
        left_grad = left_grad * skip_gain[:, :width]
        right_grad = right_grad * skip_gain[:, width:]
        first = mean(left_grad, right_grad)
        second = mean(left_grad * left, right_grad * right)
        joined[0, rows_b, :] = factor * (left_grad - first - left * second)
        joined[1, rows_b, :] = factor * (right_grad - first - right * second)


class Links:
    def __init__(self, fsdp_count):
        self.count = fsdp_count
        self.me = lax.axis_index("fsdp")
        self.core = lax.axis_index("seq")
        self.high_bits = fsdp_count.bit_length() - 3
        self.quad = 4 << (self.high_bits - 2)
        offsets = [0]
        for bit in range(self.high_bits - 2):
            offsets = offsets + [offset | (4 << bit) for offset in offsets]
        self.high_offsets = [k * self.quad | offset for k in range(4) for offset in offsets]

    def swap(self, value, mask_first, mask_second):
        pairs = []
        for index in range(self.count):
            pairs.append((2 * index, 2 * (index ^ mask_first)))
            pairs.append((2 * index + 1, 2 * (index ^ mask_second) + 1))
        return lax.ppermute(value, ("fsdp", "seq"), pairs)

    def sibling(self, value):
        return lax.ppermute(value, "seq", [(0, 1), (1, 0)])

    def pick(self, first, second):
        return jnp.where(self.core == 0, first, second)

    def offset(self, block):
        return self.high_offsets[block % (self.count // 4)] | (block // (self.count // 4))

    def place(self, offset):
        table = [0] * self.count
        for block in range(self.count):
            table[self.offset(block)] = block
        return jnp.array(table, jnp.int32)[offset]

    def columns(self, own, other):
        return self.pick(
            jnp.concatenate([own, other], axis=-1), jnp.concatenate([other, own], axis=-1)
        )

    def halves(self, value):
        half = value.shape[-1] // 2
        first, second = value[..., :half], value[..., half:]
        return self.pick(first, second), self.pick(second, first)

    def order_matrix(self, size):
        block = size // self.count
        at = lax.broadcasted_iota(jnp.int32, (size, size), 0)
        table = jnp.array([self.offset(b) for b in range(self.count)], jnp.int32)
        starts = jnp.bitwise_xor(self.me, table) * block
        wanted = (starts[:, None] + jnp.arange(block, dtype=jnp.int32)[None, :]).reshape(1, size)
        return (at == wanted).astype(bf16)

    def order_skip(self, width):
        block = width // self.count
        offsets = [
            offset & (self.count // 2 - 1) for offset in self.high_offsets[: self.count // 2 // 4 * 1]
        ]
        offsets = [offset | q for q in range(4) for offset in offsets]
        lower = jnp.bitwise_and(self.me, self.count // 2 - 1)
        starts = jnp.bitwise_xor(lower, jnp.array(offsets, jnp.int32)) * (2 * block)
        starts = jnp.stack([starts, starts + block])
        wanted = (starts[:, :, None] + jnp.arange(block, dtype=jnp.int32)).reshape(1, width)
        return (lax.broadcasted_iota(jnp.int32, (width, width), 0) == wanted).astype(bf16)

    def order_blocks(self, value):
        size = value.shape[1] // self.count
        parts = []
        for block in range(self.count):
            source = jnp.bitwise_xor(self.me, self.offset(block))
            parts.append(lax.dynamic_slice_in_dim(value, source * size, size, 1))
        return jnp.concatenate(parts, axis=1)

    def restore_blocks(self, value):
        size = value.shape[1] // self.count
        parts = []
        for shard in range(self.count):
            source = self.place(jnp.bitwise_xor(self.me, shard))
            parts.append(lax.dynamic_slice_in_dim(value, source * size, size, 1))
        return jnp.concatenate(parts, axis=1)

    def extra_gather(self, mine):
        blocks = mine
        for bit in range(self.high_bits - 2):
            blocks = jnp.concatenate([blocks, self.swap(blocks, 4 << bit, 4 << bit)], axis=0)
        return blocks

    def extra_scatter(self, value):
        for bit in reversed(range(self.high_bits - 2)):
            size = value.shape[-2] // 2
            value = value[..., :size, :] + self.swap(value[..., size:, :], 4 << bit, 4 << bit)
        return value


class Gather:
    def __init__(self, links, shards):
        self.links = links
        half = shards[0].shape[1] // 2
        self.rows = shards[0].shape[0]
        self.weights = len(shards)
        self.shards = jnp.concatenate(
            [links.pick(shard[:, :half], shard[:, half:]) for shard in shards], axis=0
        )
        self.pending = [self.shards]
        self.stage = 0

    def advance(self):
        links = self.links
        self.stage += 1
        if self.stage == 1:
            blocks = [self.pending[0]]
            for bit in range(links.high_bits - 2):
                got = links.swap(jnp.concatenate(blocks, axis=0), 4 << bit, 4 << bit)
                size = self.rows * self.weights
                blocks = blocks + [got[at * size : (at + 1) * size] for at in range(len(blocks))]
            self.low_blocks = len(blocks)
            mine = jnp.concatenate(blocks, axis=0) if len(blocks) > 1 else blocks[0]
            self.pending = [mine] + [
                links.swap(mine, k * links.quad, k * links.quad) for k in range(1, 4)
            ]
        elif self.stage == 2:
            size = self.rows * self.weights
            cuts = [
                got[at * size + w * self.rows : at * size + (w + 1) * self.rows]
                for w in range(self.weights)
                for got in self.pending
                for at in range(self.low_blocks)
            ]
            base = jnp.concatenate(cuts, axis=0)
            self.pending = [
                base, links.swap(base, 1, 2), links.swap(base, 2, 1), links.sibling(base)
            ]
        elif self.stage == 3:
            base, first, second, base_there = self.pending
            self.kept = [base, second, base_there]
            self.pending = [
                links.swap(first, 2, 1), links.sibling(first), links.sibling(second), *self.pending
            ]
        elif self.stage == 4:
            self.pending[0:1] = [links.sibling(self.pending[0]), self.pending[0]]
        elif self.stage == 5:
            both_there, both, first_there, second_there, base, first, second, base_there = self.pending
            size = base.shape[0] // self.weights
            self.result = []
            for w in range(self.weights):
                cut = slice(w * size, (w + 1) * size)
                pick = links.pick
                own = jnp.concatenate(
                    [base[cut], pick(first[cut], second[cut]), pick(second[cut], first[cut]), both[cut]],
                    axis=0,
                )
                other = jnp.concatenate(
                    [
                        base_there[cut],
                        pick(second_there[cut], first_there[cut]),
                        pick(first_there[cut], second_there[cut]),
                        both_there[cut],
                    ],
                    axis=0,
                )
                self.result.append((own, other))
            self.pending = []

    def finish(self):
        while self.stage < 5:
            self.advance()
        return self.result


class Scatter:
    def __init__(self, links, pairs):
        self.links = links
        self.pairs = pairs
        self.pending = [other for _, other in pairs]
        self.stage = 0

    def advance(self):
        links = self.links
        pick = links.pick
        self.stage += 1
        if self.stage == 1:
            self.pending = [own for own, _ in self.pairs] + [
                links.sibling(other) for other in self.pending
            ]
        elif self.stage == 2:
            count = len(self.pairs)
            send, keep = [[], []], [[], []]
            for own, got in zip(self.pending[:count], self.pending[count:]):
                size = own.shape[0] // 4
                cuts = [
                    own[q * size : (q + 1) * size].astype(f32) + got[q * size : (q + 1) * size].astype(f32)
                    for q in range(4)
                ]
                send[0].append(pick(cuts[2], cuts[1]).astype(bf16))
                send[1].append(cuts[3].astype(bf16))
                keep[0].append(cuts[0])
                keep[1].append(pick(cuts[1], cuts[2]))
            self.sizes = [part.shape[0] for part in keep[0]]
            self.keep = [jnp.concatenate(part, axis=0) for part in keep]
            self.pending = [links.swap(jnp.concatenate(send[0] + send[1], axis=0), 2, 1)]
        elif self.stage == 3:
            total = sum(self.sizes)
            got = self.pending[0].astype(f32)
            self.keep, send = self.keep[0] + got[:total], (self.keep[1] + got[total:]).astype(bf16)
            self.pending = [links.swap(send, 1, 2)]
        elif self.stage == 4:
            summed = self.keep + self.pending[0].astype(f32)
            keep, send = [], [[], [], []]
            start = 0
            for size in self.sizes:
                part = size // 4
                keep.append(summed[start : start + part])
                for k in range(1, 4):
                    send[k - 1].append(summed[start + k * part : start + (k + 1) * part].astype(bf16))
                start += size
            self.keep = jnp.concatenate(keep, axis=0)
            self.pending = [
                links.swap(jnp.concatenate(send[k - 1], axis=0), k * links.quad, k * links.quad)
                for k in range(1, 4)
            ]
        elif self.stage == 5:
            total = self.keep
            for got in self.pending:
                total = total + got.astype(f32)
            rows = [size // 4 for size in self.sizes]
            for bit in reversed(range(links.high_bits - 2)):
                keep, send, start = [], [], 0
                for at, size in enumerate(rows):
                    keep.append(total[start : start + size // 2])
                    send.append(total[start + size // 2 : start + size])
                    start += size
                    rows[at] = size // 2
                got = links.swap(jnp.concatenate(send, axis=0), 4 << bit, 4 << bit)
                total = jnp.concatenate(keep, axis=0) + got
            self.rows = rows
            self.pending = [total, links.sibling(total)]
        elif self.stage == 6:
            whole = links.columns(*self.pending)
            self.result, start = [], 0
            for size in self.rows:
                self.result.append(whole[start : start + size])
                start += size
            self.pending = []

    def finish(self):
        while self.stage < 6:
            self.advance()
        return self.result


def tie(value, *jobs):
    leaves, tree = jax.tree.flatten(value)
    flat = list(leaves)
    for job in jobs:
        flat.extend(job.pending)
    flat = list(lax.optimization_barrier(tuple(flat)))
    at = len(leaves)
    value = jax.tree.unflatten(tree, flat[:at])
    for job in jobs:
        job.pending = flat[at : at + len(job.pending)]
        at += len(job.pending)
        job.advance()
    return value


def parts_of(value):
    high = value.astype(bf16)
    return high, (value - high.astype(f32)).astype(bf16)


def sum_heads(value, heads_ref):
    high, low = parts_of(value)
    return dot_plain(high, heads_ref[...]) + dot_plain(low, heads_ref[...])


def spread_heads(value, heads_ref):
    high, low = parts_of(value)
    return dot_right_t(high, heads_ref[...]) + dot_right_t(low, heads_ref[...])


def head_norm(value, heads_ref):
    center = value - spread_heads(sum_heads(value, heads_ref) * (1.0 / HD), heads_ref)
    spread = sum_heads(center * center, heads_ref) * (1.0 / HD)
    factor = spread_heads(lax.rsqrt(spread + norm_eps), heads_ref)
    return center * factor, factor


def head_norm_back(grad, normed, factor, heads_ref):
    first = sum_heads(grad, heads_ref) * (1.0 / HD)
    second = sum_heads(grad * normed, heads_ref) * (1.0 / HD)
    return factor * (
        grad - spread_heads(first, heads_ref) - normed * spread_heads(second, heads_ref)
    )


def partner(value, former):
    quarter = HD // 4
    width = value.shape[1]
    up = pltpu.roll(value, width - quarter, 1)
    down = pltpu.roll(value, quarter, 1)
    return jnp.where(former > 0.5, up, down)


def turn(value, table_refs):
    cosine, sine, former = table_refs
    return value * cosine[...] + partner(value, former[...]) * sine[...]


def turn_back(value, table_refs):
    cosine, sine, former = table_refs
    return value * cosine[...] - partner(value, former[...]) * sine[...]


def window_of(head, width):
    start = min(head * HD // 128 * 128, width - 256)
    lane = lax.broadcasted_iota(jnp.int32, (1, 256), 1) + start
    inside = jnp.logical_and(lane >= head * HD, lane < (head + 1) * HD)
    return pl.ds(start, 256), inside.astype(f32)


def normed_rows(proj_ref, heads_ref, table_refs, rows):
    value, factor = head_norm(proj_ref[rows, :], heads_ref)
    turned = turn(value, table_refs) if table_refs else value
    return value, factor, turned


def keys_body(batch, turned, *refs):
    key_ref, value_ref, heads_ref = refs[:3]
    table_refs, out_ref = refs[3:-1], refs[-1]
    width = key_ref.shape[1]
    size = key_ref.shape[0] // batch
    for b in range(batch):
        rows = pl.ds(b * size, size)
        out_ref[rows, :width] = normed_rows(key_ref, heads_ref, table_refs, rows)[2].astype(bf16)
        out_ref[rows, width:] = value_ref[rows, :].astype(bf16)


def pair_rows(refs, b, size, lanes):
    if len(refs) == 2:
        return jnp.concatenate([ref[pl.ds(b * size, size), lanes] for ref in refs], axis=0)
    return refs[0][pl.ds(b * 2 * size, 2 * size), lanes]


def shift_lanes(lanes, width):
    return pl.ds(lanes.start + width, lanes.size)


def scores_of(query, key, lengths_ref, b, scaling):
    scores = dot_right_t(query, key) * scaling
    if lengths_ref is not None:
        column = lax.broadcasted_iota(jnp.int32, scores.shape, 1)
        scores = jnp.where(column < lengths_ref[b], scores, masked_value)
    return scores


def softmax_of(scores):
    largest = jnp.max(scores, axis=1, keepdims=True)
    raised = jnp.exp(scores - largest)
    return raised * (1.0 / jnp.sum(raised, axis=1, keepdims=True)), largest


def attention_body(batch, masked, turned, sources, scaling, *refs):
    refs = list(refs)
    lengths_ref = refs.pop(0) if masked else None
    proj_ref, heads_ref = refs.pop(0), refs.pop(0)
    table_refs = [refs.pop(0) for _ in range(3)] if turned else []
    keyval_refs = [refs.pop(0) for _ in range(sources)]
    out_ref, peak_ref, query_ref, mixed_ref = refs
    size, width = proj_ref.shape[0] // batch, proj_ref.shape[1]
    peak_ref[...] = jnp.full_like(peak_ref, masked_value)
    mixed_ref[...] = jnp.zeros_like(mixed_ref)
    for b in range(batch):
        rows = pl.ds(b * size, size)
        query_ref[rows, :] = normed_rows(proj_ref, heads_ref, table_refs, rows)[2].astype(bf16)

    @pl.loop(0, batch)
    def _(b):
        rows = pl.ds(pl.multiple_of(b * size, size), size)
        for head in range(HEADS):
            lanes, inside = window_of(head, width)
            query = query_ref[rows, lanes] * inside.astype(bf16)
            key = pair_rows(keyval_refs, b, size, lanes)
            scores = scores_of(query, key, lengths_ref, b, scaling)
            probs, largest = softmax_of(scores)
            largest = jnp.max(largest, axis=0, keepdims=True)
            peak_ref[head : head + 1, :] = jnp.maximum(
                peak_ref[head : head + 1, :], jnp.broadcast_to(largest, (1, 128))
            )
            value = pair_rows(keyval_refs, b, size, shift_lanes(lanes, width))
            mixed_ref[rows, lanes] += dot_plain(probs.astype(bf16), value) * inside

    out_ref[...] = mixed_ref[...].astype(bf16)


def attention_back_body(batch, masked, turned, sources, scaling, *refs):
    refs = list(refs)
    lengths_ref = refs.pop(0) if masked else None
    proj_ref, grad_ref, heads_ref = refs.pop(0), refs.pop(0), refs.pop(0)
    table_refs = [refs.pop(0) for _ in range(3)] if turned else []
    keyval_refs = [refs.pop(0) for _ in range(sources)]
    out_ref, here_ref, there_ref, normed_ref, factor_ref, query_ref, back_ref, total_ref = refs
    size, width = proj_ref.shape[0] // batch, proj_ref.shape[1]
    back_ref[...] = jnp.zeros_like(back_ref)
    total_ref[...] = jnp.zeros_like(total_ref)
    for b in range(batch):
        rows = pl.ds(b * size, size)
        normed, factor, query = normed_rows(proj_ref, heads_ref, table_refs, rows)
        normed_ref[rows, :] = normed
        factor_ref[rows, :] = factor
        query_ref[rows, :] = query.astype(bf16)

    @pl.loop(0, batch)
    def _(b):
        rows = pl.ds(pl.multiple_of(b * size, size), size)
        for head in range(HEADS):
            lanes, inside = window_of(head, width)
            behind = shift_lanes(lanes, width)
            query = query_ref[rows, lanes] * inside.astype(bf16)
            key = pair_rows(keyval_refs, b, size, lanes)
            probs, _ = softmax_of(scores_of(query, key, lengths_ref, b, scaling))
            grad = grad_ref[rows, lanes] * inside.astype(bf16)
            value = pair_rows(keyval_refs, b, size, behind)
            prob_grad = dot_right_t(grad, value)
            score_grad = softmax_back(probs, prob_grad).astype(bf16)
            value_grad = dot_left_t(probs.astype(bf16), grad)
            key_grad = dot_left_t(score_grad, query) * scaling
            back_ref[rows, lanes] += dot_plain(score_grad, key) * (inside * scaling)
            for at in range(2):
                part = slice(at * size, (at + 1) * size)
                total_ref[at, rows, lanes] += key_grad[part]
                total_ref[at, rows, behind] += value_grad[part]

    for b in range(batch):
        rows = pl.ds(b * size, size)
        grad = back_ref[rows, :]
        if table_refs:
            grad = turn_back(grad, table_refs)
        out_ref[rows, :] = head_norm_back(
            grad, normed_ref[rows, :], factor_ref[rows, :], heads_ref
        ).astype(bf16)
    mine = lax.axis_index("seq") if masked else 0
    here_ref[...] = total_ref[mine]
    there_ref[...] = total_ref[1 - mine].astype(bf16)


def keys_back_body(batch, turned, *refs):
    key_ref, here_ref, from_there_ref, heads_ref = refs[:4]
    table_refs, out_ref = refs[4:-1], refs[-1]
    width = key_ref.shape[1]
    size = key_ref.shape[0] // batch
    for b in range(batch):
        rows = pl.ds(b * size, size)
        normed, factor, _ = normed_rows(key_ref, heads_ref, (), rows)
        grad = here_ref[rows, :width] + from_there_ref[rows, :width].astype(f32)
        if table_refs:
            grad = turn_back(grad, table_refs)
        out_ref[rows, :width] = head_norm_back(grad, normed, factor, heads_ref).astype(bf16)
        out_ref[rows, width:] = (
            here_ref[rows, width:] + from_there_ref[rows, width:].astype(f32)
        ).astype(bf16)


def plain_call(body, outs, blocks, scratch=(), lengths=None):
    def spec(array, column):
        if column is None:
            return pl.BlockSpec(array.shape, lambda i, *_: (0,) * array.ndim)
        return pl.BlockSpec((array.shape[0], column[1]), lambda i, *_: (0, column[0]))

    def out_spec(shape):
        return pl.BlockSpec(shape.shape, lambda i, *_: (0,) * len(shape.shape))

    grid_spec = pltpu.PrefetchScalarGridSpec(
        num_scalar_prefetch=0 if lengths is None else 1,
        grid=(1,),
        in_specs=[spec(*block) for block in blocks],
        out_specs=[out_spec(shape) for shape in outs],
        scratch_shapes=list(scratch),
    )
    given = [] if lengths is None else [lengths]
    return pl.pallas_call(
        body,
        grid_spec=grid_spec,
        out_shape=list(outs),
        compiler_params=pltpu.CompilerParams(vmem_limit_bytes=50 * 2**20),
    )(*given, *[array for array, _ in blocks])


def lanes_of(value, multiple):
    size = 128 * multiple
    spare = -value.shape[-1] % size
    value = jnp.pad(value, [(0, 0)] * (value.ndim - 1) + [(0, spare)])
    return value.reshape(*value.shape[:-1], -1, 128)


def restore_order(matrix, value):
    return dot_right_t(value.astype(bf16), matrix)


def exact_restore(matrix, value):
    high = value.astype(bf16)
    low = (value - high.astype(f32)).astype(bf16)
    return dot_right_t(high, matrix) + dot_right_t(low, matrix)


def local(
    latent,
    skip_input,
    condition,
    text_encoder_states,
    text_lengths,
    out_grad,
    skip_gain,
    norm_gains,
    skip_linear,
    shift_linear,
    self_qkv,
    self_out,
    cross_query,
    cross_keyval,
    cross_out,
    mlp_up,
    mlp_down,
    thresholds,
):
    batch, tokens, width = latent.shape
    rows = batch * tokens
    text_rows = text_encoder_states.shape[1]
    text_width = text_encoder_states.shape[2]
    scaling = HD ** (-0.5)
    links = Links(lax.axis_size("fsdp"))
    me, core = links.me, links.core
    count = links.count

    positions = core * tokens + jnp.arange(tokens)
    feature = jnp.arange(width) % HD
    freqs = 10000.0 ** (-(feature % (HD // 4)).astype(f32) / (HD // 4))
    place = jnp.where(
        feature[None, :] < HD // 2, (positions // GRID_W)[:, None], (positions % GRID_W)[:, None]
    )
    angles = place.astype(f32) * freqs[None, :]
    former = (feature % (HD // 2) < HD // 4)[None, :]
    cosine = jnp.cos(angles)
    sine = jnp.where(former, -jnp.sin(angles), jnp.sin(angles))
    tables = [(cosine, None), (sine, None), (former.astype(f32), None)]
    head_at = jnp.arange(width)[:, None] // HD == jnp.arange(128)[None, :]
    head_at = (head_at.astype(bf16), None)

    gain_rows = skip_gain.shape[0]
    third = norm_gains.shape[1]
    cond_act = jax.nn.silu(condition.astype(f32)).astype(bf16)
    small = jnp.concatenate([skip_gain, norm_gains.reshape(-1), cond_act.reshape(-1)])
    small = trade(lanes_of(small, 16), count, True, 1).reshape(count, -1)
    skip_gain_all = small[:, :gain_rows].reshape(-1).astype(f32)
    cond_start = gain_rows + 3 * third
    gains = small[:, gain_rows:cond_start].reshape(count, 3, third)
    gains = gains.transpose(1, 0, 2).reshape(3, width).astype(f32)
    cond_all = small[:, cond_start : cond_start + batch * width].reshape(count * batch, width)
    shift_rows = shift_linear.shape[0]
    cond_cut = lax.dynamic_slice_in_dim(cond_all, me * shift_rows, shift_rows, 1)
    shift_parts = dot_plain(cond_cut, shift_linear).reshape(count, batch * width)
    shift_parts = trade(lanes_of(shift_parts, 8), count, False, 2)
    shift = jnp.sum(shift_parts.reshape(count, -1), axis=0)[: batch * width].reshape(batch, width)

    def columns_mine(weight):
        half = weight.shape[1] // 2
        return links.pick(weight[:, :half], weight[:, half:])

    skip_half = skip_linear.shape[0] // 2
    shards = [
        links.pick(skip_linear[:skip_half], skip_linear[skip_half:]),
        columns_mine(self_qkv),
        links.pick(self_out, cross_out),
        columns_mine(cross_query),
        columns_mine(cross_keyval),
    ]
    shards = [links.extra_gather(shard) for shard in shards]
    shards = lax.optimization_barrier((shift, *shards))
    shift = shards[0]
    gathered = gather(shards[1:], links.quad, 3)
    w_skip, w_qkv, w_pair, w_query, w_keyval = (
        g.reshape(2, 16 * g.shape[2], g.shape[3]) for g in gathered
    )
    w_self_out, w_cross_out = w_pair[0], w_pair[1]
    get_up = Gather(links, [mlp_up])
    get_down = Gather(links, [mlp_down])
    w_skip = tie(w_skip, get_up, get_down)

    order = links.order_matrix(width)
    order_skip = links.order_skip(width)
    order_text = links.order_matrix(text_width)

    def product(value, weight):
        return jnp.concatenate([dot_plain(value, weight[0]), dot_plain(value, weight[1])], axis=1)

    def product_back(grad, weight):
        half = grad.shape[1] // 2
        return dot_right_t(grad[:, :half], weight[0]) + dot_right_t(grad[:, half:], weight[1])

    def sum_twins(own, other):
        there = links.sibling(dot_left_t(*other).astype(bf16))
        return own, there

    def finish_twins(own, there):
        value = (dot_left_t(*own) + there.astype(f32)).astype(bf16)
        return value.reshape(16, value.shape[0] // 16, value.shape[1])

    def column_grad(value, grad):
        own, other = links.halves(grad)
        return sum_twins((value, own), (value, other))

    def weight_grad(value, grad_halves):
        return (
            dot_left_t(value, grad_halves[0]).astype(bf16),
            dot_left_t(value, grad_halves[1]).astype(bf16),
        )

    def relative_product(value, weight):
        return links.columns(dot_plain(value, weight[0]), dot_plain(value, weight[1]))

    def relative_back(grad_halves, weight):
        return dot_right_t(grad_halves[0], weight[0]) + dot_right_t(grad_halves[1], weight[1])

    def reorder(value):
        return dot_plain(value, order).astype(bf16)

    def restore(value):
        return dot_right_t(value.astype(bf16), order).astype(bf16)

    joined = jnp.concatenate(
        [latent.reshape(rows, width), skip_input.reshape(rows, width)], axis=1
    ).astype(f32)
    normed = gained_norm(joined, skip_gain_all).astype(bf16)
    upper_half = (me >= count // 2).astype(jnp.int32)
    near = jnp.where(upper_half == 0, normed[:, :width], normed[:, width:])
    away = jnp.where(upper_half == 0, normed[:, width:], normed[:, :width])
    near = dot_plain(near, order_skip).astype(bf16).reshape(rows, 2, 4, 1, -1)
    away = dot_plain(away, order_skip).astype(bf16).reshape(rows, 2, 4, 1, -1)
    normed = jnp.concatenate([near, away], axis=3).reshape(rows, 2, width)
    normed = (normed[:, 0], normed[:, 1])
    hidden = dot_plain(normed[0], w_skip[0]) + dot_plain(normed[1], w_skip[1])

    def shifted(values, gain, moved):
        wide = jnp.broadcast_to(moved[:, None, :], (batch, tokens, width)).reshape(rows, width)
        return layer_norm(values) * gain + wide

    attn_in = reorder(shifted(hidden, gains[0], shift).astype(bf16))
    qkv_proj = product(attn_in, w_qkv)
    query_block, key_block, value_block = ((qkv_proj, (at, width)) for at in range(3))

    def shaped(height, breadth, dtype):
        return jax.ShapeDtypeStruct((height, breadth), dtype)

    (keyval_here,) = plain_call(
        functools.partial(keys_body, batch, True),
        [shaped(rows, 2 * width, bf16)],
        [key_block, value_block, head_at, *tables],
    )
    keyval_there = links.sibling(keyval_here)
    qkv_proj = tie(qkv_proj, get_up)
    keyvals = [(keyval_here, None), (keyval_there, None)]
    attention_scratch = [pltpu.VMEM((rows, width), bf16), pltpu.VMEM((rows, width), f32)]
    attn_cat, self_peak = plain_call(
        functools.partial(attention_body, batch, False, True, 2, scaling),
        [shaped(rows, width, bf16), shaped(HEADS, 128, f32)],
        [query_block, head_at, *tables, *keyvals],
        attention_scratch,
    )
    attn_cat = reorder(attn_cat)
    attn_cat = tie(attn_cat, get_down)
    after_self = hidden + dot_plain(attn_cat, w_self_out)
    cross_in = reorder(gained_norm(after_self, gains[1]).astype(bf16))
    cq_proj = product(cross_in, w_query)

    text = text_encoder_states.reshape(batch * text_rows, text_width)
    text_ordered = dot_plain(text, order_text).astype(bf16)
    ckv_proj = product(text_ordered, w_keyval)
    (cross_keyval_all,) = plain_call(
        functools.partial(keys_body, batch, False),
        [shaped(batch * text_rows, 2 * width, bf16)],
        [(ckv_proj, (0, width)), (ckv_proj, (1, width)), head_at],
    )
    cq_proj = tie(cq_proj, get_up)
    cross_cat, cross_peak = plain_call(
        functools.partial(attention_body, batch, True, False, 1, scaling),
        [shaped(rows, width, bf16), shaped(HEADS, 128, f32)],
        [(cq_proj, None), head_at, (cross_keyval_all, None)],
        attention_scratch,
        text_lengths,
    )
    cross_cat = reorder(cross_cat)
    after_cross = after_self + dot_plain(cross_cat, w_cross_out)
    mlp_in = reorder(gained_norm(after_cross, gains[2]).astype(bf16))
    mlp_in = tie(mlp_in, get_up, get_down)
    (w_up,) = get_up.finish()
    upper = relative_product(mlp_in, w_up)
    activated = links.order_blocks(gelu_tanh(upper).astype(bf16))

    down_in = out_grad.reshape(rows, width)
    result_grad = down_in.astype(f32)
    down_halves = links.halves(down_in)
    put_down = Scatter(links, [weight_grad(activated, down_halves)])
    put_down.advance()
    activated = tie(activated, put_down)
    (w_down,) = get_down.finish()
    block_out = (after_cross + relative_product(activated, w_down)).astype(bf16)
    act_grad = links.restore_blocks(relative_back(down_halves, w_down))
    upper_grad = jax.vjp(gelu_tanh, upper)[1](act_grad)[0].astype(bf16)
    upper_halves = links.halves(upper_grad)
    put_up = Scatter(links, [weight_grad(mlp_in, upper_halves)])
    put_up.advance()
    mlp_in_grad = exact_restore(order, relative_back(upper_halves, w_up))
    cross_part, gain_third = jax.vjp(gained_norm, after_cross, gains[2])[1](mlp_in_grad)
    cross_grad = result_grad + cross_part
    cross_bf = tie(cross_grad.astype(bf16), put_up)
    cmix_grad = restore(dot_right_t(cross_bf, w_cross_out))
    cmix_grad = tie(cmix_grad, put_down)
    back_scratch = [
        pltpu.VMEM((rows, width), f32),
        pltpu.VMEM((rows, width), f32),
        pltpu.VMEM((rows, width), bf16),
        pltpu.VMEM((rows, width), f32),
        pltpu.VMEM((2, rows, 2 * width), f32),
    ]
    back_outs = [
        shaped(rows, width, bf16), shaped(rows, 2 * width, f32), shaped(rows, 2 * width, bf16)
    ]
    cq_grad, ckeyval_mine, ckeyval_theirs = plain_call(
        functools.partial(attention_back_body, batch, True, False, 1, scaling),
        back_outs,
        [(cq_proj, None), (cmix_grad, None), head_at, (cross_keyval_all, None)],
        back_scratch,
        text_lengths,
    )
    put_query = column_grad(cross_in, cq_grad)
    cq_grad = tie(cq_grad, put_up, put_down)
    cross_in_grad = exact_restore(order, product_back(cq_grad, w_query))
    self_part, gain_second = jax.vjp(gained_norm, after_self, gains[1])[1](cross_in_grad)
    self_grad = cross_grad + self_part

    text_half = text_rows // 2
    ckey_mine = lax.dynamic_slice_in_dim(
        ckv_proj.reshape(batch, text_rows, 2 * width)[:, :, :width], core * text_half, text_half, 1
    ).reshape(batch * text_half, width)
    (keyval_grad,) = plain_call(
        functools.partial(keys_back_body, batch, False),
        [shaped(batch * text_half, 2 * width, bf16)],
        [
            (ckey_mine, None),
            (ckeyval_mine, None),
            (links.sibling(ckeyval_theirs), None),
            head_at,
        ],
    )
    text_mine = lax.dynamic_slice_in_dim(
        text_ordered.reshape(batch, text_rows, text_width), core * text_half, text_half, 1
    ).reshape(-1, text_width)
    put_keyval = column_grad(text_mine, keyval_grad)
    grad_text = exact_restore(order_text, product_back(keyval_grad, w_keyval))
    grad_text = grad_text.reshape(batch, text_half, text_width)

    self_bf = self_grad.astype(bf16)
    put_pair = sum_twins(
        (links.pick(attn_cat, cross_cat), links.pick(self_bf, cross_bf)),
        (links.pick(cross_cat, attn_cat), links.pick(cross_bf, self_bf)),
    )
    self_bf = tie(self_bf, put_down)
    mix_grad = restore(dot_right_t(self_bf, w_self_out))
    mix_grad = tie(mix_grad, put_up)
    query_grad, here, there = plain_call(
        functools.partial(attention_back_body, batch, False, True, 2, scaling),
        back_outs,
        [query_block, (mix_grad, None), head_at, *tables, *keyvals],
        back_scratch,
    )
    here = tie(here, put_up)
    (key_value_grad,) = plain_call(
        functools.partial(keys_back_body, batch, True),
        [shaped(rows, 2 * width, bf16)],
        [key_block, (here, None), (links.sibling(there), None), head_at, *tables],
    )
    qkv_grad = jnp.concatenate([query_grad, key_value_grad], axis=1)
    put_qkv = column_grad(attn_in, qkv_grad)
    attn_in_grad = exact_restore(order, product_back(qkv_grad, w_qkv))
    hidden_part, gain_first, shift_grad = jax.vjp(shifted, hidden, gains[0], shift)[1](
        attn_in_grad
    )
    hidden_grad = self_grad + hidden_part
    hidden_bf = hidden_grad.astype(bf16)
    put_skip = sum_twins(
        (links.pick(*normed), hidden_bf), (links.pick(normed[1], normed[0]), hidden_bf)
    )
    normed_grad = jnp.concatenate(
        [dot_right_t(hidden_bf, w_skip[0]), dot_right_t(hidden_bf, w_skip[1])], axis=1
    ).reshape(rows, 2, 4, 2, -1)
    near_grad = exact_restore(order_skip, normed_grad[:, :, :, 0].reshape(rows, width))
    away_grad = exact_restore(order_skip, normed_grad[:, :, :, 1].reshape(rows, width))
    normed_grad = jnp.concatenate(
        [
            jnp.where(upper_half == 0, near_grad, away_grad),
            jnp.where(upper_half == 0, away_grad, near_grad),
        ],
        axis=1,
    )
    joined_grad, skip_gain_grad = jax.vjp(gained_norm, joined, skip_gain_all)[1](normed_grad)

    sums = [
        finish_twins(*put) for put in (put_pair, put_query, put_keyval, put_qkv, put_skip)
    ]
    (grad_down,) = put_down.finish()
    (grad_up,) = put_up.finish()
    scattered = [links.extra_scatter(part) for part in scatter(sums, links.quad, 4)]
    grad_self_out, grad_cross_out = scattered[0][0], scattered[0][1]
    grad_cross_query, grad_keyval, grad_qkv = (
        jnp.concatenate([part[0], part[1]], axis=1) for part in scattered[1:4]
    )
    grad_skip_linear = scattered[4].reshape(skip_linear.shape)

    gains_grad = jnp.stack([gain_first, gain_second, gain_third])
    gains_grad = gains_grad.reshape(3, count, third).transpose(1, 0, 2).reshape(count, 3 * third)
    gains_grad = jnp.concatenate([skip_gain_grad.reshape(count, gain_rows), gains_grad], axis=1)
    peaks = jnp.stack([self_peak[:, 0], cross_peak[:, 0]])
    cores = jnp.concatenate([shift_grad.reshape(-1), gains_grad.reshape(-1), peaks.reshape(-1)])
    there = links.sibling(cores)
    peaks = jnp.maximum(cores, there)[-2 * HEADS :]
    cores = cores + there
    ends = (batch * width, batch * width + count * cond_start)
    gains_grad = cores[ends[0] : ends[1]].reshape(count, cond_start)
    shift_bf = cores[: ends[0]].astype(bf16).astype(f32)
    shared = trade(lanes_of(jnp.concatenate([shift_bf, peaks]), 8), count, True, 5)
    shared = shared.reshape(count, -1)
    shift_all = shared[:, : ends[0]].reshape(count * batch, width).astype(bf16)
    peaks = jnp.max(shared[:, ends[0] : ends[0] + 2 * HEADS], axis=0).reshape(2, HEADS)
    grad_shift = dot_left_t(cond_cut, shift_all)
    cond_back = dot_right_t(shift_all, shift_linear).reshape(count, batch * shift_rows)
    owned = trade(lanes_of(jnp.concatenate([cond_back, gains_grad], axis=1), 8), count, False, 6)
    owned = owned.reshape(count, -1)
    cond_mine = owned[:, : batch * shift_rows].reshape(count, batch, shift_rows)
    cond_mine = cond_mine.transpose(1, 0, 2).reshape(batch, width)
    grad_cond = jax.vjp(jax.nn.silu, condition.astype(f32))[1](cond_mine)[0]
    own_gains = jnp.sum(owned[:, batch * shift_rows : batch * shift_rows + cond_start], axis=0)
    grad_skip_gain = own_gains[:gain_rows]
    grad_gains = own_gains[gain_rows:].reshape(3, third)

    roots = jnp.sqrt(thresholds / jnp.maximum(peaks, thresholds))
    self_cols = jnp.repeat(roots[0], HD)
    cross_cols = jnp.repeat(roots[1], HD)
    unit_cols = jnp.ones((width,), f32)
    clipped_qkv = (
        self_qkv.astype(f32) * jnp.concatenate([self_cols, self_cols, unit_cols])[None, :]
    ).astype(bf16)
    clipped_query = (cross_query.astype(f32) * cross_cols[None, :]).astype(bf16)
    clipped_keyval = (
        cross_keyval.astype(f32) * jnp.concatenate([cross_cols, unit_cols])[None, :]
    ).astype(bf16)
    return (
        block_out.reshape(batch, tokens, width),
        joined_grad[:, :width].reshape(batch, tokens, width),
        joined_grad[:, width:].reshape(batch, tokens, width),
        grad_cond,
        grad_text,
        grad_skip_gain,
        grad_gains,
        grad_skip_linear,
        grad_shift,
        grad_qkv,
        grad_self_out,
        grad_cross_query,
        grad_keyval,
        grad_cross_out,
        grad_up,
        grad_down,
        clipped_qkv,
        clipped_query,
        clipped_keyval,
        peaks,
    )


def local_sixteen(
    latent,
    skip_input,
    condition,
    text_encoder_states,
    text_lengths,
    out_grad,
    skip_gain,
    norm_gains,
    skip_linear,
    shift_linear,
    self_qkv,
    self_out,
    cross_query,
    cross_keyval,
    cross_out,
    mlp_up,
    mlp_down,
    thresholds,
):
    batch, tokens, width = latent.shape
    rows = batch * tokens
    text_rows = text_encoder_states.shape[1]
    text_width = text_encoder_states.shape[2]
    scaling = HD ** (-0.5)
    links = Links(lax.axis_size("fsdp"))
    me, core = links.me, links.core
    count = links.count

    positions = core * tokens + jnp.arange(tokens)
    feature = jnp.arange(HD)
    freqs = 10000.0 ** (-(feature % (HD // 4)).astype(f32) / (HD // 4))
    place = jnp.where(
        feature[None, :] < HD // 2, (positions // GRID_W)[:, None], (positions % GRID_W)[:, None]
    )
    angles = place.astype(f32) * freqs[None, :]
    former = (feature % (HD // 2) < HD // 4)[None, :]
    cosine = jnp.tile(jnp.cos(angles), (1, HEADS))
    sine = jnp.tile(jnp.where(former, -jnp.sin(angles), jnp.sin(angles)), (1, HEADS))
    former = jnp.tile(former, (1, HEADS))
    tables = [(cosine, None), (sine, None), (former.astype(f32), None)]
    head_at = jnp.arange(width)[:, None] // HD == jnp.arange(128)[None, :]
    head_at = (head_at.astype(bf16), None)

    gain_rows = skip_gain.shape[0]
    third = norm_gains.shape[1]
    cond_act = jax.nn.silu(condition.astype(f32)).astype(bf16)
    small = jnp.concatenate([skip_gain, norm_gains.reshape(-1), cond_act.reshape(-1)])
    small = trade(lanes_of(small, 16), count, True, 1).reshape(count, -1)
    skip_gain_all = small[:, :gain_rows].reshape(-1).astype(f32)
    cond_start = gain_rows + 3 * third
    gains = small[:, gain_rows:cond_start].reshape(count, 3, third)
    gains = gains.transpose(1, 0, 2).reshape(3, width).astype(f32)
    cond_all = small[:, cond_start : cond_start + batch * width].reshape(count * batch, width)
    shift_rows = shift_linear.shape[0]
    cond_cut = lax.dynamic_slice_in_dim(cond_all, me * shift_rows, shift_rows, 1)
    shift_parts = dot_plain(cond_cut, shift_linear).reshape(count, batch * width)
    shift_parts = trade(lanes_of(shift_parts, 8), count, False, 2)
    shift = jnp.sum(shift_parts.reshape(count, -1), axis=0)[: batch * width].reshape(batch, width)

    def halves_of(weight):
        cut = (weight.shape[1] // 2 + 127) // 128 * 128
        first, second = weight[:, :cut], weight[:, cut:]
        return first, jnp.pad(second, ((0, 0), (0, cut - second.shape[1])))

    def qkv_halves(value):
        edge = 2 * width + 768
        first = jnp.concatenate([value[:, :width], value[:, 2 * width : edge]], axis=1)
        rest = jnp.pad(value[:, edge:], ((0, 0), (0, 2 * 768 - width)))
        return first, jnp.concatenate([value[:, width : 2 * width], rest], axis=1)

    def qkv_whole(first, second):
        last = second[:, width : 2 * width - 768]
        return jnp.concatenate(
            [first[:, :width], second[:, :width], first[:, width:], last], axis=1
        )

    skip_half = skip_linear.shape[0] // 2
    shards = [
        links.pick(skip_linear[:skip_half], skip_linear[skip_half:]),
        links.pick(*qkv_halves(self_qkv)),
        links.pick(self_out, cross_out),
        links.pick(*halves_of(cross_query)),
        links.pick(*halves_of(cross_keyval)),
        links.pick(*halves_of(mlp_up)),
        links.pick(*halves_of(mlp_down)),
    ]
    block = width // 16

    def one_hot(starts, size, height):
        wanted = (starts[:, None] + jnp.arange(size, dtype=jnp.int32)).reshape(1, -1)
        rows_at = lax.broadcasted_iota(jnp.int32, (height, wanted.shape[1]), 0)
        return (rows_at == wanted).astype(bf16)

    slots = jnp.arange(16, dtype=jnp.int32)
    order = one_hot(jnp.bitwise_xor(me, slots) * block, block, width)
    text_block = text_width // 16
    order_text = one_hot(jnp.bitwise_xor(me, slots) * text_block, text_block, text_width)
    lower = jnp.bitwise_xor(jnp.bitwise_and(me, 7), slots[:8]) * (2 * block)
    order_skip = jnp.stack([one_hot(lower + at * block, block, width) for at in range(2)])
    text = text_encoder_states.reshape(batch * text_rows, text_width)
    text_ordered = dot_plain(text, order_text).astype(bf16)
    valid = (jnp.arange(text_rows)[None, :] < text_lengths[:, None]).astype(f32)
    head_at = (jnp.arange(width)[:, None] // HD == jnp.arange(128)[None, :]).astype(bf16)
    table_arrays = [table for table, _ in tables]

    def shaped(*shape, dtype=f32):
        return jax.ShapeDtypeStruct(shape, dtype)

    down_in = out_grad.reshape(rows, width)
    cut = shards[6].shape[1]
    out_halves = jnp.stack(
        [down_in[:, :cut], jnp.pad(down_in[:, cut:], ((0, 0), (0, 2 * cut - width)))]
    )
    up_shape, down_shape = shards[5].shape, shards[6].shape
    whole_down, whole_up = [shaped(4, 4, *shape, dtype=bf16) for shape in (down_shape, up_shape)]
    tile = 384

    flat, flat_low = shaped(rows, width), shaped(rows, width, dtype=bf16)
    double_low = shaped(rows, 2 * width, dtype=bf16)
    inner = mlp_down.shape[0] * 16
    given = [
        latent.reshape(rows, width),
        skip_input.reshape(rows, width),
        skip_gain_all[None, :],
        gains,
        shift,
        out_halves,
        valid,
    ]
    loaded = [order, order_skip, head_at, *table_arrays, text_ordered]

    def like(array):
        return pltpu.VMEM(array.shape, array.dtype)
    saved = [
        shaped(2, 2, rows, width // 2, dtype=bf16),
        flat,
        flat_low,
        shaped(rows, 2 * width),
        double_low,
        double_low,
        flat_low,
        flat,
        flat_low,
        flat,
        flat,
        shaped(batch * text_rows, 2 * width, dtype=bf16),
        flat_low,
        flat,
        flat_low,
        shaped(rows, inner),
        shaped(rows, inner, dtype=bf16),
        shaped(HEADS, 128),
        shaped(HEADS, 128),
    ]
    (
        *gathered,
        normed,
        hidden,
        attn_in,
        qkv_proj,
        keyval_here,
        keyval_there,
        attn_cat,
        after_self,
        cross_in,
        cq_proj,
        ckey_mine,
        cross_keyval_all,
        cross_cat,
        after_cross,
        mlp_in,
        upper,
        activated,
        self_peak,
        cross_peak,
        sums_down,
        _,
    ) = pl.pallas_call(
        functools.partial(forward_body, batch, scaling),
        out_shape=[
            *[shaped(2, 4, 4, *shard.shape, dtype=bf16) for shard in shards],
            *saved,
            whole_down,
            whole_down,
        ],
        in_specs=[IN_VMEM] * len(given) + [ANYWHERE] * 14,
        out_specs=[ANYWHERE] * (9 + len(saved)),
        scratch_shapes=[
            *[like(array) for array in saved],
            *[like(array) for array in loaded],
            pltpu.VMEM((rows, width), f32),
            pltpu.VMEM((rows, width), bf16),
            pltpu.VMEM((3, 4, 4, block, 512), bf16),
            pltpu.VMEM((2, *down_shape), bf16),
            pltpu.VMEM((2, *down_shape), bf16),
            pltpu.SemaphoreType.DMA((3,)),
            pltpu.SemaphoreType.DMA((8, 10)),
            pltpu.SemaphoreType.DMA((8, 10)),
            pltpu.SemaphoreType.DMA((8,)),
            pltpu.SemaphoreType.DMA,
            pltpu.SemaphoreType.DMA,
            pltpu.SemaphoreType.DMA((1, 16)),
            pltpu.SemaphoreType.DMA((1, 16)),
            pltpu.SemaphoreType.DMA((4,)),
            pltpu.SemaphoreType.DMA((7,)),
            pltpu.SemaphoreType.DMA((19,)),
        ],
        compiler_params=pltpu.CompilerParams(
            collective_id=7, has_side_effects=True, vmem_limit_bytes=62 * 2**20
        ),
    )(*given, *loaded, *shards)
    block_out, cross_grad, gain_third, sums_up, _, half_down = pl.pallas_call(
        functools.partial(mlp_back_body, batch),
        out_shape=[
            flat_low, flat, shaped(8, width), whole_up, whole_up,
            shaped(2, 4, *down_shape, dtype=bf16),
        ],
        in_specs=[IN_VMEM] * 7 + [ANYWHERE] * 3,
        out_specs=[IN_VMEM] * 3 + [ANYWHERE] * 3,
        scratch_shapes=[
            pltpu.VMEM((2, rows, inner // 2), bf16),
            pltpu.VMEM((width, rows), bf16),
            pltpu.VMEM((2, rows, cut), f32),
            pltpu.VMEM((3, 2, *down_shape), bf16),
            pltpu.VMEM((3, 4, 4, block, 512), bf16),
            pltpu.VMEM((2, 4, 4, block, tile), bf16),
            pltpu.VMEM((2, 4, 4, block, tile), bf16),
            pltpu.SemaphoreType.DMA((3,)),
            pltpu.SemaphoreType.DMA((1, 16)),
            pltpu.SemaphoreType.DMA((1, 16)),
            pltpu.SemaphoreType.DMA((4,)),
            pltpu.SemaphoreType.DMA((1, 8)),
            pltpu.SemaphoreType.DMA((1, 8)),
        ],
        compiler_params=pltpu.CompilerParams(
            collective_id=8, has_side_effects=True, vmem_limit_bytes=60 * 2**20
        ),
    )(
        out_halves, activated, upper, mlp_in, after_cross, order, gains,
        gathered[5], gathered[6], sums_down,
    )

    text_half = text_rows // 2
    text_mine = lax.dynamic_slice_in_dim(
        text_ordered.reshape(batch, text_rows, text_width), core * text_half, text_half, 1
    ).reshape(-1, text_width)
    parts = [shards[at].shape for at in (6, 5, 3, 4, 2, 1, 0)]
    moved = [
        *[shaped(2, *shape) for shape in parts],
        *[shaped(4, 4, *shape, dtype=bf16) for shape in parts[2:]],
        *[shaped(4, 4, *shape, dtype=bf16) for shape in parts[2:]],
        *[shaped(2, 4, *shape, dtype=bf16) for shape in parts[1:]],
        *[shaped(4, *shape, dtype=bf16) for shape in parts],
        *[shaped(4, *shape, dtype=bf16) for shape in parts],
        *[shaped(3, *shape, dtype=bf16) for shape in parts],
        *[shaped(3, *shape, dtype=bf16) for shape in parts],
    ]
    placed = [gains, valid]
    loaded = [
        cross_cat, attn_cat, cross_in, attn_in, text_mine, after_self, hidden, normed,
        order, head_at, *table_arrays,
    ]
    apart = [
        *loaded,
        *gathered[:5],
        cross_keyval_all, cq_proj, ckey_mine, qkv_proj, keyval_here, keyval_there, cross_grad,
        sums_down, sums_up, half_down,
    ]
    small_outs = [shaped(rows, text_width), shaped(8, width), shaped(8, width)]
    text_grad, gain_grads, shift_grad, normed_grad, *rest = pl.pallas_call(
        functools.partial(rest_back_body, batch, scaling),
        out_shape=[*small_outs, shaped(rows, 2 * width), *moved],
        in_specs=[IN_VMEM] * len(placed) + [ANYWHERE] * len(apart),
        out_specs=[IN_VMEM] * 3 + [ANYWHERE] * (1 + len(moved)),
        scratch_shapes=[
            *[pltpu.VMEM((rows, width), f32)] * 4,
            pltpu.VMEM((rows, width), bf16),
            pltpu.VMEM((rows, width), bf16),
            pltpu.VMEM((2, rows, 2 * width), f32),
            pltpu.VMEM((2 * rows, 2 * width), bf16),
            pltpu.VMEM((rows, 2 * width), f32),
            pltpu.VMEM((2, width, rows), bf16),
            pltpu.VMEM((2, rows, shards[1].shape[1]), bf16),
            *[like(array) for array in loaded],
            pltpu.VMEM((3, 4, 4, block, tile), bf16),
            pltpu.VMEM((2, 4, 4, block, tile), bf16),
            pltpu.VMEM((2, 4, 4, block, tile), bf16),
            pltpu.VMEM((2, 9, block, 768), bf16),
            pltpu.VMEM((2, 9, down_shape[0], 128), bf16),
            pltpu.VMEM((2, block, 768), f32),
            pltpu.VMEM((2, down_shape[0], 128), f32),
            pltpu.VMEM((2, rows, 2 * width), bf16),
            pltpu.SemaphoreType.DMA((3,)),
            pltpu.SemaphoreType.DMA((17,)),
            pltpu.SemaphoreType.DMA((5, 8)),
            pltpu.SemaphoreType.DMA((5, 8)),
            pltpu.SemaphoreType.DMA((4,)),
            pltpu.SemaphoreType.DMA((2,)),
            pltpu.SemaphoreType.DMA((2,)),
            pltpu.SemaphoreType.DMA((7, 12)),
            pltpu.SemaphoreType.DMA((7, 12)),
            pltpu.SemaphoreType.DMA((2, 9)),
            pltpu.SemaphoreType.DMA((2, 4)),
        ],
        compiler_params=pltpu.CompilerParams(
            collective_id=9, has_side_effects=True, vmem_limit_bytes=62 * 2**20
        ),
    )(*placed, *apart)
    grads = rest[:7]
    joined_grad, skip_gain_grad = pl.pallas_call(
        functools.partial(joined_back_body, batch),
        out_shape=[shaped(2, rows, width), shaped(8, 2 * width)],
        in_specs=[IN_VMEM] * 5,
        out_specs=[IN_VMEM] * 2,
        compiler_params=pltpu.CompilerParams(vmem_limit_bytes=60 * 2**20),
    )(normed_grad, latent.reshape(rows, width), skip_input.reshape(rows, width), skip_gain_all[None, :], order_skip)
    skip_gain_grad = skip_gain_grad[0]
    gain_first, gain_second, gain_third = gain_grads[0], gain_grads[1], gain_third[0]
    shift_grad = shift_grad[:batch]
    grad_text = restore_order(order_text, text_grad).reshape(batch, text_half, text_width)

    def wide_of(part):
        return jnp.concatenate([part[0], part[1]], axis=1)

    grad_down = wide_of(grads[0])[:, :width]
    grad_up = wide_of(grads[1])
    grad_cross_query = wide_of(grads[2])[:, :width]
    grad_keyval = wide_of(grads[3])
    grad_self_out, grad_cross_out = grads[4][0], grads[4][1]
    grad_qkv = qkv_whole(grads[5][0], grads[5][1])
    grad_skip_linear = grads[6].reshape(skip_linear.shape)

    gains_grad = jnp.stack([gain_first, gain_second, gain_third])
    gains_grad = gains_grad.reshape(3, count, third).transpose(1, 0, 2).reshape(count, 3 * third)
    gains_grad = jnp.concatenate([skip_gain_grad.reshape(count, gain_rows), gains_grad], axis=1)
    peaks = jnp.stack([self_peak[:, 0], cross_peak[:, 0]])
    cores = jnp.concatenate([shift_grad.reshape(-1), gains_grad.reshape(-1), peaks.reshape(-1)])
    there = links.sibling(cores)
    peaks = jnp.maximum(cores, there)[-2 * HEADS :]
    cores = cores + there
    ends = (batch * width, batch * width + count * cond_start)
    gains_grad = cores[ends[0] : ends[1]].reshape(count, cond_start)
    shift_bf = cores[: ends[0]].astype(bf16).astype(f32)
    shared = trade(lanes_of(jnp.concatenate([shift_bf, peaks]), 8), count, True, 5)
    shared = shared.reshape(count, -1)
    shift_all = shared[:, : ends[0]].reshape(count * batch, width).astype(bf16)
    peaks = jnp.max(shared[:, ends[0] : ends[0] + 2 * HEADS], axis=0).reshape(2, HEADS)
    grad_shift = dot_left_t(cond_cut, shift_all)
    cond_back = dot_right_t(shift_all, shift_linear).reshape(count, batch * shift_rows)
    owned = trade(lanes_of(jnp.concatenate([cond_back, gains_grad], axis=1), 8), count, False, 6)
    owned = owned.reshape(count, -1)
    cond_mine = owned[:, : batch * shift_rows].reshape(count, batch, shift_rows)
    cond_mine = cond_mine.transpose(1, 0, 2).reshape(batch, width)
    grad_cond = jax.vjp(jax.nn.silu, condition.astype(f32))[1](cond_mine)[0]
    own_gains = jnp.sum(owned[:, batch * shift_rows : batch * shift_rows + cond_start], axis=0)
    grad_skip_gain = own_gains[:gain_rows]
    grad_gains = own_gains[gain_rows:].reshape(3, third)

    roots = jnp.sqrt(thresholds / jnp.maximum(peaks, thresholds))
    self_cols = jnp.repeat(roots[0], HD)
    cross_cols = jnp.repeat(roots[1], HD)
    unit_cols = jnp.ones((width,), f32)
    clipped_qkv = (
        self_qkv.astype(f32) * jnp.concatenate([self_cols, self_cols, unit_cols])[None, :]
    ).astype(bf16)
    clipped_query = (cross_query.astype(f32) * cross_cols[None, :]).astype(bf16)
    clipped_keyval = (
        cross_keyval.astype(f32) * jnp.concatenate([cross_cols, unit_cols])[None, :]
    ).astype(bf16)
    return (
        block_out.reshape(batch, tokens, width),
        joined_grad[0].reshape(batch, tokens, width),
        joined_grad[1].reshape(batch, tokens, width),
        grad_cond,
        grad_text,
        grad_skip_gain,
        grad_gains,
        grad_skip_linear,
        grad_shift,
        grad_qkv,
        grad_self_out,
        grad_cross_query,
        grad_keyval,
        grad_cross_out,
        grad_up,
        grad_down,
        clipped_qkv,
        clipped_query,
        clipped_keyval,
        peaks,
    )


def solution(mesh):
    rows = P("fsdp", None)
    tokens = P("fsdp", "seq", None)
    in_specs = (
        tokens,
        tokens,
        rows,
        P("fsdp", None, None),
        P("fsdp"),
        tokens,
        P("fsdp"),
        P(None, "fsdp"),
        *([rows] * 9),
        P(),
    )
    out_specs = (
        *([tokens] * 3),
        rows,
        tokens,
        P("fsdp"),
        P(None, "fsdp"),
        *([rows] * 12),
        P(),
    )
    step = local_sixteen if mesh.shape["fsdp"] == 16 else local
    return jax.shard_map(step, mesh=mesh, in_specs=in_specs, out_specs=out_specs, check_vma=False)
```

```python
import functools

import jax
import jax.numpy as jnp
from jax import lax
from jax.experimental import pallas as pl
from jax.experimental.pallas import tpu as pltpu
from jax.sharding import PartitionSpec as P

HEADS = 16
HD = 88
GRID_W = 32

norm_eps = 1e-06
masked_value = -1e30
bf16 = jnp.bfloat16
f32 = jnp.float32
MESH = pl.DeviceIdType.MESH
ANYWHERE = pl.BlockSpec(memory_space=pl.ANY)
IN_VMEM = pl.BlockSpec(memory_space=pltpu.VMEM)


def layer_norm(values):
    center = values - jnp.mean(values, axis=-1, keepdims=True)
    spread = jnp.mean(center * center, axis=-1, keepdims=True)
    return center * lax.rsqrt(spread + norm_eps)


def gained_norm(values, gain):
    return layer_norm(values) * gain


def gelu_tanh(values):
    return jax.nn.gelu(values, approximate=True)


def dot_plain(left, right):
    return jnp.dot(left, right, preferred_element_type=f32)


def dot_left_t(left, right):
    return lax.dot_general(
        left, right, (((0,), (0,)), ((), ())), preferred_element_type=f32
    )


def dot_right_t(left, right):
    return lax.dot_general(
        left, right, (((1,), (1,)), ((), ())), preferred_element_type=f32
    )


def softmax_back(probs, prob_grad):
    return probs * (prob_grad - jnp.sum(prob_grad * probs, axis=-1, keepdims=True))


def greet(peers):
    barrier = pltpu.get_barrier_semaphore()
    for peer in peers:
        pl.semaphore_signal(barrier, inc=1, device_id=peer, device_id_type=MESH)
    pl.semaphore_wait(barrier, len(peers))


def trade_body(count, same, source, out, send, recv, local):
    me = lax.axis_index("fsdp")
    core = lax.axis_index("seq")
    greet([(jnp.bitwise_xor(me, j), core) for j in range(1, count)])

    def part(index):
        return source if same else source.at[index]

    def copy(j):
        peer = jnp.bitwise_xor(me, j)
        return pltpu.make_async_remote_copy(
            src_ref=part(peer),
            dst_ref=out.at[me],
            send_sem=send.at[j],
            recv_sem=recv.at[j],
            device_id=(peer, core),
            device_id_type=MESH,
        )

    for j in range(1, count):
        copy(j).start()
    here = pltpu.make_async_copy(part(me), out.at[me], local.at[0])
    here.start()
    here.wait()
    for j in range(1, count):
        copy(j).wait_send()
        copy(j).wait_recv()


def trade(value, count, same, identity):
    shape = value.shape if same else value.shape[1:]
    return pl.pallas_call(
        functools.partial(trade_body, count, same),
        out_shape=jax.ShapeDtypeStruct((count, *shape), value.dtype),
        in_specs=[IN_VMEM],
        out_specs=IN_VMEM,
        scratch_shapes=[
            pltpu.SemaphoreType.DMA((count,)),
            pltpu.SemaphoreType.DMA((count,)),
            pltpu.SemaphoreType.DMA((1,)),
        ],
        compiler_params=pltpu.CompilerParams(collective_id=identity, has_side_effects=True),
    )(value)


def neighbours(quad):
    me = lax.axis_index("fsdp")
    core = lax.axis_index("seq")
    first, second = 1 + core, 2 - core

    def at(mask):
        return (jnp.bitwise_xor(me, mask), core)

    return core, first, second, at, (me, 1 - core)


def gather_body(count, quad, *refs):
    mine, out = refs[:count], refs[count : 2 * count]
    send, recv, local = refs[2 * count :]
    core, first_mask, second_mask, at, sibling = neighbours(quad)
    far_peers = [at(k * quad) for k in range(1, 4)]
    greet([*far_peers, at(first_mask), at(second_mask), sibling])

    def copy(w, slot, source, target, peer):
        return pltpu.make_async_remote_copy(
            src_ref=source,
            dst_ref=target,
            send_sem=send.at[w, slot],
            recv_sem=recv.at[w, slot],
            device_id=peer,
            device_id_type=MESH,
        )

    def block(w, q):
        return out[w].at[core, pl.ds(4 * q, 4)]

    def far(w, k):
        return copy(w, k - 1, mine[w], out[w].at[core, k], far_peers[k - 1])

    def keep(w):
        return pltpu.make_async_copy(mine[w], out[w].at[core, 0], local.at[w])

    def first(w):
        return copy(w, 3, block(w, 0), block(w, first_mask), at(first_mask))

    def second(w):
        return copy(w, 4, block(w, 0), block(w, second_mask), at(second_mask))

    def both(w):
        return copy(w, 5, block(w, first_mask), block(w, 3), at(second_mask))

    def twin(w, n):
        q = (0, first_mask, second_mask, 3)[n]
        return copy(w, 6 + n, block(w, q), block(w, q), sibling)

    for w in range(count):
        keep(w).start()
        for k in range(1, 4):
            far(w, k).start()
    for step in range(count + 2):
        w = step
        if w < count:
            keep(w).wait()
            for k in range(1, 4):
                far(w, k).wait_recv()
            first(w).start()
            second(w).start()
            twin(w, 0).start()
        w = step - 1
        if 0 <= w < count:
            first(w).wait_recv()
            both(w).start()
            twin(w, 1).start()
            second(w).wait_recv()
            twin(w, 2).start()
        w = step - 2
        if 0 <= w < count:
            both(w).wait_recv()
            twin(w, 3).start()
    for w in range(count):
        for k in range(1, 4):
            far(w, k).wait_send()
        first(w).wait_send()
        second(w).wait_send()
        both(w).wait_send()
        for n in range(4):
            twin(w, n).wait_send()
            twin(w, n).wait_recv()


def gather(shards, quad, identity):
    count = len(shards)
    return pl.pallas_call(
        functools.partial(gather_body, count, quad),
        out_shape=[jax.ShapeDtypeStruct((2, 16, *s.shape), bf16) for s in shards],
        in_specs=[ANYWHERE] * count,
        out_specs=[ANYWHERE] * count,
        scratch_shapes=[
            pltpu.SemaphoreType.DMA((count, 10)),
            pltpu.SemaphoreType.DMA((count, 10)),
            pltpu.SemaphoreType.DMA((count,)),
        ],
        compiler_params=pltpu.CompilerParams(collective_id=identity, has_side_effects=True),
    )(*shards)


def scatter_body(count, quad, *refs):
    source, out = refs[:count], refs[count : 2 * count]
    kept, half, quarter, last, total = (
        refs[(2 + n) * count : (3 + n) * count] for n in range(5)
    )
    send, recv, local = refs[7 * count :]
    core, first_mask, second_mask, at, sibling = neighbours(quad)
    far_peers = [at(k * quad) for k in range(1, 4)]
    greet([*far_peers, at(first_mask), at(second_mask), sibling])

    def copy(w, slot, origin, target, peer):
        return pltpu.make_async_remote_copy(
            src_ref=origin,
            dst_ref=target,
            send_sem=send.at[w, slot],
            recv_sem=recv.at[w, slot],
            device_id=peer,
            device_id_type=MESH,
        )

    def block(w, q):
        if len(source[w].shape) == 4:
            return source[w].at[:, q]
        return source[w].at[pl.ds(4 * q, 4)]

    def give(w, n):
        q = 3 if n == 0 else second_mask
        return copy(w, n, block(w, q), half[w].at[n], at(second_mask))

    def load(w, n):
        q = first_mask if n == 0 else 0
        return pltpu.make_async_copy(block(w, q), kept[w].at[n], local.at[w, n])

    def pass_on(w):
        return copy(w, 2, half[w].at[0], quarter[w], at(first_mask))

    def far(w, k):
        return copy(w, 2 + k, half[w].at[1, k], last[w].at[k - 1], far_peers[k - 1])

    def twin(w):
        return copy(w, 6, total[w], out[w].at[core], sibling)

    def store(w):
        return pltpu.make_async_copy(total[w], out[w].at[core], local.at[w, 2])

    def lanes(w, body):
        width = total[w].shape[1]
        step = 256 if width % 256 == 0 else 128 if width % 128 == 0 else width
        if step == width:
            body(slice(None))
        else:

            @pl.loop(0, width // step)
            def _(i):
                body(pl.ds(pl.multiple_of(i * step, step), step))

    for w in range(count):
        for n in range(2):
            give(w, n).start()
            load(w, n).start()
    for step in range(count + 2):
        w = step
        if w < count:
            give(w, 0).wait_recv()
            load(w, 0).wait()

            def body(c):
                for k in range(4):
                    half[w][0, k, :, c] = (
                        half[w][0, k, :, c].astype(f32) + kept[w][0, k, :, c].astype(f32)
                    ).astype(bf16)

            lanes(w, body)
            pass_on(w).start()
        w = step - 1
        if 0 <= w < count:
            give(w, 1).wait_recv()
            load(w, 1).wait()
            pass_on(w).wait_recv()

            def body(c):
                for k in range(4):
                    value = half[w][1, k, :, c].astype(f32) + kept[w][1, k, :, c].astype(f32)
                    value = value + quarter[w][k, :, c].astype(f32)
                    if k == 0:
                        total[w][:, c] = value
                    else:
                        half[w][1, k, :, c] = value.astype(bf16)

            lanes(w, body)
            for k in range(1, 4):
                far(w, k).start()
        w = step - 2
        if 0 <= w < count:
            for k in range(1, 4):
                far(w, k).wait_recv()

            def body(c):
                value = total[w][:, c]
                for k in range(3):
                    value = value + last[w][k, :, c].astype(f32)
                total[w][:, c] = value

            lanes(w, body)
            twin(w).start()
            store(w).start()
    for w in range(count):
        give(w, 0).wait_send()
        give(w, 1).wait_send()
        pass_on(w).wait_send()
        for k in range(1, 4):
            far(w, k).wait_send()
        twin(w).wait_send()
        twin(w).wait_recv()
        store(w).wait()


def scatter(sums, quad, identity):
    count = len(sums)
    shapes = [s.shape[-2:] for s in sums]

    def buffers(*lead):
        return [pltpu.VMEM((*lead, *s), bf16) for s in shapes]

    return pl.pallas_call(
        functools.partial(scatter_body, count, quad),
        out_shape=[jax.ShapeDtypeStruct((2, *s), f32) for s in shapes],
        in_specs=[ANYWHERE] * count,
        out_specs=[ANYWHERE] * count,
        scratch_shapes=[
            *buffers(2, 4),
            *buffers(2, 4),
            *buffers(4),
            *buffers(3),
            *[pltpu.VMEM(s, f32) for s in shapes],
            pltpu.SemaphoreType.DMA((count, 7)),
            pltpu.SemaphoreType.DMA((count, 7)),
            pltpu.SemaphoreType.DMA((count, 3)),
        ],
        compiler_params=pltpu.CompilerParams(
            collective_id=identity, has_side_effects=True, vmem_limit_bytes=56 * 2**20
        ),
    )(*sums)


def gelu_parts(value):
    inner = 0.7978845608028654 * (value + 0.044715 * value * value * value)
    return jnp.tanh(inner)


def gelu_of(value):
    return 0.5 * value * (1.0 + gelu_parts(value))


class GatherPlan:
    def __init__(self, pieces, send, recv, local):
        self.pieces = pieces
        self.send, self.recv, self.local = send, recv, local
        self.core, self.first_mask, self.second_mask, self.at, self.sibling = neighbours(4)
        self.far_peers = [self.at(4 * k) for k in range(1, 4)]

    def peers(self):
        return [*self.far_peers, self.at(self.first_mask), self.at(self.second_mask), self.sibling]

    def copy(self, w, slot, source, target, peer):
        return pltpu.make_async_remote_copy(
            src_ref=source,
            dst_ref=target,
            send_sem=self.send.at[w, slot],
            recv_sem=self.recv.at[w, slot],
            device_id=peer,
            device_id_type=MESH,
        )

    def mine(self, w):
        shard, _, lanes = self.pieces[w]
        return shard.at[:, lanes]

    def block(self, w, q):
        _, out, lanes = self.pieces[w]
        return out.at[self.core, :, q, :, lanes]

    def plane(self, w, k, q):
        _, out, lanes = self.pieces[w]
        return out.at[self.core, k, q, :, lanes]

    def layer(self, w, k):
        _, out, lanes = self.pieces[w]
        return out.at[self.core, k, :, :, lanes]

    def far(self, w, k):
        return self.copy(w, k - 1, self.mine(w), self.plane(w, k, 0), self.far_peers[k - 1])

    def keep(self, w):
        return pltpu.make_async_copy(self.mine(w), self.plane(w, 0, 0), self.local.at[w])

    def first(self, w):
        mask = self.first_mask
        return self.copy(w, 3, self.block(w, 0), self.block(w, mask), self.at(mask))

    def second(self, w):
        mask = self.second_mask
        return self.copy(w, 4, self.block(w, 0), self.block(w, mask), self.at(mask))

    def both(self, w):
        return self.copy(
            w, 5, self.block(w, self.first_mask), self.block(w, 3), self.at(self.second_mask)
        )

    def twin(self, w, n):
        q = (0, self.first_mask, self.second_mask, 3)[n]
        return self.copy(w, 6 + n, self.block(w, q), self.block(w, q), self.sibling)


    def low_first(self, w):
        mask = self.first_mask
        return self.copy(w, 3, self.mine(w), self.plane(w, 0, mask), self.at(mask))

    def low_second(self, w):
        mask = self.second_mask
        return self.copy(w, 4, self.mine(w), self.plane(w, 0, mask), self.at(mask))

    def low_both(self, w):
        mask = self.second_mask
        return self.copy(
            w, 5, self.plane(w, 0, self.first_mask), self.plane(w, 0, 3), self.at(mask)
        )

    def low_far(self, w, k):
        return self.copy(w, k - 1, self.layer(w, 0), self.layer(w, k), self.far_peers[k - 1])

    def low_twin(self, w, k):
        return self.copy(w, 6 + k, self.layer(w, k), self.layer(w, k), self.sibling)

    def low_begin(self, w):
        self.keep(w).start()
        self.low_first(w).start()
        self.low_second(w).start()

    def low_cross(self, w):
        self.low_first(w).wait_recv()
        self.low_both(w).start()
        self.low_second(w).wait_recv()

    def low_spread(self, w):
        self.keep(w).wait()
        self.low_both(w).wait_recv()
        for k in range(1, 4):
            self.low_far(w, k).start()
        self.low_twin(w, 0).start()

    def low_close(self, w):
        for k in range(1, 4):
            self.low_far(w, k).wait_recv()
            self.low_twin(w, k).start()

    def low_finish(self, w):
        self.low_first(w).wait_send()
        self.low_second(w).wait_send()
        self.low_both(w).wait_send()
        for k in range(1, 4):
            self.low_far(w, k).wait_send()
        for k in range(4):
            self.low_twin(w, k).wait_send()

    def low_ready(self, w):
        for k in range(4):
            self.low_twin(w, k).wait_recv()

    def begin(self, w):
        self.keep(w).start()
        for k in range(1, 4):
            self.far(w, k).start()

    def spread(self, w):
        self.keep(w).wait()
        for k in range(1, 4):
            self.far(w, k).wait_recv()
        self.first(w).start()
        self.second(w).start()
        self.twin(w, 0).start()

    def cross(self, w):
        self.first(w).wait_recv()
        self.both(w).start()
        self.twin(w, 1).start()
        self.second(w).wait_recv()
        self.twin(w, 2).start()

    def close(self, w):
        self.both(w).wait_recv()
        self.twin(w, 3).start()

    def ready(self, w):
        for n in range(4):
            self.twin(w, n).wait_recv()

    def finish(self, w):
        for k in range(1, 4):
            self.far(w, k).wait_send()
        self.first(w).wait_send()
        self.second(w).wait_send()
        self.both(w).wait_send()
        for n in range(4):
            self.twin(w, n).wait_send()


def stream(weight, tiles, buffer, semaphore, body):
    depth = buffer.shape[0]
    height = weight.shape[3]

    def copy(index):
        half, start, size = tiles[index]
        slot = index % depth
        return pltpu.make_async_copy(
            weight.at[half, :, :, :, pl.ds(start, size)],
            buffer.at[slot, :, :, pl.ds(0, height), pl.ds(0, size)],
            semaphore.at[slot],
        )

    for index in range(min(depth - 1, len(tiles))):
        copy(index).start()
    for index, (_, _, size) in enumerate(tiles):
        if index + depth - 1 < len(tiles):
            copy(index + depth - 1).start()
        copy(index).wait()
        body(index, buffer[index % depth, :, :, :height, :size].reshape(16 * height, size))


def tiles_of(width, size, halves=(0, 1)):
    return [
        (half, start, min(size, width - start)) for half in halves for start in range(0, width, size)
    ]


def forward_body(batch, scaling, *refs):
    refs = list(refs)
    take = refs.pop
    latent, skip, skip_gain, gains, shift, out_grad, valid = (take(0) for _ in range(7))
    loaded = [take(0) for _ in range(7)]
    mine = [take(0) for _ in range(7)]
    out = [take(0) for _ in range(7)]
    saved_out = [take(0) for _ in range(19)]
    sums_down, there_down = take(0), take(0)
    saved = [take(0) for _ in range(19)]
    order, order_skip, heads_ref, *tables, text = placed = [take(0) for _ in range(7)]
    wide, narrow, buffer, out_down, in_down, semaphore, send, recv, local = (
        take(0) for _ in range(9)
    )
    twin_send, twin_recv, sum_send, sum_recv, sum_local, load_sem, save_sem = refs
    normed, hidden, attn_in, qkv, keyval_here, keyval_there = saved[:6]
    attn_cat, after_self, cross_in, cq_proj, ckey_mine, cross_keyval = saved[6:12]
    cross_cat, after_cross, mlp_in, upper, activated, self_peak, cross_peak = saved[12:]
    rows, width = hidden.shape
    size = rows // batch
    me = lax.axis_index("fsdp")
    core = lax.axis_index("seq")
    pieces = [(mine[w], out[w], pl.ds(0, mine[w].shape[1])) for w in range(6)]
    cut = mine[6].shape[1] // 2
    pieces += [(mine[6], out[6], pl.ds(at * cut, cut)) for at in range(2)]
    plan = GatherPlan(pieces, send, recv, local)
    skip_w, qkv_w, pair_w, query_w, keyval_w, up_w, down_w, last_w = range(8)

    greet(plan.peers())
    plan.low_begin(last_w)
    plan.begin(skip_w)
    plan.begin(qkv_w)
    loads = [
        pltpu.make_async_copy(source, target, load_sem.at[at])
        for at, (source, target) in enumerate(zip(loaded, placed))
    ]
    saves = [
        pltpu.make_async_copy(source, target, save_sem.at[at])
        for at, (source, target) in enumerate(zip(saved, saved_out))
    ]
    for copy in loads:
        copy.start()
    for copy in loads:
        copy.wait()

    def save(*places):
        for at in places:
            saves[at].start()

    def each(body):
        for b in range(batch):
            body(b, pl.ds(b * size, size))

    def reorder(value):
        return dot_plain(value, order[...]).astype(bf16)

    upper_half = me >= 8

    def normed_part(b, rows_b):
        left = latent[rows_b, :].astype(f32)
        right = skip[rows_b, :].astype(f32)
        mean = (
            jnp.sum(left, axis=1, keepdims=True) + jnp.sum(right, axis=1, keepdims=True)
        ) / (2 * width)
        left, right = left - mean, right - mean
        spread = (
            jnp.sum(left * left, axis=1, keepdims=True)
            + jnp.sum(right * right, axis=1, keepdims=True)
        ) / (2 * width)
        factor = lax.rsqrt(spread + norm_eps)
        left = (left * factor * skip_gain[:, :width]).astype(bf16)
        right = (right * factor * skip_gain[:, width:]).astype(bf16)
        near = jnp.where(upper_half, right, left)
        away = jnp.where(upper_half, left, right)
        for half in range(2):
            normed[half, 0, rows_b, :] = dot_plain(near, order_skip[half]).astype(bf16)
            normed[half, 1, rows_b, :] = dot_plain(away, order_skip[half]).astype(bf16)

    each(normed_part)
    save(0)
    plan.low_cross(last_w)
    plan.spread(skip_w)
    plan.begin(pair_w)
    plan.cross(skip_w)
    plan.spread(qkv_w)
    plan.begin(query_w)
    plan.close(skip_w)
    plan.ready(skip_w)

    skip_tiles = tiles_of(width, 512)

    def skip_product(index, tile):
        half, start, extent = skip_tiles[index]
        cut = tile.shape[0] // 2
        value = dot_plain(normed[half, 0], tile[:cut]) + dot_plain(normed[half, 1], tile[cut:])
        lanes = pl.ds(start, extent)
        if half == 0:
            hidden[:, lanes] = value
        else:
            hidden[:, lanes] += value

    stream(out[skip_w], skip_tiles, buffer, semaphore, skip_product)
    save(1)

    def attn_in_part(b, rows_b):
        value = layer_norm(hidden[rows_b, :]) * gains[0:1, :] + shift[b : b + 1, :]
        attn_in[rows_b, :] = reorder(value.astype(bf16))

    each(attn_in_part)
    save(2)
    plan.cross(qkv_w)
    plan.spread(pair_w)
    plan.begin(keyval_w)
    plan.spread(query_w)
    plan.begin(up_w)
    plan.close(qkv_w)
    plan.ready(qkv_w)

    qkv_tiles = tiles_of(out[qkv_w].shape[4], 512)

    def qkv_product(index, tile):
        half, start, extent = qkv_tiles[index]
        value = dot_plain(attn_in[...], tile)
        for at in range(0, extent, 128):
            lane = start + at
            piece = value[:, at : at + 128]
            if lane < width:
                qkv[:, pl.ds(half * width + lane, 128)] = piece
            else:
                place = lane - width + half * 768
                if place < width:
                    keyval_here[:, pl.ds(width + place, 128)] = piece.astype(bf16)

    stream(out[qkv_w], qkv_tiles, buffer, semaphore, qkv_product)

    def key_part(b, rows_b):
        value, _ = head_norm(qkv[rows_b, pl.ds(width, width)], heads_ref)
        keyval_here[rows_b, pl.ds(0, width)] = turn(value, tables).astype(bf16)

    each(key_part)
    save(3, 4)
    exchange = pltpu.make_async_remote_copy(
        src_ref=keyval_here,
        dst_ref=keyval_there,
        send_sem=twin_send,
        recv_sem=twin_recv,
        device_id=plan.sibling,
        device_id_type=MESH,
    )
    exchange.start()

    def query_part(b, rows_b):
        value, _ = head_norm(qkv[rows_b, pl.ds(0, width)], heads_ref)
        narrow[rows_b, :] = turn(value, tables).astype(bf16)

    each(query_part)
    plan.cross(pair_w)
    plan.spread(keyval_w)
    plan.begin(down_w)
    plan.close(pair_w)
    plan.cross(query_w)
    plan.spread(up_w)
    plan.low_spread(last_w)
    exchange.wait()
    save(5)

    def attend(sources, peak, target, masked):
        peak[...] = jnp.full_like(peak, masked_value)
        wide[...] = jnp.zeros_like(wide)

        @pl.loop(0, batch)
        def _(b):
            rows_b = pl.ds(pl.multiple_of(b * size, size), size)
            for head in range(HEADS):
                lanes, inside = window_of(head, width)
                query = narrow[rows_b, lanes] * inside.astype(bf16)
                scores = dot_right_t(query, pair_rows(sources, b, size, lanes)) * scaling
                if masked:
                    scores = jnp.where(valid[pl.ds(b, 1), :] > 0.5, scores, masked_value)
                probs, largest = softmax_of(scores)
                largest = jnp.max(largest, axis=0, keepdims=True)
                peak[head : head + 1, :] = jnp.maximum(
                    peak[head : head + 1, :], jnp.broadcast_to(largest, (1, 128))
                )
                value = pair_rows(sources, b, size, shift_lanes(lanes, width))
                wide[rows_b, lanes] += dot_plain(probs.astype(bf16), value) * inside

        target[...] = reorder(wide[...].astype(bf16))

    attend([keyval_here, keyval_there], self_peak, attn_cat, False)
    save(6, 17)
    plan.ready(pair_w)
    pair_tiles = tiles_of(width, 512)

    def out_product(source, before, after):
        def body(index, tile):
            lanes = pl.ds(pair_tiles[index][1], pair_tiles[index][2])
            after[:, lanes] = before[:, lanes] + dot_plain(source[...], tile)

        return body

    pair_body = out_product(attn_cat, hidden, after_self)
    stream(out[pair_w], tiles_of(width, 512, (0,)), buffer, semaphore, pair_body)
    save(7)

    def cross_in_part(b, rows_b):
        value = layer_norm(after_self[rows_b, :]) * gains[1:2, :]
        cross_in[rows_b, :] = reorder(value.astype(bf16))

    each(cross_in_part)
    save(8)
    plan.close(query_w)
    plan.ready(query_w)
    query_tiles = tiles_of(out[query_w].shape[4], 512)

    def query_product(index, tile):
        half, start, extent = query_tiles[index]
        place = half * out[query_w].shape[4] + start
        extent = min(extent, width - place)
        cq_proj[:, pl.ds(place, extent)] = dot_plain(cross_in[...], tile)[:, :extent]

    stream(out[query_w], query_tiles, buffer, semaphore, query_product)
    save(9)

    def cross_query_part(b, rows_b):
        narrow[rows_b, :] = head_norm(cq_proj[rows_b, :], heads_ref)[0].astype(bf16)

    each(cross_query_part)
    plan.cross(keyval_w)
    plan.spread(down_w)
    plan.close(keyval_w)
    plan.ready(keyval_w)
    keyval_tiles = tiles_of(width, 512)

    def keyval_product(index, tile):
        half, start, extent = keyval_tiles[index]
        value = dot_plain(text[...], tile)
        if half == 0:
            upper[:, pl.ds(start, extent)] = value[:rows]
            upper[:, pl.ds(width + start, extent)] = value[rows:]
        else:
            cross_keyval[:, pl.ds(width + start, extent)] = value.astype(bf16)

    stream(out[keyval_w], keyval_tiles, buffer, semaphore, keyval_product)
    for b in range(batch):
        for at in range(2):
            part = pl.ds(at * size, size)
            lanes = pl.ds(b * width, width)
            cross_keyval[pl.ds(b * 2 * size + at * size, size), pl.ds(0, width)] = head_norm(
                upper[part, lanes], heads_ref
            )[0].astype(bf16)
        ckey_mine[pl.ds(b * size, size), :] = upper[
            pl.ds(pl.multiple_of(core * size, size), size), pl.ds(b * width, width)
        ]
    attend([cross_keyval], cross_peak, cross_cat, True)
    save(10, 11, 12, 18)
    pair_body = out_product(cross_cat, after_self, after_cross)
    stream(out[pair_w], tiles_of(width, 512, (1,)), buffer, semaphore, pair_body)
    save(13)

    def mlp_in_part(b, rows_b):
        value = layer_norm(after_cross[rows_b, :]) * gains[2:3, :]
        mlp_in[rows_b, :] = reorder(value.astype(bf16))

    each(mlp_in_part)
    save(14)
    plan.cross(up_w)
    plan.cross(down_w)
    plan.close(up_w)
    plan.ready(up_w)
    block = activated.shape[1] // 16
    up_tiles = tiles_of(out[up_w].shape[4], block)

    def up_product(index, tile):
        value = dot_plain(mlp_in[...], tile)
        upper[:, pl.ds(index * block, block)] = value
        slot = jnp.bitwise_xor(me, index)
        activated[:, pl.ds(pl.multiple_of(slot * block, block), block)] = gelu_of(value).astype(bf16)

    stream(out[up_w], up_tiles, buffer, semaphore, up_product)
    save(15, 16)
    def down_part(half):
        def part(index):
            return dot_left_t(activated[:, index * block : (index + 1) * block], out_grad[half])

        return part

    planes = [lambda ref, k=k, q=q: ref.at[k, q] for k in range(4) for q in range(4)]
    down_sum = TwinSum(
        [there_down], [sums_down], sum_send, sum_recv, sum_local, out_down, in_down, plan.sibling
    )
    down_sum.run(
        0, planes, lambda index: mine[6].shape, down_part(1 - core), down_part(core)
    )
    plan.close(down_w)
    plan.low_close(last_w)
    plan.ready(down_w)
    plan.low_ready(last_w)
    for w in range(7):
        plan.finish(w)
    plan.low_finish(last_w)
    for copy in saves:
        copy.wait()


def gelu_slope(value):
    bent = gelu_parts(value)
    inner = 0.7978845608028654 * (1.0 + 3 * 0.044715 * value * value)
    return 0.5 * (1.0 + bent) + 0.5 * value * (1.0 - bent * bent) * inner


def norm_back(value, gain, grad):
    center = value - jnp.mean(value, axis=-1, keepdims=True)
    factor = lax.rsqrt(jnp.mean(center * center, axis=-1, keepdims=True) + norm_eps)
    normed = center * factor
    gain_grad = jnp.sum(grad * normed, axis=0, keepdims=True)
    grad = grad * gain
    first = jnp.mean(grad, axis=-1, keepdims=True)
    second = jnp.mean(grad * normed, axis=-1, keepdims=True)
    return factor * (grad - first - normed * second), gain_grad


class TwinSum:
    def __init__(self, there, sums, send, recv, local, out_buffer, in_buffer, sibling):
        self.there, self.sums = there, sums
        self.send, self.recv, self.local = send, recv, local
        self.out_buffer, self.in_buffer, self.sibling = out_buffer, in_buffer, sibling

    def away(self, w, index, place, source):
        return pltpu.make_async_remote_copy(
            src_ref=source,
            dst_ref=place(self.there[w]),
            send_sem=self.send.at[w, index],
            recv_sem=self.recv.at[w, index],
            device_id=self.sibling,
            device_id_type=MESH,
        )

    def run(self, w, places, shape, other, own, between=None):
        depth = self.out_buffer.shape[0]

        def slot(buffer, index):
            views = [pl.ds(0, n) for n in shape(index)]
            return buffer.at[(index % depth, *views)]

        for index, place in enumerate(places):
            if index >= depth:
                before = index - depth
                self.away(w, before, places[before], slot(self.out_buffer, before)).wait_send()
            target = slot(self.out_buffer, index)
            target[...] = other(index).astype(bf16)
            self.away(w, index, place, target).start()
        for index in range(max(0, len(places) - depth), len(places)):
            self.away(w, index, places[index], slot(self.out_buffer, index)).wait_send()
        if between is not None:
            between()

        def fetch(index):
            return pltpu.make_async_copy(
                places[index](self.there[w]),
                slot(self.in_buffer, index),
                self.local.at[index % depth],
            )

        def store(index):
            return pltpu.make_async_copy(
                slot(self.out_buffer, index),
                places[index](self.sums[w]),
                self.local.at[depth + index % depth],
            )

        def begin(index):
            self.away(w, index, places[index], slot(self.out_buffer, index)).wait_recv()
            fetch(index).start()

        begin(0)
        for index in range(len(places)):
            if index + 1 < len(places):
                begin(index + 1)
            value = own(index)
            fetch(index).wait()
            if index >= depth:
                store(index - depth).wait()
            target = slot(self.out_buffer, index)
            target[...] = (value + slot(self.in_buffer, index)[...].astype(f32)).astype(bf16)
            store(index).start()
        for index in range(max(0, len(places) - depth), len(places)):
            store(index).wait()


def lane_places(height, width, size):
    starts = [(start, min(size, width - start)) for start in range(0, width, size)]
    places = [
        lambda ref, start=start, extent=extent: ref.at[:, :, :, pl.ds(start, extent)]
        for start, extent in starts
    ]
    return starts, places, lambda index: (4, 4, height, starts[index][1])


def mlp_back_body(batch, *refs):
    refs = list(refs)
    take = refs.pop
    out_grad, activated, upper, mlp_in, after_cross, order, gains = (take(0) for _ in range(7))
    up_w, down_w, sums_down = (take(0) for _ in range(3))
    block_out, cross_grad, gain_grad = (take(0) for _ in range(3))
    sums_up, there_up, half_down = (take(0) for _ in range(3))
    upper_grad, turned, total, down_buffer, up_buffer = (take(0) for _ in range(5))
    out_up, in_up = take(0), take(0)
    semaphore, send, recv, local, give_send, give_recv = refs
    rows, width = after_cross.shape
    size = rows // batch
    block = activated.shape[1] // 16
    half_width = out_grad.shape[2]
    me = lax.axis_index("fsdp")
    core = lax.axis_index("seq")
    plan = ScatterPlan(
        [sums_down], None, [half_down], None, None, None, None, None, None,
        (give_send, give_recv, None, None),
    )
    sibling = plan.sibling
    greet([plan.at(plan.second_mask), sibling])
    plan.begin(0)

    def down_back():
        depth = down_buffer.shape[0]

        def copy(index):
            k, q = divmod(index, 4)
            return pltpu.make_async_copy(
                down_w.at[:, k, q], down_buffer.at[index % depth], semaphore.at[index % depth]
            )

        for index in range(depth - 1):
            copy(index).start()
        total[...] = jnp.zeros_like(total)
        for index in range(16):
            if index + depth - 1 < 16:
                copy(index + depth - 1).start()
            copy(index).wait()
            first, second = down_buffer[index % depth, 0], down_buffer[index % depth, 1]
            shard = jnp.bitwise_xor(me, index)
            lanes = pl.ds(pl.multiple_of(shard * block, block), block)
            grad = dot_right_t(out_grad[0], first) + dot_right_t(out_grad[1], second)
            grad = (grad * gelu_slope(upper[:, lanes])).astype(bf16)
            in_half = pl.multiple_of((shard % 8) * block, block)
            upper_grad[shard // 8, :, pl.ds(in_half, block)] = grad
            active = activated[:, index * block : (index + 1) * block]
            total[0] += dot_plain(active, first)
            total[1] += dot_plain(active, second)
        cut = width - half_width
        block_out[:, pl.ds(0, half_width)] = (
            after_cross[:, pl.ds(0, half_width)] + total[0]
        ).astype(bf16)
        block_out[:, pl.ds(half_width, cut)] = (
            after_cross[:, pl.ds(half_width, cut)] + total[1][:, :cut]
        ).astype(bf16)

    down_back()

    turned[...] = jnp.transpose(mlp_in[...])
    starts, places, shape = lane_places(width // 16, upper_grad.shape[2], out_up.shape[4])
    up = TwinSum([there_up], [sums_up], send, recv, local, out_up, in_up, sibling)

    def up_part(half):
        def part(index):
            start, extent = starts[index]
            value = dot_plain(turned[...], upper_grad[half, :, pl.ds(start, extent)])
            return value.reshape(4, 4, width // 16, extent)

        return part

    def up_back():
        tiles = tiles_of(upper_grad.shape[2], 512)

        def body(index, tile):
            half, start, extent = tiles[index]
            value = dot_right_t(upper_grad[half, :, pl.ds(start, extent)], tile)
            if index == 0:
                cross_grad[...] = value
            else:
                cross_grad[...] += value

        stream(up_w, tiles, up_buffer, semaphore, body)
        gain_grad[...] = jnp.zeros_like(gain_grad)
        for b in range(batch):
            rows_b = pl.ds(b * size, size)
            grad = restore_order(order[...], cross_grad[rows_b, :])
            value, gain_part = norm_back(after_cross[rows_b, :], gains[2:3, :], grad)
            gain_grad[0:1, :] += gain_part
            result = jnp.concatenate(
                [out_grad[0, rows_b, :], out_grad[1, rows_b, : width - half_width]], axis=1
            )
            cross_grad[rows_b, :] = result.astype(f32) + value

    up.run(0, places, shape, up_part(1 - core), up_part(core), up_back)
    for n in range(2):
        plan.give(0, n).wait_send()
        plan.give(0, n).wait_recv()


class ScatterPlan:
    def __init__(
        self, sums, out, half, passing, quarter, leaving, last, slots, totals, sems, given=()
    ):
        self.given = given
        self.sums, self.out, self.half = sums, out, half
        self.passing, self.quarter, self.leaving, self.last = passing, quarter, leaving, last
        self.slots, self.totals = slots, totals
        self.send, self.recv, self.load, self.store = sems
        self.core, self.first_mask, self.second_mask, self.at, self.sibling = neighbours(4)
        self.far_peers = [self.at(4 * k) for k in range(1, 4)]

    def peers(self):
        return [*self.far_peers, self.at(self.first_mask), self.at(self.second_mask), self.sibling]

    def copy(self, w, slot, source, target, peer):
        return pltpu.make_async_remote_copy(
            src_ref=source,
            dst_ref=target,
            send_sem=self.send.at[w, slot],
            recv_sem=self.recv.at[w, slot],
            device_id=peer,
            device_id_type=MESH,
        )

    def give(self, w, n):
        q = 3 if n == 0 else self.second_mask
        return self.copy(
            w, n, self.sums[w].at[:, q], self.half[w].at[n], self.at(self.second_mask)
        )

    def hand(self, w):
        return self.copy(w, 2, self.passing[w], self.quarter[w], self.at(self.first_mask))

    def far(self, w, k):
        return self.copy(
            w, 2 + k, self.leaving[w].at[k - 1], self.last[w].at[k - 1], self.far_peers[k - 1]
        )

    def add(self, w, groups, finish, settle):
        height, width = self.sums[w].shape[2:]
        which = 0 if height <= self.slots[0].shape[2] else 1
        slots = self.slots[which]
        size = slots.shape[3]
        chunks = [(start, min(size, width - start)) for start in range(0, width, size)]

        def loads(chunk):
            start, extent = chunks[chunk]
            bank = chunk % 2
            copies, views = [], []
            for planes in groups:
                for plane in planes:
                    at = len(copies)
                    view = slots.at[bank, at, pl.ds(0, height), pl.ds(0, extent)]
                    views.append(view)
                    copies.append(
                        pltpu.make_async_copy(
                            plane.at[:, pl.ds(start, extent)], view, self.load.at[bank, at]
                        )
                    )
            return copies, views

        def lanes_of_chunk(chunk):
            start, extent = chunks[chunk]
            return pl.ds(start, extent), extent

        for copy in loads(0)[0]:
            copy.start()
        for chunk in range(len(chunks)):
            bank = chunk % 2
            if chunk >= 1:
                settle(1 - bank, chunk - 1, *lanes_of_chunk(chunk - 1))
            if chunk + 1 < len(chunks):
                for copy in loads(chunk + 1)[0]:
                    copy.start()
            copies, views = loads(chunk)
            at = 0
            for index, planes in enumerate(groups):
                for copy in copies[at : at + len(planes)]:
                    copy.wait()
                finish(bank, chunk, index, *lanes_of_chunk(chunk), views[at : at + len(planes)])
                at += len(planes)
        last = len(chunks) - 1
        settle(last % 2, last, *lanes_of_chunk(last))

    def added(self, views, extent, kind, put):
        step = 256 if extent % 256 == 0 else 128

        @pl.loop(0, extent // step)
        def _(i):
            lanes = pl.ds(pl.multiple_of(i * step, step), step)
            value = views[0][:, lanes].astype(kind)
            for view in views[1:]:
                value = value + view[:, lanes].astype(kind)
            put(lanes, value)

    def rounded(self, w, groups, targets):
        height = self.sums[w].shape[2]
        which = 0 if height <= self.slots[0].shape[2] else 1
        starts = [sum(len(planes) for planes in groups[:at]) for at in range(len(groups))]

        def store(bank, index, lanes, extent):
            view = self.slots[which].at[bank, starts[index], pl.ds(0, height), pl.ds(0, extent)]
            return pltpu.make_async_copy(
                view, targets[index].at[:, lanes], self.store.at[bank, index]
            )

        def finish(bank, chunk, index, lanes, extent, views):
            def put(at, value):
                views[0][:, at] = value.astype(bf16)

            self.added(views, extent, bf16 if len(views) == 2 else f32, put)
            store(bank, index, lanes, extent).start()

        def settle(bank, chunk, lanes, extent):
            for index in range(len(groups)):
                store(bank, index, lanes, extent).wait()

        self.add(w, groups, finish, settle)

    def begin(self, w):
        self.give(w, 0).start()
        self.give(w, 1).start()

    def middle(self, w):
        if w not in self.given:
            self.give(w, 0).wait_recv()
        mask = self.first_mask
        groups = [[self.half[w].at[0, k], self.sums[w].at[k, mask]] for k in range(4)]
        self.rounded(w, groups, [self.passing[w].at[k] for k in range(4)])
        self.hand(w).start()

    def leave(self, w):
        if w not in self.given:
            self.give(w, 1).wait_recv()
        self.hand(w).wait_recv()
        groups = [
            [self.half[w].at[1, k], self.sums[w].at[k, 0], self.quarter[w].at[k]]
            for k in range(1, 4)
        ]
        self.rounded(w, groups, [self.leaving[w].at[k] for k in range(3)])
        for k in range(1, 4):
            self.far(w, k).start()

    def close(self, w):
        for k in range(1, 4):
            self.far(w, k).wait_recv()
        group = [self.half[w].at[1, 0], self.sums[w].at[0, 0], self.quarter[w].at[0]]
        group += [self.last[w].at[k] for k in range(3)]
        height = self.sums[w].shape[2]
        which = 0 if height <= self.slots[0].shape[2] else 1

        def moves(bank, chunk, lanes, extent):
            total = self.totals[which].at[bank, pl.ds(0, height), pl.ds(0, extent)]
            target = self.out[w].at[self.core, :, lanes]
            here = pltpu.make_async_copy(total, target, self.store.at[bank, 0])
            return total, here, self.copy(w, 6 + chunk, total, target, self.sibling)

        def finish(bank, chunk, index, lanes, extent, views):
            total, here, there = moves(bank, chunk, lanes, extent)

            def put(at, value):
                total[:, at] = value

            self.added(views, extent, f32, put)
            here.start()
            there.start()

        def settle(bank, chunk, lanes, extent):
            _, here, there = moves(bank, chunk, lanes, extent)
            here.wait()
            there.wait_send()
            there.wait_recv()

        self.add(w, [group], finish, settle)

    def finish(self, w):
        if w not in self.given:
            self.give(w, 0).wait_send()
            self.give(w, 1).wait_send()
        self.hand(w).wait_send()
        for k in range(1, 4):
            self.far(w, k).wait_send()


def rest_back_body(batch, scaling, *refs):
    refs = list(refs)
    take = refs.pop

    def several(count):
        return [take(0) for _ in range(count)]

    gains, valid = several(2)
    loaded = several(13)
    skip_w, qkv_w, pair_w, query_w, keyval_w = several(5)
    cross_keyval, cq_proj, ckey_mine, qkv, keyval_here, keyval_there, cross_grad = several(7)
    summed, half_down = several(2), take(0)
    text_grad, gain_grads, shift_grad, normed_grad = several(4)
    out = several(7)
    own_sums, there = several(5), several(5)
    half = [half_down, *several(6)]
    passing, quarter, leaving, last = (several(7) for _ in range(4))
    grad, wide, factor, back = several(4)
    query, mix_grad, total, keyval, proj, turned, halves = several(7)
    placed = several(13)
    cross_cat, attn_cat, cross_in, attn_in, text, after_self, hidden, normed = placed[:8]
    order, heads_ref, *tables = placed[8:]
    buffer, out_buffer, in_buffer = several(3)
    slots, totals = several(2), several(2)
    landed = take(0)
    semaphore, loads, twin_send, twin_recv, twin_local = several(5)
    exchange_send, exchange_recv, send, recv, add_load, add_store = several(6)
    rows, width = hidden.shape
    size = rows // batch
    block = width // 16
    core = lax.axis_index("seq")
    down, up, query_s, keyval_s, pair_s, qkv_s, skip_s = range(7)
    plan = ScatterPlan(
        summed + own_sums, out, half, passing, quarter, leaving, last, slots, totals,
        (send, recv, add_load, add_store), (0,),
    )
    twin = TwinSum(
        there, own_sums, twin_send, twin_recv, twin_local, out_buffer, in_buffer, plan.sibling
    )
    greet(plan.peers())
    plan.begin(up)

    first_lanes, last_lanes = pl.ds(0, width), pl.ds(width, width)

    def load(*pairs):
        copies = [
            pltpu.make_async_copy(source, target, loads.at[at])
            for at, (source, target) in enumerate(pairs)
        ]
        for copy in copies:
            copy.start()
        for copy in copies:
            copy.wait()

    load(
        (cross_grad, grad),
        (cross_keyval, keyval),
        (cq_proj, proj.at[:, first_lanes]),
        (ckey_mine, proj.at[:, last_lanes]),
        *zip(loaded, placed),
    )
    plan.middle(down)
    gain_grads[...] = jnp.zeros_like(gain_grads)
    shift_grad[...] = jnp.zeros_like(shift_grad)

    def each(body):
        for b in range(batch):
            body(b, pl.ds(b * size, size))

    def back_through(weight, tiles, factor_of, target):
        def body(index, tile):
            value = dot_right_t(factor_of(*tiles[index]), tile)
            if index == 0:
                target[...] = value
            else:
                target[...] += value

        stream(weight, tiles, buffer, semaphore, body)

    def restored(target):
        def part(b, rows_b):
            target[rows_b, :] = dot_right_t(wide[rows_b, :].astype(bf16), order[...]).astype(bf16)

        each(part)

    def split_lanes(value, rows_b, start):
        halves[0, rows_b, pl.ds(start, 768)] = value[:, :768]
        halves[1, rows_b, pl.ds(start, width - 768)] = value[:, 768:]
        halves[1, rows_b, pl.ds(start + width - 768, 2 * 768 - width)] = jnp.zeros(
            (value.shape[0], 2 * 768 - width), bf16
        )

    def attention_back(sources, table_refs, masked, put):
        back[...] = jnp.zeros_like(back)
        total[...] = jnp.zeros_like(total)

        def prepare(b, rows_b):
            value, scale = head_norm(proj[rows_b, first_lanes], heads_ref)
            wide[rows_b, :] = value
            factor[rows_b, :] = scale
            turned_value = turn(value, table_refs) if table_refs else value
            query[rows_b, :] = turned_value.astype(bf16)

        each(prepare)

        @pl.loop(0, batch)
        def _(b):
            rows_b = pl.ds(pl.multiple_of(b * size, size), size)
            for head in range(HEADS):
                lanes, inside = window_of(head, width)
                behind = shift_lanes(lanes, width)
                queries = query[rows_b, lanes] * inside.astype(bf16)
                keys = pair_rows(sources, b, size, lanes)
                scores = dot_right_t(queries, keys) * scaling
                if masked:
                    scores = jnp.where(valid[pl.ds(b, 1), :] > 0.5, scores, masked_value)
                probs, _ = softmax_of(scores)
                grads = mix_grad[rows_b, lanes] * inside.astype(bf16)
                prob_grad = dot_right_t(grads, pair_rows(sources, b, size, behind))
                score_grad = softmax_back(probs, prob_grad).astype(bf16)
                value_grad = dot_left_t(probs.astype(bf16), grads)
                key_grad = dot_left_t(score_grad, queries) * scaling
                back[rows_b, lanes] += dot_plain(score_grad, keys) * (inside * scaling)
                for at in range(2):
                    part = slice(at * size, (at + 1) * size)
                    total[at, rows_b, lanes] += key_grad[part]
                    total[at, rows_b, behind] += value_grad[part]

        def finish(b, rows_b):
            value = back[rows_b, :]
            if table_refs:
                value = turn_back(value, table_refs)
            value = head_norm_back(value, wide[rows_b, :], factor[rows_b, :], heads_ref)
            put(value.astype(bf16), rows_b)

        each(finish)

    def exchange(index):
        return pltpu.make_async_remote_copy(
            src_ref=keyval.at[pl.ds(0, rows), :],
            dst_ref=landed.at[index],
            send_sem=exchange_send.at[index],
            recv_sem=exchange_recv.at[index],
            device_id=plan.sibling,
            device_id_type=MESH,
        )

    def keys_back(index, mine, table_refs, put):
        def part(b, rows_b):
            normed_keys, scale = head_norm(proj[rows_b, last_lanes], heads_ref)
            value = total[mine, rows_b, first_lanes] + landed[index, rows_b, first_lanes].astype(f32)
            if table_refs:
                value = turn_back(value, table_refs)
            key_grad = head_norm_back(value, normed_keys, scale, heads_ref).astype(bf16)
            value = total[mine, rows_b, last_lanes] + landed[index, rows_b, last_lanes].astype(f32)
            put(key_grad, value.astype(bf16), rows_b)

        each(part)

    def twin_product(w, extent, height, left, right):
        starts, places, shape = lane_places(height, extent, out_buffer.shape[4])

        def part(which):
            def value(index):
                start, lanes = starts[index]
                product = dot_plain(left(which), right(which, start, lanes))
                return product.reshape(4, 4, height, lanes)

            return value

        twin.run(w, places, shape, part(1 - core), part(core))

    halves[1, :, first_lanes] = grad[...].astype(bf16)
    pair_tiles = tiles_of(width, 384, (1,))
    back_through(
        pair_w, pair_tiles, lambda at, start, extent: halves[at, :, pl.ds(start, extent)], wide
    )
    restored(mix_grad)
    attention_back([keyval], (), True, lambda value, rows_b: split_lanes(value, rows_b, width))
    keyval[pl.ds(0, rows), :] = total[1 - core].astype(bf16)
    exchange(0).start()
    plan.middle(up)
    query_tiles = tiles_of(768, 384)
    back_through(
        query_w,
        query_tiles,
        lambda at, start, extent: halves[at, :, pl.ds(width + start, extent)],
        wide,
    )

    def self_part(b, rows_b):
        value = restore_order(order[...], wide[rows_b, :])
        value, gain_part = norm_back(after_self[rows_b, :], gains[1:2, :], value)
        gain_grads[1:2, :] += gain_part
        value = grad[rows_b, :] + value
        grad[rows_b, :] = value
        halves[0, rows_b, first_lanes] = value.astype(bf16)

    each(self_part)
    pair_tiles_two = tiles_of(width, 384, (0,))
    back_through(
        pair_w, pair_tiles_two, lambda at, start, extent: halves[at, :, pl.ds(start, extent)], wide
    )
    restored(mix_grad)
    turned[0] = jnp.transpose(attn_cat[...])
    turned[1] = jnp.transpose(cross_cat[...])
    twin_product(
        2,
        width,
        block,
        lambda at: turned[at],
        lambda at, start, extent: halves[at, :, pl.ds(start, extent)],
    )
    plan.begin(pair_s)
    plan.leave(down)
    turned[0] = jnp.transpose(cross_in[...])
    twin_product(
        0,
        768,
        block,
        lambda at: turned[0],
        lambda at, start, extent: halves[at, :, pl.ds(width + start, extent)],
    )
    plan.begin(query_s)
    plan.leave(up)
    exchange(0).wait()

    def text_part(key_grad, value_grad, rows_b):
        landed[0, rows_b, first_lanes] = key_grad
        landed[0, rows_b, last_lanes] = value_grad

    keys_back(0, core, (), text_part)
    plan.middle(pair_s)

    load(
        (qkv, proj),
        (keyval_here, keyval.at[pl.ds(0, rows), :]),
        (keyval_there, keyval.at[pl.ds(rows, rows), :]),
    )

    def query_part(value, rows_b):
        halves[0, rows_b, first_lanes] = value

    sources = [keyval.at[pl.ds(0, rows), :], keyval.at[pl.ds(rows, rows), :]]
    attention_back(sources, tables, False, query_part)
    keyval[pl.ds(0, rows), :] = total[1].astype(bf16)
    exchange(1).start()
    plan.middle(query_s)
    plan.leave(pair_s)
    exchange(1).wait()

    def key_part(key_grad, value_grad, rows_b):
        halves[1, rows_b, first_lanes] = key_grad
        split_lanes(value_grad, rows_b, width)

    keys_back(1, 0, tables, key_part)
    turned[0] = jnp.transpose(attn_in[...])
    wide_half = halves.shape[2]
    twin_product(
        3,
        wide_half,
        block,
        lambda at: turned[0],
        lambda at, start, extent: halves[at, :, pl.ds(start, extent)],
    )
    plan.begin(qkv_s)
    qkv_tiles = tiles_of(wide_half, 384)
    back_through(
        qkv_w, qkv_tiles, lambda at, start, extent: halves[at, :, pl.ds(start, extent)], wide
    )

    def hidden_part(b, rows_b):
        value = restore_order(order[...], wide[rows_b, :])
        shift_grad[b : b + 1, :] = jnp.sum(value, axis=0, keepdims=True)
        value, gain_part = norm_back(hidden[rows_b, :], gains[0:1, :], value)
        gain_grads[0:1, :] += gain_part
        halves[0, rows_b, first_lanes] = (grad[rows_b, :] + value).astype(bf16)

    each(hidden_part)
    plan.leave(query_s)

    for at in range(2):
        for part in range(2):
            turned[at, pl.ds(part * (width // 2), width // 2), :] = jnp.transpose(
                normed[at, part]
            )
    twin_product(
        4,
        width,
        block,
        lambda at: turned[at],
        lambda at, start, extent: halves[0, :, pl.ds(start, extent)],
    )
    plan.begin(skip_s)

    text_width = text.shape[1]
    turned[0, pl.ds(0, text_width), :] = jnp.transpose(text[...])
    twin_product(
        1,
        width,
        text_width // 16,
        lambda at: turned[0, pl.ds(0, text_width), :],
        lambda at, start, extent: landed[0, :, pl.ds(at * width + start, extent)]
        if isinstance(at, int)
        else landed[0, :, pl.ds(pl.multiple_of(at * width + start, 128), extent)],
    )
    plan.begin(keyval_s)
    plan.middle(qkv_s)
    back_through(
        keyval_w,
        tiles_of(width, 384),
        lambda at, start, extent: landed[0, :, pl.ds(at * width + start, extent)],
        text_grad,
    )
    skip_tiles = tiles_of(width, 384)

    def skip_body(index, tile):
        at, start, extent = skip_tiles[index]
        value = dot_right_t(halves[0, :, pl.ds(start, extent)], tile)
        lanes = pl.ds(at * width, width)
        if start == 0:
            total[0, :, lanes] = value
        else:
            total[0, :, lanes] += value

    stream(skip_w, skip_tiles, buffer, semaphore, skip_body)
    keep = pltpu.make_async_copy(total.at[0], normed_grad, loads.at[0])
    keep.start()
    plan.middle(skip_s)
    plan.leave(qkv_s)
    plan.middle(keyval_s)
    plan.close(down)
    plan.leave(skip_s)
    plan.close(up)
    plan.leave(keyval_s)
    plan.close(pair_s)
    plan.close(query_s)
    plan.close(qkv_s)
    plan.close(skip_s)
    plan.close(keyval_s)
    keep.wait()
    for w in range(7):
        plan.finish(w)


def joined_back_body(batch, normed_grad, latent, skip, skip_gain, order_skip, joined, gain_grad):
    width = latent.shape[1]
    size = latent.shape[0] // batch
    upper_half = lax.axis_index("fsdp") >= 8
    gain_grad[...] = jnp.zeros_like(gain_grad)
    for b in range(batch):
        rows_b = pl.ds(b * size, size)
        near, away = 0.0, 0.0
        for at in range(2):
            part = normed_grad[rows_b, at * width : (at + 1) * width]
            near = near + restore_order(order_skip[at], part[:, : width // 2])
            away = away + restore_order(order_skip[at], part[:, width // 2 :])
        left = latent[rows_b, :].astype(f32)
        right = skip[rows_b, :].astype(f32)
        left_grad = jnp.where(upper_half, away, near)
        right_grad = jnp.where(upper_half, near, away)

        def mean(first, second):
            total = jnp.sum(first, axis=1, keepdims=True) + jnp.sum(second, axis=1, keepdims=True)
            return total / (2 * width)

        middle = mean(left, right)
        left, right = left - middle, right - middle
        factor = lax.rsqrt(mean(left * left, right * right) + norm_eps)
        left, right = left * factor, right * factor
        gain_grad[0:1, :width] += jnp.sum(left_grad * left, axis=0, keepdims=True)
        gain_grad[0:1, width:] += jnp.sum(right_grad * right, axis=0, keepdims=True)
        left_grad = left_grad * skip_gain[:, :width]
        right_grad = right_grad * skip_gain[:, width:]
        first = mean(left_grad, right_grad)
        second = mean(left_grad * left, right_grad * right)
        joined[0, rows_b, :] = factor * (left_grad - first - left * second)
        joined[1, rows_b, :] = factor * (right_grad - first - right * second)


class Links:
    def __init__(self, fsdp_count):
        self.count = fsdp_count
        self.me = lax.axis_index("fsdp")
        self.core = lax.axis_index("seq")
        self.high_bits = fsdp_count.bit_length() - 3
        self.quad = 4 << (self.high_bits - 2)
        offsets = [0]
        for bit in range(self.high_bits - 2):
            offsets = offsets + [offset | (4 << bit) for offset in offsets]
        self.high_offsets = [k * self.quad | offset for k in range(4) for offset in offsets]

    def swap(self, value, mask_first, mask_second):
        pairs = []
        for index in range(self.count):
            pairs.append((2 * index, 2 * (index ^ mask_first)))
            pairs.append((2 * index + 1, 2 * (index ^ mask_second) + 1))
        return lax.ppermute(value, ("fsdp", "seq"), pairs)

    def sibling(self, value):
        return lax.ppermute(value, "seq", [(0, 1), (1, 0)])

    def pick(self, first, second):
        return jnp.where(self.core == 0, first, second)

    def offset(self, block):
        return self.high_offsets[block % (self.count // 4)] | (block // (self.count // 4))

    def place(self, offset):
        table = [0] * self.count
        for block in range(self.count):
            table[self.offset(block)] = block
        return jnp.array(table, jnp.int32)[offset]

    def columns(self, own, other):
        return self.pick(
            jnp.concatenate([own, other], axis=-1), jnp.concatenate([other, own], axis=-1)
        )

    def halves(self, value):
        half = value.shape[-1] // 2
        first, second = value[..., :half], value[..., half:]
        return self.pick(first, second), self.pick(second, first)

    def order_matrix(self, size):
        block = size // self.count
        at = lax.broadcasted_iota(jnp.int32, (size, size), 0)
        table = jnp.array([self.offset(b) for b in range(self.count)], jnp.int32)
        starts = jnp.bitwise_xor(self.me, table) * block
        wanted = (starts[:, None] + jnp.arange(block, dtype=jnp.int32)[None, :]).reshape(1, size)
        return (at == wanted).astype(bf16)

    def order_skip(self, width):
        block = width // self.count
        offsets = [
            offset & (self.count // 2 - 1) for offset in self.high_offsets[: self.count // 2 // 4 * 1]
        ]
        offsets = [offset | q for q in range(4) for offset in offsets]
        lower = jnp.bitwise_and(self.me, self.count // 2 - 1)
        starts = jnp.bitwise_xor(lower, jnp.array(offsets, jnp.int32)) * (2 * block)
        starts = jnp.stack([starts, starts + block])
        wanted = (starts[:, :, None] + jnp.arange(block, dtype=jnp.int32)).reshape(1, width)
        return (lax.broadcasted_iota(jnp.int32, (width, width), 0) == wanted).astype(bf16)

    def order_blocks(self, value):
        size = value.shape[1] // self.count
        parts = []
        for block in range(self.count):
            source = jnp.bitwise_xor(self.me, self.offset(block))
            parts.append(lax.dynamic_slice_in_dim(value, source * size, size, 1))
        return jnp.concatenate(parts, axis=1)

    def restore_blocks(self, value):
        size = value.shape[1] // self.count
        parts = []
        for shard in range(self.count):
            source = self.place(jnp.bitwise_xor(self.me, shard))
            parts.append(lax.dynamic_slice_in_dim(value, source * size, size, 1))
        return jnp.concatenate(parts, axis=1)

    def extra_gather(self, mine):
        blocks = mine
        for bit in range(self.high_bits - 2):
            blocks = jnp.concatenate([blocks, self.swap(blocks, 4 << bit, 4 << bit)], axis=0)
        return blocks

    def extra_scatter(self, value):
        for bit in reversed(range(self.high_bits - 2)):
            size = value.shape[-2] // 2
            value = value[..., :size, :] + self.swap(value[..., size:, :], 4 << bit, 4 << bit)
        return value


class Gather:
    def __init__(self, links, shards):
        self.links = links
        half = shards[0].shape[1] // 2
        self.rows = shards[0].shape[0]
        self.weights = len(shards)
        self.shards = jnp.concatenate(
            [links.pick(shard[:, :half], shard[:, half:]) for shard in shards], axis=0
        )
        self.pending = [self.shards]
        self.stage = 0

    def advance(self):
        links = self.links
        self.stage += 1
        if self.stage == 1:
            blocks = [self.pending[0]]
            for bit in range(links.high_bits - 2):
                got = links.swap(jnp.concatenate(blocks, axis=0), 4 << bit, 4 << bit)
                size = self.rows * self.weights
                blocks = blocks + [got[at * size : (at + 1) * size] for at in range(len(blocks))]
            self.low_blocks = len(blocks)
            mine = jnp.concatenate(blocks, axis=0) if len(blocks) > 1 else blocks[0]
            self.pending = [mine] + [
                links.swap(mine, k * links.quad, k * links.quad) for k in range(1, 4)
            ]
        elif self.stage == 2:
            size = self.rows * self.weights
            cuts = [
                got[at * size + w * self.rows : at * size + (w + 1) * self.rows]
                for w in range(self.weights)
                for got in self.pending
                for at in range(self.low_blocks)
            ]
            base = jnp.concatenate(cuts, axis=0)
            self.pending = [
                base, links.swap(base, 1, 2), links.swap(base, 2, 1), links.sibling(base)
            ]
        elif self.stage == 3:
            base, first, second, base_there = self.pending
            self.kept = [base, second, base_there]
            self.pending = [
                links.swap(first, 2, 1), links.sibling(first), links.sibling(second), *self.pending
            ]
        elif self.stage == 4:
            self.pending[0:1] = [links.sibling(self.pending[0]), self.pending[0]]
        elif self.stage == 5:
            both_there, both, first_there, second_there, base, first, second, base_there = self.pending
            size = base.shape[0] // self.weights
            self.result = []
            for w in range(self.weights):
                cut = slice(w * size, (w + 1) * size)
                pick = links.pick
                own = jnp.concatenate(
                    [base[cut], pick(first[cut], second[cut]), pick(second[cut], first[cut]), both[cut]],
                    axis=0,
                )
                other = jnp.concatenate(
                    [
                        base_there[cut],
                        pick(second_there[cut], first_there[cut]),
                        pick(first_there[cut], second_there[cut]),
                        both_there[cut],
                    ],
                    axis=0,
                )
                self.result.append((own, other))
            self.pending = []

    def finish(self):
        while self.stage < 5:
            self.advance()
        return self.result


class Scatter:
    def __init__(self, links, pairs):
        self.links = links
        self.pairs = pairs
        self.pending = [other for _, other in pairs]
        self.stage = 0

    def advance(self):
        links = self.links
        pick = links.pick
        self.stage += 1
        if self.stage == 1:
            self.pending = [own for own, _ in self.pairs] + [
                links.sibling(other) for other in self.pending
            ]
        elif self.stage == 2:
            count = len(self.pairs)
            send, keep = [[], []], [[], []]
            for own, got in zip(self.pending[:count], self.pending[count:]):
                size = own.shape[0] // 4
                cuts = [
                    own[q * size : (q + 1) * size].astype(f32) + got[q * size : (q + 1) * size].astype(f32)
                    for q in range(4)
                ]
                send[0].append(pick(cuts[2], cuts[1]).astype(bf16))
                send[1].append(cuts[3].astype(bf16))
                keep[0].append(cuts[0])
                keep[1].append(pick(cuts[1], cuts[2]))
            self.sizes = [part.shape[0] for part in keep[0]]
            self.keep = [jnp.concatenate(part, axis=0) for part in keep]
            self.pending = [links.swap(jnp.concatenate(send[0] + send[1], axis=0), 2, 1)]
        elif self.stage == 3:
            total = sum(self.sizes)
            got = self.pending[0].astype(f32)
            self.keep, send = self.keep[0] + got[:total], (self.keep[1] + got[total:]).astype(bf16)
            self.pending = [links.swap(send, 1, 2)]
        elif self.stage == 4:
            summed = self.keep + self.pending[0].astype(f32)
            keep, send = [], [[], [], []]
            start = 0
            for size in self.sizes:
                part = size // 4
                keep.append(summed[start : start + part])
                for k in range(1, 4):
                    send[k - 1].append(summed[start + k * part : start + (k + 1) * part].astype(bf16))
                start += size
            self.keep = jnp.concatenate(keep, axis=0)
            self.pending = [
                links.swap(jnp.concatenate(send[k - 1], axis=0), k * links.quad, k * links.quad)
                for k in range(1, 4)
            ]
        elif self.stage == 5:
            total = self.keep
            for got in self.pending:
                total = total + got.astype(f32)
            rows = [size // 4 for size in self.sizes]
            for bit in reversed(range(links.high_bits - 2)):
                keep, send, start = [], [], 0
                for at, size in enumerate(rows):
                    keep.append(total[start : start + size // 2])
                    send.append(total[start + size // 2 : start + size])
                    start += size
                    rows[at] = size // 2
                got = links.swap(jnp.concatenate(send, axis=0), 4 << bit, 4 << bit)
                total = jnp.concatenate(keep, axis=0) + got
            self.rows = rows
            self.pending = [total, links.sibling(total)]
        elif self.stage == 6:
            whole = links.columns(*self.pending)
            self.result, start = [], 0
            for size in self.rows:
                self.result.append(whole[start : start + size])
                start += size
            self.pending = []

    def finish(self):
        while self.stage < 6:
            self.advance()
        return self.result


def tie(value, *jobs):
    leaves, tree = jax.tree.flatten(value)
    flat = list(leaves)
    for job in jobs:
        flat.extend(job.pending)
    flat = list(lax.optimization_barrier(tuple(flat)))
    at = len(leaves)
    value = jax.tree.unflatten(tree, flat[:at])
    for job in jobs:
        job.pending = flat[at : at + len(job.pending)]
        at += len(job.pending)
        job.advance()
    return value


def parts_of(value):
    high = value.astype(bf16)
    return high, (value - high.astype(f32)).astype(bf16)


def sum_heads(value, heads_ref):
    high, low = parts_of(value)
    return dot_plain(high, heads_ref[...]) + dot_plain(low, heads_ref[...])


def spread_heads(value, heads_ref):
    high, low = parts_of(value)
    return dot_right_t(high, heads_ref[...]) + dot_right_t(low, heads_ref[...])


def head_norm(value, heads_ref):
    center = value - spread_heads(sum_heads(value, heads_ref) * (1.0 / HD), heads_ref)
    spread = sum_heads(center * center, heads_ref) * (1.0 / HD)
    factor = spread_heads(lax.rsqrt(spread + norm_eps), heads_ref)
    return center * factor, factor


def head_norm_back(grad, normed, factor, heads_ref):
    first = sum_heads(grad, heads_ref) * (1.0 / HD)
    second = sum_heads(grad * normed, heads_ref) * (1.0 / HD)
    return factor * (
        grad - spread_heads(first, heads_ref) - normed * spread_heads(second, heads_ref)
    )


def partner(value, former):
    quarter = HD // 4
    width = value.shape[1]
    up = pltpu.roll(value, width - quarter, 1)
    down = pltpu.roll(value, quarter, 1)
    return jnp.where(former > 0.5, up, down)


def turn(value, table_refs):
    cosine, sine, former = table_refs
    return value * cosine[...] + partner(value, former[...]) * sine[...]


def turn_back(value, table_refs):
    cosine, sine, former = table_refs
    return value * cosine[...] - partner(value, former[...]) * sine[...]


def window_of(head, width):
    start = min(head * HD // 128 * 128, width - 256)
    lane = lax.broadcasted_iota(jnp.int32, (1, 256), 1) + start
    inside = jnp.logical_and(lane >= head * HD, lane < (head + 1) * HD)
    return pl.ds(start, 256), inside.astype(f32)


def normed_rows(proj_ref, heads_ref, table_refs, rows):
    value, factor = head_norm(proj_ref[rows, :], heads_ref)
    turned = turn(value, table_refs) if table_refs else value
    return value, factor, turned


def keys_body(batch, turned, *refs):
    key_ref, value_ref, heads_ref = refs[:3]
    table_refs, out_ref = refs[3:-1], refs[-1]
    width = key_ref.shape[1]
    size = key_ref.shape[0] // batch
    for b in range(batch):
        rows = pl.ds(b * size, size)
        out_ref[rows, :width] = normed_rows(key_ref, heads_ref, table_refs, rows)[2].astype(bf16)
        out_ref[rows, width:] = value_ref[rows, :].astype(bf16)


def pair_rows(refs, b, size, lanes):
    if len(refs) == 2:
        return jnp.concatenate([ref[pl.ds(b * size, size), lanes] for ref in refs], axis=0)
    return refs[0][pl.ds(b * 2 * size, 2 * size), lanes]


def shift_lanes(lanes, width):
    return pl.ds(lanes.start + width, lanes.size)


def scores_of(query, key, lengths_ref, b, scaling):
    scores = dot_right_t(query, key) * scaling
    if lengths_ref is not None:
        column = lax.broadcasted_iota(jnp.int32, scores.shape, 1)
        scores = jnp.where(column < lengths_ref[b], scores, masked_value)
    return scores


def softmax_of(scores):
    largest = jnp.max(scores, axis=1, keepdims=True)
    raised = jnp.exp(scores - largest)
    return raised * (1.0 / jnp.sum(raised, axis=1, keepdims=True)), largest


def attention_body(batch, masked, turned, sources, scaling, *refs):
    refs = list(refs)
    lengths_ref = refs.pop(0) if masked else None
    proj_ref, heads_ref = refs.pop(0), refs.pop(0)
    table_refs = [refs.pop(0) for _ in range(3)] if turned else []
    keyval_refs = [refs.pop(0) for _ in range(sources)]
    out_ref, peak_ref, query_ref, mixed_ref = refs
    size, width = proj_ref.shape[0] // batch, proj_ref.shape[1]
    peak_ref[...] = jnp.full_like(peak_ref, masked_value)
    mixed_ref[...] = jnp.zeros_like(mixed_ref)
    for b in range(batch):
        rows = pl.ds(b * size, size)
        query_ref[rows, :] = normed_rows(proj_ref, heads_ref, table_refs, rows)[2].astype(bf16)

    @pl.loop(0, batch)
    def _(b):
        rows = pl.ds(pl.multiple_of(b * size, size), size)
        for head in range(HEADS):
            lanes, inside = window_of(head, width)
            query = query_ref[rows, lanes] * inside.astype(bf16)
            key = pair_rows(keyval_refs, b, size, lanes)
            scores = scores_of(query, key, lengths_ref, b, scaling)
            probs, largest = softmax_of(scores)
            largest = jnp.max(largest, axis=0, keepdims=True)
            peak_ref[head : head + 1, :] = jnp.maximum(
                peak_ref[head : head + 1, :], jnp.broadcast_to(largest, (1, 128))
            )
            value = pair_rows(keyval_refs, b, size, shift_lanes(lanes, width))
            mixed_ref[rows, lanes] += dot_plain(probs.astype(bf16), value) * inside

    out_ref[...] = mixed_ref[...].astype(bf16)


def attention_back_body(batch, masked, turned, sources, scaling, *refs):
    refs = list(refs)
    lengths_ref = refs.pop(0) if masked else None
    proj_ref, grad_ref, heads_ref = refs.pop(0), refs.pop(0), refs.pop(0)
    table_refs = [refs.pop(0) for _ in range(3)] if turned else []
    keyval_refs = [refs.pop(0) for _ in range(sources)]
    out_ref, here_ref, there_ref, normed_ref, factor_ref, query_ref, back_ref, total_ref = refs
    size, width = proj_ref.shape[0] // batch, proj_ref.shape[1]
    back_ref[...] = jnp.zeros_like(back_ref)
    total_ref[...] = jnp.zeros_like(total_ref)
    for b in range(batch):
        rows = pl.ds(b * size, size)
        normed, factor, query = normed_rows(proj_ref, heads_ref, table_refs, rows)
        normed_ref[rows, :] = normed
        factor_ref[rows, :] = factor
        query_ref[rows, :] = query.astype(bf16)

    @pl.loop(0, batch)
    def _(b):
        rows = pl.ds(pl.multiple_of(b * size, size), size)
        for head in range(HEADS):
            lanes, inside = window_of(head, width)
            behind = shift_lanes(lanes, width)
            query = query_ref[rows, lanes] * inside.astype(bf16)
            key = pair_rows(keyval_refs, b, size, lanes)
            probs, _ = softmax_of(scores_of(query, key, lengths_ref, b, scaling))
            grad = grad_ref[rows, lanes] * inside.astype(bf16)
            value = pair_rows(keyval_refs, b, size, behind)
            prob_grad = dot_right_t(grad, value)
            score_grad = softmax_back(probs, prob_grad).astype(bf16)
            value_grad = dot_left_t(probs.astype(bf16), grad)
            key_grad = dot_left_t(score_grad, query) * scaling
            back_ref[rows, lanes] += dot_plain(score_grad, key) * (inside * scaling)
            for at in range(2):
                part = slice(at * size, (at + 1) * size)
                total_ref[at, rows, lanes] += key_grad[part]
                total_ref[at, rows, behind] += value_grad[part]

    for b in range(batch):
        rows = pl.ds(b * size, size)
        grad = back_ref[rows, :]
        if table_refs:
            grad = turn_back(grad, table_refs)
        out_ref[rows, :] = head_norm_back(
            grad, normed_ref[rows, :], factor_ref[rows, :], heads_ref
        ).astype(bf16)
    mine = lax.axis_index("seq") if masked else 0
    here_ref[...] = total_ref[mine]
    there_ref[...] = total_ref[1 - mine].astype(bf16)


def keys_back_body(batch, turned, *refs):
    key_ref, here_ref, from_there_ref, heads_ref = refs[:4]
    table_refs, out_ref = refs[4:-1], refs[-1]
    width = key_ref.shape[1]
    size = key_ref.shape[0] // batch
    for b in range(batch):
        rows = pl.ds(b * size, size)
        normed, factor, _ = normed_rows(key_ref, heads_ref, (), rows)
        grad = here_ref[rows, :width] + from_there_ref[rows, :width].astype(f32)
        if table_refs:
            grad = turn_back(grad, table_refs)
        out_ref[rows, :width] = head_norm_back(grad, normed, factor, heads_ref).astype(bf16)
        out_ref[rows, width:] = (
            here_ref[rows, width:] + from_there_ref[rows, width:].astype(f32)
        ).astype(bf16)


def plain_call(body, outs, blocks, scratch=(), lengths=None):
    def spec(array, column):
        if column is None:
            return pl.BlockSpec(array.shape, lambda i, *_: (0,) * array.ndim)
        return pl.BlockSpec((array.shape[0], column[1]), lambda i, *_: (0, column[0]))

    def out_spec(shape):
        return pl.BlockSpec(shape.shape, lambda i, *_: (0,) * len(shape.shape))

    grid_spec = pltpu.PrefetchScalarGridSpec(
        num_scalar_prefetch=0 if lengths is None else 1,
        grid=(1,),
        in_specs=[spec(*block) for block in blocks],
        out_specs=[out_spec(shape) for shape in outs],
        scratch_shapes=list(scratch),
    )
    given = [] if lengths is None else [lengths]
    return pl.pallas_call(
        body,
        grid_spec=grid_spec,
        out_shape=list(outs),
        compiler_params=pltpu.CompilerParams(vmem_limit_bytes=50 * 2**20),
    )(*given, *[array for array, _ in blocks])


def lanes_of(value, multiple):
    size = 128 * multiple
    spare = -value.shape[-1] % size
    value = jnp.pad(value, [(0, 0)] * (value.ndim - 1) + [(0, spare)])
    return value.reshape(*value.shape[:-1], -1, 128)


def restore_order(matrix, value):
    return dot_right_t(value.astype(bf16), matrix)


def exact_restore(matrix, value):
    high = value.astype(bf16)
    low = (value - high.astype(f32)).astype(bf16)
    return dot_right_t(high, matrix) + dot_right_t(low, matrix)


def local(
    latent,
    skip_input,
    condition,
    text_encoder_states,
    text_lengths,
    out_grad,
    skip_gain,
    norm_gains,
    skip_linear,
    shift_linear,
    self_qkv,
    self_out,
    cross_query,
    cross_keyval,
    cross_out,
    mlp_up,
    mlp_down,
    thresholds,
):
    batch, tokens, width = latent.shape
    rows = batch * tokens
    text_rows = text_encoder_states.shape[1]
    text_width = text_encoder_states.shape[2]
    scaling = HD ** (-0.5)
    links = Links(lax.axis_size("fsdp"))
    me, core = links.me, links.core
    count = links.count

    positions = core * tokens + jnp.arange(tokens)
    feature = jnp.arange(width) % HD
    freqs = 10000.0 ** (-(feature % (HD // 4)).astype(f32) / (HD // 4))
    place = jnp.where(
        feature[None, :] < HD // 2, (positions // GRID_W)[:, None], (positions % GRID_W)[:, None]
    )
    angles = place.astype(f32) * freqs[None, :]
    former = (feature % (HD // 2) < HD // 4)[None, :]
    cosine = jnp.cos(angles)
    sine = jnp.where(former, -jnp.sin(angles), jnp.sin(angles))
    tables = [(cosine, None), (sine, None), (former.astype(f32), None)]
    head_at = jnp.arange(width)[:, None] // HD == jnp.arange(128)[None, :]
    head_at = (head_at.astype(bf16), None)

    gain_rows = skip_gain.shape[0]
    third = norm_gains.shape[1]
    cond_act = jax.nn.silu(condition.astype(f32)).astype(bf16)
    small = jnp.concatenate([skip_gain, norm_gains.reshape(-1), cond_act.reshape(-1)])
    small = trade(lanes_of(small, 16), count, True, 1).reshape(count, -1)
    skip_gain_all = small[:, :gain_rows].reshape(-1).astype(f32)
    cond_start = gain_rows + 3 * third
    gains = small[:, gain_rows:cond_start].reshape(count, 3, third)
    gains = gains.transpose(1, 0, 2).reshape(3, width).astype(f32)
    cond_all = small[:, cond_start : cond_start + batch * width].reshape(count * batch, width)
    shift_rows = shift_linear.shape[0]
    cond_cut = lax.dynamic_slice_in_dim(cond_all, me * shift_rows, shift_rows, 1)
    shift_parts = dot_plain(cond_cut, shift_linear).reshape(count, batch * width)
    shift_parts = trade(lanes_of(shift_parts, 8), count, False, 2)
    shift = jnp.sum(shift_parts.reshape(count, -1), axis=0)[: batch * width].reshape(batch, width)

    def columns_mine(weight):
        half = weight.shape[1] // 2
        return links.pick(weight[:, :half], weight[:, half:])

    skip_half = skip_linear.shape[0] // 2
    shards = [
        links.pick(skip_linear[:skip_half], skip_linear[skip_half:]),
        columns_mine(self_qkv),
        links.pick(self_out, cross_out),
        columns_mine(cross_query),
        columns_mine(cross_keyval),
    ]
    shards = [links.extra_gather(shard) for shard in shards]
    shards = lax.optimization_barrier((shift, *shards))
    shift = shards[0]
    gathered = gather(shards[1:], links.quad, 3)
    w_skip, w_qkv, w_pair, w_query, w_keyval = (
        g.reshape(2, 16 * g.shape[2], g.shape[3]) for g in gathered
    )
    w_self_out, w_cross_out = w_pair[0], w_pair[1]
    get_up = Gather(links, [mlp_up])
    get_down = Gather(links, [mlp_down])
    w_skip = tie(w_skip, get_up, get_down)

    order = links.order_matrix(width)
    order_skip = links.order_skip(width)
    order_text = links.order_matrix(text_width)

    def product(value, weight):
        return jnp.concatenate([dot_plain(value, weight[0]), dot_plain(value, weight[1])], axis=1)

    def product_back(grad, weight):
        half = grad.shape[1] // 2
        return dot_right_t(grad[:, :half], weight[0]) + dot_right_t(grad[:, half:], weight[1])

    def sum_twins(own, other):
        there = links.sibling(dot_left_t(*other).astype(bf16))
        return own, there

    def finish_twins(own, there):
        value = (dot_left_t(*own) + there.astype(f32)).astype(bf16)
        return value.reshape(16, value.shape[0] // 16, value.shape[1])

    def column_grad(value, grad):
        own, other = links.halves(grad)
        return sum_twins((value, own), (value, other))

    def weight_grad(value, grad_halves):
        return (
            dot_left_t(value, grad_halves[0]).astype(bf16),
            dot_left_t(value, grad_halves[1]).astype(bf16),
        )

    def relative_product(value, weight):
        return links.columns(dot_plain(value, weight[0]), dot_plain(value, weight[1]))

    def relative_back(grad_halves, weight):
        return dot_right_t(grad_halves[0], weight[0]) + dot_right_t(grad_halves[1], weight[1])

    def reorder(value):
        return dot_plain(value, order).astype(bf16)

    def restore(value):
        return dot_right_t(value.astype(bf16), order).astype(bf16)

    joined = jnp.concatenate(
        [latent.reshape(rows, width), skip_input.reshape(rows, width)], axis=1
    ).astype(f32)
    normed = gained_norm(joined, skip_gain_all).astype(bf16)
    upper_half = (me >= count // 2).astype(jnp.int32)
    near = jnp.where(upper_half == 0, normed[:, :width], normed[:, width:])
    away = jnp.where(upper_half == 0, normed[:, width:], normed[:, :width])
    near = dot_plain(near, order_skip).astype(bf16).reshape(rows, 2, 4, 1, -1)
    away = dot_plain(away, order_skip).astype(bf16).reshape(rows, 2, 4, 1, -1)
    normed = jnp.concatenate([near, away], axis=3).reshape(rows, 2, width)
    normed = (normed[:, 0], normed[:, 1])
    hidden = dot_plain(normed[0], w_skip[0]) + dot_plain(normed[1], w_skip[1])

    def shifted(values, gain, moved):
        wide = jnp.broadcast_to(moved[:, None, :], (batch, tokens, width)).reshape(rows, width)
        return layer_norm(values) * gain + wide

    attn_in = reorder(shifted(hidden, gains[0], shift).astype(bf16))
    qkv_proj = product(attn_in, w_qkv)
    query_block, key_block, value_block = ((qkv_proj, (at, width)) for at in range(3))

    def shaped(height, breadth, dtype):
        return jax.ShapeDtypeStruct((height, breadth), dtype)

    (keyval_here,) = plain_call(
        functools.partial(keys_body, batch, True),
        [shaped(rows, 2 * width, bf16)],
        [key_block, value_block, head_at, *tables],
    )
    keyval_there = links.sibling(keyval_here)
    qkv_proj = tie(qkv_proj, get_up)
    keyvals = [(keyval_here, None), (keyval_there, None)]
    attention_scratch = [pltpu.VMEM((rows, width), bf16), pltpu.VMEM((rows, width), f32)]
    attn_cat, self_peak = plain_call(
        functools.partial(attention_body, batch, False, True, 2, scaling),
        [shaped(rows, width, bf16), shaped(HEADS, 128, f32)],
        [query_block, head_at, *tables, *keyvals],
        attention_scratch,
    )
    attn_cat = reorder(attn_cat)
    attn_cat = tie(attn_cat, get_down)
    after_self = hidden + dot_plain(attn_cat, w_self_out)
    cross_in = reorder(gained_norm(after_self, gains[1]).astype(bf16))
    cq_proj = product(cross_in, w_query)

    text = text_encoder_states.reshape(batch * text_rows, text_width)
    text_ordered = dot_plain(text, order_text).astype(bf16)
    ckv_proj = product(text_ordered, w_keyval)
    (cross_keyval_all,) = plain_call(
        functools.partial(keys_body, batch, False),
        [shaped(batch * text_rows, 2 * width, bf16)],
        [(ckv_proj, (0, width)), (ckv_proj, (1, width)), head_at],
    )
    cq_proj = tie(cq_proj, get_up)
    cross_cat, cross_peak = plain_call(
        functools.partial(attention_body, batch, True, False, 1, scaling),
        [shaped(rows, width, bf16), shaped(HEADS, 128, f32)],
        [(cq_proj, None), head_at, (cross_keyval_all, None)],
        attention_scratch,
        text_lengths,
    )
    cross_cat = reorder(cross_cat)
    after_cross = after_self + dot_plain(cross_cat, w_cross_out)
    mlp_in = reorder(gained_norm(after_cross, gains[2]).astype(bf16))
    mlp_in = tie(mlp_in, get_up, get_down)
    (w_up,) = get_up.finish()
    upper = relative_product(mlp_in, w_up)
    activated = links.order_blocks(gelu_tanh(upper).astype(bf16))

    down_in = out_grad.reshape(rows, width)
    result_grad = down_in.astype(f32)
    down_halves = links.halves(down_in)
    put_down = Scatter(links, [weight_grad(activated, down_halves)])
    put_down.advance()
    activated = tie(activated, put_down)
    (w_down,) = get_down.finish()
    block_out = (after_cross + relative_product(activated, w_down)).astype(bf16)
    act_grad = links.restore_blocks(relative_back(down_halves, w_down))
    upper_grad = jax.vjp(gelu_tanh, upper)[1](act_grad)[0].astype(bf16)
    upper_halves = links.halves(upper_grad)
    put_up = Scatter(links, [weight_grad(mlp_in, upper_halves)])
    put_up.advance()
    mlp_in_grad = exact_restore(order, relative_back(upper_halves, w_up))
    cross_part, gain_third = jax.vjp(gained_norm, after_cross, gains[2])[1](mlp_in_grad)
    cross_grad = result_grad + cross_part
    cross_bf = tie(cross_grad.astype(bf16), put_up)
    cmix_grad = restore(dot_right_t(cross_bf, w_cross_out))
    cmix_grad = tie(cmix_grad, put_down)
    back_scratch = [
        pltpu.VMEM((rows, width), f32),
        pltpu.VMEM((rows, width), f32),
        pltpu.VMEM((rows, width), bf16),
        pltpu.VMEM((rows, width), f32),
        pltpu.VMEM((2, rows, 2 * width), f32),
    ]
    back_outs = [
        shaped(rows, width, bf16), shaped(rows, 2 * width, f32), shaped(rows, 2 * width, bf16)
    ]
    cq_grad, ckeyval_mine, ckeyval_theirs = plain_call(
        functools.partial(attention_back_body, batch, True, False, 1, scaling),
        back_outs,
        [(cq_proj, None), (cmix_grad, None), head_at, (cross_keyval_all, None)],
        back_scratch,
        text_lengths,
    )
    put_query = column_grad(cross_in, cq_grad)
    cq_grad = tie(cq_grad, put_up, put_down)
    cross_in_grad = exact_restore(order, product_back(cq_grad, w_query))
    self_part, gain_second = jax.vjp(gained_norm, after_self, gains[1])[1](cross_in_grad)
    self_grad = cross_grad + self_part

    text_half = text_rows // 2
    ckey_mine = lax.dynamic_slice_in_dim(
        ckv_proj.reshape(batch, text_rows, 2 * width)[:, :, :width], core * text_half, text_half, 1
    ).reshape(batch * text_half, width)
    (keyval_grad,) = plain_call(
        functools.partial(keys_back_body, batch, False),
        [shaped(batch * text_half, 2 * width, bf16)],
        [
            (ckey_mine, None),
            (ckeyval_mine, None),
            (links.sibling(ckeyval_theirs), None),
            head_at,
        ],
    )
    text_mine = lax.dynamic_slice_in_dim(
        text_ordered.reshape(batch, text_rows, text_width), core * text_half, text_half, 1
    ).reshape(-1, text_width)
    put_keyval = column_grad(text_mine, keyval_grad)
    grad_text = exact_restore(order_text, product_back(keyval_grad, w_keyval))
    grad_text = grad_text.reshape(batch, text_half, text_width)

    self_bf = self_grad.astype(bf16)
    put_pair = sum_twins(
        (links.pick(attn_cat, cross_cat), links.pick(self_bf, cross_bf)),
        (links.pick(cross_cat, attn_cat), links.pick(cross_bf, self_bf)),
    )
    self_bf = tie(self_bf, put_down)
    mix_grad = restore(dot_right_t(self_bf, w_self_out))
    mix_grad = tie(mix_grad, put_up)
    query_grad, here, there = plain_call(
        functools.partial(attention_back_body, batch, False, True, 2, scaling),
        back_outs,
        [query_block, (mix_grad, None), head_at, *tables, *keyvals],
        back_scratch,
    )
    here = tie(here, put_up)
    (key_value_grad,) = plain_call(
        functools.partial(keys_back_body, batch, True),
        [shaped(rows, 2 * width, bf16)],
        [key_block, (here, None), (links.sibling(there), None), head_at, *tables],
    )
    qkv_grad = jnp.concatenate([query_grad, key_value_grad], axis=1)
    put_qkv = column_grad(attn_in, qkv_grad)
    attn_in_grad = exact_restore(order, product_back(qkv_grad, w_qkv))
    hidden_part, gain_first, shift_grad = jax.vjp(shifted, hidden, gains[0], shift)[1](
        attn_in_grad
    )
    hidden_grad = self_grad + hidden_part
    hidden_bf = hidden_grad.astype(bf16)
    put_skip = sum_twins(
        (links.pick(*normed), hidden_bf), (links.pick(normed[1], normed[0]), hidden_bf)
    )
    normed_grad = jnp.concatenate(
        [dot_right_t(hidden_bf, w_skip[0]), dot_right_t(hidden_bf, w_skip[1])], axis=1
    ).reshape(rows, 2, 4, 2, -1)
    near_grad = exact_restore(order_skip, normed_grad[:, :, :, 0].reshape(rows, width))
    away_grad = exact_restore(order_skip, normed_grad[:, :, :, 1].reshape(rows, width))
    normed_grad = jnp.concatenate(
        [
            jnp.where(upper_half == 0, near_grad, away_grad),
            jnp.where(upper_half == 0, away_grad, near_grad),
        ],
        axis=1,
    )
    joined_grad, skip_gain_grad = jax.vjp(gained_norm, joined, skip_gain_all)[1](normed_grad)

    sums = [
        finish_twins(*put) for put in (put_pair, put_query, put_keyval, put_qkv, put_skip)
    ]
    (grad_down,) = put_down.finish()
    (grad_up,) = put_up.finish()
    scattered = [links.extra_scatter(part) for part in scatter(sums, links.quad, 4)]
    grad_self_out, grad_cross_out = scattered[0][0], scattered[0][1]
    grad_cross_query, grad_keyval, grad_qkv = (
        jnp.concatenate([part[0], part[1]], axis=1) for part in scattered[1:4]
    )
    grad_skip_linear = scattered[4].reshape(skip_linear.shape)

    gains_grad = jnp.stack([gain_first, gain_second, gain_third])
    gains_grad = gains_grad.reshape(3, count, third).transpose(1, 0, 2).reshape(count, 3 * third)
    gains_grad = jnp.concatenate([skip_gain_grad.reshape(count, gain_rows), gains_grad], axis=1)
    peaks = jnp.stack([self_peak[:, 0], cross_peak[:, 0]])
    cores = jnp.concatenate([shift_grad.reshape(-1), gains_grad.reshape(-1), peaks.reshape(-1)])
    there = links.sibling(cores)
    peaks = jnp.maximum(cores, there)[-2 * HEADS :]
    cores = cores + there
    ends = (batch * width, batch * width + count * cond_start)
    gains_grad = cores[ends[0] : ends[1]].reshape(count, cond_start)
    shift_bf = cores[: ends[0]].astype(bf16).astype(f32)
    shared = trade(lanes_of(jnp.concatenate([shift_bf, peaks]), 8), count, True, 5)
    shared = shared.reshape(count, -1)
    shift_all = shared[:, : ends[0]].reshape(count * batch, width).astype(bf16)
    peaks = jnp.max(shared[:, ends[0] : ends[0] + 2 * HEADS], axis=0).reshape(2, HEADS)
    grad_shift = dot_left_t(cond_cut, shift_all)
    cond_back = dot_right_t(shift_all, shift_linear).reshape(count, batch * shift_rows)
    owned = trade(lanes_of(jnp.concatenate([cond_back, gains_grad], axis=1), 8), count, False, 6)
    owned = owned.reshape(count, -1)
    cond_mine = owned[:, : batch * shift_rows].reshape(count, batch, shift_rows)
    cond_mine = cond_mine.transpose(1, 0, 2).reshape(batch, width)
    grad_cond = jax.vjp(jax.nn.silu, condition.astype(f32))[1](cond_mine)[0]
    own_gains = jnp.sum(owned[:, batch * shift_rows : batch * shift_rows + cond_start], axis=0)
    grad_skip_gain = own_gains[:gain_rows]
    grad_gains = own_gains[gain_rows:].reshape(3, third)

    roots = jnp.sqrt(thresholds / jnp.maximum(peaks, thresholds))
    self_cols = jnp.repeat(roots[0], HD)
    cross_cols = jnp.repeat(roots[1], HD)
    unit_cols = jnp.ones((width,), f32)
    clipped_qkv = (
        self_qkv.astype(f32) * jnp.concatenate([self_cols, self_cols, unit_cols])[None, :]
    ).astype(bf16)
    clipped_query = (cross_query.astype(f32) * cross_cols[None, :]).astype(bf16)
    clipped_keyval = (
        cross_keyval.astype(f32) * jnp.concatenate([cross_cols, unit_cols])[None, :]
    ).astype(bf16)
    return (
        block_out.reshape(batch, tokens, width),
        joined_grad[:, :width].reshape(batch, tokens, width),
        joined_grad[:, width:].reshape(batch, tokens, width),
        grad_cond,
        grad_text,
        grad_skip_gain,
        grad_gains,
        grad_skip_linear,
        grad_shift,
        grad_qkv,
        grad_self_out,
        grad_cross_query,
        grad_keyval,
        grad_cross_out,
        grad_up,
        grad_down,
        clipped_qkv,
        clipped_query,
        clipped_keyval,
        peaks,
    )


def local_sixteen(
    latent,
    skip_input,
    condition,
    text_encoder_states,
    text_lengths,
    out_grad,
    skip_gain,
    norm_gains,
    skip_linear,
    shift_linear,
    self_qkv,
    self_out,
    cross_query,
    cross_keyval,
    cross_out,
    mlp_up,
    mlp_down,
    thresholds,
):
    batch, tokens, width = latent.shape
    rows = batch * tokens
    text_rows = text_encoder_states.shape[1]
    text_width = text_encoder_states.shape[2]
    scaling = HD ** (-0.5)
    links = Links(lax.axis_size("fsdp"))
    me, core = links.me, links.core
    count = links.count

    positions = core * tokens + jnp.arange(tokens)
    feature = jnp.arange(HD)
    freqs = 10000.0 ** (-(feature % (HD // 4)).astype(f32) / (HD // 4))
    place = jnp.where(
        feature[None, :] < HD // 2, (positions // GRID_W)[:, None], (positions % GRID_W)[:, None]
    )
    angles = place.astype(f32) * freqs[None, :]
    former = (feature % (HD // 2) < HD // 4)[None, :]
    cosine = jnp.tile(jnp.cos(angles), (1, HEADS))
    sine = jnp.tile(jnp.where(former, -jnp.sin(angles), jnp.sin(angles)), (1, HEADS))
    former = jnp.tile(former, (1, HEADS))
    tables = [(cosine, None), (sine, None), (former.astype(f32), None)]
    head_at = jnp.arange(width)[:, None] // HD == jnp.arange(128)[None, :]
    head_at = (head_at.astype(bf16), None)

    gain_rows = skip_gain.shape[0]
    third = norm_gains.shape[1]
    cond_act = jax.nn.silu(condition.astype(f32)).astype(bf16)
    small = jnp.concatenate([skip_gain, norm_gains.reshape(-1), cond_act.reshape(-1)])
    small = trade(lanes_of(small, 16), count, True, 1).reshape(count, -1)
    skip_gain_all = small[:, :gain_rows].reshape(-1).astype(f32)
    cond_start = gain_rows + 3 * third
    gains = small[:, gain_rows:cond_start].reshape(count, 3, third)
    gains = gains.transpose(1, 0, 2).reshape(3, width).astype(f32)
    cond_all = small[:, cond_start : cond_start + batch * width].reshape(count * batch, width)
    shift_rows = shift_linear.shape[0]
    cond_cut = lax.dynamic_slice_in_dim(cond_all, me * shift_rows, shift_rows, 1)
    shift_parts = dot_plain(cond_cut, shift_linear).reshape(count, batch * width)
    shift_parts = trade(lanes_of(shift_parts, 8), count, False, 2)
    shift = jnp.sum(shift_parts.reshape(count, -1), axis=0)[: batch * width].reshape(batch, width)

    def halves_of(weight):
        cut = (weight.shape[1] // 2 + 127) // 128 * 128
        first, second = weight[:, :cut], weight[:, cut:]
        return first, jnp.pad(second, ((0, 0), (0, cut - second.shape[1])))

    def qkv_halves(value):
        edge = 2 * width + 768
        first = jnp.concatenate([value[:, :width], value[:, 2 * width : edge]], axis=1)
        rest = jnp.pad(value[:, edge:], ((0, 0), (0, 2 * 768 - width)))
        return first, jnp.concatenate([value[:, width : 2 * width], rest], axis=1)

    def qkv_whole(first, second):
        last = second[:, width : 2 * width - 768]
        return jnp.concatenate(
            [first[:, :width], second[:, :width], first[:, width:], last], axis=1
        )

    skip_half = skip_linear.shape[0] // 2
    shards = [
        links.pick(skip_linear[:skip_half], skip_linear[skip_half:]),
        links.pick(*qkv_halves(self_qkv)),
        links.pick(self_out, cross_out),
        links.pick(*halves_of(cross_query)),
        links.pick(*halves_of(cross_keyval)),
        links.pick(*halves_of(mlp_up)),
        links.pick(*halves_of(mlp_down)),
    ]
    block = width // 16

    def one_hot(starts, size, height):
        wanted = (starts[:, None] + jnp.arange(size, dtype=jnp.int32)).reshape(1, -1)
        rows_at = lax.broadcasted_iota(jnp.int32, (height, wanted.shape[1]), 0)
        return (rows_at == wanted).astype(bf16)

    slots = jnp.arange(16, dtype=jnp.int32)
    order = one_hot(jnp.bitwise_xor(me, slots) * block, block, width)
    text_block = text_width // 16
    order_text = one_hot(jnp.bitwise_xor(me, slots) * text_block, text_block, text_width)
    lower = jnp.bitwise_xor(jnp.bitwise_and(me, 7), slots[:8]) * (2 * block)
    order_skip = jnp.stack([one_hot(lower + at * block, block, width) for at in range(2)])
    text = text_encoder_states.reshape(batch * text_rows, text_width)
    text_ordered = dot_plain(text, order_text).astype(bf16)
    valid = (jnp.arange(text_rows)[None, :] < text_lengths[:, None]).astype(f32)
    head_at = (jnp.arange(width)[:, None] // HD == jnp.arange(128)[None, :]).astype(bf16)
    table_arrays = [table for table, _ in tables]

    def shaped(*shape, dtype=f32):
        return jax.ShapeDtypeStruct(shape, dtype)

    down_in = out_grad.reshape(rows, width)
    cut = shards[6].shape[1]
    out_halves = jnp.stack(
        [down_in[:, :cut], jnp.pad(down_in[:, cut:], ((0, 0), (0, 2 * cut - width)))]
    )
    up_shape, down_shape = shards[5].shape, shards[6].shape
    whole_down, whole_up = [shaped(4, 4, *shape, dtype=bf16) for shape in (down_shape, up_shape)]
    tile = 384

    flat, flat_low = shaped(rows, width), shaped(rows, width, dtype=bf16)
    double_low = shaped(rows, 2 * width, dtype=bf16)
    inner = mlp_down.shape[0] * 16
    given = [
        latent.reshape(rows, width),
        skip_input.reshape(rows, width),
        skip_gain_all[None, :],
        gains,
        shift,
        out_halves,
        valid,
    ]
    loaded = [order, order_skip, head_at, *table_arrays, text_ordered]

    def like(array):
        return pltpu.VMEM(array.shape, array.dtype)
    saved = [
        shaped(2, 2, rows, width // 2, dtype=bf16),
        flat,
        flat_low,
        shaped(rows, 2 * width),
        double_low,
        double_low,
        flat_low,
        flat,
        flat_low,
        flat,
        flat,
        shaped(batch * text_rows, 2 * width, dtype=bf16),
        flat_low,
        flat,
        flat_low,
        shaped(rows, inner),
        shaped(rows, inner, dtype=bf16),
        shaped(HEADS, 128),
        shaped(HEADS, 128),
    ]
    (
        *gathered,
        normed,
        hidden,
        attn_in,
        qkv_proj,
        keyval_here,
        keyval_there,
        attn_cat,
        after_self,
        cross_in,
        cq_proj,
        ckey_mine,
        cross_keyval_all,
        cross_cat,
        after_cross,
        mlp_in,
        upper,
        activated,
        self_peak,
        cross_peak,
        sums_down,
        _,
    ) = pl.pallas_call(
        functools.partial(forward_body, batch, scaling),
        out_shape=[
            *[shaped(2, 4, 4, *shard.shape, dtype=bf16) for shard in shards],
            *saved,
            whole_down,
            whole_down,
        ],
        in_specs=[IN_VMEM] * len(given) + [ANYWHERE] * 14,
        out_specs=[ANYWHERE] * (9 + len(saved)),
        scratch_shapes=[
            *[like(array) for array in saved],
            *[like(array) for array in loaded],
            pltpu.VMEM((rows, width), f32),
            pltpu.VMEM((rows, width), bf16),
            pltpu.VMEM((3, 4, 4, block, 512), bf16),
            pltpu.VMEM((2, *down_shape), bf16),
            pltpu.VMEM((2, *down_shape), bf16),
            pltpu.SemaphoreType.DMA((3,)),
            pltpu.SemaphoreType.DMA((8, 10)),
            pltpu.SemaphoreType.DMA((8, 10)),
            pltpu.SemaphoreType.DMA((8,)),
            pltpu.SemaphoreType.DMA,
            pltpu.SemaphoreType.DMA,
            pltpu.SemaphoreType.DMA((1, 16)),
            pltpu.SemaphoreType.DMA((1, 16)),
            pltpu.SemaphoreType.DMA((4,)),
            pltpu.SemaphoreType.DMA((7,)),
            pltpu.SemaphoreType.DMA((19,)),
        ],
        compiler_params=pltpu.CompilerParams(
            collective_id=7, has_side_effects=True, vmem_limit_bytes=62 * 2**20
        ),
    )(*given, *loaded, *shards)
    block_out, cross_grad, gain_third, sums_up, _, half_down = pl.pallas_call(
        functools.partial(mlp_back_body, batch),
        out_shape=[
            flat_low, flat, shaped(8, width), whole_up, whole_up,
            shaped(2, 4, *down_shape, dtype=bf16),
        ],
        in_specs=[IN_VMEM] * 7 + [ANYWHERE] * 3,
        out_specs=[IN_VMEM] * 3 + [ANYWHERE] * 3,
        scratch_shapes=[
            pltpu.VMEM((2, rows, inner // 2), bf16),
            pltpu.VMEM((width, rows), bf16),
            pltpu.VMEM((2, rows, cut), f32),
            pltpu.VMEM((3, 2, *down_shape), bf16),
            pltpu.VMEM((3, 4, 4, block, 512), bf16),
            pltpu.VMEM((2, 4, 4, block, tile), bf16),
            pltpu.VMEM((2, 4, 4, block, tile), bf16),
            pltpu.SemaphoreType.DMA((3,)),
            pltpu.SemaphoreType.DMA((1, 16)),
            pltpu.SemaphoreType.DMA((1, 16)),
            pltpu.SemaphoreType.DMA((4,)),
            pltpu.SemaphoreType.DMA((1, 8)),
            pltpu.SemaphoreType.DMA((1, 8)),
        ],
        compiler_params=pltpu.CompilerParams(
            collective_id=8, has_side_effects=True, vmem_limit_bytes=60 * 2**20
        ),
    )(
        out_halves, activated, upper, mlp_in, after_cross, order, gains,
        gathered[5], gathered[6], sums_down,
    )

    text_half = text_rows // 2
    text_mine = lax.dynamic_slice_in_dim(
        text_ordered.reshape(batch, text_rows, text_width), core * text_half, text_half, 1
    ).reshape(-1, text_width)
    parts = [shards[at].shape for at in (6, 5, 3, 4, 2, 1, 0)]
    moved = [
        *[shaped(2, *shape) for shape in parts],
        *[shaped(4, 4, *shape, dtype=bf16) for shape in parts[2:]],
        *[shaped(4, 4, *shape, dtype=bf16) for shape in parts[2:]],
        *[shaped(2, 4, *shape, dtype=bf16) for shape in parts[1:]],
        *[shaped(4, *shape, dtype=bf16) for shape in parts],
        *[shaped(4, *shape, dtype=bf16) for shape in parts],
        *[shaped(3, *shape, dtype=bf16) for shape in parts],
        *[shaped(3, *shape, dtype=bf16) for shape in parts],
    ]
    placed = [gains, valid]
    loaded = [
        cross_cat, attn_cat, cross_in, attn_in, text_mine, after_self, hidden, normed,
        order, head_at, *table_arrays,
    ]
    apart = [
        *loaded,
        *gathered[:5],
        cross_keyval_all, cq_proj, ckey_mine, qkv_proj, keyval_here, keyval_there, cross_grad,
        sums_down, sums_up, half_down,
    ]
    small_outs = [shaped(rows, text_width), shaped(8, width), shaped(8, width)]
    text_grad, gain_grads, shift_grad, normed_grad, *rest = pl.pallas_call(
        functools.partial(rest_back_body, batch, scaling),
        out_shape=[*small_outs, shaped(rows, 2 * width), *moved],
        in_specs=[IN_VMEM] * len(placed) + [ANYWHERE] * len(apart),
        out_specs=[IN_VMEM] * 3 + [ANYWHERE] * (1 + len(moved)),
        scratch_shapes=[
            *[pltpu.VMEM((rows, width), f32)] * 4,
            pltpu.VMEM((rows, width), bf16),
            pltpu.VMEM((rows, width), bf16),
            pltpu.VMEM((2, rows, 2 * width), f32),
            pltpu.VMEM((2 * rows, 2 * width), bf16),
            pltpu.VMEM((rows, 2 * width), f32),
            pltpu.VMEM((2, width, rows), bf16),
            pltpu.VMEM((2, rows, shards[1].shape[1]), bf16),
            *[like(array) for array in loaded],
            pltpu.VMEM((3, 4, 4, block, tile), bf16),
            pltpu.VMEM((2, 4, 4, block, tile), bf16),
            pltpu.VMEM((2, 4, 4, block, tile), bf16),
            pltpu.VMEM((2, 9, block, 768), bf16),
            pltpu.VMEM((2, 9, down_shape[0], 128), bf16),
            pltpu.VMEM((2, block, 768), f32),
            pltpu.VMEM((2, down_shape[0], 128), f32),
            pltpu.VMEM((2, rows, 2 * width), bf16),
            pltpu.SemaphoreType.DMA((3,)),
            pltpu.SemaphoreType.DMA((17,)),
            pltpu.SemaphoreType.DMA((5, 8)),
            pltpu.SemaphoreType.DMA((5, 8)),
            pltpu.SemaphoreType.DMA((4,)),
            pltpu.SemaphoreType.DMA((2,)),
            pltpu.SemaphoreType.DMA((2,)),
            pltpu.SemaphoreType.DMA((7, 12)),
            pltpu.SemaphoreType.DMA((7, 12)),
            pltpu.SemaphoreType.DMA((2, 9)),
            pltpu.SemaphoreType.DMA((2, 4)),
        ],
        compiler_params=pltpu.CompilerParams(
            collective_id=9, has_side_effects=True, vmem_limit_bytes=62 * 2**20
        ),
    )(*placed, *apart)
    grads = rest[:7]
    joined_grad, skip_gain_grad = pl.pallas_call(
        functools.partial(joined_back_body, batch),
        out_shape=[shaped(2, rows, width), shaped(8, 2 * width)],
        in_specs=[IN_VMEM] * 5,
        out_specs=[IN_VMEM] * 2,
        compiler_params=pltpu.CompilerParams(vmem_limit_bytes=60 * 2**20),
    )(normed_grad, latent.reshape(rows, width), skip_input.reshape(rows, width), skip_gain_all[None, :], order_skip)
    skip_gain_grad = skip_gain_grad[0]
    gain_first, gain_second, gain_third = gain_grads[0], gain_grads[1], gain_third[0]
    shift_grad = shift_grad[:batch]
    grad_text = restore_order(order_text, text_grad).reshape(batch, text_half, text_width)

    def wide_of(part):
        return jnp.concatenate([part[0], part[1]], axis=1)

    grad_down = wide_of(grads[0])[:, :width]
    grad_up = wide_of(grads[1])
    grad_cross_query = wide_of(grads[2])[:, :width]
    grad_keyval = wide_of(grads[3])
    grad_self_out, grad_cross_out = grads[4][0], grads[4][1]
    grad_qkv = qkv_whole(grads[5][0], grads[5][1])
    grad_skip_linear = grads[6].reshape(skip_linear.shape)

    gains_grad = jnp.stack([gain_first, gain_second, gain_third])
    gains_grad = gains_grad.reshape(3, count, third).transpose(1, 0, 2).reshape(count, 3 * third)
    gains_grad = jnp.concatenate([skip_gain_grad.reshape(count, gain_rows), gains_grad], axis=1)
    peaks = jnp.stack([self_peak[:, 0], cross_peak[:, 0]])
    cores = jnp.concatenate([shift_grad.reshape(-1), gains_grad.reshape(-1), peaks.reshape(-1)])
    there = links.sibling(cores)
    peaks = jnp.maximum(cores, there)[-2 * HEADS :]
    cores = cores + there
    ends = (batch * width, batch * width + count * cond_start)
    gains_grad = cores[ends[0] : ends[1]].reshape(count, cond_start)
    shift_bf = cores[: ends[0]].astype(bf16).astype(f32)
    shared = trade(lanes_of(jnp.concatenate([shift_bf, peaks]), 8), count, True, 5)
    shared = shared.reshape(count, -1)
    shift_all = shared[:, : ends[0]].reshape(count * batch, width).astype(bf16)
    peaks = jnp.max(shared[:, ends[0] : ends[0] + 2 * HEADS], axis=0).reshape(2, HEADS)
    grad_shift = dot_left_t(cond_cut, shift_all)
    cond_back = dot_right_t(shift_all, shift_linear).reshape(count, batch * shift_rows)
    owned = trade(lanes_of(jnp.concatenate([cond_back, gains_grad], axis=1), 8), count, False, 6)
    owned = owned.reshape(count, -1)
    cond_mine = owned[:, : batch * shift_rows].reshape(count, batch, shift_rows)
    cond_mine = cond_mine.transpose(1, 0, 2).reshape(batch, width)
    grad_cond = jax.vjp(jax.nn.silu, condition.astype(f32))[1](cond_mine)[0]
    own_gains = jnp.sum(owned[:, batch * shift_rows : batch * shift_rows + cond_start], axis=0)
    grad_skip_gain = own_gains[:gain_rows]
    grad_gains = own_gains[gain_rows:].reshape(3, third)

    roots = jnp.sqrt(thresholds / jnp.maximum(peaks, thresholds))
    self_cols = jnp.repeat(roots[0], HD)
    cross_cols = jnp.repeat(roots[1], HD)
    unit_cols = jnp.ones((width,), f32)
    clipped_qkv = (
        self_qkv.astype(f32) * jnp.concatenate([self_cols, self_cols, unit_cols])[None, :]
    ).astype(bf16)
    clipped_query = (cross_query.astype(f32) * cross_cols[None, :]).astype(bf16)
    clipped_keyval = (
        cross_keyval.astype(f32) * jnp.concatenate([cross_cols, unit_cols])[None, :]
    ).astype(bf16)
    return (
        block_out.reshape(batch, tokens, width),
        joined_grad[0].reshape(batch, tokens, width),
        joined_grad[1].reshape(batch, tokens, width),
        grad_cond,
        grad_text,
        grad_skip_gain,
        grad_gains,
        grad_skip_linear,
        grad_shift,
        grad_qkv,
        grad_self_out,
        grad_cross_query,
        grad_keyval,
        grad_cross_out,
        grad_up,
        grad_down,
        clipped_qkv,
        clipped_query,
        clipped_keyval,
        peaks,
    )


def solution(mesh):
    rows = P("fsdp", None)
    tokens = P("fsdp", "seq", None)
    in_specs = (
        tokens,
        tokens,
        rows,
        P("fsdp", None, None),
        P("fsdp"),
        tokens,
        P("fsdp"),
        P(None, "fsdp"),
        *([rows] * 9),
        P(),
    )
    out_specs = (
        *([tokens] * 3),
        rows,
        tokens,
        P("fsdp"),
        P(None, "fsdp"),
        *([rows] * 12),
        P(),
    )
    step = local_sixteen if mesh.shape["fsdp"] == 16 else local
    return jax.shard_map(step, mesh=mesh, in_specs=in_specs, out_specs=out_specs, check_vma=False)
```
